32 devices in a mesh: dp: 8 (over z, x), tensor: 4 (over y, core).
Axes of the slice: x: 2, y: 2, z: 4, core: 2. Of those that a mesh axis runs over, the one named last changes fastest.
Arguments:
- tokens: bfloat16 [8192, 768], P(('dp', 'tensor')), may hold values from -6 to 6
- cotangent: bfloat16 [8192, 768], P(('dp', 'tensor')), may hold values from -6 to 6
- lengths: int32 [8, 4], P('dp'), may hold values from 0 to 1024, as said below
- timesteps: int32 [8, 4], P('dp'), may hold values from 0 to 999
- w_self: bfloat16 [1536, 768], replicated, may hold values from -0.15625 to 0.15625
- ln_gain: float32 [2, 768], replicated, may hold values from 0.5 to 1.5
- ln_bias: float32 [2, 768], replicated, may hold values from -1.8 to 1.8
- w_qkv: bfloat16 [2, 3, 768, 768], P(None, None, None, 'tensor'), may hold values from -0.21875 to 0.21875
- w_out: bfloat16 [2, 768, 768], P(None, 'tensor'), may hold values from -0.875 to 0.875
- w_ada: float32 [2, 768, 1536], replicated, may hold values from -0.21875 to 0.21875
- b_ada: float32 [2, 1536], replicated, may hold values from -1.8 to 1.8
- w_up: bfloat16 [2, 768, 3072], P(None, None, 'tensor'), may hold values from -0.21875 to 0.21875
- w_down: bfloat16 [2, 3072, 768], P(None, 'tensor'), may hold values from -0.109375 to 0.109375
- b_down: float32 [2, 768], replicated, may hold values from -1.8 to 1.8
Outputs:
- activations: bfloat16 [8192, 768], P(('dp', 'tensor'))
- grad_tokens: float32 [8192, 768], P(('dp', 'tensor'))
- grad_ln_gain: float32 [2, 768], replicated
- grad_ln_bias: float32 [2, 768], replicated
- grad_qkv: float32 [2, 3, 768, 768], P(None, None, 'dp', 'tensor')
- grad_out: float32 [2, 768, 768], P(None, 'tensor', 'dp')
- grad_ada: float32 [2, 768, 1536], replicated
- grad_ada_bias: float32 [2, 1536], replicated
- grad_up: float32 [2, 768, 3072], P(None, 'dp', 'tensor')
- grad_down: float32 [2, 3072, 768], P(None, 'tensor', 'dp')
- grad_down_bias: float32 [2, 768], replicated
- grad_self: float32 [1536, 768], replicated
The draws below stay inside these ranges and needn't reach their ends.
Inputs may be any that keep to these rules, and one draw needn't show every extreme that they name: `lengths`: each row is either one sequence of 1024 tokens followed by zeros, or 4 sequences of 256 tokens; at least one row is of the first kind.
All inputs are finite; a program needn't handle non-finite values.
Results may differ from the reference program's by a relative error of at most 0.018.
Values may be sent and summed in bfloat16 or wider, within the bound.
A program may use at most 192 MiB of HBM per device.

```python
import jax
import jax.numpy as jnp
from jax import lax

D = 768
H = 12
HD = 64
FF = 3072
LAYERS = 2
SLOTS = 4
GROUP = 1024
SHORT = 256
TOKENS = 8192
N_DP = 8


def draw_lengths(key, part):
    key = jax.random.fold_in(key, 11)
    key_kind, key_force = jax.random.split(key)
    group_kinds = jax.random.randint(key_kind, (N_DP,), 0, 3)
    forced = jax.random.randint(key_force, (), 0, N_DP)
    single = (group_kinds < 2) | (jnp.arange(N_DP) == forced)
    places = jnp.arange(SLOTS)
    single_row = jnp.where(places == 0, GROUP, 0)
    packed_row = jnp.full((SLOTS,), SHORT)
    return jnp.where(single[:, None], single_row[None, :], packed_row[None, :]).astype(jnp.int32)


def place_ends(values, own_key, low, top_value):
    longest = values.shape.index(max(values.shape))
    spots = []
    for shift in (0, 1):
        where = [jax.random.randint(jax.random.fold_in(own_key, axis), (), 0, length) for axis, length in enumerate(values.shape)]
        where[longest] = (where[longest] + shift) % values.shape[longest]
        spots.append(tuple(where))
    return values.at[spots[0]].set(low).at[spots[1]].set(top_value)


def block_scale(stream_key, extent, shards, least, top_value):
    def one(dim, shards_of):
        steps = jax.random.uniform(jax.random.fold_in(jax.random.fold_in(stream_key, 6), dim), (shards_of,), jnp.float32, least / len(shards), top_value / len(shards))
        return jnp.repeat(jnp.exp(steps), extent[dim] // shards_of).reshape((-1,) + (1,) * (len(extent) - dim - 1))

    factor_of = one(*shards[0])
    for cut in shards[1:]:
        factor_of = factor_of * one(*cut)
    return factor_of


def normal_values(own_key, dims, scale, limit, cuts=(), kind=jnp.bfloat16):
    factor_of = block_scale(own_key, dims, cuts, -0.22, 0.18) if cuts else 1.0
    values = jax.random.normal(own_key, dims, jnp.float32) * scale * factor_of
    return jnp.minimum(jnp.maximum(values, -limit), limit).astype(kind)


def setup_inputs(seed: int = 0) -> dict:
    seeds = jax.random.split(jax.random.key(seed), 15)
    tokens = normal_values(seeds[0], (TOKENS, D), 1.0, 6.0, ((0, 32),))
    cotangent = normal_values(seeds[1], (TOKENS, D), 1.0, 6.0, ((0, 32),))
    lengths = draw_lengths(jax.random.fold_in(seeds[14], 71), 0)
    timesteps = place_ends(jax.random.randint(seeds[3], (N_DP, SLOTS), 0, 1000), jax.random.fold_in(seeds[3], 1), 0, 999).astype(jnp.int32)
    w_self = normal_values(seeds[4], (2 * D, D), (2 * D) ** -0.5, 0.15625)
    ln_gain = jnp.clip(1.0 + 0.1 * jax.random.normal(seeds[5], (LAYERS, D), jnp.float32), 0.5, 1.5)
    ln_bias = normal_values(seeds[6], (LAYERS, D), 0.3, 1.8, (), jnp.float32)
    w_qkv = normal_values(seeds[7], (LAYERS, 3, D, H * HD), D ** -0.5, 0.21875, ((3, 4),))
    w_out = normal_values(seeds[8], (LAYERS, H * HD, D), (H * HD // 16) ** -0.5, 0.875, ((1, 4),))
    w_ada = normal_values(seeds[9], (LAYERS, D, 2 * D), D ** -0.5, 0.21875, (), jnp.float32)
    b_ada = normal_values(seeds[10], (LAYERS, 2 * D), 0.3, 1.8, (), jnp.float32)
    w_up = normal_values(seeds[11], (LAYERS, D, FF), D ** -0.5, 0.21875, ((2, 4),))
    w_down = normal_values(seeds[12], (LAYERS, FF, D), FF ** -0.5, 0.109375, ((1, 4),))
    b_down = normal_values(seeds[13], (LAYERS, D), 0.3, 1.8, (), jnp.float32)
    return dict(tokens=tokens, cotangent=cotangent, lengths=lengths, timesteps=timesteps, w_self=w_self, ln_gain=ln_gain, ln_bias=ln_bias, w_qkv=w_qkv, w_out=w_out, w_ada=w_ada, b_ada=b_ada, w_up=w_up, w_down=w_down, b_down=b_down)


@jax.custom_vjp
def low(v):
    return lax.optimization_barrier(v.astype(jnp.bfloat16)).astype(jnp.float32)

@jax.custom_vjp
def low_back(v):
    return v

def low_keep(v):
    return (low(v), None)

def low_pass(kept, grad):
    return (grad,)

def back_keep(v):
    return (v, None)

def back_low(kept, grad):
    return (low(grad),)
low.defvjp(low_keep, low_pass)
low_back.defvjp(back_keep, back_low)

def layout(lengths, index):
    ends = jnp.cumsum(lengths, axis=-1).astype(jnp.int32)
    starts = ends - lengths
    segment = lax.optimization_barrier(jnp.sum((index[:, None] >= ends[..., None, :]).astype(jnp.int32), axis=-1))
    segment = jnp.minimum(segment, lengths.shape[-1] - 1)
    onehot = (segment[..., None] == jnp.arange(lengths.shape[-1], dtype=jnp.int32)).astype(jnp.int32)
    position = index - lax.optimization_barrier(jnp.sum(onehot * starts[..., None, :], axis=-1))
    return (segment, onehot, position)

def embed_time(steps, width):
    half = width // 2
    freqs = jnp.exp(-jnp.log(10000.0) * jnp.arange(half).astype(jnp.float32) / half)
    angle = steps.astype(jnp.float32)[..., None] * freqs
    return jnp.concatenate([jnp.cos(angle), jnp.sin(angle)], axis=-1)

def rotary_tables(position, head_size):
    half = head_size // 2
    freqs = jnp.exp(-jnp.log(10000.0) * jnp.arange(half).astype(jnp.float32) / half)
    angle = position.astype(jnp.float32)[..., None] * freqs
    return (jnp.cos(angle), jnp.sin(angle))

def rotate(values, cosine, sine):
    half = values.shape[-1] // 2
    first = values[..., :half]
    second = values[..., half:]
    cosine = cosine[..., None, :]
    sine = sine[..., None, :]
    return jnp.concatenate([first * cosine - second * sine, second * cosine + first * sine], axis=-1)

def normalize(rows):
    centred = rows - lax.optimization_barrier(jnp.mean(rows, axis=-1, keepdims=True))
    variance = lax.optimization_barrier(jnp.mean(centred * centred, axis=-1, keepdims=True))
    return centred * lax.rsqrt(variance + 1e-05)

def attend(args):
    queries, key_rows, value_rows, segment = args
    scale = HD ** (-0.5)
    scores = jnp.einsum('qhd,khd->hqk', queries, key_rows, precision=lax.Precision.HIGHEST) * scale
    same = segment[:, None] == segment[None, :]
    scores = low_back(jnp.where(same[None], scores, -1000000000.0))
    shares = jax.nn.softmax(scores, axis=-1)
    return jnp.einsum('hqk,khd->qhd', low(shares), value_rows, precision=lax.Precision.HIGHEST)

def forward(rows, ln_gain, ln_bias, w_qkv, w_out, w_ada, b_ada, w_up, w_down, b_down, segment, onehot, cosine, sine, temb):
    hp = lax.Precision.HIGHEST
    groups, length, width = rows.shape
    for layer in range(LAYERS):
        normed = low(normalize(rows) * ln_gain[layer] + ln_bias[layer])
        mixed = low_back(jnp.einsum('ngd,jde->njge', normed, w_qkv[layer], precision=hp))
        queries = low(rotate(mixed[:, 0].reshape(groups, length, H, HD), cosine, sine))
        key_rows = low(rotate(mixed[:, 1].reshape(groups, length, H, HD), cosine, sine))
        value_rows = low(mixed[:, 2].reshape(groups, length, H, HD))
        attended = lax.map(jax.checkpoint(attend), (queries, key_rows, value_rows, segment))
        attended = low_back(low(attended.reshape(groups, length, H * HD)))
        after = rows + low_back(jnp.einsum('nge,ed->ngd', attended, w_out[layer], precision=hp))
        cond = jnp.einsum('nsd,de->nse', temb, w_ada[layer], precision=hp) + b_ada[layer]
        cond_rows = jnp.einsum('ngs,nse->nge', onehot, cond, precision=hp)
        modulated = low(normalize(after) * (1.0 + cond_rows[..., width:]) + cond_rows[..., :width])
        hidden = low_back(jnp.einsum('ngd,df->ngf', modulated, w_up[layer], precision=hp))
        gated = low(jax.nn.gelu(hidden, approximate=False))
        rows = after + low_back(jnp.einsum('ngf,fd->ngd', gated, w_down[layer], precision=hp)) + b_down[layer]
    return rows

def project(rows, self_weight, extra):
    joined = jnp.concatenate([rows, extra], axis=-1)
    return jnp.einsum('ngc,cd->ngd', joined, self_weight, precision=lax.Precision.HIGHEST)

def reference(tokens, cotangent, lengths, timesteps, w_self, ln_gain, ln_bias, w_qkv, w_out, w_ada, b_ada, w_up, w_down, b_down):
    groups = lengths.shape[0]
    length = tokens.shape[0] // groups
    width = tokens.shape[1]
    index = jnp.arange(length, dtype=jnp.int32)
    segment, onehot, position = layout(lengths, index)
    cosine, sine = rotary_tables(position, HD)
    temb = embed_time(timesteps, width)
    onehot = onehot.astype(jnp.float32)
    rows = tokens.astype(jnp.float32).reshape(groups, length, width)
    self_weight = w_self.astype(jnp.float32)
    params = (ln_gain.astype(jnp.float32), ln_bias.astype(jnp.float32), w_qkv.astype(jnp.float32), w_out.astype(jnp.float32), w_ada.astype(jnp.float32), b_ada.astype(jnp.float32), w_up.astype(jnp.float32), w_down.astype(jnp.float32), b_down.astype(jnp.float32))
    first = forward(project(rows, self_weight, jnp.zeros_like(rows)), *params, segment, onehot, cosine, sine, temb)
    extra = low(first)

    def run(rows, self_weight, *weights):
        start = low_back(project(rows, self_weight, extra))
        return forward(start, *weights, segment, onehot, cosine, sine, temb)
    result, pullback = jax.vjp(run, rows, self_weight, *params)
    grads = pullback(cotangent.astype(jnp.float32).reshape(groups, length, width))
    activations = result.reshape(-1, width).astype(jnp.bfloat16)
    grad_tokens = grads[0].reshape(-1, width)
    return (activations, grad_tokens, grads[2], grads[3], grads[4], grads[5], grads[6], grads[7], grads[8], grads[9], grads[10], grads[1])
```

```python
import functools

import jax
import jax.numpy as jnp
from jax import lax
from jax.experimental import pallas as pl
from jax.experimental.pallas import tpu as pltpu
from jax.sharding import PartitionSpec as P

HD = 64
HALF = HD // 2
BF = jnp.bfloat16
F32 = jnp.float32
MESH = pl.DeviceIdType.MESH
EPS = 1e-05
LIMIT = 60 << 20


def norm(rows):
    centred = rows - jnp.mean(rows, axis=-1, keepdims=True)
    rstd = lax.rsqrt(jnp.mean(centred * centred, axis=-1, keepdims=True) + EPS)
    return (centred * rstd, rstd)


def norm_back(grad, hat, rstd):
    return rstd * (
        grad
        - jnp.mean(grad, axis=-1, keepdims=True)
        - hat * jnp.mean(grad * hat, axis=-1, keepdims=True)
    )


def dot(left, right, dims=((1,), (0,))):
    return lax.dot_general(left, right, (dims, ((), ())), preferred_element_type=F32)


NT = ((1,), (1,))
TN = ((0,), (0,))


def head_mask(head, rotary):
    lane = lax.broadcasted_iota(jnp.int32, (1, 256), 1)
    if rotary:
        return (lane % 128) // HALF == head
    return lane // HD == head


class Group:
    def __init__(self, sems, ids, gathered, pair_out, pair_in, own_out, own_in, far_out, far_in):
        self.sems = sems
        self.ids = ids
        self.gathered = gathered
        self.pair_out, self.pair_in = pair_out, pair_in
        self.own_out, self.own_in = own_out, own_in
        self.far_out, self.far_in = far_out, far_in
        self.half = gathered.shape[0] // 8

    def copy(self, src, dst, kind, part, far):
        send, recv = self.sems
        return pltpu.make_async_remote_copy(
            src_ref=src,
            dst_ref=dst,
            send_sem=send.at[kind, part],
            recv_sem=recv.at[kind, part],
            device_id=self.ids[1] if far else self.ids[0],
            device_id_type=MESH,
        )

    def rows(self, start):
        return pl.ds(pl.multiple_of(start, self.half), self.half)

    def pair(self, part):
        return 6 * self.half - 2 * self.half * part

    def far_copy(self, part):
        own = self.gathered.at[self.rows(part * self.half)]
        return self.copy(own, self.gathered.at[self.rows(self.pair(part))], 0, part, True)

    def sibling_copy(self, part):
        own = self.gathered.at[self.rows(part * self.half)]
        place = self.gathered.at[self.rows((2 + part) * self.half)]
        return self.copy(own, place, 1, part, False)

    def forward_copy(self, part):
        src = self.gathered.at[self.rows(self.pair(part))]
        dst = self.gathered.at[self.rows(self.pair(part) + self.half)]
        return self.copy(src, dst, 2, part, False)

    def send(self, part):
        self.far_copy(part).start()
        self.sibling_copy(part).start()

    def receive(self, step):
        @pl.when(step == 1)
        def _():
            self.sibling_copy(0).wait_recv()
            self.sibling_copy(1).wait_recv()

        @pl.when(step >= 2)
        def _():
            part = step - 2
            self.far_copy(part).wait_recv()
            self.forward_copy(part).start()
            self.forward_copy(part).wait_recv()

    def pair_copy(self, part):
        return self.copy(self.pair_out.at[part], self.pair_in.at[part], 3, part, False)

    def own_copy(self):
        return self.copy(self.own_out, self.own_in, 4, 0, False)

    def sum_copy(self, part):
        return self.copy(self.far_out.at[part], self.far_in.at[part], 5, part, True)

    def scatter(self, unit, total, own):
        @pl.when(unit == 0)
        def _():
            own[...] = total[...]

        @pl.when(unit == 1)
        def _():
            self.own_out[...] = total[...].astype(BF)
            self.own_copy().start()

        @pl.when(unit >= 2)
        def _():
            part = 3 - unit
            self.pair_out[part] = total[self.half :, :].astype(BF)
            self.pair_copy(part).start()
            self.pair_copy(part).wait_recv()
            self.far_out[part] = (
                total[: self.half, :] + self.pair_in[part].astype(F32)
            ).astype(BF)
            self.sum_copy(part).start()

    def collect(self, part, own):
        if part == 0:
            self.own_copy().wait_recv()
        self.sum_copy(part).wait_recv()
        rows = pl.ds(part * self.half, self.half)
        return own[rows, :] + self.own_in[rows, :].astype(F32) + self.far_in[part].astype(F32)

    def finish(self):
        for part in range(2):
            self.far_copy(part).wait_send()
            self.sibling_copy(part).wait_send()
            self.forward_copy(part).wait_send()
            self.pair_copy(part).wait_send()
            self.sum_copy(part).wait_send()
        self.own_copy().wait_send()


def neighbours():
    group = lax.axis_index("dp")
    place = lax.axis_index("tensor")
    core = lax.rem(place, 2)
    return ((group, place + 1 - 2 * core), (group, lax.rem(place + 2, 4)))


def meet(ids):
    barrier = pltpu.get_barrier_semaphore()
    for device in ids:
        pl.semaphore_signal(barrier, inc=1, device_id=device, device_id_type=MESH)
    pl.semaphore_wait(barrier, 2)


def group_scratch(rows, width):
    half = rows // 8
    return [
        pltpu.VMEM((rows, width), BF),
        pltpu.VMEM((2, half, width), BF),
        pltpu.VMEM((2, half, width), BF),
        pltpu.VMEM((2 * half, width), BF),
        pltpu.VMEM((2 * half, width), BF),
        pltpu.VMEM((2, half, width), BF),
        pltpu.VMEM((2, half, width), BF),
    ]


def gelu_parts(hidden):
    cdf = 0.5 * (1.0 + lax.erf(hidden * (0.5**0.5)))
    density = jnp.exp(hidden * hidden * -0.5) * 0.3989422804014327
    return (hidden * cdf, cdf + hidden * density)


def forward_kernel(layer, save, heads, refs):
    (x_ref, gain_ref, bias_ref, cond_ref, bdown_ref, cos_ref, sin_ref, neg_ref) = refs[:8]
    hbm_weights = refs[8:12]
    count = 10 if save else 0
    next_ref = refs[12]
    saves = refs[13 : 13 + count]
    scratch = refs[13 + count :]
    weights = scratch[:4]
    (wqkv, wout, wup, wdown) = weights
    first = scratch[4:11]
    second = scratch[11:18]
    (qb, kb, vb, lse, ob, x1, gb, gpb, total, own) = scratch[18:28]
    (send, recv, send2, recv2, wsem, osem) = scratch[28:]
    ids = neighbours()
    meet(ids)
    loads = [
        pltpu.make_async_copy(src.at[layer], dst, wsem.at[i])
        for i, (src, dst) in enumerate(zip(hbm_weights, weights))
    ]
    for load in loads:
        load.start()
    attn = Group((send, recv), ids, *first)
    feed = Group((send2, recv2), ids, *second)
    abuf, mbuf = first[0], second[0]
    half = attn.half
    unit_rows = 2 * half
    width = x_ref.shape[1]
    for part in range(2):
        rows = pl.ds(part * half, half)
        hat = norm(x_ref[rows, :])[0]
        abuf[rows, :] = (hat * gain_ref[...] + bias_ref[...]).astype(BF)
        attn.send(part)
    loads[0].wait()

    def project(step, carry):
        attn.receive(step)
        unit = jnp.where(step < 2, step, 5 - step)
        rows = pl.ds(pl.multiple_of(unit * unit_rows, unit_rows), unit_rows)
        mixed = dot(abuf[rows, :], wqkv[...])
        cosine = cos_ref[rows, :]
        sine = sin_ref[rows, :]
        for place, dst, scale in ((0, qb, HD**-0.5), (256, kb, 1.0)):
            first_half = mixed[:, place : place + 128]
            second_half = mixed[:, place + 128 : place + 256]
            dst[rows, :128] = ((first_half * cosine - second_half * sine) * scale).astype(BF)
            dst[rows, 128:] = ((second_half * cosine + first_half * sine) * scale).astype(BF)
        vb[rows, :] = mixed[:, 512:].astype(BF)
        return carry

    lax.fori_loop(0, 4, project, 0)
    loads[1].wait()
    lane = lax.broadcasted_iota(jnp.int32, (1, 128), 1)

    def attend(step, carry):
        unit = 3 - step
        rows = pl.ds(pl.multiple_of(unit * unit_rows, unit_rows), unit_rows)
        queries = qb[rows, :]
        attended = jnp.zeros((unit_rows, 256), F32)
        logs = jnp.zeros((unit_rows, 128), F32)
        for head in range(heads):
            masked = jnp.where(head_mask(head, True), queries, jnp.zeros_like(queries))
            scores = dot(masked, kb[...], NT)
            scores = scores.reshape(2, half, 8 * half) + neg_ref[unit]
            scores = scores.reshape(unit_rows, 8 * half)
            largest = jnp.max(scores, axis=-1, keepdims=True)
            shares = jnp.exp(scores - largest)
            sums = jnp.sum(shares, axis=-1, keepdims=True)
            output = dot(shares.astype(BF), vb[...]) * (1.0 / sums)
            attended = jnp.where(head_mask(head, False), output, attended)
            if save:
                logs = jnp.where(lane == head, largest + jnp.log(sums), logs)
        if save:
            lse[unit] = logs.T[:8, :]
        attended = attended.astype(BF)
        ob[rows, :] = attended
        total[...] = dot(attended, wout[...])
        attn.scatter(unit, total, own)
        return carry

    lax.fori_loop(0, 4, attend, 0)
    loads[2].wait()
    loads[3].wait()
    shift = cond_ref[:, :width]
    scale = cond_ref[:, width:]
    for part in range(2):
        rows = pl.ds(part * half, half)
        after = x_ref[rows, :] + attn.collect(part, own)
        x1[rows, :] = after
        mbuf[rows, :] = (norm(after)[0] * (1.0 + scale) + shift).astype(BF)
        feed.send(part)

    def expand(step, carry):
        feed.receive(step)
        unit = jnp.where(step < 2, step, 5 - step)
        rows = pl.ds(pl.multiple_of(unit * unit_rows, unit_rows), unit_rows)
        hidden = dot(mbuf[rows, :], wup[...])
        gated, slope = gelu_parts(hidden)
        gated = gated.astype(BF)
        if save:
            gb[rows, :] = gated
            gpb[rows, :] = slope.astype(BF)
        total[...] = dot(gated, wdown[...])
        feed.scatter(unit, total, own)
        return carry

    lax.fori_loop(0, 4, expand, 0)
    stores = []
    if save:
        made = (abuf, qb, kb, vb, lse, ob, x1, mbuf, gb, gpb)
        for i, (src, dst) in enumerate(zip(made, saves)):
            stores.append(pltpu.make_async_copy(src, dst, osem.at[i]))
            stores[-1].start()
    for part in range(2):
        rows = pl.ds(part * half, half)
        next_ref[rows, :] = x1[rows, :] + feed.collect(part, own) + bdown_ref[...]
    attn.finish()
    feed.finish()
    for store in stores:
        store.wait()


def any_spec():
    return pl.BlockSpec(memory_space=pl.ANY)


def vmem_spec():
    return pl.BlockSpec(memory_space=pltpu.VMEM)


def forward_layer(layer, save, heads, rows, small, tables, weights):
    gain, bias, cond, bdown = small
    cosine, sine, neg = tables
    block, width = rows.shape
    length = 4 * block
    units = weights[2].shape[2]
    saved_shapes = [
        ((length, width), BF),
        ((length, 256), BF),
        ((length, 256), BF),
        ((length, 256), BF),
        ((4, 8, block), F32),
        ((length, 256), BF),
        ((block, width), F32),
        ((length, width), BF),
        ((length, units), BF),
        ((length, units), BF),
    ]
    out_shape = [jax.ShapeDtypeStruct((block, width), F32)]
    out_specs = [vmem_spec()]
    if save:
        out_shape += [jax.ShapeDtypeStruct(*each) for each in saved_shapes]
        out_specs += [any_spec()] * len(saved_shapes)
    scratch = [pltpu.VMEM(each.shape[1:], BF) for each in weights]
    scratch += group_scratch(length, width) + group_scratch(length, width)
    scratch += [
        pltpu.VMEM((length, 256), BF),
        pltpu.VMEM((length, 256), BF),
        pltpu.VMEM((length, 256), BF),
        pltpu.VMEM((4, 8, block), F32),
        pltpu.VMEM((length, 256), BF),
        pltpu.VMEM((block, width), F32),
        pltpu.VMEM((length, units) if save else (16, 128), BF),
        pltpu.VMEM((length, units) if save else (16, 128), BF),
        pltpu.VMEM((block, width), F32),
        pltpu.VMEM((block, width), F32),
    ]
    scratch += [pltpu.SemaphoreType.DMA((6, 2))] * 4
    scratch += [pltpu.SemaphoreType.DMA((4,)), pltpu.SemaphoreType.DMA((10,))]

    def kernel(*refs):
        forward_kernel(layer, save, heads, refs)

    return pl.pallas_call(
        kernel,
        out_shape=out_shape,
        in_specs=[vmem_spec()] * 8 + [any_spec()] * 4,
        out_specs=out_specs,
        scratch_shapes=scratch,
        compiler_params=pltpu.CompilerParams(
            collective_id=1 + 2 * layer + int(save), has_side_effects=True, vmem_limit_bytes=LIMIT
        ),
        name="layer_forward",
    )(rows, gain, bias, cond, bdown, cosine, sine, neg, *weights)


def backward_kernel(layer, heads, refs):
    (dx_ref, x_ref, x1_ref, gain_ref, cond_ref, cos_ref, sin_ref, neg_ref, lse_ref) = refs[:9]
    hbm = refs[9:21]
    (out_ref, small_ref, grads_ref) = refs[21:24]
    scratch = refs[24:]
    local = scratch[:12]
    (wqkv, wout, wup, wdown, abuf, qb, kb, vb, ob, mbuf, gb, gpb) = local
    first = scratch[12:19]
    second = scratch[19:26]
    (dhb, qmask, domask, dsb, pb, dqkv, total, own, dx1, grads) = scratch[26:36]
    (send, recv, send2, recv2, lsem, osem) = scratch[36:]
    ids = neighbours()
    meet(ids)
    order = (3, 11, 2, 9, 10, 1, 5, 6, 7, 0, 4, 8)
    loads = [
        pltpu.make_async_copy(src.at[layer] if i < 4 else src, dst, lsem.at[i])
        for i, (src, dst) in enumerate(zip(hbm, local))
    ]
    for i in order:
        loads[i].start()
    feed = Group((send, recv), ids, *first)
    attn = Group((send2, recv2), ids, *second)
    ebuf, fbuf = first[0], second[0]
    half = feed.half
    unit_rows = 2 * half
    width = x_ref.shape[1]
    for part in range(2):
        rows = pl.ds(part * half, half)
        ebuf[rows, :] = dx_ref[rows, :].astype(BF)
        feed.send(part)
    small_ref[...] = jnp.zeros_like(small_ref)
    small_ref[4:5, :] = jnp.sum(dx_ref[...], axis=0, keepdims=True)
    for i in (3, 11, 2):
        loads[i].wait()

    def contract(step, carry):
        feed.receive(step)
        unit = jnp.where(step < 2, step, 5 - step)
        rows = pl.ds(pl.multiple_of(unit * unit_rows, unit_rows), unit_rows)
        grad = dot(ebuf[rows, :], wdown[...], NT)
        grad = (grad * gpb[rows, :].astype(F32)).astype(BF)
        dhb[rows, :] = grad
        total[...] = dot(grad, wup[...], NT)
        feed.scatter(unit, total, own)
        return carry

    lax.fori_loop(0, 4, contract, 0)
    tiles = width // 256

    def outer(left, right, place, columns):
        def tile(index, carry):
            start = pl.multiple_of(index * 256, 256)
            grads[pl.ds(start, 256), place : place + columns] = dot(
                left[:, pl.ds(start, 256)], right[...], TN
            ).astype(BF)
            return carry

        lax.fori_loop(0, tiles, tile, 0)

    units = gb.shape[1]
    shift_sum = jnp.zeros((1, width), F32)
    scale_sum = jnp.zeros((1, width), F32)
    for part in range(2):
        if part == 0:
            loads[9].wait()
            loads[10].wait()
            outer(mbuf, dhb, 1024, units)
        else:
            outer(ebuf, gb, 1024 + units, units)
        rows = pl.ds(part * half, half)
        grad = feed.collect(part, own)
        hat, rstd = norm(x1_ref[rows, :])
        shift_sum += jnp.sum(grad, axis=0, keepdims=True)
        scale_sum += jnp.sum(grad * hat, axis=0, keepdims=True)
        after = dx_ref[rows, :] + norm_back(grad * (1.0 + cond_ref[:, width:]), hat, rstd)
        dx1[rows, :] = after
        fbuf[rows, :] = after.astype(BF)
        attn.send(part)
    small_ref[0:1, :] = shift_sum
    small_ref[1:2, :] = scale_sum
    for i in (1, 5, 6, 7):
        loads[i].wait()

    def turn_back(grad, rows, scale):
        cosine = cos_ref[rows, :]
        sine = sin_ref[rows, :]
        first_half = grad[:, :128]
        second_half = grad[:, 128:]
        return (
            ((first_half * cosine + second_half * sine) * scale).astype(BF),
            ((second_half * cosine - first_half * sine) * scale).astype(BF),
        )

    def attend(step, carry):
        attn.receive(step)
        unit = jnp.where(step < 2, step, 5 - step)
        rows = pl.ds(pl.multiple_of(unit * unit_rows, unit_rows), unit_rows)
        grad_out = dot(fbuf[rows, :], wout[...], NT).astype(BF)
        queries = qb[rows, :]
        grad_queries = jnp.zeros((unit_rows, 256), F32)
        for head in range(heads):
            masked = jnp.where(head_mask(head, True), queries, jnp.zeros_like(queries))
            masked_out = jnp.where(head_mask(head, False), grad_out, jnp.zeros_like(grad_out))
            start = pl.multiple_of((unit * heads + head) * unit_rows, unit_rows)
            place = pl.ds(start, unit_rows)
            qmask[place, :] = masked
            domask[place, :] = masked_out
            scores = dot(kb[...], masked, NT).reshape(8, half, unit_rows)
            shares = jnp.exp(scores - (lse_ref[unit, head : head + 1, :] - neg_ref[unit]))
            shares = shares.reshape(8 * half, unit_rows)
            grad_shares = dot(vb[...], masked_out, NT)
            centre = jnp.sum(shares * grad_shares, axis=0, keepdims=True)
            grad_scores = (shares * (grad_shares - centre)).astype(BF)
            pb[:, place] = shares.astype(BF)
            dsb[:, place] = grad_scores
            keys = jnp.where(head_mask(head, True), kb[...], jnp.zeros(kb.shape, BF))
            grad_queries = grad_queries + dot(grad_scores, keys, TN)
        low, high = turn_back(grad_queries, rows, HD**-0.5)
        dqkv[rows, :128] = low
        dqkv[rows, 128:256] = high
        return carry

    lax.fori_loop(0, 4, attend, 0)
    loads[0].wait()

    def spread(step, carry):
        unit = 3 - step
        rows = pl.ds(pl.multiple_of(unit * unit_rows, unit_rows), unit_rows)
        low, high = turn_back(dot(dsb[rows, :], qmask[...]), rows, 1.0)
        dqkv[rows, 256:384] = low
        dqkv[rows, 384:512] = high
        dqkv[rows, 512:768] = dot(pb[rows, :], domask[...]).astype(BF)
        total[...] = dot(dqkv[rows, :], wqkv[...], NT)
        attn.scatter(unit, total, own)
        return carry

    lax.fori_loop(0, 4, spread, 0)
    gain_sum = jnp.zeros((1, width), F32)
    bias_sum = jnp.zeros((1, width), F32)
    for part in range(2):
        if part == 0:
            loads[4].wait()
            outer(abuf, dqkv, 0, 768)
        else:
            loads[8].wait()
            outer(fbuf, ob, 768, 256)
            store = pltpu.make_async_copy(grads, grads_ref, osem)
            store.start()
        rows = pl.ds(part * half, half)
        grad = attn.collect(part, own)
        hat, rstd = norm(x_ref[rows, :])
        gain_sum += jnp.sum(grad * hat, axis=0, keepdims=True)
        bias_sum += jnp.sum(grad, axis=0, keepdims=True)
        out_ref[rows, :] = dx1[rows, :] + norm_back(grad * gain_ref[...], hat, rstd)
    small_ref[2:3, :] = gain_sum
    small_ref[3:4, :] = bias_sum
    feed.finish()
    attn.finish()
    store.wait()


def backward_layer(layer, heads, grad_rows, rows, gain, cond, tables, weights, saved):
    cosine, sine, neg = tables
    (normed, queries, keys, values, logs, attended, after, modulated, gated, slope) = saved
    block, width = rows.shape
    length = 4 * block
    units = weights[2].shape[2]
    columns = 1024 + 2 * units
    held = [*weights, normed, queries, keys, values, attended, modulated, gated, slope]
    scratch = [pltpu.VMEM(each.shape[1:], BF) for each in weights]
    scratch += [pltpu.VMEM(each.shape, BF) for each in held[4:]]
    scratch += group_scratch(length, width) + group_scratch(length, width)
    scratch += [
        pltpu.VMEM((length, units), BF),
        pltpu.VMEM((heads * length, 256), BF),
        pltpu.VMEM((heads * length, 256), BF),
        pltpu.VMEM((length, heads * length), BF),
        pltpu.VMEM((length, heads * length), BF),
        pltpu.VMEM((length, 768), BF),
        pltpu.VMEM((block, width), F32),
        pltpu.VMEM((block, width), F32),
        pltpu.VMEM((block, width), F32),
        pltpu.VMEM((width, columns), BF),
    ]
    scratch += [pltpu.SemaphoreType.DMA((6, 2))] * 4
    scratch += [pltpu.SemaphoreType.DMA((12,)), pltpu.SemaphoreType.DMA]

    def kernel(*refs):
        backward_kernel(layer, heads, refs)

    return pl.pallas_call(
        kernel,
        out_shape=[
            jax.ShapeDtypeStruct((block, width), F32),
            jax.ShapeDtypeStruct((8, width), F32),
            jax.ShapeDtypeStruct((width, columns), BF),
        ],
        in_specs=[vmem_spec()] * 9 + [any_spec()] * 12,
        out_specs=[vmem_spec(), vmem_spec(), any_spec()],
        scratch_shapes=scratch,
        compiler_params=pltpu.CompilerParams(
            collective_id=9 + layer, has_side_effects=True, vmem_limit_bytes=LIMIT
        ),
        name="layer_backward",
    )(grad_rows, rows, after, gain, cond, cosine, sine, neg, logs, *held)


def rotary_columns(weights, heads):
    parts = weights.reshape(*weights.shape[:-1], heads, 2, HALF)
    parts = jnp.swapaxes(parts, -3, -2)
    parts = jnp.pad(parts, [(0, 0)] * (parts.ndim - 2) + [(0, 4 - heads), (0, 0)])
    return parts.reshape(*weights.shape[:-1], 256)


def plain_columns(grads, heads):
    parts = grads.reshape(*grads.shape[:-1], 2, 4, HALF)[..., :heads, :]
    return jnp.swapaxes(parts, -3, -2).reshape(*grads.shape[:-1], heads * HD)


def local(
    tokens,
    cotangent,
    lengths,
    timesteps,
    w_self,
    ln_gain,
    ln_bias,
    w_qkv,
    w_out,
    w_ada,
    b_ada,
    w_up,
    w_down,
    b_down,
):
    hp = lax.Precision.HIGHEST
    block, width = tokens.shape
    depth = w_qkv.shape[0]
    heads = w_qkv.shape[3] // HD
    units = w_up.shape[2]
    place = lax.axis_index("tensor")
    core = place % 2
    sibling = place + 1 - 2 * core
    far = (place + 2) % 4
    far_other = (sibling + 2) % 4
    half = block // 2
    owners = jnp.stack([place, place, sibling, sibling, far, far_other, far, far_other])
    halves = jnp.array([0, 1, 0, 1, 1, 1, 0, 0], jnp.int32)
    starts = owners * block + halves * half
    index = (starts[:, None] + jnp.arange(half, dtype=jnp.int32)).reshape(-1)
    packed = lengths[0, 0] < 4 * block
    position = jnp.where(packed, index % block, index)
    freqs = jnp.exp(-jnp.log(10000.0) * jnp.arange(HALF).astype(F32) / HALF)
    angle = position.astype(F32)[:, None] * freqs
    cosine = jnp.tile(jnp.cos(angle), (1, 4))
    sine = jnp.tile(jnp.sin(angle), (1, 4))
    chunk = jnp.array([0, 0, 1, 1, 2, 3, 2, 3], jnp.int32)
    apart = (chunk[:, None] != chunk[None, :]).astype(F32) * jnp.where(packed, -1e9, 0.0)
    neg_keys = jnp.repeat(apart, half, axis=1).reshape(4, 2, 1, 4 * block)
    neg_queries = jnp.repeat(apart, half, axis=1).reshape(8, 4, 1, block).swapaxes(0, 1)
    slot = jnp.where(packed, place, 0)
    freqs = jnp.exp(-jnp.log(10000.0) * jnp.arange(width // 2).astype(F32) / (width // 2))
    angle = lax.dynamic_slice_in_dim(timesteps, slot, 1, 1).astype(F32) * freqs
    temb = jnp.concatenate([jnp.cos(angle), jnp.sin(angle)], axis=-1)
    conds = [jnp.dot(temb, w_ada[l], precision=hp) + b_ada[l] for l in range(depth)]
    value_pad = [(0, 0), (0, 0), (0, 256 - heads * HD)]
    weights = (
        jnp.concatenate(
            [
                rotary_columns(w_qkv[:, 0], heads),
                rotary_columns(w_qkv[:, 1], heads),
                jnp.pad(w_qkv[:, 2], value_pad),
            ],
            axis=-1,
        ),
        jnp.pad(w_out, [(0, 0), (0, 256 - heads * HD), (0, 0)]),
        w_up,
        w_down,
    )

    def run(rows, save):
        kept = []
        for layer in range(depth):
            small = (
                ln_gain[layer][None],
                ln_bias[layer][None],
                conds[layer],
                b_down[layer][None],
            )
            made = forward_layer(
                layer, save, heads, rows, small, (cosine, sine, neg_keys), weights
            )
            kept.append((rows, made[1:]))
            rows = made[0]
        return (rows, kept)

    start = jnp.dot(tokens, w_self[:width], preferred_element_type=F32)
    estimate = run(start, False)[0].astype(BF)
    start = start + jnp.dot(estimate, w_self[width:], preferred_element_type=F32)
    rows, kept = run(start, True)
    activations = rows.astype(BF)
    grad_rows = cotangent.astype(F32)
    smalls = [None] * depth
    shards = [None] * depth
    for layer in reversed(range(depth)):
        rows_in, saved = kept[layer]
        grad_rows, smalls[layer], grads = backward_layer(
            layer,
            heads,
            grad_rows,
            rows_in,
            ln_gain[layer][None],
            conds[layer],
            (cosine, sine, neg_queries),
            weights,
            saved,
        )
        shards[layer] = lax.psum_scatter(grads, "dp", scatter_dimension=0, tiled=True).astype(F32)
    low = grad_rows.astype(BF)
    grad_tokens = dot(low, w_self[:width], NT)
    joined = jnp.concatenate([tokens, estimate], axis=1)
    grad_self = lax.psum(dot(joined, low, TN).astype(BF), ("dp", "tensor")).astype(F32)
    shard = jnp.stack(shards)
    grad_qkv = jnp.stack(
        [
            plain_columns(shard[..., :256], heads),
            plain_columns(shard[..., 256:512], heads),
            shard[..., 512 : 512 + heads * HD],
        ],
        axis=1,
    )
    grad_out = jnp.swapaxes(shard[..., 768 : 768 + heads * HD], 1, 2)
    grad_up = shard[..., 1024 : 1024 + units]
    grad_down = jnp.swapaxes(shard[..., 1024 + units :], 1, 2)
    vectors = jnp.concatenate([temb] + [each[:5].reshape(1, -1) for each in smalls], axis=1)
    vectors = lax.all_gather(vectors, ("dp", "tensor"), axis=0, tiled=True)
    times = vectors[:, :width]
    rest = vectors[:, width:].reshape(-1, depth, 5 * width)
    grad_ada = jnp.einsum("nd,nle->lde", times, rest[..., : 2 * width], precision=hp)
    sums = jnp.sum(rest, axis=0)
    return (
        activations,
        grad_tokens,
        sums[:, 2 * width : 3 * width],
        sums[:, 3 * width : 4 * width],
        grad_qkv,
        grad_out,
        grad_ada,
        sums[:, : 2 * width],
        grad_up,
        grad_down,
        sums[:, 4 * width :],
        grad_self,
    )


def solution(mesh):
    return jax.shard_map(
        local,
        mesh=mesh,
        in_specs=(
            P(("dp", "tensor"), None),
            P(("dp", "tensor"), None),
            P("dp", None),
            P("dp", None),
            P(),
            P(),
            P(),
            P(None, None, None, "tensor"),
            P(None, "tensor", None),
            P(),
            P(),
            P(None, None, "tensor"),
            P(None, "tensor", None),
            P(),
        ),
        out_specs=(
            P(("dp", "tensor"), None),
            P(("dp", "tensor"), None),
            P(),
            P(),
            P(None, None, "dp", "tensor"),
            P(None, "tensor", "dp"),
            P(),
            P(),
            P(None, "dp", "tensor"),
            P(None, "tensor", "dp"),
            P(),
            P(),
        ),
        check_vma=False,
    )
```

```python
import functools

import jax
import jax.numpy as jnp
from jax import lax
from jax.experimental import pallas as pl
from jax.experimental.pallas import tpu as pltpu
from jax.sharding import PartitionSpec as P

HD = 64
HALF = HD // 2
BF = jnp.bfloat16
F32 = jnp.float32
MESH = pl.DeviceIdType.MESH
EPS = 1e-05
LIMIT = 60 << 20


def norm(rows):
    centred = rows - jnp.mean(rows, axis=-1, keepdims=True)
    rstd = lax.rsqrt(jnp.mean(centred * centred, axis=-1, keepdims=True) + EPS)
    return (centred * rstd, rstd)


def norm_back(grad, hat, rstd):
    return rstd * (
        grad
        - jnp.mean(grad, axis=-1, keepdims=True)
        - hat * jnp.mean(grad * hat, axis=-1, keepdims=True)
    )


def dot(left, right, dims=((1,), (0,))):
    return lax.dot_general(left, right, (dims, ((), ())), preferred_element_type=F32)


NT = ((1,), (1,))
TN = ((0,), (0,))


def head_mask(head, columns, rotary):
    lane = lax.broadcasted_iota(jnp.int32, (1, columns), 1)
    if rotary:
        return (lane % 128) // HALF == head
    return lane // HD == head


def keep_head(rows, head, rotary):
    return jnp.where(head_mask(head, rows.shape[1], rotary), rows, jnp.zeros_like(rows))


def turned_place(columns, start, total):
    row = lax.broadcasted_iota(jnp.int32, (256, total), 0)
    column = lax.broadcasted_iota(jnp.int32, (256, total), 1) - start
    source = column // HD * HALF + column % HD // HALF * 128 + column % HALF
    fits = (source == row) & (column >= 0) & (column < columns)
    return fits.astype(F32).astype(BF)


def plain_place(columns, start, total):
    row = lax.broadcasted_iota(jnp.int32, (columns, total), 0)
    column = lax.broadcasted_iota(jnp.int32, (columns, total), 1) - start
    return (row == column).astype(F32).astype(BF)


class Group:
    def __init__(self, sems, ids, gathered, pair_out, pair_in, own_out, own_in, far_out, far_in):
        self.sems = sems
        self.ids = ids
        self.gathered = gathered
        self.pair_out, self.pair_in = pair_out, pair_in
        self.own_out, self.own_in = own_out, own_in
        self.far_out, self.far_in = far_out, far_in
        self.half = gathered.shape[0] // 8

    def copy(self, src, dst, kind, part, far):
        send, recv = self.sems
        return pltpu.make_async_remote_copy(
            src_ref=src,
            dst_ref=dst,
            send_sem=send.at[kind, part],
            recv_sem=recv.at[kind, part],
            device_id=self.ids[1] if far else self.ids[0],
            device_id_type=MESH,
        )

    def rows(self, start):
        return pl.ds(pl.multiple_of(start, self.half), self.half)

    def pair(self, part):
        return 6 * self.half - 2 * self.half * part

    def far_copy(self, part):
        own = self.gathered.at[self.rows(part * self.half)]
        return self.copy(own, self.gathered.at[self.rows(self.pair(part))], 0, part, True)

    def sibling_copy(self, part):
        own = self.gathered.at[self.rows(part * self.half)]
        place = self.gathered.at[self.rows((2 + part) * self.half)]
        return self.copy(own, place, 1, part, False)

    def forward_copy(self, part):
        src = self.gathered.at[self.rows(self.pair(part))]
        dst = self.gathered.at[self.rows(self.pair(part) + self.half)]
        return self.copy(src, dst, 2, part, False)

    def send(self, part):
        self.far_copy(part).start()
        self.sibling_copy(part).start()

    def receive(self, step):
        @pl.when(step == 1)
        def _():
            self.sibling_copy(0).wait_recv()
            self.sibling_copy(1).wait_recv()

        @pl.when(step >= 2)
        def _():
            part = step - 2
            self.far_copy(part).wait_recv()
            self.forward_copy(part).start()
            self.forward_copy(part).wait_recv()

    def pair_copy(self, part):
        return self.copy(self.pair_out.at[part], self.pair_in.at[part], 3, part, False)

    def own_copy(self):
        return self.copy(self.own_out, self.own_in, 4, 0, False)

    def sum_copy(self, part):
        return self.copy(self.far_out.at[part], self.far_in.at[part], 5, part, True)

    def scatter(self, unit, total, own):
        @pl.when(unit == 0)
        def _():
            own[...] = total[...]

        @pl.when(unit == 1)
        def _():
            self.own_out[...] = total[...].astype(BF)
            self.own_copy().start()

        @pl.when(unit >= 2)
        def _():
            part = 3 - unit
            self.pair_out[part] = total[self.half :, :].astype(BF)
            self.pair_copy(part).start()
            self.pair_copy(part).wait_recv()
            self.far_out[part] = (
                total[: self.half, :] + self.pair_in[part].astype(F32)
            ).astype(BF)
            self.sum_copy(part).start()

    def collect(self, part, own):
        if part == 0:
            self.own_copy().wait_recv()
        self.sum_copy(part).wait_recv()
        rows = pl.ds(part * self.half, self.half)
        return own[rows, :] + self.own_in[rows, :].astype(F32) + self.far_in[part].astype(F32)

    def finish(self):
        for part in range(2):
            self.far_copy(part).wait_send()
            self.sibling_copy(part).wait_send()
            self.forward_copy(part).wait_send()
            self.pair_copy(part).wait_send()
            self.sum_copy(part).wait_send()
        self.own_copy().wait_send()


def neighbours():
    group = lax.axis_index("dp")
    place = lax.axis_index("tensor")
    core = lax.rem(place, 2)
    return ((group, place + 1 - 2 * core), (group, lax.rem(place + 2, 4)))


class Spot:
    def __init__(self, deep):
        group = lax.axis_index("dp")
        self.place = lax.axis_index("tensor")
        self.deep = deep
        self.z = group // 2
        self.x = lax.rem(group, 2)
        self.across = (2 * self.z + 1 - self.x, self.place)

    def level(self, ahead):
        return lax.rem(self.z + ahead, self.deep)

    def along(self, ahead):
        return (2 * self.level(ahead) + self.x, self.place)

    def partners(self):
        return [self.across] + [self.along(ahead) for ahead in range(1, self.deep)]


def meet(ids):
    barrier = pltpu.get_barrier_semaphore()
    for device in ids:
        pl.semaphore_signal(barrier, inc=1, device_id=device, device_id_type=MESH)
    pl.semaphore_wait(barrier, len(ids))


class DpSum:
    def __init__(self, spot, src, out, scratch):
        self.spot, self.src, self.out = spot, src, out
        self.pairs, self.rest, self.sems = scratch
        self.block = self.pairs.shape[1]

    @staticmethod
    def scratch(deep, block, columns):
        return [
            pltpu.VMEM((deep, block, columns), BF),
            pltpu.VMEM((deep - 1, block, columns), BF),
            pltpu.SemaphoreType.DMA((4, deep)),
        ]

    def rows(self, ahead, x):
        start = (2 * self.spot.level(ahead) + x) * self.block
        return pl.ds(pl.multiple_of(start, self.block), self.block)

    def x_copy(self, ahead):
        return pltpu.make_async_remote_copy(
            src_ref=self.src.at[self.rows(ahead, 1 - self.spot.x)],
            dst_ref=self.pairs.at[ahead],
            send_sem=self.sems.at[0, ahead],
            recv_sem=self.sems.at[1, ahead],
            device_id=self.spot.across,
            device_id_type=MESH,
        )

    def z_copy(self, ahead):
        return pltpu.make_async_remote_copy(
            src_ref=self.pairs.at[ahead],
            dst_ref=self.rest.at[ahead - 1],
            send_sem=self.sems.at[2, ahead],
            recv_sem=self.sems.at[3, ahead],
            device_id=self.spot.along(ahead),
            device_id_type=MESH,
        )

    def order(self):
        return [*range(1, self.spot.deep), 0]

    def start(self):
        for ahead in self.order():
            self.x_copy(ahead).start()

    def middle(self):
        for ahead in self.order():
            self.x_copy(ahead).wait_recv()
            total = self.src[self.rows(ahead, self.spot.x), :].astype(F32)
            total = total + self.pairs[ahead].astype(F32)
            if ahead:
                self.pairs[ahead] = total.astype(BF)
                self.z_copy(ahead).start()
            else:
                self.out[...] = total

    def end(self):
        for ahead in range(1, self.spot.deep):
            self.z_copy(ahead).wait_recv()
        total = self.out[...]
        for ahead in range(1, self.spot.deep):
            total = total + self.rest[ahead - 1].astype(F32)
        self.out[...] = total
        for ahead in range(self.spot.deep):
            self.x_copy(ahead).wait_send()
            if ahead:
                self.z_copy(ahead).wait_send()


def group_scratch(rows, width):
    half = rows // 8
    return [
        pltpu.VMEM((rows, width), BF),
        pltpu.VMEM((2, half, width), BF),
        pltpu.VMEM((2, half, width), BF),
        pltpu.VMEM((2 * half, width), BF),
        pltpu.VMEM((2 * half, width), BF),
        pltpu.VMEM((2, half, width), BF),
        pltpu.VMEM((2, half, width), BF),
    ]


def gelu_parts(hidden):
    cdf = 0.5 * (1.0 + lax.erf(hidden * (0.5**0.5)))
    density = jnp.exp(hidden * hidden * -0.5) * 0.3989422804014327
    return (hidden * cdf, cdf + hidden * density)


def load_turned(wq, wk, wqk):
    turn = turned_place(wq.shape[1], 0, wq.shape[1])
    wqk[:, :256] = dot(wq[...], turn, NT).astype(BF)
    wqk[:, 256:] = dot(wk[...], turn, NT).astype(BF)


def forward_kernel(layer, save, heads, refs):
    (x_ref, gain_ref, bias_ref, cond_ref, bdown_ref, cos_ref, sin_ref, neg_ref) = refs[:8]
    (wqkv_hbm, wout_hbm, wup_hbm, wdown_hbm, wada_hbm) = refs[8:13]
    count = 10 if save else 1
    next_ref = refs[13]
    saves = refs[14 : 14 + count]
    scratch = refs[14 + count :]
    (wq, wk, wv, wout, wup, wdown, wada, wqk) = scratch[:8]
    first = scratch[8:15]
    second = scratch[15:22]
    (qb, kb, vb, lse, ob, x1, gb, gpb, total, own, cond) = scratch[22:33]
    (send, recv, send2, recv2, wsem, osem) = scratch[33:]
    ids = neighbours()
    meet(ids)
    sources = [wqkv_hbm.at[layer, part] for part in range(3)]
    sources += [wout_hbm.at[layer], wup_hbm.at[layer], wdown_hbm.at[layer]]
    places = [wq, wk, wv, wout, wup, wdown]
    if not save:
        sources.append(wada_hbm.at[layer])
        places.append(wada)
    loads = [
        pltpu.make_async_copy(src, dst, wsem.at[i])
        for i, (src, dst) in enumerate(zip(sources, places))
    ]
    for load in loads:
        load.start()
    attn = Group((send, recv), ids, *first)
    feed = Group((send2, recv2), ids, *second)
    abuf, mbuf = first[0], second[0]
    half = attn.half
    unit_rows = 2 * half
    width = x_ref.shape[1]
    for part in range(2):
        rows = pl.ds(part * half, half)
        hat = norm(x_ref[rows, :])[0]
        abuf[rows, :] = (hat * gain_ref[...] + bias_ref[...]).astype(BF)
        attn.send(part)
    for load in loads[:3]:
        load.wait()
    load_turned(wq, wk, wqk)

    def project(step, carry):
        attn.receive(step)
        unit = jnp.where(step < 2, step, 5 - step)
        rows = pl.ds(pl.multiple_of(unit * unit_rows, unit_rows), unit_rows)
        normed = abuf[rows, :]
        mixed = dot(normed, wqk[...])
        cosine = cos_ref[rows, :]
        sine = sin_ref[rows, :]
        for place, dst, scale in ((0, qb, HD**-0.5), (256, kb, 1.0)):
            first_half = mixed[:, place : place + 128]
            second_half = mixed[:, place + 128 : place + 256]
            dst[rows, :128] = ((first_half * cosine - second_half * sine) * scale).astype(BF)
            dst[rows, 128:] = ((second_half * cosine + first_half * sine) * scale).astype(BF)
        vb[rows, :] = dot(normed, wv[...]).astype(BF)
        return carry

    lax.fori_loop(0, 4, project, 0)
    loads[3].wait()
    lane = lax.broadcasted_iota(jnp.int32, (1, 128), 1)

    def attend(step, carry):
        unit = 3 - step
        rows = pl.ds(pl.multiple_of(unit * unit_rows, unit_rows), unit_rows)
        queries = qb[rows, :]
        columns = heads * HD
        attended = jnp.zeros((unit_rows, columns), F32)
        logs = jnp.zeros((unit_rows, 128), F32)
        for head in range(heads):
            scores = dot(keep_head(queries, head, True), kb[...], NT)
            scores = scores.reshape(2, half, 8 * half) + neg_ref[unit]
            scores = scores.reshape(unit_rows, 8 * half)
            largest = jnp.max(scores, axis=-1, keepdims=True)
            shares = jnp.exp(scores - largest)
            sums = jnp.sum(shares, axis=-1, keepdims=True)
            output = dot(shares.astype(BF), vb[...]) * (1.0 / sums)
            attended = jnp.where(head_mask(head, columns, False), output, attended)
            if save:
                logs = jnp.where(lane == head, largest + jnp.log(sums), logs)
        if save:
            lse[unit] = logs.T[:8, :]
        attended = attended.astype(BF)
        ob[rows, :] = attended
        total[...] = dot(attended, wout[...])
        attn.scatter(unit, total, own)
        return carry

    lax.fori_loop(0, 4, attend, 0)
    for load in loads[4:]:
        load.wait()
    if save:
        shift = cond_ref[:1, :width]
        scale = cond_ref[:1, width:]
    else:
        embedding, ada_bias = cond_ref
        made = jnp.sum(wada[...] * embedding[...], axis=0, keepdims=True) + ada_bias[...]
        cond[...] = jnp.broadcast_to(made, cond.shape)
        shift = made[:, :width]
        scale = made[:, width:]
    for part in range(2):
        rows = pl.ds(part * half, half)
        after = x_ref[rows, :] + attn.collect(part, own)
        x1[rows, :] = after
        mbuf[rows, :] = (norm(after)[0] * (1.0 + scale) + shift).astype(BF)
        feed.send(part)

    def expand(step, carry):
        feed.receive(step)
        unit = jnp.where(step < 2, step, 5 - step)
        rows = pl.ds(pl.multiple_of(unit * unit_rows, unit_rows), unit_rows)
        hidden = dot(mbuf[rows, :], wup[...])
        gated, slope = gelu_parts(hidden)
        gated = gated.astype(BF)
        if save:
            gb[rows, :] = gated
            gpb[rows, :] = slope.astype(BF)
        total[...] = dot(gated, wdown[...])
        feed.scatter(unit, total, own)
        return carry

    lax.fori_loop(0, 4, expand, 0)
    stores = []
    made = (abuf, qb, kb, vb, lse, ob, x1, mbuf, gb, gpb) if save else (cond,)
    for i, (src, dst) in enumerate(zip(made, saves)):
        stores.append(pltpu.make_async_copy(src, dst, osem.at[i]))
        stores[-1].start()
    for part in range(2):
        rows = pl.ds(part * half, half)
        next_ref[rows, :] = x1[rows, :] + feed.collect(part, own) + bdown_ref[...]
    attn.finish()
    feed.finish()
    for store in stores:
        store.wait()


def any_spec():
    return pl.BlockSpec(memory_space=pl.ANY)


def vmem_spec():
    return pl.BlockSpec(memory_space=pltpu.VMEM)


def forward_layer(layer, save, heads, rows, small, tables, weights):
    gain, bias, cond, bdown = small
    cosine, sine, neg = tables
    block, width = rows.shape
    length = 4 * block
    columns = heads * HD
    units = weights[2].shape[2]
    saved_shapes = [
        ((length, width), BF),
        ((length, 256), BF),
        ((length, 256), BF),
        ((length, columns), BF),
        ((4, 8, block), F32),
        ((length, columns), BF),
        ((block, width), F32),
        ((length, width), BF),
        ((length, units), BF),
        ((length, units), BF),
    ]
    if not save:
        saved_shapes = [((8, 2 * width), F32)]
    out_shape = [jax.ShapeDtypeStruct((block, width), F32)]
    out_specs = [vmem_spec()]
    out_shape += [jax.ShapeDtypeStruct(*each) for each in saved_shapes]
    out_specs += [any_spec()] * len(saved_shapes)
    scratch = [pltpu.VMEM((width, columns), BF)] * 3
    scratch += [pltpu.VMEM(each.shape[1:], BF) for each in weights[1:4]]
    scratch += [pltpu.VMEM((8, 128) if save else (width, 2 * width), F32)]
    scratch += [pltpu.VMEM((width, 512), BF)]
    scratch += group_scratch(length, width) + group_scratch(length, width)
    scratch += [
        pltpu.VMEM((length, 256), BF),
        pltpu.VMEM((length, 256), BF),
        pltpu.VMEM((length, columns), BF),
        pltpu.VMEM((4, 8, block), F32),
        pltpu.VMEM((length, columns), BF),
        pltpu.VMEM((block, width), F32),
        pltpu.VMEM((length, units) if save else (16, 128), BF),
        pltpu.VMEM((length, units) if save else (16, 128), BF),
        pltpu.VMEM((block, width), F32),
        pltpu.VMEM((block, width), F32),
        pltpu.VMEM((8, 2 * width), F32),
    ]
    scratch += [pltpu.SemaphoreType.DMA((6, 2))] * 4
    scratch += [pltpu.SemaphoreType.DMA((7,)), pltpu.SemaphoreType.DMA((10,))]

    def kernel(*refs):
        if not save:
            refs = (*refs[:3], refs[3:5], *refs[5:])
        forward_kernel(layer, save, heads, refs)

    conds = (cond,) if save else cond
    return pl.pallas_call(
        kernel,
        out_shape=out_shape,
        in_specs=[vmem_spec()] * (7 + len(conds)) + [any_spec()] * 5,
        out_specs=out_specs,
        scratch_shapes=scratch,
        compiler_params=pltpu.CompilerParams(
            collective_id=1 + 2 * layer + int(save), has_side_effects=True, vmem_limit_bytes=LIMIT
        ),
        name="layer_forward",
    )(rows, gain, bias, *conds, bdown, cosine, sine, neg, *weights)


def backward_kernel(layer, heads, deep, carried, refs):
    (dx_ref, x_ref, x1_ref, gain_ref, cond_ref, cos_ref, sin_ref, neg_ref, lse_ref) = refs[:9]
    refs = refs[9:]
    if carried:
        carry_ref, refs = refs[0], refs[1:]
    hbm = refs[:13]
    (wqkv_hbm, wout_hbm, wup_hbm, wdown_hbm, wada_hbm) = hbm[:5]
    refs = refs[13:]
    saved_hbm = hbm[5:13]
    (out_ref, small_ref, attn_out, feed_out) = refs[:4]
    refs = refs[4:]
    if carried:
        carry_out, refs = refs[0], refs[1:]
    (wq, wk, wv, wout, wup, wdown, abuf, qb, kb, vb, ob, mbuf, gb, gpb) = refs[:14]
    first = refs[14:21]
    second = refs[21:28]
    (wqk, dhb, qmask, domask, dsb, pb, dkb, dvb, dqk, dvv, total, own, dx1) = refs[28:41]
    (feed_grads, attn_grads) = refs[41:43]
    refs = refs[43:]
    (send, recv, send2, recv2, lsem, osem) = refs[:6]
    refs = refs[6:]
    ids = neighbours()
    sums = []
    if deep:
        spot = Spot(deep)
        meet([*ids, *spot.partners()])
        up_sum = DpSum(spot, feed_grads.at[0], feed_out.at[0], refs[0:3])
        down_sum = DpSum(spot, feed_grads.at[1], feed_out.at[1], refs[3:6])
        if carried:
            carry_sum = DpSum(spot, carry_ref, carry_out, refs[6:9])
            carry_sum.start()
    else:
        meet(ids)
    sources = [wqkv_hbm.at[layer, part] for part in range(3)]
    sources += [wout_hbm.at[layer], wup_hbm.at[layer], wdown_hbm.at[layer], *saved_hbm]
    places = (wq, wk, wv, wout, wup, wdown, abuf, qb, kb, vb, ob, mbuf, gb, gpb)
    loads = [
        pltpu.make_async_copy(src, dst, lsem.at[i])
        for i, (src, dst) in enumerate(zip(sources, places))
    ]
    for i in (5, 13, 4, 11, 12, 3, 7, 8, 9, 0, 1, 2, 6, 10):
        loads[i].start()
    feed = Group((send, recv), ids, *first)
    attn = Group((send2, recv2), ids, *second)
    ebuf, fbuf = first[0], second[0]
    half = feed.half
    unit_rows = 2 * half
    width = x_ref.shape[1]
    columns = heads * HD
    for part in range(2):
        rows = pl.ds(part * half, half)
        ebuf[rows, :] = dx_ref[rows, :].astype(BF)
        feed.send(part)
    small_ref[...] = jnp.zeros_like(small_ref)
    small_ref[4:5, :] = jnp.sum(dx_ref[...].astype(F32), axis=0, keepdims=True)
    dkb[...] = jnp.zeros_like(dkb)
    dvb[...] = jnp.zeros_like(dvb)
    for i in (5, 13, 4):
        loads[i].wait()

    def contract(step, carry):
        feed.receive(step)
        unit = jnp.where(step < 2, step, 5 - step)
        rows = pl.ds(pl.multiple_of(unit * unit_rows, unit_rows), unit_rows)
        grad = dot(ebuf[rows, :], wdown[...], NT)
        grad = (grad * gpb[rows, :].astype(F32)).astype(BF)
        dhb[rows, :] = grad
        total[...] = dot(grad, wup[...], NT)
        feed.scatter(unit, total, own)
        return carry

    lax.fori_loop(0, 4, contract, 0)
    tiles = width // 256

    def outer(left, right, dst):
        def tile(index, carry):
            start = pl.multiple_of(index * 256, 256)
            dst[pl.ds(start, 256), :] = dot(left[:, pl.ds(start, 256)], right[...], TN).astype(BF)
            return carry

        lax.fori_loop(0, tiles, tile, 0)

    shift_sum = jnp.zeros((1, width), F32)
    scale_sum = jnp.zeros((1, width), F32)
    for part in range(2):
        if part == 0:
            loads[11].wait()
            outer(mbuf, dhb, feed_grads.at[0])
        else:
            loads[12].wait()
            outer(ebuf, gb, feed_grads.at[1])
        rows = pl.ds(part * half, half)
        grad = feed.collect(part, own)
        hat, rstd = norm(x1_ref[rows, :])
        shift_sum += jnp.sum(grad, axis=0, keepdims=True)
        scale_sum += jnp.sum(grad * hat, axis=0, keepdims=True)
        after = dx_ref[rows, :].astype(F32)
        after = after + norm_back(grad * (1.0 + cond_ref[:1, width:]), hat, rstd)
        dx1[rows, :] = after
        fbuf[rows, :] = after.astype(BF)
        attn.send(part)
    small_ref[0:1, :] = shift_sum
    small_ref[1:2, :] = scale_sum
    if deep:
        if carried:
            carry_sum.middle()
        up_sum.start()
        down_sum.start()
    for i in (3, 7, 8, 9):
        loads[i].wait()

    def turn_back(grad, rows, scale):
        cosine = cos_ref[rows, :]
        sine = sin_ref[rows, :]
        first_half = grad[:, :128]
        second_half = grad[:, 128:]
        return (
            ((first_half * cosine + second_half * sine) * scale).astype(BF),
            ((second_half * cosine - first_half * sine) * scale).astype(BF),
        )

    def attend(step, carry):
        attn.receive(step)
        unit = jnp.where(step < 2, step, 5 - step)
        rows = pl.ds(pl.multiple_of(unit * unit_rows, unit_rows), unit_rows)
        grad_out = dot(fbuf[rows, :], wout[...], NT).astype(BF)
        queries = qb[rows, :]
        grad_queries = jnp.zeros((unit_rows, 256), F32)
        for head in range(heads):
            place = pl.ds(head * unit_rows, unit_rows)
            masked = keep_head(queries, head, True)
            masked_out = keep_head(grad_out, head, False)
            qmask[place, :] = masked
            domask[place, :] = masked_out
            scores = dot(kb[...], masked, NT).reshape(8, half, unit_rows)
            shares = jnp.exp(scores - (lse_ref[unit, head : head + 1, :] - neg_ref[unit]))
            shares = shares.reshape(8 * half, unit_rows)
            grad_shares = dot(vb[...], masked_out, NT)
            centre = jnp.sum(shares * grad_shares, axis=0, keepdims=True)
            grad_scores = (shares * (grad_shares - centre)).astype(BF)
            pb[:, place] = shares.astype(BF)
            dsb[:, place] = grad_scores
            grad_queries = grad_queries + dot(grad_scores, keep_head(kb[...], head, True), TN)
        dkb[...] += dot(dsb[...], qmask[...])
        dvb[...] += dot(pb[...], domask[...])
        low, high = turn_back(grad_queries, rows, HD**-0.5)
        dqk[rows, :128] = low
        dqk[rows, 128:256] = high
        return carry

    lax.fori_loop(0, 4, attend, 0)
    if deep:
        if carried:
            carry_sum.end()
        up_sum.middle()
    for i in (0, 1, 2):
        loads[i].wait()
    load_turned(wq, wk, wqk)

    def spread(step, carry):
        unit = 3 - step
        rows = pl.ds(pl.multiple_of(unit * unit_rows, unit_rows), unit_rows)
        low, high = turn_back(dkb[rows, :], rows, 1.0)
        dqk[rows, 256:384] = low
        dqk[rows, 384:512] = high
        values = dvb[rows, :].astype(BF)
        dvv[rows, :] = values
        total[...] = dot(dqk[rows, :], wqk[...], NT) + dot(values, wv[...], NT)
        attn.scatter(unit, total, own)
        return carry

    lax.fori_loop(0, 4, spread, 0)
    loads[6].wait()
    loads[10].wait()
    places = (
        turned_place(columns, 0, 4 * columns),
        turned_place(columns, columns, 4 * columns),
        plain_place(columns, 2 * columns, 4 * columns),
        plain_place(columns, 3 * columns, 4 * columns),
    )

    def attn_tile(index, carry):
        start = pl.multiple_of(index * 256, 256)
        normed = abuf[:, pl.ds(start, 256)]
        both = dot(normed, dqk[...], TN).astype(BF)
        made = dot(both[:, :256], places[0]) + dot(both[:, 256:], places[1])
        made = made + dot(dot(normed, dvv[...], TN).astype(BF), places[2])
        outs = dot(fbuf[:, pl.ds(start, 256)], ob[...], TN).astype(BF)
        attn_grads[pl.ds(start, 256), :] = (made + dot(outs, places[3])).astype(BF)
        return carry

    lax.fori_loop(0, tiles, attn_tile, 0)
    store = pltpu.make_async_copy(attn_grads, attn_out, osem.at[0])
    store.start()
    if deep:
        down_sum.middle()
    gain_sum = jnp.zeros((1, width), F32)
    bias_sum = jnp.zeros((1, width), F32)
    for part in range(2):
        rows = pl.ds(part * half, half)
        grad = attn.collect(part, own)
        hat, rstd = norm(x_ref[rows, :])
        gain_sum += jnp.sum(grad * hat, axis=0, keepdims=True)
        bias_sum += jnp.sum(grad, axis=0, keepdims=True)
        out_ref[rows, :] = dx1[rows, :] + norm_back(grad * gain_ref[...], hat, rstd)
    small_ref[2:3, :] = gain_sum
    small_ref[3:4, :] = bias_sum
    if deep:
        up_sum.end()
        down_sum.end()
    else:
        whole = pltpu.make_async_copy(feed_grads, feed_out, osem.at[1])
        whole.start()
        whole.wait()
    feed.finish()
    attn.finish()
    store.wait()


def backward_layer(layer, heads, deep, grad_rows, rows, gain, cond, tables, weights, saved, carry):
    cosine, sine, neg = tables
    (normed, queries, keys, values, logs, attended, after, modulated, gated, slope) = saved
    block, width = rows.shape
    length = 4 * block
    units = weights[2].shape[2]
    columns = heads * HD
    part = width // (2 * deep) if deep else 0
    held = [normed, queries, keys, values, attended, modulated, gated, slope]
    scratch = [pltpu.VMEM((width, columns), BF)] * 3
    scratch += [pltpu.VMEM(each.shape[1:], BF) for each in weights[1:4]]
    scratch += [pltpu.VMEM(each.shape, BF) for each in held]
    scratch += group_scratch(length, width) + group_scratch(length, width)
    scratch += [
        pltpu.VMEM((width, 512), BF),
        pltpu.VMEM((length, units), BF),
        pltpu.VMEM((heads * block, 256), BF),
        pltpu.VMEM((heads * block, columns), BF),
        pltpu.VMEM((length, heads * block), BF),
        pltpu.VMEM((length, heads * block), BF),
        pltpu.VMEM((length, 256), F32),
        pltpu.VMEM((length, columns), F32),
        pltpu.VMEM((length, 512), BF),
        pltpu.VMEM((length, columns), BF),
        pltpu.VMEM((block, width), F32),
        pltpu.VMEM((block, width), F32),
        pltpu.VMEM((block, width), F32),
        pltpu.VMEM((2, width, units), BF),
        pltpu.VMEM((width, 4 * columns), BF),
    ]
    scratch += [pltpu.SemaphoreType.DMA((6, 2))] * 4
    scratch += [pltpu.SemaphoreType.DMA((14,)), pltpu.SemaphoreType.DMA((2,))]
    carried = carry is not None
    if deep:
        scratch += DpSum.scratch(deep, part, units) + DpSum.scratch(deep, part, units)
        if carried:
            scratch += DpSum.scratch(deep, part, 4 * columns)
    out_shape = [
        jax.ShapeDtypeStruct((block, width), F32),
        jax.ShapeDtypeStruct((8, width), F32),
        jax.ShapeDtypeStruct((width, 4 * columns), BF),
        jax.ShapeDtypeStruct((2, part, units), F32)
        if deep
        else jax.ShapeDtypeStruct((2, width, units), BF),
    ]
    out_specs = [vmem_spec(), vmem_spec(), any_spec(), vmem_spec() if deep else any_spec()]
    more = []
    if carried:
        more.append(carry)
        out_shape.append(jax.ShapeDtypeStruct((part, 4 * columns), F32))
        out_specs.append(vmem_spec())

    def kernel(*refs):
        backward_kernel(layer, heads, deep, carried, refs)

    return pl.pallas_call(
        kernel,
        out_shape=out_shape,
        in_specs=[vmem_spec()] * (9 + len(more)) + [any_spec()] * 13,
        out_specs=out_specs,
        scratch_shapes=scratch,
        compiler_params=pltpu.CompilerParams(
            collective_id=9 + layer, has_side_effects=True, vmem_limit_bytes=LIMIT
        ),
        name="layer_backward",
    )(grad_rows, rows, after, gain, cond, cosine, sine, neg, logs, *more, *weights, *held)


class Ladder:
    def __init__(self, spot, ids, sems, sem_count):
        self.spot, self.ids = spot, ids
        self.send, self.recv = sems
        self.used = 0
        self.count = sem_count
        self.open = []

    def copy(self, src, dst, device):
        made = pltpu.make_async_remote_copy(
            src_ref=src,
            dst_ref=dst,
            send_sem=self.send.at[self.used],
            recv_sem=self.recv.at[self.used],
            device_id=device,
            device_id_type=MESH,
        )
        self.used += 1
        assert self.used <= self.count
        made.start()
        self.open.append(made)
        return made

    def finish(self):
        for each in self.open:
            each.wait_send()


SELF_COPIES = 32


def tail_kernel(deep, carried, refs):
    (dx_ref, joined_ref, small_ref, small2_ref, temb_ref, carry_ref) = refs[:6]
    (sum_ref, vec_ref, carry_out) = refs[6:9]
    (ebuf, jbuf, part, near_out, near_in, next_out, next_in, z_out, z_in, mid, result, vecs) = refs[
        9:21
    ]
    (send, recv, osem) = refs[21:24]
    ids = neighbours()
    sibling, far = ids
    spot = Spot(deep)
    meet([*ids, *spot.partners()])
    place = lax.axis_index("tensor")
    core = lax.rem(place, 2)
    y = place // 2
    x, z = spot.x, spot.z
    block, width = dx_ref.shape
    ladder = Ladder(spot, ids, (send, recv), SELF_COPIES)
    ebuf[0] = dx_ref[...].astype(BF)
    rows_copy = ladder.copy(ebuf.at[0], ebuf.at[1], sibling)
    joined_copy = ladder.copy(joined_ref.at[1 - core], jbuf.at[1], sibling)
    mine = vecs.at[core, y, x, z]
    stacked = jnp.concatenate([small_ref[...], small2_ref[...]], axis=0)
    row = lax.broadcasted_iota(jnp.int32, stacked.shape, 0)
    mine[...] = jnp.where(row == 5, temb_ref[...], stacked).astype(BF)
    vec_z = [ladder.copy(mine, mine, spot.along(ahead)) for ahead in range(1, deep)]
    jbuf[0] = joined_ref[core]
    rows_copy.wait_recv()
    joined_copy.wait_recv()
    rest = width // 2
    tiles = width // 256

    def tile(index, carry):
        start = pl.multiple_of(index * 256, 256)
        made = dot(jbuf[0, :, pl.ds(start, 256)], ebuf[0], TN)
        made = made + dot(jbuf[1, :, pl.ds(start, 256)], ebuf[1], TN)
        part[0, pl.ds(start, 256), :] = made[:, :rest]
        part[1, pl.ds(start, 256), :] = made[:, rest:]
        return carry

    lax.fori_loop(0, tiles, tile, 0)

    def span(start, size):
        return pl.ds(pl.multiple_of(start, size), size)

    half, quarter = width // 2, width // 4
    piece = quarter // deep
    ways = (((far, y), (spot.across, x)), ((spot.across, x), (far, y)))
    firsts = []
    for side, ((device, bit), _) in enumerate(ways):
        near_out[side] = part[side, span((1 - bit) * half, half), :].astype(BF)
        firsts.append(ladder.copy(near_out.at[side], near_in.at[side], device))
    if carried:
        carry_sum = DpSum(spot, carry_ref, carry_out, refs[24:27])
        carry_sum.start()
    for each in vec_z:
        each.wait_recv()
    row_z = vecs.at[core, y, x]
    vec_x = ladder.copy(row_z, row_z, spot.across)
    seconds = []
    for side, ((_, bit), (device, bit2)) in enumerate(ways):
        firsts[side].wait_recv()
        total = part[side, span(bit * half, half), :] + near_in[side].astype(F32)
        part[side, span(bit * half, half), :] = total
        send_rows = span(bit * half + (1 - bit2) * quarter, quarter)
        next_out[side] = part[side, send_rows, :].astype(BF)
        seconds.append(ladder.copy(next_out.at[side], next_in.at[side], device))
    vec_x.wait_recv()
    plane = vecs.at[core, y]
    vec_y = ladder.copy(plane, plane, far)
    thirds = []
    for side, ((_, bit), (_, bit2)) in enumerate(ways):
        seconds[side].wait_recv()
        start = bit * half + bit2 * quarter
        total = part[side, span(start, quarter), :] + next_in[side].astype(F32)
        mid[side] = total
        z_out[side] = total.astype(BF).reshape(deep, piece, rest)
        for ahead in range(1, deep):
            thirds.append(
                ladder.copy(
                    z_out.at[side, spot.level(ahead)], z_in.at[side, ahead - 1], spot.along(ahead)
                )
            )
    if carried:
        carry_sum.middle()
    vec_y.wait_recv()
    every = vecs.at[core]
    vec_core = ladder.copy(every, every, sibling)
    lasts = []
    for side, ((_, bit), (_, bit2)) in enumerate(ways):
        for ahead in range(1, deep):
            thirds[side * (deep - 1) + ahead - 1].wait_recv()
        total = mid[side, span(z * piece, piece), :]
        for ahead in range(1, deep):
            total = total + z_in[side, ahead - 1].astype(F32)
        own = result.at[core, side, span(bit * half + bit2 * quarter + z * piece, piece)]
        own[...] = total.astype(BF)
        lasts += [ladder.copy(own, own, spot.along(ahead)) for ahead in range(1, deep)]
    backs = []
    for side, ((_, bit), (device, bit2)) in enumerate(ways):
        for ahead in range(1, deep):
            lasts[side * (deep - 1) + ahead - 1].wait_recv()
        own = result.at[core, side, span(bit * half + bit2 * quarter, quarter)]
        backs.append(ladder.copy(own, own, device))
    ends = []
    for side, ((device, bit), _) in enumerate(ways):
        backs[side].wait_recv()
        own = result.at[core, side, span(bit * half, half)]
        ends.append(ladder.copy(own, own, device))
    if carried:
        carry_sum.end()
    vec_core.wait_recv()
    vec_store = pltpu.make_async_copy(vecs, vec_ref, osem.at[0])
    vec_store.start()
    for each in ends:
        each.wait_recv()
    whole = ladder.copy(result.at[core], result.at[core], sibling)
    whole.wait_recv()
    sum_store = pltpu.make_async_copy(result, sum_ref, osem.at[1])
    sum_store.start()
    ladder.finish()
    vec_store.wait()
    sum_store.wait()


def tail(deep, grad_rows, joined, smalls, temb, carry):
    block, width = grad_rows.shape
    half, quarter = width // 2, width // 4
    piece = quarter // deep
    part = width // (2 * deep)
    vec_shape = (2, 2, 2, deep, 16, width)
    scratch = [
        pltpu.VMEM((2, block, width), BF),
        pltpu.VMEM((2, block, width), BF),
        pltpu.VMEM((2, width, half), F32),
        pltpu.VMEM((2, half, half), BF),
        pltpu.VMEM((2, half, half), BF),
        pltpu.VMEM((2, quarter, half), BF),
        pltpu.VMEM((2, quarter, half), BF),
        pltpu.VMEM((2, deep, piece, half), BF),
        pltpu.VMEM((2, deep - 1, piece, half), BF),
        pltpu.VMEM((2, quarter, half), F32),
        pltpu.VMEM((2, 2, width, half), BF),
        pltpu.VMEM(vec_shape, BF),
        pltpu.SemaphoreType.DMA((SELF_COPIES,)),
        pltpu.SemaphoreType.DMA((SELF_COPIES,)),
        pltpu.SemaphoreType.DMA((2,)),
    ]
    scratch += DpSum.scratch(deep, part, carry.shape[1])

    def kernel(*refs):
        tail_kernel(deep, True, refs)

    return pl.pallas_call(
        kernel,
        out_shape=[
            jax.ShapeDtypeStruct((2, 2, width, half), BF),
            jax.ShapeDtypeStruct(vec_shape, BF),
            jax.ShapeDtypeStruct((part, carry.shape[1]), F32),
        ],
        in_specs=[vmem_spec()] * 6,
        out_specs=[any_spec(), any_spec(), vmem_spec()],
        scratch_shapes=scratch,
        compiler_params=pltpu.CompilerParams(
            collective_id=20, has_side_effects=True, vmem_limit_bytes=LIMIT
        ),
        name="sum_tail",
    )(grad_rows, joined, *smalls, temb, carry)


def finish_kernel(depth, refs):
    (low_ref, wself_ref, sum_ref, vec_ref) = refs[:4]
    attn_refs = refs[4 : 4 + depth]
    feed_refs = refs[4 + depth : 4 + 2 * depth]
    (tokens_ref, small_ref, qkv_ref, out_ref, ada_ref, up_ref, down_ref, self_ref) = refs[
        4 + 2 * depth :
    ]
    step = pl.program_id(0)
    members = vec_ref.shape[0] // 16
    width = vec_ref.shape[1]

    def pick(row):
        device = lax.broadcasted_iota(jnp.int32, (members, vec_ref.shape[0]), 0)
        column = lax.broadcasted_iota(jnp.int32, (members, vec_ref.shape[0]), 1)
        wanted = (column == device * 16 + row).astype(F32).astype(BF)
        return dot(wanted, vec_ref[...]).astype(BF)

    rows = ada_ref.shape[1]
    times = pick(5)
    device = lax.broadcasted_iota(jnp.int32, (width, rows), 0)
    column = lax.broadcasted_iota(jnp.int32, (width, rows), 1)
    chosen = (device == column + step * rows).astype(F32).astype(BF)
    times = dot(times, chosen).astype(BF)
    for layer in range(depth):
        for place in range(2):
            ada_ref[layer, :, place * width : (place + 1) * width] = dot(
                times, pick(8 * layer + place), TN
            )
    self_ref[:, : width // 2] = sum_ref[0].astype(F32)
    self_ref[:, width // 2 :] = sum_ref[1].astype(F32)

    @pl.when(step == 0)
    def _():
        row = lax.broadcasted_iota(jnp.int32, (16, vec_ref.shape[0]), 0)
        column = lax.broadcasted_iota(jnp.int32, (16, vec_ref.shape[0]), 1)
        small_ref[...] = dot((column % 16 == row).astype(F32).astype(BF), vec_ref[...])

    @pl.when(step == 1)
    def _():
        tokens_ref[...] = dot(low_ref[...].astype(BF), wself_ref[...], NT)

    @pl.when(step == 2)
    def _():
        for layer in range(depth):
            grads = attn_refs[layer][...]
            columns = grads.shape[1] // 4
            for place in range(3):
                qkv_ref[layer, place] = grads[:, place * columns : (place + 1) * columns]
            out_ref[layer] = grads[:, 3 * columns :].T

    @pl.when(step == 3)
    def _():
        for layer in range(depth):
            up_ref[layer] = feed_refs[layer][0]
            down_ref[layer] = feed_refs[layer][1].T


def finish(depth, low, w_self, sums, vectors, attn_shards, feed_shards):
    block, width = low.shape
    part, columns = attn_shards[0].shape
    columns //= 4
    units = feed_shards[0].shape[2]
    steps = 4
    rows = 2 * width // steps

    def fixed(shape):
        return pl.BlockSpec(shape, lambda step: (0,) * len(shape))

    def kernel(*refs):
        finish_kernel(depth, refs)

    return pl.pallas_call(
        kernel,
        grid=(steps,),
        out_shape=[
            jax.ShapeDtypeStruct((block, width), F32),
            jax.ShapeDtypeStruct((16, width), F32),
            jax.ShapeDtypeStruct((depth, 3, part, columns), F32),
            jax.ShapeDtypeStruct((depth, columns, part), F32),
            jax.ShapeDtypeStruct((depth, width, 2 * width), F32),
            jax.ShapeDtypeStruct((depth, part, units), F32),
            jax.ShapeDtypeStruct((depth, units, part), F32),
            jax.ShapeDtypeStruct((2 * width, width), F32),
        ],
        in_specs=[
            fixed((block, width)),
            fixed((width, width)),
            pl.BlockSpec((None, 2, rows, width // 2), lambda step: (step // 2, 0, step % 2, 0)),
            fixed(vectors.shape),
            *[fixed(each.shape) for each in attn_shards],
            *[fixed(each.shape) for each in feed_shards],
        ],
        out_specs=[
            fixed((block, width)),
            fixed((16, width)),
            fixed((depth, 3, part, columns)),
            fixed((depth, columns, part)),
            pl.BlockSpec((depth, width // steps, 2 * width), lambda step: (0, step, 0)),
            fixed((depth, part, units)),
            fixed((depth, units, part)),
            pl.BlockSpec((rows, width), lambda step: (step, 0)),
        ],
        compiler_params=pltpu.CompilerParams(vmem_limit_bytes=LIMIT),
        name="write_grads",
    )(low, w_self, sums, vectors, *attn_shards, *feed_shards)


def local(
    tokens,
    cotangent,
    lengths,
    timesteps,
    w_self,
    ln_gain,
    ln_bias,
    w_qkv,
    w_out,
    w_ada,
    b_ada,
    w_up,
    w_down,
    b_down,
):
    hp = lax.Precision.HIGHEST
    block, width = tokens.shape
    depth = w_qkv.shape[0]
    heads = w_qkv.shape[3] // HD
    groups = lax.axis_size("dp")
    deep = 4 if groups == 8 else 0
    place = lax.axis_index("tensor")
    core = place % 2
    sibling = place + 1 - 2 * core
    far = (place + 2) % 4
    far_other = (sibling + 2) % 4
    half = block // 2
    owners = jnp.stack([place, place, sibling, sibling, far, far_other, far, far_other])
    halves = jnp.array([0, 1, 0, 1, 1, 1, 0, 0], jnp.int32)
    starts = owners * block + halves * half
    index = (starts[:, None] + jnp.arange(half, dtype=jnp.int32)).reshape(-1)
    packed = lengths[0, 0] < 4 * block
    position = jnp.where(packed, index % block, index)
    lanes = jnp.arange(128) % HALF
    freqs = jnp.exp(-jnp.log(10000.0) * lanes.astype(F32) / HALF)
    angle = position.astype(F32)[:, None] * freqs
    cosine = jnp.cos(angle)
    sine = jnp.sin(angle)
    chunk = jnp.array([0, 0, 1, 1, 2, 3, 2, 3], jnp.int32)
    apart = (chunk[:, None] != chunk[None, :]).astype(F32) * jnp.where(packed, -1e9, 0.0)
    neg_keys = jnp.repeat(apart, half, axis=1).reshape(4, 2, 1, 4 * block)
    neg_queries = jnp.repeat(apart, half, axis=1).reshape(8, 4, 1, block).swapaxes(0, 1)
    slot = jnp.where(packed, place, 0)
    freqs = jnp.exp(-jnp.log(10000.0) * jnp.arange(width // 2).astype(F32) / (width // 2))
    angle = lax.dynamic_slice_in_dim(timesteps, slot, 1, 1).astype(F32) * freqs
    temb = jnp.concatenate([jnp.cos(angle), jnp.sin(angle)], axis=-1)
    weights = (w_qkv, w_out, w_up, w_down, w_ada)

    def run(rows, conds):
        kept = []
        for layer in range(depth):
            save = conds is not None
            cond = conds[layer] if save else (temb.reshape(width, 1), b_ada[layer][None])
            small = (ln_gain[layer][None], ln_bias[layer][None], cond, b_down[layer][None])
            made = forward_layer(
                layer, save, heads, rows, small, (cosine, sine, neg_keys), weights
            )
            kept.append((rows, made[1:]))
            rows = made[0]
        return (rows, kept)

    start = jnp.dot(tokens, w_self[:width], preferred_element_type=F32)
    rows, kept = run(start, None)
    conds = [each[1][0] for each in kept]
    estimate = rows.astype(BF)
    start = start + jnp.dot(estimate, w_self[width:], preferred_element_type=F32)
    rows, kept = run(start, conds)
    activations = rows.astype(BF)
    grad_rows = cotangent
    smalls = [None] * depth
    attn_shards = [None] * depth
    feed_shards = [None] * depth
    carry = None
    for layer in reversed(range(depth)):
        rows_in, saved = kept[layer]
        made = backward_layer(
            layer,
            heads,
            deep,
            grad_rows,
            rows_in,
            ln_gain[layer][None],
            conds[layer],
            (cosine, sine, neg_queries),
            weights,
            saved,
            carry,
        )
        grad_rows, smalls[layer], attn_grads, feed_shards[layer] = made[:4]
        if deep:
            if carry is not None:
                attn_shards[layer + 1] = made[4]
            carry = attn_grads
        else:
            attn_shards[layer] = lax.psum_scatter(
                attn_grads, "dp", scatter_dimension=0, tiled=True
            ).astype(F32)
            feed_shards[layer] = lax.psum_scatter(
                feed_shards[layer], "dp", scatter_dimension=1, tiled=True
            ).astype(F32)
    if deep:
        joined = jnp.stack([tokens, estimate])
        sums, vectors, attn_shards[0] = tail(deep, grad_rows, joined, smalls, temb, carry)
        vectors = vectors.reshape(-1, width)
    else:
        joined = jnp.concatenate([tokens, estimate], axis=1)
        sums = lax.psum(dot(joined, grad_rows.astype(BF), TN).astype(BF), ("dp", "tensor"))
        sums = sums.reshape(2, width, 2, width // 2).swapaxes(1, 2)
        vectors = jnp.concatenate(smalls, axis=0).at[5].set(temb[0]).astype(BF)
        vectors = lax.all_gather(vectors, ("dp", "tensor"), axis=0, tiled=True)
    (grad_tokens, totals, grad_qkv, grad_out, grad_ada, grad_up, grad_down, grad_self) = finish(
        depth, grad_rows, w_self, sums, vectors, attn_shards, feed_shards
    )
    totals = totals.reshape(depth, 8, width)
    return (
        activations,
        grad_tokens,
        totals[:, 2],
        totals[:, 3],
        grad_qkv,
        grad_out,
        grad_ada,
        totals[:, :2].reshape(depth, 2 * width),
        grad_up,
        grad_down,
        totals[:, 4],
        grad_self,
    )


def solution(mesh):
    return jax.shard_map(
        local,
        mesh=mesh,
        in_specs=(
            P(("dp", "tensor"), None),
            P(("dp", "tensor"), None),
            P("dp", None),
            P("dp", None),
            P(),
            P(),
            P(),
            P(None, None, None, "tensor"),
            P(None, "tensor", None),
            P(),
            P(),
            P(None, None, "tensor"),
            P(None, "tensor", None),
            P(),
        ),
        out_specs=(
            P(("dp", "tensor"), None),
            P(("dp", "tensor"), None),
            P(),
            P(),
            P(None, None, "dp", "tensor"),
            P(None, "tensor", "dp"),
            P(),
            P(),
            P(None, "dp", "tensor"),
            P(None, "tensor", "dp"),
            P(),
            P(),
        ),
        check_vma=False,
    )
```

```python
import functools

import jax
import jax.numpy as jnp
from jax import lax
from jax.experimental import pallas as pl
from jax.experimental.pallas import tpu as pltpu
from jax.sharding import PartitionSpec as P

HD = 64
HALF = HD // 2
BF = jnp.bfloat16
F32 = jnp.float32
MESH = pl.DeviceIdType.MESH
EPS = 1e-05
LIMIT = 60 << 20


def norm(rows):
    centred = rows - jnp.mean(rows, axis=-1, keepdims=True)
    rstd = lax.rsqrt(jnp.mean(centred * centred, axis=-1, keepdims=True) + EPS)
    return (centred * rstd, rstd)


def norm_back(grad, hat, rstd):
    return rstd * (
        grad
        - jnp.mean(grad, axis=-1, keepdims=True)
        - hat * jnp.mean(grad * hat, axis=-1, keepdims=True)
    )


def dot(left, right, dims=((1,), (0,))):
    return lax.dot_general(left, right, (dims, ((), ())), preferred_element_type=F32)


NT = ((1,), (1,))
TN = ((0,), (0,))


def head_mask(head, columns, rotary):
    lane = lax.broadcasted_iota(jnp.int32, (1, columns), 1)
    if rotary:
        return (lane % 128) // HALF == head
    return lane // HD == head


def keep_head(rows, head, rotary):
    return jnp.where(head_mask(head, rows.shape[1], rotary), rows, jnp.zeros_like(rows))


def turned_place(columns, start, total):
    row = lax.broadcasted_iota(jnp.int32, (256, total), 0)
    column = lax.broadcasted_iota(jnp.int32, (256, total), 1) - start
    source = column // HD * HALF + column % HD // HALF * 128 + column % HALF
    fits = (source == row) & (column >= 0) & (column < columns)
    return fits.astype(F32).astype(BF)


def plain_place(columns, start, total):
    row = lax.broadcasted_iota(jnp.int32, (columns, total), 0)
    column = lax.broadcasted_iota(jnp.int32, (columns, total), 1) - start
    return (row == column).astype(F32).astype(BF)


class Group:
    def __init__(self, sems, ids, gathered, pair_out, pair_in, own_out, own_in, far_out, far_in):
        self.sems = sems
        self.ids = ids
        self.gathered = gathered
        self.pair_out, self.pair_in = pair_out, pair_in
        self.own_out, self.own_in = own_out, own_in
        self.far_out, self.far_in = far_out, far_in
        self.half = gathered.shape[0] // 8

    def copy(self, src, dst, kind, part, far):
        send, recv = self.sems
        return pltpu.make_async_remote_copy(
            src_ref=src,
            dst_ref=dst,
            send_sem=send.at[kind, part],
            recv_sem=recv.at[kind, part],
            device_id=self.ids[1] if far else self.ids[0],
            device_id_type=MESH,
        )

    def rows(self, start):
        return pl.ds(pl.multiple_of(start, self.half), self.half)

    def pair(self, part):
        return 6 * self.half - 2 * self.half * part

    def far_copy(self, part):
        own = self.gathered.at[self.rows(part * self.half)]
        return self.copy(own, self.gathered.at[self.rows(self.pair(part))], 0, part, True)

    def sibling_copy(self, part):
        own = self.gathered.at[self.rows(part * self.half)]
        place = self.gathered.at[self.rows((2 + part) * self.half)]
        return self.copy(own, place, 1, part, False)

    def forward_copy(self, part):
        src = self.gathered.at[self.rows(self.pair(part))]
        dst = self.gathered.at[self.rows(self.pair(part) + self.half)]
        return self.copy(src, dst, 2, part, False)

    def send(self, part):
        self.far_copy(part).start()
        self.sibling_copy(part).start()

    def receive(self, step):
        @pl.when(step == 1)
        def _():
            self.sibling_copy(0).wait_recv()
            self.sibling_copy(1).wait_recv()

        @pl.when(step >= 2)
        def _():
            part = step - 2
            self.far_copy(part).wait_recv()
            self.forward_copy(part).start()
            self.forward_copy(part).wait()

    def pair_copy(self, part):
        return self.copy(self.pair_out.at[part], self.pair_in.at[part], 3, part, False)

    def own_copy(self):
        return self.copy(self.own_out, self.own_in, 4, 0, False)

    def sum_copy(self, part):
        return self.copy(self.far_out.at[part], self.far_in.at[part], 5, part, True)

    def scatter(self, unit, total, own):
        @pl.when(unit == 0)
        def _():
            own[...] = total[...]

        @pl.when(unit == 1)
        def _():
            self.own_out[...] = total[...].astype(BF)
            self.own_copy().start()

        @pl.when(unit >= 2)
        def _():
            part = 3 - unit
            self.pair_out[part] = total[self.half :, :].astype(BF)
            self.pair_copy(part).start()
            self.pair_copy(part).wait_recv()
            self.far_out[part] = (
                total[: self.half, :] + self.pair_in[part].astype(F32)
            ).astype(BF)
            self.sum_copy(part).start()

    def collect(self, part, own):
        if part == 0:
            self.own_copy().wait_recv()
        self.sum_copy(part).wait_recv()
        rows = pl.ds(part * self.half, self.half)
        return own[rows, :] + self.own_in[rows, :].astype(F32) + self.far_in[part].astype(F32)

    def finish(self):
        for part in range(2):
            self.far_copy(part).wait_send()
            self.sibling_copy(part).wait_send()
            self.pair_copy(part).wait_send()
            self.sum_copy(part).wait_send()
        self.own_copy().wait_send()


def neighbours():
    group = lax.axis_index("dp")
    place = lax.axis_index("tensor")
    core = lax.rem(place, 2)
    return ((group, place + 1 - 2 * core), (group, lax.rem(place + 2, 4)))


class Spot:
    def __init__(self, deep):
        group = lax.axis_index("dp")
        self.place = lax.axis_index("tensor")
        self.deep = deep
        self.z = group // 2
        self.x = lax.rem(group, 2)
        self.across = (2 * self.z + 1 - self.x, self.place)

    def level(self, ahead):
        return lax.rem(self.z + ahead, self.deep)

    def along(self, ahead):
        return (2 * self.level(ahead) + self.x, self.place)

    def partners(self):
        return [self.across] + [self.along(ahead) for ahead in range(1, self.deep)]


def meet(ids):
    barrier = pltpu.get_barrier_semaphore()
    for device in ids:
        pl.semaphore_signal(barrier, inc=1, device_id=device, device_id_type=MESH)
    pl.semaphore_wait(barrier, len(ids))


class DpSum:
    def __init__(self, spot, src, out, scratch):
        self.spot, self.src, self.out = spot, src, out
        self.pairs, self.rest, self.sems = scratch
        self.block = self.pairs.shape[1]

    @staticmethod
    def scratch(deep, block, columns):
        return [
            pltpu.VMEM((deep, block, columns), BF),
            pltpu.VMEM((deep - 1, block, columns), BF),
            pltpu.SemaphoreType.DMA((4, deep)),
        ]

    def rows(self, ahead, x):
        start = (2 * self.spot.level(ahead) + x) * self.block
        return pl.ds(pl.multiple_of(start, self.block), self.block)

    def x_copy(self, ahead):
        return pltpu.make_async_remote_copy(
            src_ref=self.src.at[self.rows(ahead, 1 - self.spot.x)],
            dst_ref=self.pairs.at[ahead],
            send_sem=self.sems.at[0, ahead],
            recv_sem=self.sems.at[1, ahead],
            device_id=self.spot.across,
            device_id_type=MESH,
        )

    def z_copy(self, ahead):
        return pltpu.make_async_remote_copy(
            src_ref=self.pairs.at[ahead],
            dst_ref=self.rest.at[ahead - 1],
            send_sem=self.sems.at[2, ahead],
            recv_sem=self.sems.at[3, ahead],
            device_id=self.spot.along(ahead),
            device_id_type=MESH,
        )

    def order(self):
        return [*range(1, self.spot.deep), 0]

    def start(self):
        for ahead in self.order():
            self.x_copy(ahead).start()

    def middle(self):
        for ahead in self.order():
            self.x_copy(ahead).wait_recv()
            total = self.src[self.rows(ahead, self.spot.x), :].astype(F32)
            total = total + self.pairs[ahead].astype(F32)
            if ahead:
                self.pairs[ahead] = total.astype(BF)
                self.z_copy(ahead).start()
            else:
                self.out[...] = total
        for ahead in self.order():
            self.x_copy(ahead).wait_send()

    def end(self):
        for ahead in range(1, self.spot.deep):
            self.z_copy(ahead).wait_recv()
        total = self.out[...]
        for ahead in range(1, self.spot.deep):
            total = total + self.rest[ahead - 1].astype(F32)
        self.out[...] = total
        for ahead in range(1, self.spot.deep):
            self.z_copy(ahead).wait_send()


def group_scratch(rows, width):
    half = rows // 8
    return [
        pltpu.VMEM((rows, width), BF),
        pltpu.VMEM((2, half, width), BF),
        pltpu.VMEM((2, half, width), BF),
        pltpu.VMEM((2 * half, width), BF),
        pltpu.VMEM((2 * half, width), BF),
        pltpu.VMEM((2, half, width), BF),
        pltpu.VMEM((2, half, width), BF),
    ]


def gelu_parts(hidden):
    cdf = 0.5 * (1.0 + lax.erf(hidden * (0.5**0.5)))
    density = jnp.exp(hidden * hidden * -0.5) * 0.3989422804014327
    return (hidden * cdf, cdf + hidden * density)


def load_turned(wq, wk, wqk):
    turn = turned_place(wq.shape[1], 0, wq.shape[1])
    wqk[:, :256] = dot(wq[...], turn, NT).astype(BF)
    wqk[:, 256:] = dot(wk[...], turn, NT).astype(BF)


def forward_kernel(layer, save, heads, refs):
    (x_ref, gain_ref, bias_ref, cond_ref, bdown_ref, cos_ref, sin_ref, neg_ref) = refs[:8]
    (wqkv_hbm, wout_hbm, wup_hbm, wdown_hbm, wada_hbm) = refs[8:13]
    count = 10 if save else 1
    next_ref = refs[13]
    saves = refs[14 : 14 + count]
    scratch = refs[14 + count :]
    (wq, wk, wv, wout, wup, wdown, wada, wqk) = scratch[:8]
    first = scratch[8:15]
    second = scratch[15:22]
    (qb, kb, vb, lse, ob, x1, gb, gpb, total, own, cond) = scratch[22:33]
    (send, recv, send2, recv2, wsem, osem) = scratch[33:]
    ids = neighbours()
    meet(ids)
    sources = [wqkv_hbm.at[layer, part] for part in range(3)]
    sources += [wout_hbm.at[layer], wup_hbm.at[layer], wdown_hbm.at[layer]]
    places = [wq, wk, wv, wout, wup, wdown]
    if not save:
        sources.append(wada_hbm.at[layer])
        places.append(wada)
    loads = [
        pltpu.make_async_copy(src, dst, wsem.at[i])
        for i, (src, dst) in enumerate(zip(sources, places))
    ]
    for load in loads:
        load.start()
    attn = Group((send, recv), ids, *first)
    feed = Group((send2, recv2), ids, *second)
    abuf, mbuf = first[0], second[0]
    half = attn.half
    unit_rows = 2 * half
    width = x_ref.shape[1]
    for part in range(2):
        rows = pl.ds(part * half, half)
        hat = norm(x_ref[rows, :])[0]
        abuf[rows, :] = (hat * gain_ref[...] + bias_ref[...]).astype(BF)
        attn.send(part)
    for load in loads[:3]:
        load.wait()
    load_turned(wq, wk, wqk)

    def project(step, carry):
        attn.receive(step)
        unit = jnp.where(step < 2, step, 5 - step)
        rows = pl.ds(pl.multiple_of(unit * unit_rows, unit_rows), unit_rows)
        normed = abuf[rows, :]
        mixed = dot(normed, wqk[...])
        cosine = cos_ref[rows, :]
        sine = sin_ref[rows, :]
        for place, dst, scale in ((0, qb, HD**-0.5), (256, kb, 1.0)):
            first_half = mixed[:, place : place + 128]
            second_half = mixed[:, place + 128 : place + 256]
            dst[rows, :128] = ((first_half * cosine - second_half * sine) * scale).astype(BF)
            dst[rows, 128:] = ((second_half * cosine + first_half * sine) * scale).astype(BF)
        vb[rows, :] = dot(normed, wv[...]).astype(BF)
        return carry

    lax.fori_loop(0, 4, project, 0)
    loads[3].wait()
    lane = lax.broadcasted_iota(jnp.int32, (1, 128), 1)

    def attend(step, carry):
        unit = 3 - step
        rows = pl.ds(pl.multiple_of(unit * unit_rows, unit_rows), unit_rows)
        queries = qb[rows, :]
        columns = heads * HD
        attended = jnp.zeros((unit_rows, columns), F32)
        logs = jnp.zeros((unit_rows, 128), F32)
        for head in range(heads):
            scores = dot(keep_head(queries, head, True), kb[...], NT)
            scores = scores.reshape(2, half, 8 * half) + neg_ref[unit]
            scores = scores.reshape(unit_rows, 8 * half)
            largest = jnp.max(scores, axis=-1, keepdims=True)
            shares = jnp.exp(scores - largest)
            sums = jnp.sum(shares, axis=-1, keepdims=True)
            output = dot(shares.astype(BF), vb[...]) * (1.0 / sums)
            attended = jnp.where(head_mask(head, columns, False), output, attended)
            if save:
                logs = jnp.where(lane == head, largest + jnp.log(sums), logs)
        if save:
            lse[unit] = logs.T[:8, :]
        attended = attended.astype(BF)
        ob[rows, :] = attended
        total[...] = dot(attended, wout[...])
        attn.scatter(unit, total, own)
        return carry

    lax.fori_loop(0, 4, attend, 0)
    for load in loads[4:]:
        load.wait()
    if save:
        shift = cond_ref[:1, :width]
        scale = cond_ref[:1, width:]
    else:
        embedding, ada_bias = cond_ref
        made = jnp.sum(wada[...] * embedding[...], axis=0, keepdims=True) + ada_bias[...]
        cond[...] = jnp.broadcast_to(made, cond.shape)
        shift = made[:, :width]
        scale = made[:, width:]
    for part in range(2):
        rows = pl.ds(part * half, half)
        after = x_ref[rows, :] + attn.collect(part, own)
        x1[rows, :] = after
        mbuf[rows, :] = (norm(after)[0] * (1.0 + scale) + shift).astype(BF)
        feed.send(part)

    def expand(step, carry):
        feed.receive(step)
        unit = jnp.where(step < 2, step, 5 - step)
        rows = pl.ds(pl.multiple_of(unit * unit_rows, unit_rows), unit_rows)
        hidden = dot(mbuf[rows, :], wup[...])
        gated, slope = gelu_parts(hidden)
        gated = gated.astype(BF)
        if save:
            gb[rows, :] = gated
            gpb[rows, :] = slope.astype(BF)
        total[...] = dot(gated, wdown[...])
        feed.scatter(unit, total, own)
        return carry

    lax.fori_loop(0, 4, expand, 0)
    stores = []
    made = (abuf, qb, kb, vb, lse, ob, x1, mbuf, gb, gpb) if save else (cond,)
    for i, (src, dst) in enumerate(zip(made, saves)):
        stores.append(pltpu.make_async_copy(src, dst, osem.at[i]))
        stores[-1].start()
    for part in range(2):
        rows = pl.ds(part * half, half)
        next_ref[rows, :] = x1[rows, :] + feed.collect(part, own) + bdown_ref[...]
    attn.finish()
    feed.finish()
    for store in stores:
        store.wait()


def any_spec():
    return pl.BlockSpec(memory_space=pl.ANY)


def vmem_spec():
    return pl.BlockSpec(memory_space=pltpu.VMEM)


def forward_layer(layer, save, heads, rows, small, tables, weights):
    gain, bias, cond, bdown = small
    cosine, sine, neg = tables
    block, width = rows.shape
    length = 4 * block
    columns = heads * HD
    units = weights[2].shape[2]
    saved_shapes = [
        ((length, width), BF),
        ((length, 256), BF),
        ((length, 256), BF),
        ((length, columns), BF),
        ((4, 8, block), F32),
        ((length, columns), BF),
        ((block, width), F32),
        ((length, width), BF),
        ((length, units), BF),
        ((length, units), BF),
    ]
    if not save:
        saved_shapes = [((8, 2 * width), F32)]
    out_shape = [jax.ShapeDtypeStruct((block, width), F32)]
    out_specs = [vmem_spec()]
    out_shape += [jax.ShapeDtypeStruct(*each) for each in saved_shapes]
    out_specs += [any_spec()] * len(saved_shapes)
    scratch = [pltpu.VMEM((width, columns), BF)] * 3
    scratch += [pltpu.VMEM(each.shape[1:], BF) for each in weights[1:4]]
    scratch += [pltpu.VMEM((8, 128) if save else (width, 2 * width), F32)]
    scratch += [pltpu.VMEM((width, 512), BF)]
    scratch += group_scratch(length, width) + group_scratch(length, width)
    scratch += [
        pltpu.VMEM((length, 256), BF),
        pltpu.VMEM((length, 256), BF),
        pltpu.VMEM((length, columns), BF),
        pltpu.VMEM((4, 8, block), F32),
        pltpu.VMEM((length, columns), BF),
        pltpu.VMEM((block, width), F32),
        pltpu.VMEM((length, units) if save else (16, 128), BF),
        pltpu.VMEM((length, units) if save else (16, 128), BF),
        pltpu.VMEM((block, width), F32),
        pltpu.VMEM((block, width), F32),
        pltpu.VMEM((8, 2 * width), F32),
    ]
    scratch += [pltpu.SemaphoreType.DMA((6, 2))] * 4
    scratch += [pltpu.SemaphoreType.DMA((7,)), pltpu.SemaphoreType.DMA((10,))]

    def kernel(*refs):
        if not save:
            refs = (*refs[:3], refs[3:5], *refs[5:])
        forward_kernel(layer, save, heads, refs)

    conds = (cond,) if save else cond
    return pl.pallas_call(
        kernel,
        out_shape=out_shape,
        in_specs=[vmem_spec()] * (7 + len(conds)) + [any_spec()] * 5,
        out_specs=out_specs,
        scratch_shapes=scratch,
        compiler_params=pltpu.CompilerParams(
            collective_id=1 + 2 * layer + int(save), has_side_effects=True, vmem_limit_bytes=LIMIT
        ),
        name="layer_forward",
    )(rows, gain, bias, *conds, bdown, cosine, sine, neg, *weights)


class Ladder:
    def __init__(self, sems):
        self.send, self.recv = sems
        self.used = 0
        self.open = []

    def copy(self, src, dst, device):
        made = pltpu.make_async_remote_copy(
            src_ref=src,
            dst_ref=dst,
            send_sem=self.send.at[self.used],
            recv_sem=self.recv.at[self.used],
            device_id=device,
            device_id_type=MESH,
        )
        self.used += 1
        assert self.used <= LADDER_COPIES
        made.start()
        self.open.append(made)
        return made

    def finish(self):
        for each in self.open:
            each.wait_send()


LADDER_COPIES = 34


class Loads:
    def __init__(self, sems):
        self.sems = sems
        self.names = {}

    def add(self, name, sources, buffer):
        self.names[name] = (sources, buffer, len(self.names))
        return buffer

    def copy(self, name, layer):
        sources, buffer, place = self.names[name]
        return pltpu.make_async_copy(sources[layer], buffer, self.sems.at[place])

    def start(self, layer, *names):
        if layer >= 0:
            for name in names:
                self.copy(name, layer).start()

    def wait(self, layer, *names):
        for name in names:
            self.copy(name, layer).wait()


SAVED = ("a", "q", "k", "v", "o", "x1", "m", "g", "slope", "x")


def span(start, size):
    return pl.ds(pl.multiple_of(start, size), size)


def backward_kernel(depth, heads, deep, refs):
    refs = list(refs)

    def take(count):
        made = refs[:count]
        del refs[:count]
        return made

    cot_ref, gain_ref, cos_ref, sin_ref, neg_ref, temb_ref = take(6)
    cond_refs, lse_refs = take(depth), take(depth)
    joined_hbm = take(2)
    wqkv_hbm, wout_hbm, wup_hbm, wdown_hbm, _ = take(5)
    saved_hbm = [dict(zip(SAVED, take(len(SAVED)))) for _ in range(depth)]
    (out_ref, small_ref) = take(2)
    attn_outs, feed_outs = take(depth), take(depth)
    if deep:
        sum_ref, vec_ref = take(2)
    send, recv, send2, recv2, load_sems, store_sems = take(6)
    loads = Loads(load_sems)
    wq, wk, wv = (
        loads.add(name, [wqkv_hbm.at[layer, part] for layer in range(depth)], take(1)[0])
        for part, name in enumerate(("wq", "wk", "wv"))
    )
    wout, wup, wdown = (
        loads.add(name, [src.at[layer] for layer in range(depth)], take(1)[0])
        for name, src in (("wout", wout_hbm), ("wup", wup_hbm), ("wdown", wdown_hbm))
    )
    abuf, qb, kb, vb, ob, x1b, mbuf, gb, gpb, xb = (
        loads.add(name, [saved_hbm[layer][name] for layer in range(depth)], take(1)[0])
        for name in SAVED
    )
    first = take(7)
    second = take(7)
    (wqk, dhb, qmask, domask, dsb, pb, dkb, dvb, dqk, dvv, work, dxb) = take(12)
    (feed_grads, attn_grads) = take(2)
    ids = neighbours()
    sums = {}
    if deep:
        spot = Spot(deep)
        meet([*ids, *spot.partners()])
        for layer in range(depth):
            for name, src, out in (
                ("up", feed_grads.at[0], feed_outs[layer].at[0]),
                ("down", feed_grads.at[1], feed_outs[layer].at[1]),
                ("attn", attn_grads, attn_outs[layer]),
            ):
                sums[name, layer] = DpSum(spot, src, out, take(3))
        tail_refs = take(10)
        joined = tail_refs[0]
        joined_loads = [
            pltpu.make_async_copy(src, joined.at[i], store_sems.at[i])
            for i, src in enumerate(joined_hbm)
        ]
        for each in joined_loads:
            each.start()
    else:
        meet(ids)
    feed = Group((send, recv), ids, *first)
    attn = Group((send2, recv2), ids, *second)
    ebuf, fbuf = first[0], second[0]
    half = feed.half
    unit_rows = 2 * half
    width = cot_ref.shape[1]
    columns = heads * HD
    tiles = width // 256
    total, own, dx1 = (work.at[pl.ds(i * unit_rows, unit_rows)] for i in range(3))
    top = depth - 1
    for part in range(2):
        rows = pl.ds(part * half, half)
        ebuf[rows, :] = cot_ref[rows, :]
        feed.send(part)
    loads.start(top, "wdown", "slope", "wup", "m", "g", "x1", "wout", "q", "k", "v")
    loads.start(top, "wq", "wk", "wv", "a", "o", "x")
    dxb[...] = cot_ref[...].astype(F32)
    small_ref[...] = jnp.zeros_like(small_ref)

    def outer(left, right, dst):
        def tile(index, carry):
            place = span(index * 256, 256)
            dst[place, :] = dot(left[:, place], right[...], TN).astype(BF)
            return carry

        lax.fori_loop(0, tiles, tile, 0)

    def turn_back(grad, rows, scale):
        cosine = cos_ref[rows, :]
        sine = sin_ref[rows, :]
        first_half = grad[:, :128]
        second_half = grad[:, 128:]
        return (
            ((first_half * cosine + second_half * sine) * scale).astype(BF),
            ((second_half * cosine - first_half * sine) * scale).astype(BF),
        )

    def event(name, layer, kind):
        if (name, layer) in sums:
            getattr(sums[name, layer], kind)()

    for layer in reversed(range(depth)):
        lse_ref, cond_ref = lse_refs[layer], cond_refs[layer]

        def note(row, value):
            small_ref[8 * layer + row : 8 * layer + row + 1, :] = value

        note(4, jnp.sum(dxb[...], axis=0, keepdims=True))
        dkb[...] = jnp.zeros_like(dkb)
        dvb[...] = jnp.zeros_like(dvb)
        loads.wait(layer, "wdown", "slope", "wup")

        def contract(step, carry):
            feed.receive(step)
            unit = jnp.where(step < 2, step, 5 - step)
            rows = span(unit * unit_rows, unit_rows)
            grad = dot(ebuf[rows, :], wdown[...], NT)
            grad = (grad * gpb[rows, :].astype(F32)).astype(BF)
            dhb[rows, :] = grad
            total[...] = dot(grad, wup[...], NT)
            feed.scatter(unit, total, own)
            return carry

        lax.fori_loop(0, 4, contract, 0)
        loads.start(layer - 1, "wdown", "slope", "wup")
        event("attn", layer + 1, "middle")
        event("up", layer + 1, "end")
        if layer < top:
            attn.finish()
        shift_sum = jnp.zeros((1, width), F32)
        scale_sum = jnp.zeros((1, width), F32)
        for part in range(2):
            if part == 0:
                loads.wait(layer, "m", "x1")
                outer(mbuf, dhb, feed_grads.at[0])
                event("up", layer, "start")
            else:
                loads.wait(layer, "g")
                outer(ebuf, gb, feed_grads.at[1])
                event("down", layer, "start")
            rows = pl.ds(part * half, half)
            grad = feed.collect(part, own)
            hat, rstd = norm(x1b[rows, :])
            shift_sum += jnp.sum(grad, axis=0, keepdims=True)
            scale_sum += jnp.sum(grad * hat, axis=0, keepdims=True)
            after = dxb[rows, :]
            after = after + norm_back(grad * (1.0 + cond_ref[:1, width:]), hat, rstd)
            dx1[rows, :] = after
            fbuf[rows, :] = after.astype(BF)
            attn.send(part)
        note(0, shift_sum)
        note(1, scale_sum)
        loads.start(layer - 1, "m", "g", "x1")
        loads.wait(layer, "wout", "q", "k", "v")

        def attend(step, carry):
            attn.receive(step)
            unit = jnp.where(step < 2, step, 5 - step)
            rows = span(unit * unit_rows, unit_rows)
            grad_out = dot(fbuf[rows, :], wout[...], NT).astype(BF)
            queries = qb[rows, :]
            grad_queries = jnp.zeros((unit_rows, 256), F32)
            for head in range(heads):
                place = pl.ds(head * unit_rows, unit_rows)
                masked = keep_head(queries, head, True)
                masked_out = keep_head(grad_out, head, False)
                qmask[place, :] = masked
                domask[place, :] = masked_out
                scores = dot(kb[...], masked, NT).reshape(8, half, unit_rows)
                shares = jnp.exp(scores - (lse_ref[unit, head : head + 1, :] - neg_ref[unit]))
                shares = shares.reshape(8 * half, unit_rows)
                grad_shares = dot(vb[...], masked_out, NT)
                centre = jnp.sum(shares * grad_shares, axis=0, keepdims=True)
                grad_scores = (shares * (grad_shares - centre)).astype(BF)
                pb[:, place] = shares.astype(BF)
                dsb[:, place] = grad_scores
                grad_queries = grad_queries + dot(grad_scores, keep_head(kb[...], head, True), TN)
            dkb[...] += dot(dsb[...], qmask[...])
            dvb[...] += dot(pb[...], domask[...])
            low, high = turn_back(grad_queries, rows, HD**-0.5)
            dqk[rows, :128] = low
            dqk[rows, 128:256] = high
            return carry

        lax.fori_loop(0, 4, attend, 0)
        loads.start(layer - 1, "wout", "q", "k", "v")
        event("down", layer + 1, "end")
        event("attn", layer + 1, "end")
        event("up", layer, "middle")
        loads.wait(layer, "wq", "wk", "wv")
        load_turned(wq, wk, wqk)

        def spread(step, carry):
            unit = 3 - step
            rows = span(unit * unit_rows, unit_rows)
            low, high = turn_back(dkb[rows, :], rows, 1.0)
            dqk[rows, 256:384] = low
            dqk[rows, 384:512] = high
            values = dvb[rows, :].astype(BF)
            dvv[rows, :] = values
            total[...] = dot(dqk[rows, :], wqk[...], NT) + dot(values, wv[...], NT)
            attn.scatter(unit, total, own)
            return carry

        lax.fori_loop(0, 4, spread, 0)
        loads.start(layer - 1, "wq", "wk", "wv")
        event("down", layer, "middle")
        loads.wait(layer, "a", "o")
        places = (
            turned_place(columns, 0, 4 * columns),
            turned_place(columns, columns, 4 * columns),
            plain_place(columns, 2 * columns, 4 * columns),
            plain_place(columns, 3 * columns, 4 * columns),
        )

        def attn_tile(index, carry):
            place = span(index * 256, 256)
            normed = abuf[:, place]
            both = dot(normed, dqk[...], TN).astype(BF)
            made = dot(both[:, :256], places[0]) + dot(both[:, 256:], places[1])
            made = made + dot(dot(normed, dvv[...], TN).astype(BF), places[2])
            outs = dot(fbuf[:, place], ob[...], TN).astype(BF)
            attn_grads[place, :] = (made + dot(outs, places[3])).astype(BF)
            return carry

        lax.fori_loop(0, tiles, attn_tile, 0)
        loads.start(layer - 1, "a", "o")
        event("attn", layer, "start")
        if not deep:
            stores = [
                pltpu.make_async_copy(attn_grads, attn_outs[layer], store_sems.at[0]),
                pltpu.make_async_copy(feed_grads, feed_outs[layer], store_sems.at[1]),
            ]
            for each in stores:
                each.start()
            for each in stores:
                each.wait()
        feed.finish()
        loads.wait(layer, "x")
        gain_sum = jnp.zeros((1, width), F32)
        bias_sum = jnp.zeros((1, width), F32)
        for part in range(2):
            rows = pl.ds(part * half, half)
            grad = attn.collect(part, own)
            hat, rstd = norm(xb[rows, :])
            gain_sum += jnp.sum(grad * hat, axis=0, keepdims=True)
            bias_sum += jnp.sum(grad, axis=0, keepdims=True)
            made = dx1[rows, :] + norm_back(
                grad * gain_ref[layer : layer + 1, :], hat, rstd
            )
            dxb[rows, :] = made
            if layer:
                ebuf[rows, :] = made.astype(BF)
                feed.send(part)
        note(2, gain_sum)
        note(3, bias_sum)
        loads.start(layer - 1, "x")
    out_ref[...] = dxb[...]
    if deep:
        for each in joined_loads:
            each.wait()
        tail(deep, spot, ids, sums, dxb, small_ref, temb_ref, work, dsb, tail_refs,
             sum_ref, vec_ref, store_sems)
    attn.finish()


def tail(deep, spot, ids, sums, dxb, small_ref, temb_ref, work, dsb, scratch, sum_ref, vec_ref,
         store_sems):
    (joined, ebuf, jbuf, near_in, next_in, z_in, result, vecs, send, recv) = scratch
    sibling, far = ids
    place = lax.axis_index("tensor")
    core = lax.rem(place, 2)
    y = place // 2
    x, z = spot.x, spot.z
    width = dxb.shape[1]
    ladder = Ladder((send, recv))
    ebuf[0] = dxb[...].astype(BF)
    rows_copy = ladder.copy(ebuf.at[0], ebuf.at[1], sibling)
    joined_copy = ladder.copy(joined.at[1 - core], jbuf, sibling)
    mine = vecs.at[core, y, x, z]
    row = lax.broadcasted_iota(jnp.int32, small_ref.shape, 0)
    mine[...] = jnp.where(row == 5, temb_ref[...], small_ref[...]).astype(BF)
    vec_z = [ladder.copy(mine, mine, spot.along(ahead)) for ahead in range(1, deep)]
    rows_copy.wait_recv()
    joined_copy.wait_recv()
    rest = width // 2

    def tile(index, carry):
        rows = span(index * 256, 256)
        made = dot(joined[core, :, rows], ebuf[0], TN)
        work[rows, :] = made + dot(jbuf[:, rows], ebuf[1], TN)
        return carry

    lax.fori_loop(0, width // 256, tile, 0)
    half, quarter = width // 2, width // 4
    piece = quarter // deep
    ways = (((far, y), (spot.across, x)), ((spot.across, x), (far, y)))
    lanes = (pl.ds(0, rest), pl.ds(rest, rest))
    firsts = []
    for side, ((device, bit), _) in enumerate(ways):
        out = dsb.at[pl.ds(0, half), lanes[side]]
        out[...] = work[span((1 - bit) * half, half), lanes[side]].astype(BF)
        firsts.append(ladder.copy(out, near_in.at[side], device))
    for each in vec_z:
        each.wait_recv()
    row_z = vecs.at[core, y, x]
    vec_x = ladder.copy(row_z, row_z, spot.across)
    seconds = []
    for side, ((_, bit), (device, bit2)) in enumerate(ways):
        firsts[side].wait_recv()
        kept = work.at[span(bit * half, half), lanes[side]]
        kept[...] = kept[...] + near_in[side].astype(F32)
        out = dsb.at[pl.ds(half, quarter), lanes[side]]
        out[...] = work[span(bit * half + (1 - bit2) * quarter, quarter), lanes[side]].astype(BF)
        seconds.append(ladder.copy(out, next_in.at[side], device))
    vec_x.wait_recv()
    plane = vecs.at[core, y]
    vec_y = ladder.copy(plane, plane, far)
    sums["attn", 0].middle()
    thirds = []
    for side, ((_, bit), (_, bit2)) in enumerate(ways):
        seconds[side].wait_recv()
        kept = work.at[span(bit * half + bit2 * quarter, quarter), lanes[side]]
        kept[...] = kept[...] + next_in[side].astype(F32)
        out = dsb.at[pl.ds(half + quarter, quarter), lanes[side]]
        out[...] = kept[...].astype(BF)
        for ahead in range(1, deep):
            start = half + quarter + spot.level(ahead) * piece
            thirds.append(
                ladder.copy(
                    dsb.at[span(start, piece), lanes[side]],
                    z_in.at[side, ahead - 1],
                    spot.along(ahead),
                )
            )
    sums["up", 0].end()
    sums["down", 0].end()
    vec_y.wait_recv()
    every = vecs.at[core]
    vec_core = ladder.copy(every, every, sibling)
    lasts = []
    for side, ((_, bit), (_, bit2)) in enumerate(ways):
        for ahead in range(1, deep):
            thirds[side * (deep - 1) + ahead - 1].wait_recv()
        start = bit * half + bit2 * quarter + z * piece
        made = work[span(start, piece), lanes[side]]
        for ahead in range(1, deep):
            made = made + z_in[side, ahead - 1].astype(F32)
        own = result.at[core, side, span(start, piece)]
        own[...] = made.astype(BF)
        lasts += [ladder.copy(own, own, spot.along(ahead)) for ahead in range(1, deep)]
    backs = []
    for side, ((_, bit), (device, bit2)) in enumerate(ways):
        for ahead in range(1, deep):
            lasts[side * (deep - 1) + ahead - 1].wait_recv()
        own = result.at[core, side, span(bit * half + bit2 * quarter, quarter)]
        backs.append(ladder.copy(own, own, device))
    ends = []
    for side, ((device, bit), _) in enumerate(ways):
        backs[side].wait_recv()
        own = result.at[core, side, span(bit * half, half)]
        ends.append(ladder.copy(own, own, device))
    sums["attn", 0].end()
    vec_core.wait_recv()
    vec_store = pltpu.make_async_copy(vecs, vec_ref, store_sems.at[0])
    vec_store.start()
    for each in ends:
        each.wait_recv()
    whole = ladder.copy(result.at[core], result.at[core], sibling)
    whole.wait_recv()
    sum_store = pltpu.make_async_copy(result, sum_ref, store_sems.at[1])
    sum_store.start()
    ladder.finish()
    vec_store.wait()
    sum_store.wait()


def backward(heads, deep, cotangent, gains, conds, temb, tables, weights, kept, joined):
    depth = len(kept)
    block, width = cotangent.shape
    length = 4 * block
    units = weights[2].shape[2]
    columns = heads * HD
    part = width // (2 * deep) if deep else width
    half, quarter = width // 2, width // 4
    logs = []
    held = []
    for rows, (normed, queries, keys, values, log, attended, after, modulated, gated, slope) in kept:
        logs.append(log)
        held.append(
            [normed, queries, keys, values, attended, after, modulated, gated, slope, rows]
        )
    scratch = [pltpu.SemaphoreType.DMA((6, 2))] * 4
    scratch += [pltpu.SemaphoreType.DMA((16,)), pltpu.SemaphoreType.DMA((2,))]
    scratch += [pltpu.VMEM((width, columns), BF)] * 3
    scratch += [pltpu.VMEM(each.shape[1:], BF) for each in weights[1:4]]
    scratch += [pltpu.VMEM(each.shape, each.dtype) for each in held[0]]
    scratch += group_scratch(length, width) + group_scratch(length, width)
    scratch += [
        pltpu.VMEM((width, 512), BF),
        pltpu.VMEM((length, units), BF),
        pltpu.VMEM((heads * block, 256), BF),
        pltpu.VMEM((heads * block, columns), BF),
        pltpu.VMEM((length, heads * block), BF),
        pltpu.VMEM((length, heads * block), BF),
        pltpu.VMEM((length, 256), F32),
        pltpu.VMEM((length, columns), F32),
        pltpu.VMEM((length, 512), BF),
        pltpu.VMEM((length, columns), BF),
        pltpu.VMEM((3 * block, width), F32),
        pltpu.VMEM((block, width), F32),
        pltpu.VMEM((2, width, units), BF),
        pltpu.VMEM((width, 4 * columns), BF),
    ]
    out_shape = [
        jax.ShapeDtypeStruct((block, width), F32),
        jax.ShapeDtypeStruct((8 * depth, width), F32),
    ]
    kind = F32 if deep else BF
    out_shape += [jax.ShapeDtypeStruct((part, 4 * columns), kind)] * depth
    out_shape += [jax.ShapeDtypeStruct((2, part, units), kind)] * depth
    out_specs = [vmem_spec()] * 2 + [vmem_spec() if deep else any_spec()] * (2 * depth)
    if deep:
        for _ in range(depth):
            scratch += DpSum.scratch(deep, part, units) + DpSum.scratch(deep, part, units)
            scratch += DpSum.scratch(deep, part, 4 * columns)
        vec_shape = (2, 2, 2, deep, 8 * depth, width)
        scratch += [
            pltpu.VMEM((2, block, width), BF),
            pltpu.VMEM((2, block, width), BF),
            pltpu.VMEM((block, width), BF),
            pltpu.VMEM((2, half, half), BF),
            pltpu.VMEM((2, quarter, half), BF),
            pltpu.VMEM((2, deep - 1, quarter // deep, half), BF),
            pltpu.VMEM((2, 2, width, half), BF),
            pltpu.VMEM(vec_shape, BF),
            pltpu.SemaphoreType.DMA((LADDER_COPIES,)),
            pltpu.SemaphoreType.DMA((LADDER_COPIES,)),
        ]
        out_shape += [
            jax.ShapeDtypeStruct((2, 2, width, half), BF),
            jax.ShapeDtypeStruct(vec_shape, BF),
        ]
        out_specs += [any_spec(), any_spec()]

    def kernel(*refs):
        backward_kernel(depth, heads, deep, refs)

    operands = [cotangent, gains, *tables, temb, *conds, *logs]
    in_specs = [vmem_spec()] * len(operands)
    remote = [*joined, *weights, *[each for layer in held for each in layer]]
    in_specs += [any_spec()] * len(remote)
    return pl.pallas_call(
        kernel,
        out_shape=out_shape,
        in_specs=in_specs,
        out_specs=out_specs,
        scratch_shapes=scratch,
        compiler_params=pltpu.CompilerParams(
            collective_id=9, has_side_effects=True, vmem_limit_bytes=LIMIT
        ),
        name="layers_backward",
    )(*operands, *remote)


def finish_kernel(depth, refs):
    (low_ref, wself_ref, sum_ref, vec_ref) = refs[:4]
    attn_refs = refs[4 : 4 + depth]
    feed_refs = refs[4 + depth : 4 + 2 * depth]
    (tokens_ref, small_ref, qkv_ref, out_ref, ada_ref, up_ref, down_ref, self_ref) = refs[
        4 + 2 * depth :
    ]
    step = pl.program_id(0)
    members = vec_ref.shape[0] // 16
    width = vec_ref.shape[1]

    def pick(row):
        device = lax.broadcasted_iota(jnp.int32, (members, vec_ref.shape[0]), 0)
        column = lax.broadcasted_iota(jnp.int32, (members, vec_ref.shape[0]), 1)
        wanted = (column == device * 16 + row).astype(F32).astype(BF)
        return dot(wanted, vec_ref[...]).astype(BF)

    rows = ada_ref.shape[1]
    times = pick(5)
    device = lax.broadcasted_iota(jnp.int32, (width, rows), 0)
    column = lax.broadcasted_iota(jnp.int32, (width, rows), 1)
    chosen = (device == column + step * rows).astype(F32).astype(BF)
    times = dot(times, chosen).astype(BF)
    for layer in range(depth):
        for place in range(2):
            ada_ref[layer, :, place * width : (place + 1) * width] = dot(
                times, pick(8 * layer + place), TN
            )
    self_ref[:, : width // 2] = sum_ref[0].astype(F32)
    self_ref[:, width // 2 :] = sum_ref[1].astype(F32)

    @pl.when(step == 0)
    def _():
        row = lax.broadcasted_iota(jnp.int32, (16, vec_ref.shape[0]), 0)
        column = lax.broadcasted_iota(jnp.int32, (16, vec_ref.shape[0]), 1)
        small_ref[...] = dot((column % 16 == row).astype(F32).astype(BF), vec_ref[...])

    @pl.when(step == 1)
    def _():
        tokens_ref[...] = dot(low_ref[...].astype(BF), wself_ref[...], NT)

    @pl.when(step == 2)
    def _():
        for layer in range(depth):
            grads = attn_refs[layer][...]
            columns = grads.shape[1] // 4
            for place in range(3):
                qkv_ref[layer, place] = grads[:, place * columns : (place + 1) * columns]
            out_ref[layer] = grads[:, 3 * columns :].T

    @pl.when(step == 3)
    def _():
        for layer in range(depth):
            up_ref[layer] = feed_refs[layer][0]
            down_ref[layer] = feed_refs[layer][1].T


def finish(depth, low, w_self, sums, vectors, attn_shards, feed_shards):
    block, width = low.shape
    part, columns = attn_shards[0].shape
    columns //= 4
    units = feed_shards[0].shape[2]
    steps = 4
    rows = 2 * width // steps

    def fixed(shape):
        return pl.BlockSpec(shape, lambda step: (0,) * len(shape))

    def kernel(*refs):
        finish_kernel(depth, refs)

    return pl.pallas_call(
        kernel,
        grid=(steps,),
        out_shape=[
            jax.ShapeDtypeStruct((block, width), F32),
            jax.ShapeDtypeStruct((16, width), F32),
            jax.ShapeDtypeStruct((depth, 3, part, columns), F32),
            jax.ShapeDtypeStruct((depth, columns, part), F32),
            jax.ShapeDtypeStruct((depth, width, 2 * width), F32),
            jax.ShapeDtypeStruct((depth, part, units), F32),
            jax.ShapeDtypeStruct((depth, units, part), F32),
            jax.ShapeDtypeStruct((2 * width, width), F32),
        ],
        in_specs=[
            fixed((block, width)),
            fixed((width, width)),
            pl.BlockSpec((None, 2, rows, width // 2), lambda step: (step // 2, 0, step % 2, 0)),
            fixed(vectors.shape),
            *[fixed(each.shape) for each in attn_shards],
            *[fixed(each.shape) for each in feed_shards],
        ],
        out_specs=[
            fixed((block, width)),
            fixed((16, width)),
            fixed((depth, 3, part, columns)),
            fixed((depth, columns, part)),
            pl.BlockSpec((depth, width // steps, 2 * width), lambda step: (0, step, 0)),
            fixed((depth, part, units)),
            fixed((depth, units, part)),
            pl.BlockSpec((rows, width), lambda step: (step, 0)),
        ],
        compiler_params=pltpu.CompilerParams(vmem_limit_bytes=LIMIT),
        name="write_grads",
    )(low, w_self, sums, vectors, *attn_shards, *feed_shards)


def local(
    tokens,
    cotangent,
    lengths,
    timesteps,
    w_self,
    ln_gain,
    ln_bias,
    w_qkv,
    w_out,
    w_ada,
    b_ada,
    w_up,
    w_down,
    b_down,
):
    hp = lax.Precision.HIGHEST
    block, width = tokens.shape
    depth = w_qkv.shape[0]
    heads = w_qkv.shape[3] // HD
    groups = lax.axis_size("dp")
    deep = 4 if groups == 8 else 0
    place = lax.axis_index("tensor")
    core = place % 2
    sibling = place + 1 - 2 * core
    far = (place + 2) % 4
    far_other = (sibling + 2) % 4
    half = block // 2
    owners = jnp.stack([place, place, sibling, sibling, far, far_other, far, far_other])
    halves = jnp.array([0, 1, 0, 1, 1, 1, 0, 0], jnp.int32)
    starts = owners * block + halves * half
    index = (starts[:, None] + jnp.arange(half, dtype=jnp.int32)).reshape(-1)
    packed = lengths[0, 0] < 4 * block
    position = jnp.where(packed, index % block, index)
    lanes = jnp.arange(128) % HALF
    freqs = jnp.exp(-jnp.log(10000.0) * lanes.astype(F32) / HALF)
    angle = position.astype(F32)[:, None] * freqs
    cosine = jnp.cos(angle)
    sine = jnp.sin(angle)
    chunk = jnp.array([0, 0, 1, 1, 2, 3, 2, 3], jnp.int32)
    apart = (chunk[:, None] != chunk[None, :]).astype(F32) * jnp.where(packed, -1e9, 0.0)
    neg_keys = jnp.repeat(apart, half, axis=1).reshape(4, 2, 1, 4 * block)
    neg_queries = jnp.repeat(apart, half, axis=1).reshape(8, 4, 1, block).swapaxes(0, 1)
    slot = jnp.where(packed, place, 0)
    freqs = jnp.exp(-jnp.log(10000.0) * jnp.arange(width // 2).astype(F32) / (width // 2))
    angle = lax.dynamic_slice_in_dim(timesteps, slot, 1, 1).astype(F32) * freqs
    temb = jnp.concatenate([jnp.cos(angle), jnp.sin(angle)], axis=-1)
    weights = (w_qkv, w_out, w_up, w_down, w_ada)

    def run(rows, conds):
        kept = []
        for layer in range(depth):
            save = conds is not None
            cond = conds[layer] if save else (temb.reshape(width, 1), b_ada[layer][None])
            small = (ln_gain[layer][None], ln_bias[layer][None], cond, b_down[layer][None])
            made = forward_layer(
                layer, save, heads, rows, small, (cosine, sine, neg_keys), weights
            )
            kept.append((rows, made[1:]))
            rows = made[0]
        return (rows, kept)

    start = jnp.dot(tokens, w_self[:width], preferred_element_type=F32)
    rows, kept = run(start, None)
    conds = [each[1][0] for each in kept]
    estimate = rows.astype(BF)
    start = start + jnp.dot(estimate, w_self[width:], preferred_element_type=F32)
    rows, kept = run(start, conds)
    activations = rows.astype(BF)
    made = backward(
        heads,
        deep,
        cotangent,
        ln_gain,
        conds,
        temb,
        (cosine, sine, neg_queries),
        weights,
        kept,
        (tokens, estimate),
    )
    grad_rows, smalls = made[:2]
    attn_shards = made[2 : 2 + depth]
    feed_shards = made[2 + depth : 2 + 2 * depth]
    if deep:
        sums, vectors = made[2 + 2 * depth :]
        vectors = vectors.reshape(-1, width)
    else:
        attn_shards = [
            lax.psum_scatter(each, "dp", scatter_dimension=0, tiled=True).astype(F32)
            for each in attn_shards
        ]
        feed_shards = [
            lax.psum_scatter(each, "dp", scatter_dimension=1, tiled=True).astype(F32)
            for each in feed_shards
        ]
        joined = jnp.concatenate([tokens, estimate], axis=1)
        sums = lax.psum(dot(joined, grad_rows.astype(BF), TN).astype(BF), ("dp", "tensor"))
        sums = sums.reshape(2, width, 2, width // 2).swapaxes(1, 2)
        vectors = smalls.at[5].set(temb[0]).astype(BF)
        vectors = lax.all_gather(vectors, ("dp", "tensor"), axis=0, tiled=True)
    (grad_tokens, totals, grad_qkv, grad_out, grad_ada, grad_up, grad_down, grad_self) = finish(
        depth, grad_rows, w_self, sums, vectors, attn_shards, feed_shards
    )
    totals = totals.reshape(depth, 8, width)
    return (
        activations,
        grad_tokens,
        totals[:, 2],
        totals[:, 3],
        grad_qkv,
        grad_out,
        grad_ada,
        totals[:, :2].reshape(depth, 2 * width),
        grad_up,
        grad_down,
        totals[:, 4],
        grad_self,
    )


def solution(mesh):
    return jax.shard_map(
        local,
        mesh=mesh,
        in_specs=(
            P(("dp", "tensor"), None),
            P(("dp", "tensor"), None),
            P("dp", None),
            P("dp", None),
            P(),
            P(),
            P(),
            P(None, None, None, "tensor"),
            P(None, "tensor", None),
            P(),
            P(),
            P(None, None, "tensor"),
            P(None, "tensor", None),
            P(),
        ),
        out_specs=(
            P(("dp", "tensor"), None),
            P(("dp", "tensor"), None),
            P(),
            P(),
            P(None, None, "dp", "tensor"),
            P(None, "tensor", "dp"),
            P(),
            P(),
            P(None, "dp", "tensor"),
            P(None, "tensor", "dp"),
            P(),
            P(),
        ),
        check_vma=False,
    )
```

```python
import functools

import jax
import jax.numpy as jnp
from jax import lax
from jax.experimental import pallas as pl
from jax.experimental.pallas import tpu as pltpu
from jax.sharding import PartitionSpec as P

HD = 64
HALF = HD // 2
BF = jnp.bfloat16
F32 = jnp.float32
MESH = pl.DeviceIdType.MESH
EPS = 1e-05
LIMIT = 60 << 20


def norm(rows):
    centred = rows - jnp.mean(rows, axis=-1, keepdims=True)
    rstd = lax.rsqrt(jnp.mean(centred * centred, axis=-1, keepdims=True) + EPS)
    return (centred * rstd, rstd)


def norm_back(grad, hat, rstd):
    return rstd * (
        grad
        - jnp.mean(grad, axis=-1, keepdims=True)
        - hat * jnp.mean(grad * hat, axis=-1, keepdims=True)
    )


def dot(left, right, dims=((1,), (0,))):
    return lax.dot_general(left, right, (dims, ((), ())), preferred_element_type=F32)


NT = ((1,), (1,))
TN = ((0,), (0,))


def head_mask(head, columns, rotary):
    lane = lax.broadcasted_iota(jnp.int32, (1, columns), 1)
    if rotary:
        return (lane % 128) // HALF == head
    return lane // HD == head


def keep_head(rows, head, rotary):
    return jnp.where(head_mask(head, rows.shape[1], rotary), rows, jnp.zeros_like(rows))


def turned_place(columns, start, total):
    row = lax.broadcasted_iota(jnp.int32, (256, total), 0)
    column = lax.broadcasted_iota(jnp.int32, (256, total), 1) - start
    source = column // HD * HALF + column % HD // HALF * 128 + column % HALF
    fits = (source == row) & (column >= 0) & (column < columns)
    return fits.astype(F32).astype(BF)


def plain_place(columns, start, total):
    row = lax.broadcasted_iota(jnp.int32, (columns, total), 0)
    column = lax.broadcasted_iota(jnp.int32, (columns, total), 1) - start
    return (row == column).astype(F32).astype(BF)


def span(start, size):
    return pl.ds(pl.multiple_of(start, size), size)


class Group:
    def __init__(self, sems, ids, gathered, pair_out, pair_in, own_out, own_in, far_out, far_in):
        self.sems = sems
        self.ids = ids
        self.gathered = gathered
        self.pair_out, self.pair_in = pair_out, pair_in
        self.own_out, self.own_in = own_out, own_in
        self.far_out, self.far_in = far_out, far_in
        self.half = gathered.shape[0] // 8

    def copy(self, src, dst, kind, part, far):
        send, recv = self.sems
        return pltpu.make_async_remote_copy(
            src_ref=src,
            dst_ref=dst,
            send_sem=send.at[kind, part],
            recv_sem=recv.at[kind, part],
            device_id=self.ids[1] if far else self.ids[0],
            device_id_type=MESH,
        )

    def rows(self, start):
        return pl.ds(pl.multiple_of(start, self.half), self.half)

    def pair(self, part):
        return 6 * self.half - 2 * self.half * part

    def far_copy(self, part):
        own = self.gathered.at[self.rows(part * self.half)]
        return self.copy(own, self.gathered.at[self.rows(self.pair(part))], 0, part, True)

    def sibling_copy(self, part):
        own = self.gathered.at[self.rows(part * self.half)]
        place = self.gathered.at[self.rows((2 + part) * self.half)]
        return self.copy(own, place, 1, part, False)

    def forward_copy(self, part):
        src = self.gathered.at[self.rows(self.pair(part))]
        dst = self.gathered.at[self.rows(self.pair(part) + self.half)]
        return self.copy(src, dst, 2, part, False)

    def send(self, part):
        self.far_copy(part).start()
        self.sibling_copy(part).start()

    def receive(self, step):
        @pl.when(step == 1)
        def _():
            self.sibling_copy(0).wait_recv()
            self.sibling_copy(1).wait_recv()

        @pl.when(step >= 2)
        def _():
            part = step - 2
            self.far_copy(part).wait_recv()
            self.forward_copy(part).start()
            self.forward_copy(part).wait()

    def pair_copy(self, part):
        return self.copy(self.pair_out.at[part], self.pair_in.at[part], 3, part, False)

    def own_copy(self):
        return self.copy(self.own_out, self.own_in, 4, 0, False)

    def sum_copy(self, part):
        return self.copy(self.far_out.at[part], self.far_in.at[part], 5, part, True)

    def scatter(self, unit, total, own):
        @pl.when(unit == 0)
        def _():
            own[...] = total[...]

        @pl.when(unit == 1)
        def _():
            self.own_out[...] = total[...].astype(BF)
            self.own_copy().start()

        @pl.when(unit >= 2)
        def _():
            part = 3 - unit
            self.pair_out[part] = total[self.half :, :].astype(BF)
            self.pair_copy(part).start()
            self.pair_copy(part).wait_recv()
            self.far_out[part] = (
                total[: self.half, :] + self.pair_in[part].astype(F32)
            ).astype(BF)
            self.sum_copy(part).start()

    def collect(self, part, own):
        if part == 0:
            self.own_copy().wait_recv()
        self.sum_copy(part).wait_recv()
        rows = pl.ds(part * self.half, self.half)
        return own[rows, :] + self.own_in[rows, :].astype(F32) + self.far_in[part].astype(F32)

    def finish(self):
        for part in range(2):
            self.far_copy(part).wait_send()
            self.sibling_copy(part).wait_send()
            self.pair_copy(part).wait_send()
            self.sum_copy(part).wait_send()
        self.own_copy().wait_send()


def neighbours():
    group = lax.axis_index("dp")
    place = lax.axis_index("tensor")
    core = lax.rem(place, 2)
    return ((group, place + 1 - 2 * core), (group, lax.rem(place + 2, 4)))


class Spot:
    def __init__(self, deep):
        group = lax.axis_index("dp")
        self.place = lax.axis_index("tensor")
        self.deep = deep
        self.z = group // 2
        self.x = lax.rem(group, 2)
        self.across = (2 * self.z + 1 - self.x, self.place)

    def level(self, ahead):
        return lax.rem(self.z + ahead, self.deep)

    def along(self, ahead):
        return (2 * self.level(ahead) + self.x, self.place)

    def partners(self):
        return [self.across] + [self.along(ahead) for ahead in range(1, self.deep)]


def meet(ids):
    barrier = pltpu.get_barrier_semaphore()
    for device in ids:
        pl.semaphore_signal(barrier, inc=1, device_id=device, device_id_type=MESH)
    pl.semaphore_wait(barrier, len(ids))


class DpSum:
    def __init__(self, spot, src, out, scratch):
        self.spot, self.src, self.out = spot, src, out
        self.pairs, self.rest, self.sems = scratch
        self.block = self.pairs.shape[1]

    @staticmethod
    def scratch(deep, block, columns):
        return [
            pltpu.VMEM((deep, block, columns), BF),
            pltpu.VMEM((deep - 1, block, columns), BF),
            pltpu.SemaphoreType.DMA((4, deep)),
        ]

    def rows(self, ahead, x):
        start = (2 * self.spot.level(ahead) + x) * self.block
        return pl.ds(pl.multiple_of(start, self.block), self.block)

    def x_copy(self, ahead):
        return pltpu.make_async_remote_copy(
            src_ref=self.src.at[self.rows(ahead, 1 - self.spot.x)],
            dst_ref=self.pairs.at[ahead],
            send_sem=self.sems.at[0, ahead],
            recv_sem=self.sems.at[1, ahead],
            device_id=self.spot.across,
            device_id_type=MESH,
        )

    def z_copy(self, ahead):
        return pltpu.make_async_remote_copy(
            src_ref=self.pairs.at[ahead],
            dst_ref=self.rest.at[ahead - 1],
            send_sem=self.sems.at[2, ahead],
            recv_sem=self.sems.at[3, ahead],
            device_id=self.spot.along(ahead),
            device_id_type=MESH,
        )

    def order(self):
        return [*range(1, self.spot.deep), 0]

    def start(self):
        for ahead in self.order():
            self.x_copy(ahead).start()

    def middle(self):
        for ahead in self.order():
            self.x_copy(ahead).wait_recv()
            total = self.src[self.rows(ahead, self.spot.x), :].astype(F32)
            total = total + self.pairs[ahead].astype(F32)
            if ahead:
                self.pairs[ahead] = total.astype(BF)
                self.z_copy(ahead).start()
            else:
                self.out[...] = total
        for ahead in self.order():
            self.x_copy(ahead).wait_send()

    def end(self):
        for ahead in range(1, self.spot.deep):
            self.z_copy(ahead).wait_recv()
        total = self.out[...]
        for ahead in range(1, self.spot.deep):
            total = total + self.rest[ahead - 1].astype(F32)
        self.out[...] = total
        for ahead in range(1, self.spot.deep):
            self.z_copy(ahead).wait_send()


def group_scratch(rows, width):
    half = rows // 8
    return [
        pltpu.VMEM((rows, width), BF),
        pltpu.VMEM((2, half, width), BF),
        pltpu.VMEM((2, half, width), BF),
        pltpu.VMEM((2 * half, width), BF),
        pltpu.VMEM((2 * half, width), BF),
        pltpu.VMEM((2, half, width), BF),
        pltpu.VMEM((2, half, width), BF),
    ]


def gelu_parts(hidden):
    cdf = 0.5 * (1.0 + lax.erf(hidden * (0.5**0.5)))
    density = jnp.exp(hidden * hidden * -0.5) * 0.3989422804014327
    return (hidden * cdf, cdf + hidden * density)


def load_turned(wq, wk, wqk):
    turn = turned_place(wq.shape[0], 0, wq.shape[0])
    wqk[:256, :] = dot(turn, wq[...]).astype(BF)
    wqk[256:, :] = dot(turn, wk[...]).astype(BF)


def is_packed(lengths_ref, length):
    return (lengths_ref[:, 0:1] < length).astype(jnp.int32).astype(F32)


def owner(chunk):
    return jnp.where(chunk < 4, chunk // 2, 2 + chunk % 2)


def apart(keys, queries, packed):
    return (keys != queries).astype(jnp.int32).astype(F32) * (packed * -1e9)


def unit_owner(unit, half):
    return jnp.where(unit < 2, unit, 2 + half)


SAVED = ("a", "q", "k", "v", "o", "x1", "m", "g", "slope", "x", "lse")


def forward_kernel(depth, heads, refs):
    refs = list(refs)

    def take(count):
        made = refs[:count]
        del refs[:count]
        return made

    (gain_ref, bias_ref, bdown_ref, bada_ref, lengths_ref, steps_ref) = take(6)
    (rotary_ref, time_ref) = take(2)
    (tokens_hbm, wself_hbm, wqkv_hbm, wout_hbm, wup_hbm, wdown_hbm, wada_hbm) = take(7)
    (acts_ref, est_ref, cond_ref, cos_ref, sin_ref, temb_ref) = take(6)
    saved_hbm = [dict(zip(SAVED, take(len(SAVED)))) for _ in range(depth)]
    (send, recv, send2, recv2, load_sems, store_sems) = take(6)
    (tokens, wself, wada) = take(3)
    weights = [take(6) for _ in range(depth)]
    wqks = take(depth)
    first, second = take(7), take(7)
    (qb, kb, vb, lse, ob, x1, gb, gpb, total, own, xb, start) = take(12)
    ids = neighbours()
    sources = [tokens_hbm, wself_hbm.at[0], wself_hbm.at[1]]
    places = [tokens, wself.at[0], wself.at[1]]
    for layer in range(depth):
        sources += [wqkv_hbm.at[layer, part] for part in range(3)]
        sources += [wout_hbm.at[layer], wup_hbm.at[layer], wdown_hbm.at[layer]]
        places += weights[layer]
    loads = [
        pltpu.make_async_copy(src, dst, load_sems.at[i])
        for i, (src, dst) in enumerate(zip(sources, places))
    ]
    ada_loads = [
        pltpu.make_async_copy(wada_hbm.at[layer], wada, load_sems.at[len(loads)])
        for layer in range(depth)
    ]
    order = [0, 1, *range(3, 9)]
    for i in order:
        loads[i].start()
    ada_loads[0].start()
    for i in range(len(loads)):
        if i not in order:
            loads[i].start()
    meet(ids)
    attn = Group((send, recv), ids, *first)
    feed = Group((send2, recv2), ids, *second)
    abuf, mbuf = first[0], second[0]
    half = attn.half
    unit_rows = 2 * half
    length = 8 * half
    width = xb.shape[1]
    columns = heads * HD
    packed = is_packed(lengths_ref, length)
    buffers = dict(zip(SAVED, (abuf, qb, kb, vb, ob, x1, mbuf, gb, gpb, xb, lse)))
    pending = []

    def store(layer, *names):
        for name in names:
            made = pltpu.make_async_copy(
                buffers[name], saved_hbm[layer][name], store_sems.at[SAVED.index(name)]
            )
            made.start()
            pending.append((name, made))

    def stored(*names):
        for each in list(pending):
            if each[0] in names:
                each[1].wait()
                pending.remove(each)

    def begin(layer, part, rows, values):
        xb[rows, :] = values
        hat = norm(values)[0]
        gain = gain_ref[layer : layer + 1, :]
        abuf[rows, :] = (hat * gain + bias_ref[layer : layer + 1, :]).astype(BF)
        attn.send(part)

    loads[0].wait()
    loads[1].wait()
    for part in range(2):
        rows = pl.ds(part * half, half)
        made = dot(tokens[rows, :], wself[0])
        start[rows, :] = made
        begin(0, part, rows, made)

    def make_tables():
        place = lax.axis_index("tensor")
        sibling = ids[0][1]
        far = ids[1][1]
        far_other = lax.rem(sibling + 2, 4)
        row = lax.broadcasted_iota(jnp.int32, (half, 128), 0).astype(F32)
        for chunk, (block, part) in enumerate(
            zip(
                (place, place, sibling, sibling, far, far_other, far, far_other),
                (0, 1, 0, 1, 1, 1, 0, 0),
            )
        ):
            rows = pl.ds(chunk * half, half)
            offset = (block * unit_rows).astype(F32)
            position = row + part * half + (1.0 - packed) * offset
            angle = position * rotary_ref[...]
            cos_ref[rows, :] = jnp.cos(angle)
            sin_ref[rows, :] = jnp.sin(angle)
        steps = steps_ref[...].astype(F32)
        slot = lax.broadcasted_iota(jnp.int32, steps.shape, 1)
        mine = jnp.sum(jnp.where(slot == place, steps, 0.0), axis=1, keepdims=True)
        step = packed * mine + (1.0 - packed) * steps[:, 0:1]
        angle = jnp.broadcast_to(step * time_ref[...], (8, width // 2))
        temb_ref[:, : width // 2] = jnp.cos(angle)
        temb_ref[:, width // 2 :] = jnp.sin(angle)

    def make_cond(layer):
        ada_loads[layer].wait()
        column = temb_ref[...].T[:, 0:1]
        made = jnp.sum(wada[...] * column, axis=0, keepdims=True)
        made = made + bada_ref[layer : layer + 1, :]
        cond_ref[8 * layer : 8 * layer + 8, :] = jnp.broadcast_to(made, (8, 2 * width))
        if layer + 1 < depth:
            ada_loads[layer + 1].start()

    def run(layer, save, after_layer):
        (wq, wk, wv, wout, wup, wdown) = weights[layer]
        wqk = wqks[layer]
        if not save:
            if layer == 0:
                make_tables()
            for i in range(3 + 6 * layer, 6 + 6 * layer):
                loads[i].wait()
            load_turned(wq, wk, wqk)
        stored("q", "k", "v")

        def project(step, carry):
            attn.receive(step)
            unit = jnp.where(step < 2, step, 5 - step)
            rows = span(unit * unit_rows, unit_rows)
            normed = abuf[rows, :]
            mixed = dot(normed, wqk[...], NT)
            cosine = cos_ref[rows, :]
            sine = sin_ref[rows, :]
            for place, dst, scale in ((0, qb, HD**-0.5), (256, kb, 1.0)):
                first_half = mixed[:, place : place + 128]
                second_half = mixed[:, place + 128 : place + 256]
                dst[rows, :128] = ((first_half * cosine - second_half * sine) * scale).astype(BF)
                dst[rows, 128:] = ((second_half * cosine + first_half * sine) * scale).astype(BF)
            vb[rows, :] = dot(normed, wv[...], NT).astype(BF)
            return carry

        lax.fori_loop(0, 4, project, 0)
        stored("o", "lse", "m", "x1", "g", "slope")
        if save:
            store(layer, "a", "x", "q", "k", "v")
        elif layer == 0:
            for i in (6, 7, 8):
                loads[i].wait()
        else:
            for i in range(6 + 6 * layer, 9 + 6 * layer):
                loads[i].wait()
        lane = lax.broadcasted_iota(jnp.int32, (1, 128), 1)

        def attend(step, carry):
            unit = 3 - step
            rows = span(unit * unit_rows, unit_rows)
            queries = qb[rows, :]
            attended = jnp.zeros((unit_rows, columns), F32)
            logs = jnp.zeros((unit_rows, 128), F32)
            part = lax.broadcasted_iota(jnp.int32, (2, 1, length), 0)
            chunk = lax.broadcasted_iota(jnp.int32, (2, 1, length), 2) // half
            neg = apart(owner(chunk), unit_owner(unit, part), packed.reshape(1, 1, 1))
            for head in range(heads):
                scores = dot(keep_head(queries, head, True), kb[...], NT)
                scores = scores.reshape(2, half, length) + neg
                scores = scores.reshape(unit_rows, length)
                largest = jnp.max(scores, axis=-1, keepdims=True)
                shares = jnp.exp(scores - largest)
                sums = jnp.sum(shares, axis=-1, keepdims=True)
                output = dot(shares.astype(BF), vb[...]) * (1.0 / sums)
                attended = jnp.where(head_mask(head, columns, False), output, attended)
                if save:
                    logs = jnp.where(lane == head, largest + jnp.log(sums), logs)
            if save:
                lse[unit] = logs.T[:8, :]
            attended = attended.astype(BF)
            ob[rows, :] = attended
            total[...] = dot(attended, wout[...])
            attn.scatter(unit, total, own)
            return carry

        lax.fori_loop(0, 4, attend, 0)
        if not save:
            make_cond(layer)
        shift = cond_ref[8 * layer : 8 * layer + 1, :width]
        scale = cond_ref[8 * layer : 8 * layer + 1, width:]
        if save or layer:
            feed.finish()
        for part in range(2):
            rows = pl.ds(part * half, half)
            after = xb[rows, :] + attn.collect(part, own)
            x1[rows, :] = after
            mbuf[rows, :] = (norm(after)[0] * (1.0 + scale) + shift).astype(BF)
            feed.send(part)
        stored("a", "x")
        if save:
            store(layer, "o", "lse", "x1")

        def expand(step, carry):
            feed.receive(step)
            unit = jnp.where(step < 2, step, 5 - step)
            rows = span(unit * unit_rows, unit_rows)
            hidden = dot(mbuf[rows, :], wup[...])
            gated, slope = gelu_parts(hidden)
            gated = gated.astype(BF)
            if save:
                gb[rows, :] = gated
                gpb[rows, :] = slope.astype(BF)
            total[...] = dot(gated, wdown[...])
            feed.scatter(unit, total, own)
            return carry

        lax.fori_loop(0, 4, expand, 0)
        if save:
            store(layer, "m", "g", "slope")
        attn.finish()
        for part in range(2):
            rows = pl.ds(part * half, half)
            made = x1[rows, :] + feed.collect(part, own) + bdown_ref[layer : layer + 1, :]
            after_layer(part, rows, made)

    def between(part, rows, made):
        estimate = made.astype(BF)
        est_ref[rows, :] = estimate
        begin(0, part, rows, start[rows, :] + dot(estimate, wself[1]))

    def close(part, rows, made):
        acts_ref[rows, :] = made.astype(BF)

    for save in (False, True):
        for layer in range(depth):
            if layer + 1 < depth:
                run(layer, save, functools.partial(begin, layer + 1))
            elif save:
                run(layer, save, close)
            else:
                loads[2].wait()
                run(layer, save, between)
    feed.finish()
    stored(*SAVED)


def any_spec():
    return pl.BlockSpec(memory_space=pl.ANY)


def vmem_spec():
    return pl.BlockSpec(memory_space=pltpu.VMEM)


def forward(heads, tokens, w_self, vectors, weights):
    depth = weights[0].shape[0]
    block, width = tokens.shape
    length = 4 * block
    columns = heads * HD
    units = weights[2].shape[2]
    lanes = jnp.arange(128) % HALF
    rotary = jnp.exp(-jnp.log(10000.0) * lanes.astype(F32) / HALF)[None]
    halves = jnp.arange(width // 2).astype(F32)
    times = jnp.exp(-jnp.log(10000.0) * halves / (width // 2))[None]
    kept = {
        "a": ((length, width), BF),
        "q": ((length, 256), BF),
        "k": ((length, 256), BF),
        "v": ((length, columns), BF),
        "o": ((length, columns), BF),
        "x1": ((block, width), F32),
        "m": ((length, width), BF),
        "g": ((length, units), BF),
        "slope": ((length, units), BF),
        "x": ((block, width), F32),
        "lse": ((4, 8, block), F32),
    }
    kept_shapes = [jax.ShapeDtypeStruct(*kept[name]) for name in SAVED]
    out_shape = [
        jax.ShapeDtypeStruct((block, width), BF),
        jax.ShapeDtypeStruct((block, width), BF),
        jax.ShapeDtypeStruct((8 * depth, 2 * width), F32),
        jax.ShapeDtypeStruct((length, 128), F32),
        jax.ShapeDtypeStruct((length, 128), F32),
        jax.ShapeDtypeStruct((8, width), F32),
    ] + kept_shapes * depth
    out_specs = [vmem_spec()] * 6 + [any_spec()] * (depth * len(SAVED))
    scratch = [pltpu.SemaphoreType.DMA((6, 2))] * 4
    scratch += [
        pltpu.SemaphoreType.DMA((4 + 6 * depth,)),
        pltpu.SemaphoreType.DMA((len(SAVED),)),
        pltpu.VMEM((block, width), BF),
        pltpu.VMEM((2, width, width), BF),
        pltpu.VMEM((width, 2 * width), F32),
    ]
    for _ in range(depth):
        scratch += [pltpu.VMEM((columns, width), BF)] * 3
        scratch += [pltpu.VMEM(each.shape[1:], BF) for each in weights[1:4]]
    scratch += [pltpu.VMEM((512, width), BF)] * depth
    scratch += group_scratch(length, width) + group_scratch(length, width)
    for name in ("q", "k", "v", "lse", "o", "x1", "g", "slope"):
        scratch.append(pltpu.VMEM(*kept[name]))
    scratch += [pltpu.VMEM((block, width), F32)] * 4

    def kernel(*refs):
        forward_kernel(depth, heads, refs)

    operands = [*vectors, rotary, times]
    remote = [tokens, w_self.reshape(2, width, width), *weights]
    made = pl.pallas_call(
        kernel,
        out_shape=out_shape,
        in_specs=[vmem_spec()] * len(operands) + [any_spec()] * len(remote),
        out_specs=out_specs,
        scratch_shapes=scratch,
        compiler_params=pltpu.CompilerParams(
            collective_id=1, has_side_effects=True, vmem_limit_bytes=LIMIT
        ),
        name="layers_forward",
    )(*operands, *remote)
    count = len(SAVED)
    saved = [made[6 + count * layer : 6 + count * (layer + 1)] for layer in range(depth)]
    return (made[:6], [dict(zip(SAVED, each)) for each in saved])


class Ladder:
    def __init__(self, sems):
        self.send, self.recv = sems
        self.used = 0
        self.open = []

    def copy(self, src, dst, device):
        made = pltpu.make_async_remote_copy(
            src_ref=src,
            dst_ref=dst,
            send_sem=self.send.at[self.used],
            recv_sem=self.recv.at[self.used],
            device_id=device,
            device_id_type=MESH,
        )
        self.used += 1
        assert self.used <= LADDER_COPIES
        made.start()
        self.open.append(made)
        return made

    def finish(self):
        for each in self.open:
            each.wait_send()


LADDER_COPIES = 34


class Loads:
    def __init__(self, sems):
        self.sems = sems
        self.names = {}

    def add(self, name, sources, buffer):
        self.names[name] = (sources, buffer, len(self.names))
        return buffer

    def copy(self, name, layer):
        sources, buffer, place = self.names[name]
        return pltpu.make_async_copy(sources[layer], buffer, self.sems.at[place])

    def start(self, layer, *names):
        if layer >= 0:
            for name in names:
                self.copy(name, layer).start()

    def wait(self, layer, *names):
        for name in names:
            self.copy(name, layer).wait()


def backward_kernel(depth, heads, deep, refs):
    refs = list(refs)

    def take(count):
        made = refs[:count]
        del refs[:count]
        return made

    cot_ref, gain_ref, lengths_ref, cos_ref, sin_ref, temb_ref, cond_ref = take(7)
    joined_hbm = take(2)
    wqkv_hbm, wout_hbm, wup_hbm, wdown_hbm, _ = take(5)
    saved_hbm = [dict(zip(SAVED, take(len(SAVED)))) for _ in range(depth)]
    (out_ref, small_ref) = take(2)
    attn_outs, feed_outs = take(depth), take(depth)
    if deep:
        sum_ref, vec_ref = take(2)
    send, recv, send2, recv2, load_sems, store_sems = take(6)
    loads = Loads(load_sems)
    wq, wk, wv = (
        loads.add(name, [wqkv_hbm.at[layer, part] for layer in range(depth)], take(1)[0])
        for part, name in enumerate(("wq", "wk", "wv"))
    )
    wout, wup, wdown = (
        loads.add(name, [src.at[layer] for layer in range(depth)], take(1)[0])
        for name, src in (("wout", wout_hbm), ("wup", wup_hbm), ("wdown", wdown_hbm))
    )
    abuf, qb, kb, vb, ob, x1b, mbuf, gb, gpb, xb, lse = (
        loads.add(name, [saved_hbm[layer][name] for layer in range(depth)], take(1)[0])
        for name in SAVED
    )
    first = take(7)
    second = take(7)
    (wqk, dhb, qmask, domask, dsb, pb, dkb, dvb, dqk, dvv, work, dxb) = take(12)
    (feed_grads, attn_grads) = take(2)
    ids = neighbours()
    sums = {}
    if deep:
        spot = Spot(deep)
        meet([*ids, *spot.partners()])
        for layer in range(depth):
            for name, src, out in (
                ("up", feed_grads.at[0], feed_outs[layer].at[0]),
                ("down", feed_grads.at[1], feed_outs[layer].at[1]),
                ("attn", attn_grads, attn_outs[layer]),
            ):
                sums[name, layer] = DpSum(spot, src, out, take(3))
        tail_refs = take(10)
        joined = tail_refs[0]
        joined_loads = [
            pltpu.make_async_copy(src, joined.at[i], store_sems.at[i])
            for i, src in enumerate(joined_hbm)
        ]
        for each in joined_loads:
            each.start()
    else:
        meet(ids)
    feed = Group((send, recv), ids, *first)
    attn = Group((send2, recv2), ids, *second)
    ebuf, fbuf = first[0], second[0]
    half = feed.half
    unit_rows = 2 * half
    width = cot_ref.shape[1]
    columns = heads * HD
    tiles = width // 256
    total, own, dx1 = (work.at[pl.ds(i * unit_rows, unit_rows)] for i in range(3))
    top = depth - 1
    packed = is_packed(lengths_ref, 8 * half)
    for part in range(2):
        rows = pl.ds(part * half, half)
        ebuf[rows, :] = cot_ref[rows, :]
        feed.send(part)
    loads.start(top, "wdown", "slope", "wup", "m", "g", "x1", "wout", "q", "k", "v", "lse")
    loads.start(top, "wq", "wk", "wv", "a", "o", "x")
    dxb[...] = cot_ref[...].astype(F32)
    small_ref[...] = jnp.zeros_like(small_ref)

    def outer(left, right, dst):
        def tile(index, carry):
            place = span(index * 256, 256)
            dst[place, :] = dot(left[:, place], right[...], TN).astype(BF)
            return carry

        lax.fori_loop(0, tiles, tile, 0)

    def turn_back(grad, rows, scale):
        cosine = cos_ref[rows, :]
        sine = sin_ref[rows, :]
        first_half = grad[:, :128]
        second_half = grad[:, 128:]
        return (
            ((first_half * cosine + second_half * sine) * scale).astype(BF),
            ((second_half * cosine - first_half * sine) * scale).astype(BF),
        )

    def event(name, layer, kind):
        if (name, layer) in sums:
            getattr(sums[name, layer], kind)()

    for layer in reversed(range(depth)):
        def note(row, value):
            small_ref[8 * layer + row : 8 * layer + row + 1, :] = value

        note(4, jnp.sum(dxb[...], axis=0, keepdims=True))
        dkb[...] = jnp.zeros_like(dkb)
        dvb[...] = jnp.zeros_like(dvb)
        loads.wait(layer, "wdown", "slope", "wup")

        def contract(step, carry):
            feed.receive(step)
            unit = jnp.where(step < 2, step, 5 - step)
            rows = span(unit * unit_rows, unit_rows)
            grad = dot(ebuf[rows, :], wdown[...], NT)
            grad = (grad * gpb[rows, :].astype(F32)).astype(BF)
            dhb[rows, :] = grad
            total[...] = dot(grad, wup[...], NT)
            feed.scatter(unit, total, own)
            return carry

        lax.fori_loop(0, 4, contract, 0)
        loads.start(layer - 1, "wdown", "slope", "wup")
        event("attn", layer + 1, "middle")
        event("up", layer + 1, "end")
        if layer < top:
            attn.finish()
        shift_sum = jnp.zeros((1, width), F32)
        scale_sum = jnp.zeros((1, width), F32)
        for part in range(2):
            if part == 0:
                loads.wait(layer, "m", "x1")
                outer(mbuf, dhb, feed_grads.at[0])
                event("up", layer, "start")
            else:
                loads.wait(layer, "g")
                outer(ebuf, gb, feed_grads.at[1])
                event("down", layer, "start")
            rows = pl.ds(part * half, half)
            grad = feed.collect(part, own)
            hat, rstd = norm(x1b[rows, :])
            shift_sum += jnp.sum(grad, axis=0, keepdims=True)
            scale_sum += jnp.sum(grad * hat, axis=0, keepdims=True)
            after = dxb[rows, :]
            after = after + norm_back(grad * (1.0 + cond_ref[8 * layer : 8 * layer + 1, width:]), hat, rstd)
            dx1[rows, :] = after
            fbuf[rows, :] = after.astype(BF)
            attn.send(part)
        note(0, shift_sum)
        note(1, scale_sum)
        loads.start(layer - 1, "m", "g", "x1")
        loads.wait(layer, "wout", "q", "k", "v", "lse")

        def attend(step, carry):
            attn.receive(step)
            unit = jnp.where(step < 2, step, 5 - step)
            rows = span(unit * unit_rows, unit_rows)
            grad_out = dot(fbuf[rows, :], wout[...], NT).astype(BF)
            queries = qb[rows, :]
            grad_queries = jnp.zeros((unit_rows, 256), F32)
            chunk = lax.broadcasted_iota(jnp.int32, (8, 1, unit_rows), 0)
            part = lax.broadcasted_iota(jnp.int32, (8, 1, unit_rows), 2) // half
            neg = apart(owner(chunk), unit_owner(unit, part), packed.reshape(1, 1, 1))
            for head in range(heads):
                place = pl.ds(head * unit_rows, unit_rows)
                masked = keep_head(queries, head, True)
                masked_out = keep_head(grad_out, head, False)
                qmask[place, :] = masked
                domask[place, :] = masked_out
                scores = dot(kb[...], masked, NT).reshape(8, half, unit_rows)
                shares = jnp.exp(scores - (lse[unit, head : head + 1, :] - neg))
                shares = shares.reshape(8 * half, unit_rows)
                grad_shares = dot(vb[...], masked_out, NT)
                centre = jnp.sum(shares * grad_shares, axis=0, keepdims=True)
                grad_scores = (shares * (grad_shares - centre)).astype(BF)
                pb[:, place] = shares.astype(BF)
                dsb[:, place] = grad_scores
                grad_queries = grad_queries + dot(grad_scores, keep_head(kb[...], head, True), TN)
            dkb[...] += dot(dsb[...], qmask[...])
            dvb[...] += dot(pb[...], domask[...])
            low, high = turn_back(grad_queries, rows, HD**-0.5)
            dqk[rows, :128] = low
            dqk[rows, 128:256] = high
            return carry

        lax.fori_loop(0, 4, attend, 0)
        loads.start(layer - 1, "wout", "q", "k", "v", "lse")
        event("down", layer + 1, "end")
        event("attn", layer + 1, "end")
        event("up", layer, "middle")
        loads.wait(layer, "wq", "wk", "wv")
        load_turned(wq, wk, wqk)

        def spread(step, carry):
            unit = 3 - step
            rows = span(unit * unit_rows, unit_rows)
            low, high = turn_back(dkb[rows, :], rows, 1.0)
            dqk[rows, 256:384] = low
            dqk[rows, 384:512] = high
            values = dvb[rows, :].astype(BF)
            dvv[rows, :] = values
            total[...] = dot(dqk[rows, :], wqk[...]) + dot(values, wv[...])
            attn.scatter(unit, total, own)
            return carry

        lax.fori_loop(0, 4, spread, 0)
        loads.start(layer - 1, "wq", "wk", "wv")
        event("down", layer, "middle")
        loads.wait(layer, "a", "o")
        places = (
            turned_place(columns, 0, 4 * columns),
            turned_place(columns, columns, 4 * columns),
            plain_place(columns, 2 * columns, 4 * columns),
            plain_place(columns, 3 * columns, 4 * columns),
        )

        def attn_tile(index, carry):
            place = span(index * 256, 256)
            normed = abuf[:, place]
            both = dot(normed, dqk[...], TN).astype(BF)
            made = dot(both[:, :256], places[0]) + dot(both[:, 256:], places[1])
            made = made + dot(dot(normed, dvv[...], TN).astype(BF), places[2])
            outs = dot(fbuf[:, place], ob[...], TN).astype(BF)
            attn_grads[place, :] = (made + dot(outs, places[3])).astype(BF)
            return carry

        lax.fori_loop(0, tiles, attn_tile, 0)
        loads.start(layer - 1, "a", "o")
        event("attn", layer, "start")
        if not deep:
            stores = [
                pltpu.make_async_copy(attn_grads, attn_outs[layer], store_sems.at[0]),
                pltpu.make_async_copy(feed_grads, feed_outs[layer], store_sems.at[1]),
            ]
            for each in stores:
                each.start()
            for each in stores:
                each.wait()
        feed.finish()
        loads.wait(layer, "x")
        gain_sum = jnp.zeros((1, width), F32)
        bias_sum = jnp.zeros((1, width), F32)
        for part in range(2):
            rows = pl.ds(part * half, half)
            grad = attn.collect(part, own)
            hat, rstd = norm(xb[rows, :])
            gain_sum += jnp.sum(grad * hat, axis=0, keepdims=True)
            bias_sum += jnp.sum(grad, axis=0, keepdims=True)
            made = dx1[rows, :] + norm_back(
                grad * gain_ref[layer : layer + 1, :], hat, rstd
            )
            dxb[rows, :] = made
            if layer:
                ebuf[rows, :] = made.astype(BF)
                feed.send(part)
        note(2, gain_sum)
        note(3, bias_sum)
        loads.start(layer - 1, "x")
    out_ref[...] = dxb[...]
    if deep:
        for each in joined_loads:
            each.wait()
        tail(deep, spot, ids, sums, dxb, small_ref, temb_ref, work, dsb, tail_refs,
             sum_ref, vec_ref, store_sems)
    attn.finish()


def tail(deep, spot, ids, sums, dxb, small_ref, temb_ref, work, dsb, scratch, sum_ref, vec_ref,
         store_sems):
    (joined, ebuf, jbuf, near_in, next_in, z_in, result, vecs, send, recv) = scratch
    sibling, far = ids
    place = lax.axis_index("tensor")
    core = lax.rem(place, 2)
    y = place // 2
    x, z = spot.x, spot.z
    width = dxb.shape[1]
    ladder = Ladder((send, recv))
    ebuf[0] = dxb[...].astype(BF)
    rows_copy = ladder.copy(ebuf.at[0], ebuf.at[1], sibling)
    joined_copy = ladder.copy(joined.at[1 - core], jbuf, sibling)
    mine = vecs.at[core, y, x, z]
    row = lax.broadcasted_iota(jnp.int32, small_ref.shape, 0)
    mine[...] = jnp.where(row == 5, temb_ref[0:1, :], small_ref[...]).astype(BF)
    vec_z = [ladder.copy(mine, mine, spot.along(ahead)) for ahead in range(1, deep)]
    rows_copy.wait_recv()
    joined_copy.wait_recv()
    rest = width // 2

    def tile(index, carry):
        rows = span(index * 256, 256)
        made = dot(joined[core, :, rows], ebuf[0], TN)
        work[rows, :] = made + dot(jbuf[:, rows], ebuf[1], TN)
        return carry

    lax.fori_loop(0, width // 256, tile, 0)
    half, quarter = width // 2, width // 4
    piece = quarter // deep
    ways = (((far, y), (spot.across, x)), ((spot.across, x), (far, y)))
    lanes = (pl.ds(0, rest), pl.ds(rest, rest))
    firsts = []
    for side, ((device, bit), _) in enumerate(ways):
        out = dsb.at[pl.ds(0, half), lanes[side]]
        out[...] = work[span((1 - bit) * half, half), lanes[side]].astype(BF)
        firsts.append(ladder.copy(out, near_in.at[side], device))
    for each in vec_z:
        each.wait_recv()
    row_z = vecs.at[core, y, x]
    vec_x = ladder.copy(row_z, row_z, spot.across)
    seconds = []
    for side, ((_, bit), (device, bit2)) in enumerate(ways):
        firsts[side].wait_recv()
        kept = work.at[span(bit * half, half), lanes[side]]
        kept[...] = kept[...] + near_in[side].astype(F32)
        out = dsb.at[pl.ds(half, quarter), lanes[side]]
        out[...] = work[span(bit * half + (1 - bit2) * quarter, quarter), lanes[side]].astype(BF)
        seconds.append(ladder.copy(out, next_in.at[side], device))
    vec_x.wait_recv()
    plane = vecs.at[core, y]
    vec_y = ladder.copy(plane, plane, far)
    sums["attn", 0].middle()
    thirds = []
    for side, ((_, bit), (_, bit2)) in enumerate(ways):
        seconds[side].wait_recv()
        kept = work.at[span(bit * half + bit2 * quarter, quarter), lanes[side]]
        kept[...] = kept[...] + next_in[side].astype(F32)
        out = dsb.at[pl.ds(half + quarter, quarter), lanes[side]]
        out[...] = kept[...].astype(BF)
        for ahead in range(1, deep):
            start = half + quarter + spot.level(ahead) * piece
            thirds.append(
                ladder.copy(
                    dsb.at[span(start, piece), lanes[side]],
                    z_in.at[side, ahead - 1],
                    spot.along(ahead),
                )
            )
    sums["up", 0].end()
    sums["down", 0].end()
    vec_y.wait_recv()
    every = vecs.at[core]
    vec_core = ladder.copy(every, every, sibling)
    lasts = []
    for side, ((_, bit), (_, bit2)) in enumerate(ways):
        for ahead in range(1, deep):
            thirds[side * (deep - 1) + ahead - 1].wait_recv()
        start = bit * half + bit2 * quarter + z * piece
        made = work[span(start, piece), lanes[side]]
        for ahead in range(1, deep):
            made = made + z_in[side, ahead - 1].astype(F32)
        own = result.at[core, side, span(start, piece)]
        own[...] = made.astype(BF)
        lasts += [ladder.copy(own, own, spot.along(ahead)) for ahead in range(1, deep)]
    backs = []
    for side, ((_, bit), (device, bit2)) in enumerate(ways):
        for ahead in range(1, deep):
            lasts[side * (deep - 1) + ahead - 1].wait_recv()
        own = result.at[core, side, span(bit * half + bit2 * quarter, quarter)]
        backs.append(ladder.copy(own, own, device))
    ends = []
    for side, ((device, bit), _) in enumerate(ways):
        backs[side].wait_recv()
        own = result.at[core, side, span(bit * half, half)]
        ends.append(ladder.copy(own, own, device))
    sums["attn", 0].end()
    vec_core.wait_recv()
    vec_store = pltpu.make_async_copy(vecs, vec_ref, store_sems.at[0])
    vec_store.start()
    for each in ends:
        each.wait_recv()
    whole = ladder.copy(result.at[core], result.at[core], sibling)
    whole.wait_recv()
    sum_store = pltpu.make_async_copy(result, sum_ref, store_sems.at[1])
    sum_store.start()
    ladder.finish()
    vec_store.wait()
    sum_store.wait()


def backward(heads, deep, cotangent, gains, lengths, tables, weights, kept, joined):
    depth = len(kept)
    block, width = cotangent.shape
    length = 4 * block
    units = weights[2].shape[2]
    columns = heads * HD
    part = width // (2 * deep) if deep else width
    half, quarter = width // 2, width // 4
    held = [[each[name] for name in SAVED] for each in kept]
    scratch = [pltpu.SemaphoreType.DMA((6, 2))] * 4
    scratch += [pltpu.SemaphoreType.DMA((6 + len(SAVED),)), pltpu.SemaphoreType.DMA((2,))]
    scratch += [pltpu.VMEM((columns, width), BF)] * 3
    scratch += [pltpu.VMEM(each.shape[1:], BF) for each in weights[1:4]]
    scratch += [pltpu.VMEM(each.shape, each.dtype) for each in held[0]]
    scratch += group_scratch(length, width) + group_scratch(length, width)
    scratch += [
        pltpu.VMEM((512, width), BF),
        pltpu.VMEM((length, units), BF),
        pltpu.VMEM((heads * block, 256), BF),
        pltpu.VMEM((heads * block, columns), BF),
        pltpu.VMEM((length, heads * block), BF),
        pltpu.VMEM((length, heads * block), BF),
        pltpu.VMEM((length, 256), F32),
        pltpu.VMEM((length, columns), F32),
        pltpu.VMEM((length, 512), BF),
        pltpu.VMEM((length, columns), BF),
        pltpu.VMEM((3 * block, width), F32),
        pltpu.VMEM((block, width), F32),
        pltpu.VMEM((2, width, units), BF),
        pltpu.VMEM((width, 4 * columns), BF),
    ]
    out_shape = [
        jax.ShapeDtypeStruct((block, width), F32),
        jax.ShapeDtypeStruct((8 * depth, width), F32),
    ]
    kind = F32 if deep else BF
    out_shape += [jax.ShapeDtypeStruct((part, 4 * columns), kind)] * depth
    out_shape += [jax.ShapeDtypeStruct((2, part, units), kind)] * depth
    out_specs = [vmem_spec()] * 2 + [vmem_spec() if deep else any_spec()] * (2 * depth)
    if deep:
        for _ in range(depth):
            scratch += DpSum.scratch(deep, part, units) + DpSum.scratch(deep, part, units)
            scratch += DpSum.scratch(deep, part, 4 * columns)
        vec_shape = (2, 2, 2, deep, 8 * depth, width)
        scratch += [
            pltpu.VMEM((2, block, width), BF),
            pltpu.VMEM((2, block, width), BF),
            pltpu.VMEM((block, width), BF),
            pltpu.VMEM((2, half, half), BF),
            pltpu.VMEM((2, quarter, half), BF),
            pltpu.VMEM((2, deep - 1, quarter // deep, half), BF),
            pltpu.VMEM((2, 2, width, half), BF),
            pltpu.VMEM(vec_shape, BF),
            pltpu.SemaphoreType.DMA((LADDER_COPIES,)),
            pltpu.SemaphoreType.DMA((LADDER_COPIES,)),
        ]
        out_shape += [
            jax.ShapeDtypeStruct((2, 2, width, half), BF),
            jax.ShapeDtypeStruct(vec_shape, BF),
        ]
        out_specs += [any_spec(), any_spec()]

    def kernel(*refs):
        backward_kernel(depth, heads, deep, refs)

    operands = [cotangent, gains, lengths, *tables]
    in_specs = [vmem_spec()] * len(operands)
    remote = [*joined, *weights, *[each for layer in held for each in layer]]
    in_specs += [any_spec()] * len(remote)
    return pl.pallas_call(
        kernel,
        out_shape=out_shape,
        in_specs=in_specs,
        out_specs=out_specs,
        scratch_shapes=scratch,
        compiler_params=pltpu.CompilerParams(
            collective_id=9, has_side_effects=True, vmem_limit_bytes=LIMIT
        ),
        name="layers_backward",
    )(*operands, *remote)


def finish_kernel(depth, refs):
    (low_ref, wself_ref, sum_ref, vec_ref) = refs[:4]
    attn_refs = refs[4 : 4 + depth]
    feed_refs = refs[4 + depth : 4 + 2 * depth]
    (tokens_ref, gain_ref, bias_ref, bada_ref, bdown_ref) = refs[4 + 2 * depth : 9 + 2 * depth]
    (qkv_ref, out_ref, ada_ref, up_ref, down_ref, self_ref) = refs[9 + 2 * depth :]
    step = pl.program_id(0)
    members = vec_ref.shape[0] // (8 * depth)
    width = vec_ref.shape[1]

    def pick(row):
        device = lax.broadcasted_iota(jnp.int32, (members, vec_ref.shape[0]), 0)
        column = lax.broadcasted_iota(jnp.int32, (members, vec_ref.shape[0]), 1)
        wanted = (column == device * 8 * depth + row).astype(F32).astype(BF)
        return dot(wanted, vec_ref[...]).astype(BF)

    rows = ada_ref.shape[1]
    times = pick(5)
    device = lax.broadcasted_iota(jnp.int32, (width, rows), 0)
    column = lax.broadcasted_iota(jnp.int32, (width, rows), 1)
    chosen = (device == column + step * rows).astype(F32).astype(BF)
    times = dot(times, chosen).astype(BF)
    for layer in range(depth):
        for place in range(2):
            ada_ref[layer, :, place * width : (place + 1) * width] = dot(
                times, pick(8 * layer + place), TN
            )
    self_ref[:, : width // 2] = sum_ref[0].astype(F32)
    self_ref[:, width // 2 :] = sum_ref[1].astype(F32)

    @pl.when(step == 0)
    def _():
        row = lax.broadcasted_iota(jnp.int32, (8 * depth, vec_ref.shape[0]), 0)
        column = lax.broadcasted_iota(jnp.int32, (8 * depth, vec_ref.shape[0]), 1)
        ones = (column % (8 * depth) == row).astype(F32).astype(BF)
        totals = dot(ones, vec_ref[...])
        for layer in range(depth):
            here = slice(layer, layer + 1)
            base = 8 * layer
            bada_ref[here, :width] = totals[base : base + 1]
            bada_ref[here, width:] = totals[base + 1 : base + 2]
            gain_ref[here, :] = totals[base + 2 : base + 3]
            bias_ref[here, :] = totals[base + 3 : base + 4]
            bdown_ref[here, :] = totals[base + 4 : base + 5]

    @pl.when(step == 1)
    def _():
        tokens_ref[...] = dot(low_ref[...].astype(BF), wself_ref[...], NT)

    @pl.when(step == 2)
    def _():
        for layer in range(depth):
            grads = attn_refs[layer][...]
            columns = grads.shape[1] // 4
            for place in range(3):
                qkv_ref[layer, place] = grads[:, place * columns : (place + 1) * columns]
            out_ref[layer] = grads[:, 3 * columns :].T

    @pl.when(step == 3)
    def _():
        for layer in range(depth):
            up_ref[layer] = feed_refs[layer][0]
            down_ref[layer] = feed_refs[layer][1]


def finish(depth, low, w_self, sums, vectors, attn_shards, feed_shards):
    block, width = low.shape
    part, columns = attn_shards[0].shape
    columns //= 4
    units = feed_shards[0].shape[2]
    steps = 4
    rows = 2 * width // steps

    def fixed(*shape):
        return pl.BlockSpec(shape, lambda step: (0,) * len(shape))

    def kernel(*refs):
        finish_kernel(depth, refs)

    fixed_shapes = [
        (block, width),
        (depth, width),
        (depth, width),
        (depth, 2 * width),
        (depth, width),
        (depth, 3, part, columns),
        (depth, columns, part),
    ]
    shard = (depth, part, units)
    return pl.pallas_call(
        kernel,
        grid=(steps,),
        out_shape=[
            *[jax.ShapeDtypeStruct(each, F32) for each in fixed_shapes],
            jax.ShapeDtypeStruct((depth, width, 2 * width), F32),
            jax.ShapeDtypeStruct(shard, F32),
            jax.ShapeDtypeStruct(shard, F32),
            jax.ShapeDtypeStruct((2 * width, width), F32),
        ],
        in_specs=[
            fixed(block, width),
            fixed(width, width),
            pl.BlockSpec((None, 2, rows, width // 2), lambda step: (step // 2, 0, step % 2, 0)),
            fixed(*vectors.shape),
            *[fixed(*each.shape) for each in attn_shards],
            *[fixed(*each.shape) for each in feed_shards],
        ],
        out_specs=[
            *[fixed(*each) for each in fixed_shapes],
            pl.BlockSpec((depth, width // steps, 2 * width), lambda step: (0, step, 0)),
            fixed(*shard),
            fixed(*shard),
            pl.BlockSpec((rows, width), lambda step: (step, 0)),
        ],
        compiler_params=pltpu.CompilerParams(vmem_limit_bytes=LIMIT),
        name="write_grads",
    )(low, w_self, sums, vectors, *attn_shards, *feed_shards)


def local(
    tokens,
    cotangent,
    lengths,
    timesteps,
    w_self,
    ln_gain,
    ln_bias,
    w_qkv,
    w_out,
    w_ada,
    b_ada,
    w_up,
    w_down,
    b_down,
):
    width = tokens.shape[1]
    depth = w_qkv.shape[0]
    heads = w_qkv.shape[3] // HD
    deep = 4 if lax.axis_size("dp") == 8 else 0
    weights = (jnp.swapaxes(w_qkv, 2, 3), w_out, w_up, w_down, w_ada)
    vectors = (ln_gain, ln_bias, b_down, b_ada, lengths, timesteps)
    made, kept = forward(heads, tokens, w_self, vectors, weights)
    (activations, estimate, conds, cosine, sine, temb) = made
    made = backward(
        heads,
        deep,
        cotangent,
        ln_gain,
        lengths,
        (cosine, sine, temb, conds),
        weights,
        kept,
        (tokens, estimate),
    )
    grad_rows, smalls = made[:2]
    attn_shards = made[2 : 2 + depth]
    feed_shards = made[2 + depth : 2 + 2 * depth]
    if deep:
        sums, vectors = made[2 + 2 * depth :]
        vectors = vectors.reshape(-1, width)
    else:
        attn_shards = [
            lax.psum_scatter(each, "dp", scatter_dimension=0, tiled=True).astype(F32)
            for each in attn_shards
        ]
        feed_shards = [
            lax.psum_scatter(each, "dp", scatter_dimension=1, tiled=True).astype(F32)
            for each in feed_shards
        ]
        joined = jnp.concatenate([tokens, estimate], axis=1)
        sums = lax.psum(dot(joined, grad_rows.astype(BF), TN).astype(BF), ("dp", "tensor"))
        sums = sums.reshape(2, width, 2, width // 2).swapaxes(1, 2)
        vectors = smalls.at[5].set(temb[0]).astype(BF)
        vectors = lax.all_gather(vectors, ("dp", "tensor"), axis=0, tiled=True)
    made = finish(depth, grad_rows, w_self, sums, vectors, attn_shards, feed_shards)
    (grad_tokens, gain, bias, bias_ada, bias_down, qkv, out, ada, up, down, own) = made
    return (
        activations,
        grad_tokens,
        gain,
        bias,
        qkv,
        out,
        ada,
        bias_ada,
        up,
        jnp.swapaxes(down, 1, 2),
        bias_down,
        own,
    )


def solution(mesh):
    return jax.shard_map(
        local,
        mesh=mesh,
        in_specs=(
            P(("dp", "tensor"), None),
            P(("dp", "tensor"), None),
            P("dp", None),
            P("dp", None),
            P(),
            P(),
            P(),
            P(None, None, None, "tensor"),
            P(None, "tensor", None),
            P(),
            P(),
            P(None, None, "tensor"),
            P(None, "tensor", None),
            P(),
        ),
        out_specs=(
            P(("dp", "tensor"), None),
            P(("dp", "tensor"), None),
            P(),
            P(),
            P(None, None, "dp", "tensor"),
            P(None, "tensor", "dp"),
            P(),
            P(),
            P(None, "dp", "tensor"),
            P(None, "tensor", "dp"),
            P(),
            P(),
        ),
        check_vma=False,
    )
```

```python
import functools

import jax
import jax.numpy as jnp
from jax import lax
from jax.experimental import pallas as pl
from jax.experimental.pallas import tpu as pltpu
from jax.sharding import PartitionSpec as P

HD = 64
HALF = HD // 2
BF = jnp.bfloat16
F32 = jnp.float32
MESH = pl.DeviceIdType.MESH
EPS = 1e-05
LIMIT = 60 << 20

def norm(rows):
    centred = rows - jnp.mean(rows, axis=-1, keepdims=True)
    rstd = lax.rsqrt(jnp.mean(centred * centred, axis=-1, keepdims=True) + EPS)
    return (centred * rstd, rstd)


def norm_back(grad, hat, rstd):
    return rstd * (
        grad
        - jnp.mean(grad, axis=-1, keepdims=True)
        - hat * jnp.mean(grad * hat, axis=-1, keepdims=True)
    )


def dot(left, right, dims=((1,), (0,))):
    return lax.dot_general(left, right, (dims, ((), ())), preferred_element_type=F32)


NT = ((1,), (1,))
TN = ((0,), (0,))


def head_mask(head, columns, rotary):
    lane = lax.broadcasted_iota(jnp.int32, (1, columns), 1)
    if rotary:
        return (lane % 128) // HALF == head
    return lane // HD == head


def keep_head(rows, head, rotary):
    return jnp.where(head_mask(head, rows.shape[1], rotary), rows, jnp.zeros_like(rows))


def turned_place(columns, start, total):
    row = lax.broadcasted_iota(jnp.int32, (256, total), 0)
    column = lax.broadcasted_iota(jnp.int32, (256, total), 1) - start
    source = column // HD * HALF + column % HD // HALF * 128 + column % HALF
    fits = (source == row) & (column >= 0) & (column < columns)
    return fits.astype(F32).astype(BF)


def plain_place(columns, start, total):
    row = lax.broadcasted_iota(jnp.int32, (columns, total), 0)
    column = lax.broadcasted_iota(jnp.int32, (columns, total), 1) - start
    return (row == column).astype(F32).astype(BF)


def span(start, size):
    return pl.ds(pl.multiple_of(start, size), size)


class Gather:
    def __init__(self, sems, ids, rows):
        self.sems, self.ids, self.rows = sems, ids, rows
        self.half = rows.shape[0] // 8

    def copy(self, src, dst, kind, part, far):
        send, recv = self.sems
        return pltpu.make_async_remote_copy(
            src_ref=self.rows.at[span(src, self.half)],
            dst_ref=self.rows.at[span(dst, self.half)],
            send_sem=send.at[kind, part],
            recv_sem=recv.at[kind, part],
            device_id=self.ids[1] if far else self.ids[0],
            device_id_type=MESH,
        )

    def own(self, part):
        return span(2 * self.half * part, self.half)

    def pair(self, part):
        return 6 * self.half - 2 * self.half * part

    def far_copy(self, part):
        return self.copy(2 * self.half * part, self.pair(part), 0, part, True)

    def sibling_copy(self, part):
        start = 2 * self.half * part
        return self.copy(start, start + self.half, 1, part, False)

    def forward_copy(self, part):
        return self.copy(self.pair(part), self.pair(part) + self.half, 2, part, False)

    def send(self, part):
        self.far_copy(part).start()
        self.sibling_copy(part).start()

    def near(self, part):
        self.sibling_copy(part).wait_recv()

    def far(self, part):
        self.far_copy(part).wait_recv()
        self.forward_copy(part).start()
        self.forward_copy(part).wait()

    def receive(self, step):
        @pl.when(step < 2)
        def _():
            self.near(step)

        @pl.when(step >= 2)
        def _():
            self.far(step - 2)

    def finish(self, far=True):
        for part in range(2):
            self.sibling_copy(part).wait_send()
            if far:
                self.far_copy(part).wait_send()


class Scatter:
    def __init__(self, sems, ids, own, buffers):
        self.sems, self.ids, self.own_sum = sems, ids, own
        self.pair_out, self.pair_in, self.own_out, self.own_in, self.far_out, self.far_in = buffers
        self.half = self.pair_out.shape[1]

    def copy(self, src, dst, kind, part, far):
        send, recv = self.sems
        return pltpu.make_async_remote_copy(
            src_ref=src.at[part],
            dst_ref=dst.at[part],
            send_sem=send.at[kind, part],
            recv_sem=recv.at[kind, part],
            device_id=self.ids[1] if far else self.ids[0],
            device_id_type=MESH,
        )

    def pair_copy(self, part):
        return self.copy(self.pair_out, self.pair_in, 0, part, False)

    def own_copy(self, part):
        return self.copy(self.own_out, self.own_in, 1, part, False)

    def sum_copy(self, part):
        return self.copy(self.far_out, self.far_in, 2, part, True)

    def send(self, unit, total):
        @pl.when(unit < 2)
        def _():
            self.own_sum[span(self.half * unit, self.half), :] = total[: self.half, :]
            self.own_out[unit] = total[self.half :, :].astype(BF)
            self.own_copy(unit).start()

        @pl.when(unit >= 2)
        def _():
            part = 3 - unit
            self.pair_out[part] = total[self.half :, :].astype(BF)
            self.pair_copy(part).start()
            self.pair_copy(part).wait_recv()
            self.far_out[part] = (
                total[: self.half, :] + self.pair_in[part].astype(F32)
            ).astype(BF)
            self.sum_copy(part).start()

    def collect(self, part):
        self.own_copy(part).wait_recv()
        self.sum_copy(part).wait_recv()
        rows = pl.ds(part * self.half, self.half)
        made = self.own_sum[rows, :] + self.own_in[part].astype(F32)
        return made + self.far_in[part].astype(F32)

    def finish(self):
        for part in range(2):
            self.pair_copy(part).wait_send()
            self.own_copy(part).wait_send()
            self.sum_copy(part).wait_send()


class Near:
    def __init__(self, sems, ids, own, out, into):
        self.sems, self.ids = sems, ids
        self.own, self.out, self.into = own, out, into
        self.half = out.shape[1]

    def copy(self, part):
        return pltpu.make_async_remote_copy(
            src_ref=self.out.at[part],
            dst_ref=self.into.at[part],
            send_sem=self.sems.at[0, part],
            recv_sem=self.sems.at[1, part],
            device_id=self.ids[0],
            device_id_type=MESH,
        )

    def send(self, part, total):
        self.own[span(self.half * part, self.half), :] = total[: self.half, :]
        self.out[part] = total[self.half :, :].astype(BF)
        self.copy(part).start()

    def collect(self, part):
        self.copy(part).wait_recv()
        return self.own[pl.ds(part * self.half, self.half), :] + self.into[part].astype(F32)

    def drain(self):
        for part in range(2):
            self.copy(part).wait_send()


class Fetch:
    def __init__(self, sems, ids, square, shards):
        self.sems, self.shards = sems, shards
        self.far = ids[1]
        self.x, self.z, self.x_peer, self.z_peer = square
        self.piece = shards.shape[1] // 8

    def copy(self, index, src, start, size, device):
        place = span(start * self.piece, size * self.piece)
        return pltpu.make_async_remote_copy(
            src_ref=self.shards.at[src, place],
            dst_ref=self.shards.at[1, place],
            send_sem=self.sems.at[0, index],
            recv_sem=self.sems.at[1, index],
            device_id=device,
            device_id_type=MESH,
        )

    def hop(self, index):
        x_first = 2 * self.z + self.x
        z_first = 4 + 2 * self.x + self.z
        return (
            lambda: self.copy(0, 0, x_first, 1, self.far),
            lambda: self.copy(1, 0, z_first, 1, self.far),
            lambda: self.copy(2, 1, x_first, 1, self.x_peer),
            lambda: self.copy(3, 1, z_first, 1, self.z_peer),
            lambda: self.copy(4, 1, 2 * self.z, 2, self.z_peer),
            lambda: self.copy(5, 1, 4 + 2 * self.x, 2, self.x_peer),
        )[index]()

    def step(self, count):
        if count == 1:
            self.hop(0).start()
            self.hop(1).start()
        elif count < 4:
            for index in (2 * count - 4, 2 * count - 3):
                self.hop(index).wait_recv()
                self.hop(index + 2).start()
        else:
            self.hop(4).wait_recv()
            self.hop(5).wait_recv()

    def finish(self):
        for index in range(6):
            self.hop(index).wait_send()


def square():
    group = lax.axis_index("dp")
    place = lax.axis_index("tensor")
    x = lax.rem(group, 2)
    z = lax.rem(group // 2, 2)
    return (x, z, (group + 1 - 2 * x, place), (group + 2 - 4 * z, place))


def neighbours():
    group = lax.axis_index("dp")
    place = lax.axis_index("tensor")
    core = lax.rem(place, 2)
    return ((group, place + 1 - 2 * core), (group, lax.rem(place + 2, 4)))


class Spot:
    def __init__(self, deep):
        group = lax.axis_index("dp")
        self.place = lax.axis_index("tensor")
        self.deep = deep
        self.z = group // 2
        self.x = lax.rem(group, 2)
        self.across = (2 * self.z + 1 - self.x, self.place)

    def level(self, ahead):
        return lax.rem(self.z + ahead, self.deep)

    def along(self, ahead):
        return (2 * self.level(ahead) + self.x, self.place)

    def partners(self):
        return [self.across] + [self.along(ahead) for ahead in range(1, self.deep)]


def meet(ids):
    barrier = pltpu.get_barrier_semaphore()
    for device in ids:
        pl.semaphore_signal(barrier, inc=1, device_id=device, device_id_type=MESH)
    pl.semaphore_wait(barrier, len(ids))


class DpSum:
    def __init__(self, spot, src, out, scratch):
        self.spot, self.src, self.out = spot, src, out
        self.pairs, self.rest, self.sems = scratch
        self.block = self.pairs.shape[1]

    @staticmethod
    def scratch(deep, block, columns):
        return [
            pltpu.VMEM((deep, block, columns), BF),
            pltpu.VMEM((deep - 1, block, columns), BF),
            pltpu.SemaphoreType.DMA((4, deep)),
        ]

    def rows(self, ahead, x):
        start = (2 * self.spot.level(ahead) + x) * self.block
        return pl.ds(pl.multiple_of(start, self.block), self.block)

    def x_copy(self, ahead):
        return pltpu.make_async_remote_copy(
            src_ref=self.src.at[self.rows(ahead, 1 - self.spot.x)],
            dst_ref=self.pairs.at[ahead],
            send_sem=self.sems.at[0, ahead],
            recv_sem=self.sems.at[1, ahead],
            device_id=self.spot.across,
            device_id_type=MESH,
        )

    def z_copy(self, ahead):
        return pltpu.make_async_remote_copy(
            src_ref=self.pairs.at[ahead],
            dst_ref=self.rest.at[ahead - 1],
            send_sem=self.sems.at[2, ahead],
            recv_sem=self.sems.at[3, ahead],
            device_id=self.spot.along(ahead),
            device_id_type=MESH,
        )

    def order(self):
        return [*range(1, self.spot.deep), 0]

    def start(self):
        for ahead in self.order():
            self.x_copy(ahead).start()

    def middle(self):
        for ahead in self.order():
            self.x_copy(ahead).wait_recv()
            total = self.src[self.rows(ahead, self.spot.x), :].astype(F32)
            total = total + self.pairs[ahead].astype(F32)
            if ahead:
                self.pairs[ahead] = total.astype(BF)
                self.z_copy(ahead).start()
            else:
                self.out[...] = total
        for ahead in self.order():
            self.x_copy(ahead).wait_send()

    def end(self):
        for ahead in range(1, self.spot.deep):
            self.z_copy(ahead).wait_recv()
        total = self.out[...]
        for ahead in range(1, self.spot.deep):
            total = total + self.rest[ahead - 1].astype(F32)
        self.out[...] = total
        for ahead in range(1, self.spot.deep):
            self.z_copy(ahead).wait_send()


def scatter_scratch(rows, width):
    return [pltpu.VMEM((2, rows // 8, width), BF)] * 6


def gelu_parts(hidden):
    cdf = 0.5 * (1.0 + lax.erf(hidden * (0.5**0.5)))
    density = jnp.exp(hidden * hidden * -0.5) * 0.3989422804014327
    return (hidden * cdf, cdf + hidden * density)


def load_turned(wq, wk, wqk):
    turn = turned_place(wq.shape[0], 0, wq.shape[0])
    wqk[:256, :] = dot(turn, wq[...]).astype(BF)
    wqk[256:, :] = dot(turn, wk[...]).astype(BF)


def is_packed(lengths_ref, length):
    return (lengths_ref[:, 0:1] < length).astype(jnp.int32).astype(F32)


def owner(chunk):
    return 2 * (chunk // 4) + chunk % 2


def apart(keys, queries, packed):
    return (keys != queries).astype(jnp.int32).astype(F32) * (packed * -1e9)


def unit_owner(unit, half):
    return jnp.where(unit < 2, 0, 2) + half


SAVED = ("a", "q", "k", "v", "o", "x1", "m", "g", "slope", "x", "lse")


def forward_kernel(depth, heads, refs):
    refs = list(refs)

    def take(count):
        made = refs[:count]
        del refs[:count]
        return made

    (gain_ref, bias_ref, bdown_ref, bada_ref, lengths_ref, steps_ref) = take(6)
    (rotary_ref, time_ref, cot_ref) = take(3)
    (tokens_hbm, wself_hbm, wqkv_hbm, wout_hbm, wup_hbm, wdown_hbm, wada_hbm) = take(7)
    (acts_ref, est_ref, cond_ref, cos_ref, sin_ref, temb_ref, grad_hbm) = take(7)
    saved_hbm = [dict(zip(SAVED, take(len(SAVED)))) for _ in range(depth)]
    gather_sems = [take(2) for _ in range(5)]
    (near_a_sems, near_f_sems, fetch_sems, cross_send, cross_recv) = take(5)
    (load_sems, store_sems) = take(2)
    (tokens, wself, wada) = take(3)
    wa, wu, wd, wqk = take(depth), take(depth), take(depth), take(depth)
    abufs, mbufs, (ebuf,) = take(2), take(2), take(1)
    (q2, k2, v2, ob2, lse2, accs, stats, gb, gpb) = take(9)
    (x1, xb, start, own_a, own_f, sums) = take(6)
    near_a_bufs, near_f_bufs = take(2), take(2)
    ids = neighbours()
    corner = square()
    columns = heads * HD
    width = xb.shape[1]
    half = xb.shape[0] // 2
    unit_rows = 2 * half
    length = 8 * half
    part_a = [pl.ds(part * columns, columns) for part in range(4)]
    sources = [tokens_hbm, wself_hbm.at[0], wself_hbm.at[1]]
    places = [tokens, wself.at[0], wself.at[1]]
    for layer in range(depth):
        sources += [wqkv_hbm.at[layer, part] for part in range(3)] + [wout_hbm.at[layer]]
        places += [wa[layer].at[0, rows] for rows in part_a]
        sources += [wup_hbm.at[layer], wdown_hbm.at[layer]]
        places += [wu[layer].at[0], wd[layer].at[0]]
    loads = [
        pltpu.make_async_copy(src, dst, load_sems.at[i])
        for i, (src, dst) in enumerate(zip(sources, places))
    ]
    ada_loads = [
        pltpu.make_async_copy(wada_hbm.at[layer], wada, load_sems.at[len(loads)])
        for layer in range(depth)
    ]
    order = [0, 1, *range(3, 9)]
    for i in order:
        loads[i].start()
    ada_loads[0].start()
    for i in range(len(loads)):
        if i not in order:
            loads[i].start()
    meet([*ids, *corner[2:]])
    fetches = []
    for layer in range(depth):
        for shards in (wa[layer], wu[layer], wd[layer]):
            fetches.append(Fetch(fetch_sems.at[len(fetches)], ids, corner, shards))
    gathers = [Gather(gather_sems[i], ids, abufs[i]) for i in range(2)]
    mixes = [Gather(gather_sems[2 + i], ids, mbufs[i]) for i in range(2)]
    grads = Gather(gather_sems[4], ids, ebuf)
    near_a = Near(near_a_sems, ids, own_a, *near_a_bufs)
    near_f = Near(near_f_sems, ids, own_f, *near_f_bufs)
    packed = is_packed(lengths_ref, length)
    pending = []

    def store(name, src, dst):
        made = pltpu.make_async_copy(src, dst, store_sems.at[len(pending)])
        made.start()
        pending.append([name, made, False])

    def stored(*names):
        for each in pending:
            if each[0] in names and not each[2]:
                each[1].wait()
                each[2] = True

    def begin(number, part, made):
        layer = number % depth
        rows = pl.ds(part * half, half)
        if number >= 2 and part == 0:
            gathers[number % 2].finish()
        xb[rows, :] = made
        hat = norm(made)[0]
        gain = gain_ref[layer : layer + 1, :]
        normed = hat * gain + bias_ref[layer : layer + 1, :]
        abufs[number % 2][pl.ds(2 * half * part, half), :] = normed.astype(BF)
        gathers[number % 2].send(part)

    for i in (3, 4, 5, 6):
        loads[i].wait()
    fetches[0].step(1)
    loads[0].wait()
    loads[1].wait()
    for part in range(2):
        rows = pl.ds(part * half, half)
        made = dot(tokens[rows, :], wself[0])
        start[rows, :] = made
        begin(0, part, made)

    def make_tables():
        place = lax.axis_index("tensor")
        sibling = ids[0][1]
        far = ids[1][1]
        far_other = lax.rem(sibling + 2, 4)
        row = lax.broadcasted_iota(jnp.int32, (half, 128), 0).astype(F32)
        for chunk, (block, part) in enumerate(
            zip(
                (place, sibling, place, sibling, far, far_other, far, far_other),
                (0, 0, 1, 1, 1, 1, 0, 0),
            )
        ):
            rows = pl.ds(chunk * half, half)
            offset = (block * unit_rows).astype(F32)
            position = row + part * half + (1.0 - packed) * offset
            angle = position * rotary_ref[...]
            cos_ref[rows, :] = jnp.cos(angle)
            sin_ref[rows, :] = jnp.sin(angle)
        steps = steps_ref[...].astype(F32)
        slot = lax.broadcasted_iota(jnp.int32, steps.shape, 1)
        mine = jnp.sum(jnp.where(slot == place, steps, 0.0), axis=1, keepdims=True)
        step = packed * mine + (1.0 - packed) * steps[:, 0:1]
        angle = jnp.broadcast_to(step * time_ref[...], (8, width // 2))
        temb_ref[:, : width // 2] = jnp.cos(angle)
        temb_ref[:, width // 2 :] = jnp.sin(angle)

    def make_cond(layer):
        ada_loads[layer].wait()
        column = temb_ref[...].T[:, 0:1]
        made = jnp.sum(wada[...] * column, axis=0, keepdims=True)
        made = made + bada_ref[layer : layer + 1, :]
        cond_ref[8 * layer : 8 * layer + 8, :] = jnp.broadcast_to(made, (8, 2 * width))
        if layer + 1 < depth:
            ada_loads[layer + 1].start()

    def project(number, count, pick, before):
        layer = number % depth
        abuf = abufs[number % 2]

        def body(step, carry):
            before(step)
            shard, unit = pick(step)
            rows = span(unit * unit_rows, unit_rows)
            normed = abuf[rows, :]
            mixed = dot(normed, wqk[layer][shard], NT)
            cosine = cos_ref[rows, :]
            sine = sin_ref[rows, :]
            for place, dst, scale in ((0, q2, HD**-0.5), (256, k2, 1.0)):
                first = mixed[:, place : place + 128]
                second = mixed[:, place + 128 : place + 256]
                dst[shard, rows, :128] = ((first * cosine - second * sine) * scale).astype(BF)
                dst[shard, rows, 128:] = ((second * cosine + first * sine) * scale).astype(BF)
            v2[shard, rows, :] = dot(normed, wa[layer][shard, part_a[2], :], NT).astype(BF)
            return carry

        lax.fori_loop(0, count, body, 0)

    lane = lax.broadcasted_iota(jnp.int32, (1, 128), 1)

    def scores_of(shard, unit, head, keys):
        rows = span(unit * unit_rows, unit_rows)
        made = dot(keep_head(q2[shard, rows, :], head, True), k2[shard, keys, :], NT)
        part = lax.broadcasted_iota(jnp.int32, (2, 1, length // 2), 0)
        chunk = lax.broadcasted_iota(jnp.int32, (2, 1, length // 2), 2) // half
        neg = apart(owner(chunk + keys.start // half), part, packed.reshape(1, 1, 1))
        return (made.reshape(2, half, length // 2) + neg).reshape(unit_rows, length // 2)

    def attend_near(number, count, pick, before):
        keys = pl.ds(0, length // 2)

        def body(step, carry):
            before(step)
            shard, unit = pick(step)
            place = 2 * unit + shard
            attended = jnp.zeros((unit_rows, columns), F32)
            tops = jnp.zeros((unit_rows, 128), F32)
            totals = jnp.zeros((unit_rows, 128), F32)
            for head in range(heads):
                scores = scores_of(shard, unit, head, keys)
                largest = jnp.max(scores, axis=-1, keepdims=True)
                shares = jnp.exp(scores - largest)
                output = dot(shares.astype(BF), v2[shard, keys, :])
                attended = jnp.where(head_mask(head, columns, False), output, attended)
                tops = jnp.where(lane == head, largest, tops)
                totals = jnp.where(lane == head, jnp.sum(shares, axis=-1, keepdims=True), totals)
            accs[place] = attended
            stats[place, 0] = tops
            stats[place, 1] = totals
            return carry

        lax.fori_loop(0, count, body, 0)

    def attend_far(number, save, before):
        keys = pl.ds(length // 2, length // 2)
        layer, slot = number % depth, number % 2

        def body(step, carry):
            before(step)
            shard, unit = by_unit(step)
            place = 2 * unit + shard
            rows = span(unit * unit_rows, unit_rows)
            attended = jnp.zeros((unit_rows, columns), F32)
            logs = jnp.zeros((unit_rows, 128), F32)
            for head in range(heads):
                scores = scores_of(shard, unit, head, keys)
                earlier = stats[place, 0][:, head : head + 1]
                largest = jnp.maximum(earlier, jnp.max(scores, axis=-1, keepdims=True))
                shares = jnp.exp(scores - largest)
                shrink = jnp.exp(earlier - largest)
                totals = stats[place, 1][:, head : head + 1] * shrink
                totals = totals + jnp.sum(shares, axis=-1, keepdims=True)
                output = dot(shares.astype(BF), v2[shard, keys, :])
                output = (accs[place] * shrink + output) * (1.0 / totals)
                attended = jnp.where(head_mask(head, columns, False), output, attended)
                if save:
                    logs = jnp.where(lane == head, largest + jnp.log(totals), logs)
            if save:
                lse2[slot, shard, unit] = logs.T[:8, :]
            attended = attended.astype(BF)
            ob2[slot, shard, rows, :] = attended

            @pl.when(shard == 1)
            def _():
                total = dot(ob2[slot, 0, rows, :], wa[layer][0, part_a[3], :])
                near_a.send(unit, total + dot(attended, wa[layer][1, part_a[3], :]))

            return carry

        lax.fori_loop(0, 4, body, 0)

    def feed(number, save, pick, before):
        layer = number % depth
        mbuf = mbufs[number % 2]

        def body(step, carry):
            before(step)
            shard, unit = pick(step)
            rows = span(unit * unit_rows, unit_rows)
            hidden = dot(mbuf[rows, :], wu[layer][shard])
            gated, slope = gelu_parts(hidden)
            gated = gated.astype(BF)
            made = dot(gated, wd[layer][shard])

            @pl.when(shard == 0)
            def _():
                if save:
                    gb[rows, :] = gated
                    gpb[rows, :] = slope.astype(BF)
                sums[rows, :] = made

            @pl.when(shard == 1)
            def _():
                near_f.send(unit, sums[rows, :] + made)

            return carry

        lax.fori_loop(0, 4, body, 0)

    crossings = {}

    def cross(number):
        slot = number % 2
        made = []
        for part in range(2):
            pairs = (
                (
                    ob2.at[slot, 1, pl.ds(part * unit_rows, unit_rows)],
                    ob2.at[slot, 0, pl.ds((3 - part) * unit_rows, unit_rows)],
                ),
                (lse2.at[slot, 1, part], lse2.at[slot, 0, 3 - part]),
            )
            for kind, (src, dst) in enumerate(pairs):
                place = 4 * slot + 2 * part + kind
                made.append(
                    pltpu.make_async_remote_copy(
                        src_ref=src,
                        dst_ref=dst,
                        send_sem=cross_send.at[place],
                        recv_sem=cross_recv.at[place],
                        device_id=ids[1],
                        device_id_type=MESH,
                    )
                )
                made[-1].start()
        crossings[number] = made

    def late(number):
        slot = number % 2
        saved = saved_hbm[number % depth]
        if number == depth:
            for part in range(2):
                grads.near(part)
                grads.far(part)
            store("grad", ebuf, grad_hbm)
        for part in range(2):
            mixes[slot].far(part)
        store("m", mbufs[slot], saved["m"])
        for each in crossings[number]:
            each.wait_recv()
        store("o", ob2.at[slot, 0], saved["o"])
        store("lse", lse2.at[slot, 0], saved["lse"])

    def steps_of(*pairs):
        for index, count in pairs:
            if index < len(fetches):
                fetches[index].step(count)

    def events(table):
        def before(step):
            for when, actions in table.items():

                @pl.when(step == when)
                def _():
                    for action in actions:
                        if isinstance(action, tuple):
                            if action[0] < len(fetches):
                                fetches[action[0]].step(action[1])
                        else:
                            action()

        return before

    def waits(*indices):
        def action():
            for index in indices:
                loads[index].wait()

        return action

    def by_unit(step):
        return (lax.rem(step, 2), step // 2)

    def by_shard(step):
        return (step // 2, lax.rem(step, 2))

    def run(number, after_layer):
        layer, slot = number % depth, number % 2
        save = number >= depth
        group, mix = gathers[slot], mixes[slot]
        mix_rows = mbufs[slot]
        base = 3 * layer

        def after_attend(part):
            def action():
                if part == 0 and number >= 2:
                    mix.finish(far=False)
                if part == 0:
                    stored("x1")
                rows = pl.ds(part * half, half)
                after = xb[rows, :] + near_a.collect(part)
                x1[rows, :] = after
                shift = cond_ref[8 * layer : 8 * layer + 1, :width]
                scale = cond_ref[8 * layer : 8 * layer + 1, width:]
                made = norm(after)[0] * (1.0 + scale) + shift
                mix_rows[pl.ds(2 * half * part, half), :] = made.astype(BF)
                mix.sibling_copy(part).start()
                if save:
                    mix.far_copy(part).start()

            return action

        def after_feed(part):
            def action():
                if part == 0:
                    stored("x")
                rows = pl.ds(part * half, half)
                made = x1[rows, :] + near_f.collect(part) + bdown_ref[layer : layer + 1, :]
                after_layer(part, rows, made)

            return action

        def near_rows(part):
            return lambda: group.near(part)

        def far_rows(part):
            return lambda: group.far(part)

        def mixed(part):
            return lambda: mix.near(part)

        if number:
            near_a.drain()
            near_f.drain()
        stored("q", "k", "v")
        if save:
            if number == depth:
                for part in range(2):
                    ebuf[grads.own(part), :] = cot_ref[pl.ds(part * half, half), :]
                    grads.send(part)
            arrive = events({0: [near_rows(0)], 1: [near_rows(1)]})
            project(number, 4, by_shard, arrive)
            attend_near(number, 4, by_unit, events({}))
            if number > depth:
                late(number - 1)
            arrive = events({0: [far_rows(0)], 2: [far_rows(1)]})
            project(number, 4, lambda step: (lax.rem(step, 2), 3 - step // 2), arrive)
            store("a", abufs[slot], saved_hbm[layer]["a"])
            store("x", xb, saved_hbm[layer]["x"])
            for name, src in (("q", q2), ("k", k2), ("v", v2)):
                store(name, src.at[0], saved_hbm[layer][name])
            far_table = {3: [after_attend(0)]}
            feed_table = {
                0: [mixed(0)],
                1: [after_attend(1)],
                2: [mixed(1)],
                3: [after_feed(0)],
            }
            order = by_unit
        else:
            if layer == 0:
                make_tables()
            load_turned(
                wa[layer].at[0, part_a[0]], wa[layer].at[0, part_a[1]], wqk[layer].at[0]
            )
            rows_table = {
                0: [near_rows(0)],
                1: [near_rows(1)],
                2: [far_rows(0)],
                3: [far_rows(1)],
            }
            if layer == 0:
                rows_table[2] = [(0, 2), far_rows(0)]
                rows_table[3] = [far_rows(1), waits(7), (1, 1)]
                first_near = {0: [(0, 3)]}
                second_near = {1: [(1, 3)]}
                far_table = {0: [(2, 2), waits(9, 10, 11, 12), (3, 1)], 3: [after_attend(0)]}
                feed_table = {
                    0: [mixed(0), (3, 2), waits(13), (4, 1)],
                    1: [after_attend(1), mixed(1), (2, 3), (1, 4)],
                    2: [(2, 4), (3, 3), (4, 2), waits(14), (5, 1)],
                    3: [after_feed(0)],
                }
                order = by_shard
            else:
                rows_table[2] = [(base + 1, 3), *rows_table[2]]
                rows_table[3] = [*rows_table[3], (base + 2, 2)]
                first_near = {}
                second_near = {0: [(base + 2, 3)]}
                far_table = {3: [after_attend(0)]}
                feed_table = {
                    0: [mixed(0), (base + 1, 4)],
                    1: [after_attend(1), (base + 2, 4)],
                    2: [mixed(1)],
                    3: [after_feed(0)],
                }
                order = by_unit

            def in_order(step):
                return jnp.where(step < 2, step, 5 - step)

            project(number, 4, lambda step: (0, in_order(step)), events(rows_table))
            attend_near(number, 2, lambda step: (0, step), events(first_near))
            make_cond(layer)
            if layer == 0:
                events({0: [waits(8), (2, 1), (1, 2)]})(0)
            events({0: [(base, 4)]})(0)
            load_turned(
                wa[layer].at[1, part_a[0]], wa[layer].at[1, part_a[1]], wqk[layer].at[1]
            )
            project(number, 4, lambda step: (1, in_order(step)), events({}))
            attend_near(number, 2, lambda step: (1, step), events(second_near))
        attend_far(number, save, events(far_table))
        if save:
            cross(number)
        stored("g", "slope")
        feed(number, save, order, events(feed_table))
        if save:
            store("x1", x1, saved_hbm[layer]["x1"])
            store("g", gb, saved_hbm[layer]["g"])
            store("slope", gpb, saved_hbm[layer]["slope"])
        after_feed(1)()

    def between(part, rows, made):
        estimate = made.astype(BF)
        est_ref[rows, :] = estimate
        begin(depth, part, start[rows, :] + dot(estimate, wself[1]))

    def close(part, rows, made):
        acts_ref[rows, :] = made.astype(BF)

    def enter(number):
        return lambda part, rows, made: begin(number, part, made)

    for number in range(2 * depth):
        if number + 1 == 2 * depth:
            run(number, close)
        elif number + 1 == depth:
            loads[2].wait()
            run(number, between)
        else:
            run(number, enter(number + 1))
    late(2 * depth - 1)
    for each in gathers:
        each.finish()
    for each in (*mixes, grads):
        each.finish()
    near_a.drain()
    near_f.drain()
    for each in fetches:
        each.finish()
    for each in crossings.values():
        for copy in each:
            copy.wait_send()
    stored("grad", *SAVED)


def any_spec():
    return pl.BlockSpec(memory_space=pl.ANY)


def vmem_spec():
    return pl.BlockSpec(memory_space=pltpu.VMEM)


def forward(heads, tokens, cotangent, w_self, vectors, weights):
    depth = weights[0].shape[0]
    block, width = tokens.shape
    length = 4 * block
    half = block // 2
    columns = heads * HD
    units = weights[2].shape[2]
    lanes = jnp.arange(128) % HALF
    rotary = jnp.exp(-jnp.log(10000.0) * lanes.astype(F32) / HALF)[None]
    halves = jnp.arange(width // 2).astype(F32)
    times = jnp.exp(-jnp.log(10000.0) * halves / (width // 2))[None]
    kept = {
        "a": ((length, width), BF),
        "q": ((length, 256), BF),
        "k": ((length, 256), BF),
        "v": ((length, columns), BF),
        "o": ((length, columns), BF),
        "x1": ((block, width), F32),
        "m": ((length, width), BF),
        "g": ((length // 2, units), BF),
        "slope": ((length // 2, units), BF),
        "x": ((block, width), F32),
        "lse": ((4, 8, block), F32),
    }
    kept_shapes = [jax.ShapeDtypeStruct(*kept[name]) for name in SAVED]
    out_shape = [
        jax.ShapeDtypeStruct((block, width), BF),
        jax.ShapeDtypeStruct((block, width), BF),
        jax.ShapeDtypeStruct((8 * depth, 2 * width), F32),
        jax.ShapeDtypeStruct((length, 128), F32),
        jax.ShapeDtypeStruct((length, 128), F32),
        jax.ShapeDtypeStruct((8, width), F32),
        jax.ShapeDtypeStruct((length, width), BF),
    ] + kept_shapes * depth
    out_specs = [vmem_spec()] * 6 + [any_spec()] * (1 + depth * len(SAVED))
    dma = pltpu.SemaphoreType.DMA
    scratch = [dma((3, 2))] * 10
    scratch += [dma((2, 2))] * 2 + [dma((3 * depth, 2, 6)), dma((8,)), dma((8,))]
    scratch += [dma((4 + 6 * depth,)), dma((1 + depth * len(SAVED),))]
    scratch += [
        pltpu.VMEM((block, width), BF),
        pltpu.VMEM((2, width, width), BF),
        pltpu.VMEM((width, 2 * width), F32),
    ]
    scratch += [pltpu.VMEM((2, 4 * columns, width), BF)] * depth
    scratch += [pltpu.VMEM((2, width, units), BF)] * depth
    scratch += [pltpu.VMEM((2, units, width), BF)] * depth
    scratch += [pltpu.VMEM((2, 512, width), BF)] * depth
    scratch += [pltpu.VMEM((length, width), BF)] * 5
    scratch += [
        pltpu.VMEM((2, length, 256), BF),
        pltpu.VMEM((2, length, 256), BF),
        pltpu.VMEM((2, length, columns), BF),
        pltpu.VMEM((2, 2, length, columns), BF),
        pltpu.VMEM((2, 2, 4, 8, block), F32),
        pltpu.VMEM((4, block, columns), F32),
        pltpu.VMEM((4, 2, block, 128), F32),
        pltpu.VMEM((length // 2, units), BF),
        pltpu.VMEM((length // 2, units), BF),
    ]
    scratch += [pltpu.VMEM((block, width), F32)] * 5
    scratch += [pltpu.VMEM((2 * block, width), F32)]
    scratch += [pltpu.VMEM((2, half, width), BF)] * 4

    def kernel(*refs):
        forward_kernel(depth, heads, refs)

    operands = [*vectors, rotary, times, cotangent]
    remote = [tokens, w_self.reshape(2, width, width), *weights]
    made = pl.pallas_call(
        kernel,
        out_shape=out_shape,
        in_specs=[vmem_spec()] * len(operands) + [any_spec()] * len(remote),
        out_specs=out_specs,
        scratch_shapes=scratch,
        compiler_params=pltpu.CompilerParams(
            collective_id=1, has_side_effects=True, vmem_limit_bytes=LIMIT
        ),
        name="layers_forward",
    )(*operands, *remote)
    count = len(SAVED)
    saved = [made[7 + count * layer : 7 + count * (layer + 1)] for layer in range(depth)]
    return (made[:7], [dict(zip(SAVED, each)) for each in saved])


class Ladder:
    def __init__(self, sems):
        self.send, self.recv = sems
        self.used = 0
        self.open = []

    def copy(self, src, dst, device):
        made = pltpu.make_async_remote_copy(
            src_ref=src,
            dst_ref=dst,
            send_sem=self.send.at[self.used],
            recv_sem=self.recv.at[self.used],
            device_id=device,
            device_id_type=MESH,
        )
        self.used += 1
        assert self.used <= LADDER_COPIES
        made.start()
        self.open.append(made)
        return made

    def finish(self):
        for each in self.open:
            each.wait_send()


LADDER_COPIES = 34


class Loads:
    def __init__(self, sems):
        self.sems = sems
        self.names = {}

    def add(self, name, sources, buffer):
        self.names[name] = (sources, buffer, len(self.names))
        return buffer

    def copy(self, name, layer):
        sources, buffer, place = self.names[name]
        return pltpu.make_async_copy(sources[layer], buffer, self.sems.at[place])

    def start(self, layer, *names):
        if layer >= 0:
            for name in names:
                self.copy(name, layer).start()

    def wait(self, layer, *names):
        for name in names:
            self.copy(name, layer).wait()


def backward_kernel(depth, heads, deep, refs):
    refs = list(refs)

    def take(count):
        made = refs[:count]
        del refs[:count]
        return made

    cot_ref, gain_ref, lengths_ref, cos_ref, sin_ref, temb_ref, cond_ref = take(7)
    joined_hbm = take(2)
    (grad_hbm,) = take(1)
    wqkv_hbm, wout_hbm, wup_hbm, wdown_hbm, _ = take(5)
    saved_hbm = [dict(zip(SAVED, take(len(SAVED)))) for _ in range(depth)]
    (out_ref, small_ref) = take(2)
    attn_outs, feed_outs = take(depth), take(depth)
    if deep:
        sum_ref, vec_ref = take(2)
    feed_sems, attn_sems = [take(2), take(2)], [take(2), take(2)]
    load_sems, store_sems = take(2)
    loads = Loads(load_sems)
    wq, wk, wv = (
        loads.add(name, [wqkv_hbm.at[layer, part] for layer in range(depth)], take(1)[0])
        for part, name in enumerate(("wq", "wk", "wv"))
    )
    wout, wup, wdown = (
        loads.add(name, [src.at[layer] for layer in range(depth)], take(1)[0])
        for name, src in (("wout", wout_hbm), ("wup", wup_hbm), ("wdown", wdown_hbm))
    )
    buffers = dict(zip(SAVED, take(len(SAVED))))
    for name in SAVED:
        rows = saved_hbm[0][name].shape[0]
        buffer = buffers[name]
        if rows < buffer.shape[0]:
            buffer = buffer.at[pl.ds(0, rows)]
        loads.add(name, [saved_hbm[layer][name] for layer in range(depth)], buffer)
    abuf, qb, kb, vb, ob, x1b, mbuf, gb, gpb, xb, lse = (buffers[name] for name in SAVED)
    ebuf, fbuf = take(2)
    feed_bufs, attn_bufs = take(6), take(6)
    (wqk, dhb, qmask, domask, dsb, pb, dkb, dvb, dqk, dvv, work, dxb) = take(12)
    (feed_grads, attn_grads) = take(2)
    ids = neighbours()
    sums = {}
    if deep:
        spot = Spot(deep)
        meet([*ids, *spot.partners()])
        for layer in range(depth):
            for name, src, out in (
                ("up", feed_grads.at[0], feed_outs[layer].at[0]),
                ("down", feed_grads.at[1], feed_outs[layer].at[1]),
                ("attn", attn_grads, attn_outs[layer]),
            ):
                sums[name, layer] = DpSum(spot, src, out, take(3))
        tail_refs = take(10)
        joined = tail_refs[0]
        joined_loads = [
            pltpu.make_async_copy(src, joined.at[i], store_sems.at[i])
            for i, src in enumerate(joined_hbm)
        ]
        for each in joined_loads:
            each.start()
    else:
        meet(ids)
    width = cot_ref.shape[1]
    half = cot_ref.shape[0] // 2
    unit_rows = 2 * half
    total, own, dx1 = (work.at[pl.ds(i * unit_rows, unit_rows)] for i in range(3))
    feed_rows = Gather(feed_sems[0], ids, ebuf)
    feed_sum = Scatter(feed_sems[1], ids, own, feed_bufs)
    attn_rows = Gather(attn_sems[0], ids, fbuf)
    attn_sum = Scatter(attn_sems[1], ids, own, attn_bufs)
    columns = heads * HD
    tiles = width // 256
    top = depth - 1
    packed = is_packed(lengths_ref, 8 * half)
    loads.add("grad", [grad_hbm] * depth, ebuf)
    loads.start(top, "m", "wup", "grad", "wdown", "slope", "x1", "wout", "q", "k", "v", "lse", "g")
    loads.start(top, "wq", "wk", "wv", "a", "o", "x")
    dxb[...] = cot_ref[...].astype(F32)
    small_ref[...] = jnp.zeros_like(small_ref)

    def outer(left, right, dst):
        def tile(index, carry):
            place = span(index * 256, 256)
            dst[place, :] = dot(left[:, place], right[...], TN).astype(BF)
            return carry

        lax.fori_loop(0, tiles, tile, 0)

    def turn_back(grad, rows, scale):
        cosine = cos_ref[rows, :]
        sine = sin_ref[rows, :]
        first_half = grad[:, :128]
        second_half = grad[:, 128:]
        return (
            ((first_half * cosine + second_half * sine) * scale).astype(BF),
            ((second_half * cosine - first_half * sine) * scale).astype(BF),
        )

    def event(name, layer, kind):
        if (name, layer) in sums:
            getattr(sums[name, layer], kind)()

    for layer in reversed(range(depth)):
        def note(row, value):
            small_ref[8 * layer + row : 8 * layer + row + 1, :] = value

        note(4, jnp.sum(dxb[...], axis=0, keepdims=True))
        dkb[...] = jnp.zeros_like(dkb)
        dvb[...] = jnp.zeros_like(dvb)
        loads.wait(layer, "m", "wup")

        def expand(step, carry):
            rows = span((3 - step) * unit_rows, unit_rows)
            gated, slope = gelu_parts(dot(mbuf[rows, :], wup[...]))
            gb[rows, :] = gated.astype(BF)
            gpb[rows, :] = slope.astype(BF)
            return carry

        lax.fori_loop(0, 2, expand, 0)
        loads.wait(layer, "wdown", "slope")
        if layer == top:
            loads.wait(layer, "grad")

        def contract(step, carry):
            if layer == top:
                unit = jnp.where(step < 2, 3 - step, step - 2)
            else:
                feed_rows.receive(step)
                unit = jnp.where(step < 2, step, 5 - step)
            rows = span(unit * unit_rows, unit_rows)
            grad = dot(ebuf[rows, :], wdown[...], NT)
            grad = (grad * gpb[rows, :].astype(F32)).astype(BF)
            dhb[rows, :] = grad
            total[...] = dot(grad, wup[...], NT)
            feed_sum.send(unit, total)
            return carry

        lax.fori_loop(0, 4, contract, 0)
        loads.start(layer - 1, "wdown", "slope")
        event("attn", layer + 1, "middle")
        event("up", layer + 1, "end")
        if layer < top:
            attn_rows.finish()
            attn_sum.finish()
        shift_sum = jnp.zeros((1, width), F32)
        scale_sum = jnp.zeros((1, width), F32)
        for part in range(2):
            if part == 0:
                loads.wait(layer, "x1")
                outer(mbuf, dhb, feed_grads.at[0])
                event("up", layer, "start")
            else:
                loads.wait(layer, "g")
                outer(ebuf, gb, feed_grads.at[1])
                event("down", layer, "start")
            rows = pl.ds(part * half, half)
            grad = feed_sum.collect(part)
            hat, rstd = norm(x1b[rows, :])
            shift_sum += jnp.sum(grad, axis=0, keepdims=True)
            scale_sum += jnp.sum(grad * hat, axis=0, keepdims=True)
            after = dxb[rows, :]
            after = after + norm_back(grad * (1.0 + cond_ref[8 * layer : 8 * layer + 1, width:]), hat, rstd)
            dx1[rows, :] = after
            fbuf[attn_rows.own(part), :] = after.astype(BF)
            attn_rows.send(part)
        note(0, shift_sum)
        note(1, scale_sum)
        loads.start(layer - 1, "m", "g", "x1", "wup")
        loads.wait(layer, "wout", "q", "k", "v", "lse")

        def attend(step, carry):
            attn_rows.receive(step)
            unit = jnp.where(step < 2, step, 5 - step)
            rows = span(unit * unit_rows, unit_rows)
            grad_out = dot(fbuf[rows, :], wout[...], NT).astype(BF)
            queries = qb[rows, :]
            grad_queries = jnp.zeros((unit_rows, 256), F32)
            chunk = lax.broadcasted_iota(jnp.int32, (8, 1, unit_rows), 0)
            part = lax.broadcasted_iota(jnp.int32, (8, 1, unit_rows), 2) // half
            neg = apart(owner(chunk), unit_owner(unit, part), packed.reshape(1, 1, 1))
            for head in range(heads):
                place = pl.ds(head * unit_rows, unit_rows)
                masked = keep_head(queries, head, True)
                masked_out = keep_head(grad_out, head, False)
                qmask[place, :] = masked
                domask[place, :] = masked_out
                scores = dot(kb[...], masked, NT).reshape(8, half, unit_rows)
                shares = jnp.exp(scores - (lse[unit, head : head + 1, :] - neg))
                shares = shares.reshape(8 * half, unit_rows)
                grad_shares = dot(vb[...], masked_out, NT)
                centre = jnp.sum(shares * grad_shares, axis=0, keepdims=True)
                grad_scores = (shares * (grad_shares - centre)).astype(BF)
                pb[:, place] = shares.astype(BF)
                dsb[:, place] = grad_scores
                grad_queries = grad_queries + dot(grad_scores, keep_head(kb[...], head, True), TN)
            dkb[...] += dot(dsb[...], qmask[...])
            dvb[...] += dot(pb[...], domask[...])
            low, high = turn_back(grad_queries, rows, HD**-0.5)
            dqk[rows, :128] = low
            dqk[rows, 128:256] = high
            return carry

        lax.fori_loop(0, 4, attend, 0)
        loads.start(layer - 1, "wout", "q", "k", "v", "lse")
        event("down", layer + 1, "end")
        event("attn", layer + 1, "end")
        event("up", layer, "middle")
        loads.wait(layer, "wq", "wk", "wv")
        load_turned(wq, wk, wqk)

        def spread(step, carry):
            unit = jnp.where(step < 2, 3 - step, step - 2)
            rows = span(unit * unit_rows, unit_rows)
            low, high = turn_back(dkb[rows, :], rows, 1.0)
            dqk[rows, 256:384] = low
            dqk[rows, 384:512] = high
            values = dvb[rows, :].astype(BF)
            dvv[rows, :] = values
            total[...] = dot(dqk[rows, :], wqk[...]) + dot(values, wv[...])
            attn_sum.send(unit, total)
            return carry

        lax.fori_loop(0, 4, spread, 0)
        loads.start(layer - 1, "wq", "wk", "wv")
        event("down", layer, "middle")
        loads.wait(layer, "a", "o")
        places = (
            turned_place(columns, 0, 4 * columns),
            turned_place(columns, columns, 4 * columns),
            plain_place(columns, 2 * columns, 4 * columns),
            plain_place(columns, 3 * columns, 4 * columns),
        )

        def attn_tile(index, carry):
            place = span(index * 256, 256)
            normed = abuf[:, place]
            both = dot(normed, dqk[...], TN).astype(BF)
            made = dot(both[:, :256], places[0]) + dot(both[:, 256:], places[1])
            made = made + dot(dot(normed, dvv[...], TN).astype(BF), places[2])
            outs = dot(fbuf[:, place], ob[...], TN).astype(BF)
            attn_grads[place, :] = (made + dot(outs, places[3])).astype(BF)
            return carry

        lax.fori_loop(0, tiles, attn_tile, 0)
        loads.start(layer - 1, "a", "o")
        event("attn", layer, "start")
        if not deep:
            stores = [
                pltpu.make_async_copy(attn_grads, attn_outs[layer], store_sems.at[0]),
                pltpu.make_async_copy(feed_grads, feed_outs[layer], store_sems.at[1]),
            ]
            for each in stores:
                each.start()
            for each in stores:
                each.wait()
        if layer < top:
            feed_rows.finish()
        feed_sum.finish()
        loads.wait(layer, "x")
        gain_sum = jnp.zeros((1, width), F32)
        bias_sum = jnp.zeros((1, width), F32)
        for part in range(2):
            rows = pl.ds(part * half, half)
            grad = attn_sum.collect(part)
            hat, rstd = norm(xb[rows, :])
            gain_sum += jnp.sum(grad * hat, axis=0, keepdims=True)
            bias_sum += jnp.sum(grad, axis=0, keepdims=True)
            made = dx1[rows, :] + norm_back(
                grad * gain_ref[layer : layer + 1, :], hat, rstd
            )
            dxb[rows, :] = made
            if layer:
                ebuf[feed_rows.own(part), :] = made.astype(BF)
                feed_rows.send(part)
        note(2, gain_sum)
        note(3, bias_sum)
        loads.start(layer - 1, "x")
    out_ref[...] = dxb[...]
    if deep:
        for each in joined_loads:
            each.wait()
        tail(deep, spot, ids, sums, dxb, small_ref, temb_ref, work, dsb, tail_refs,
             sum_ref, vec_ref, store_sems)
    attn_rows.finish()
    attn_sum.finish()


def tail(deep, spot, ids, sums, dxb, small_ref, temb_ref, work, dsb, scratch, sum_ref, vec_ref,
         store_sems):
    (joined, ebuf, jbuf, near_in, next_in, z_in, result, vecs, send, recv) = scratch
    sibling, far = ids
    place = lax.axis_index("tensor")
    core = lax.rem(place, 2)
    y = place // 2
    x, z = spot.x, spot.z
    width = dxb.shape[1]
    ladder = Ladder((send, recv))
    ebuf[0] = dxb[...].astype(BF)
    rows_copy = ladder.copy(ebuf.at[0], ebuf.at[1], sibling)
    joined_copy = ladder.copy(joined.at[1 - core], jbuf, sibling)
    mine = vecs.at[core, y, x, z]
    row = lax.broadcasted_iota(jnp.int32, small_ref.shape, 0)
    mine[...] = jnp.where(row == 5, temb_ref[0:1, :], small_ref[...]).astype(BF)
    vec_z = [ladder.copy(mine, mine, spot.along(ahead)) for ahead in range(1, deep)]
    rows_copy.wait_recv()
    joined_copy.wait_recv()
    rest = width // 2

    def tile(index, carry):
        rows = span(index * 256, 256)
        made = dot(joined[core, :, rows], ebuf[0], TN)
        work[rows, :] = made + dot(jbuf[:, rows], ebuf[1], TN)
        return carry

    lax.fori_loop(0, width // 256, tile, 0)
    half, quarter = width // 2, width // 4
    piece = quarter // deep
    ways = (((far, y), (spot.across, x)), ((spot.across, x), (far, y)))
    lanes = (pl.ds(0, rest), pl.ds(rest, rest))
    firsts = []
    for side, ((device, bit), _) in enumerate(ways):
        out = dsb.at[pl.ds(0, half), lanes[side]]
        out[...] = work[span((1 - bit) * half, half), lanes[side]].astype(BF)
        firsts.append(ladder.copy(out, near_in.at[side], device))
    for each in vec_z:
        each.wait_recv()
    row_z = vecs.at[core, y, x]
    vec_x = ladder.copy(row_z, row_z, spot.across)
    seconds = []
    for side, ((_, bit), (device, bit2)) in enumerate(ways):
        firsts[side].wait_recv()
        kept = work.at[span(bit * half, half), lanes[side]]
        kept[...] = kept[...] + near_in[side].astype(F32)
        out = dsb.at[pl.ds(half, quarter), lanes[side]]
        out[...] = work[span(bit * half + (1 - bit2) * quarter, quarter), lanes[side]].astype(BF)
        seconds.append(ladder.copy(out, next_in.at[side], device))
    vec_x.wait_recv()
    plane = vecs.at[core, y]
    vec_y = ladder.copy(plane, plane, far)
    sums["attn", 0].middle()
    thirds = []
    for side, ((_, bit), (_, bit2)) in enumerate(ways):
        seconds[side].wait_recv()
        kept = work.at[span(bit * half + bit2 * quarter, quarter), lanes[side]]
        kept[...] = kept[...] + next_in[side].astype(F32)
        out = dsb.at[pl.ds(half + quarter, quarter), lanes[side]]
        out[...] = kept[...].astype(BF)
        for ahead in range(1, deep):
            start = half + quarter + spot.level(ahead) * piece
            thirds.append(
                ladder.copy(
                    dsb.at[span(start, piece), lanes[side]],
                    z_in.at[side, ahead - 1],
                    spot.along(ahead),
                )
            )
    sums["up", 0].end()
    sums["down", 0].end()
    vec_y.wait_recv()
    every = vecs.at[core]
    vec_core = ladder.copy(every, every, sibling)
    lasts = []
    for side, ((_, bit), (_, bit2)) in enumerate(ways):
        for ahead in range(1, deep):
            thirds[side * (deep - 1) + ahead - 1].wait_recv()
        start = bit * half + bit2 * quarter + z * piece
        made = work[span(start, piece), lanes[side]]
        for ahead in range(1, deep):
            made = made + z_in[side, ahead - 1].astype(F32)
        own = result.at[core, side, span(start, piece)]
        own[...] = made.astype(BF)
        lasts += [ladder.copy(own, own, spot.along(ahead)) for ahead in range(1, deep)]
    backs = []
    for side, ((_, bit), (device, bit2)) in enumerate(ways):
        for ahead in range(1, deep):
            lasts[side * (deep - 1) + ahead - 1].wait_recv()
        own = result.at[core, side, span(bit * half + bit2 * quarter, quarter)]
        backs.append(ladder.copy(own, own, device))
    ends = []
    for side, ((device, bit), _) in enumerate(ways):
        backs[side].wait_recv()
        own = result.at[core, side, span(bit * half, half)]
        ends.append(ladder.copy(own, own, device))
    sums["attn", 0].end()
    vec_core.wait_recv()
    vec_store = pltpu.make_async_copy(vecs, vec_ref, store_sems.at[0])
    vec_store.start()
    for each in ends:
        each.wait_recv()
    whole = ladder.copy(result.at[core], result.at[core], sibling)
    whole.wait_recv()
    sum_store = pltpu.make_async_copy(result, sum_ref, store_sems.at[1])
    sum_store.start()
    ladder.finish()
    vec_store.wait()
    sum_store.wait()


def backward(heads, deep, cotangent, grad_all, gains, lengths, tables, weights, kept, joined):
    depth = len(kept)
    block, width = cotangent.shape
    length = 4 * block
    units = weights[2].shape[2]
    columns = heads * HD
    part = width // (2 * deep) if deep else width
    half, quarter = width // 2, width // 4
    held = [[each[name] for name in SAVED] for each in kept]
    scratch = [pltpu.SemaphoreType.DMA((3, 2))] * 8
    scratch += [pltpu.SemaphoreType.DMA((7 + len(SAVED),)), pltpu.SemaphoreType.DMA((2,))]
    scratch += [pltpu.VMEM((columns, width), BF)] * 3
    scratch += [pltpu.VMEM(each.shape[1:], BF) for each in weights[1:4]]
    for name, each in zip(SAVED, held[0]):
        shape = (length, units) if name in ("g", "slope") else each.shape
        scratch.append(pltpu.VMEM(shape, each.dtype))
    scratch += [pltpu.VMEM((length, width), BF)] * 2
    scratch += scatter_scratch(length, width) + scatter_scratch(length, width)
    scratch += [
        pltpu.VMEM((512, width), BF),
        pltpu.VMEM((length, units), BF),
        pltpu.VMEM((heads * block, 256), BF),
        pltpu.VMEM((heads * block, columns), BF),
        pltpu.VMEM((length, heads * block), BF),
        pltpu.VMEM((length, heads * block), BF),
        pltpu.VMEM((length, 256), F32),
        pltpu.VMEM((length, columns), F32),
        pltpu.VMEM((length, 512), BF),
        pltpu.VMEM((length, columns), BF),
        pltpu.VMEM((3 * block, width), F32),
        pltpu.VMEM((block, width), F32),
        pltpu.VMEM((2, width, units), BF),
        pltpu.VMEM((width, 4 * columns), BF),
    ]
    out_shape = [
        jax.ShapeDtypeStruct((block, width), F32),
        jax.ShapeDtypeStruct((8 * depth, width), F32),
    ]
    kind = F32 if deep else BF
    out_shape += [jax.ShapeDtypeStruct((part, 4 * columns), kind)] * depth
    out_shape += [jax.ShapeDtypeStruct((2, part, units), kind)] * depth
    out_specs = [vmem_spec()] * 2 + [vmem_spec() if deep else any_spec()] * (2 * depth)
    if deep:
        for _ in range(depth):
            scratch += DpSum.scratch(deep, part, units) + DpSum.scratch(deep, part, units)
            scratch += DpSum.scratch(deep, part, 4 * columns)
        vec_shape = (2, 2, 2, deep, 8 * depth, width)
        scratch += [
            pltpu.VMEM((2, block, width), BF),
            pltpu.VMEM((2, block, width), BF),
            pltpu.VMEM((block, width), BF),
            pltpu.VMEM((2, half, half), BF),
            pltpu.VMEM((2, quarter, half), BF),
            pltpu.VMEM((2, deep - 1, quarter // deep, half), BF),
            pltpu.VMEM((2, 2, width, half), BF),
            pltpu.VMEM(vec_shape, BF),
            pltpu.SemaphoreType.DMA((LADDER_COPIES,)),
            pltpu.SemaphoreType.DMA((LADDER_COPIES,)),
        ]
        out_shape += [
            jax.ShapeDtypeStruct((2, 2, width, half), BF),
            jax.ShapeDtypeStruct(vec_shape, BF),
        ]
        out_specs += [any_spec(), any_spec()]

    def kernel(*refs):
        backward_kernel(depth, heads, deep, refs)

    operands = [cotangent, gains, lengths, *tables]
    in_specs = [vmem_spec()] * len(operands)
    remote = [*joined, grad_all, *weights, *[each for layer in held for each in layer]]
    in_specs += [any_spec()] * len(remote)
    return pl.pallas_call(
        kernel,
        out_shape=out_shape,
        in_specs=in_specs,
        out_specs=out_specs,
        scratch_shapes=scratch,
        compiler_params=pltpu.CompilerParams(
            collective_id=9, has_side_effects=True, vmem_limit_bytes=LIMIT
        ),
        name="layers_backward",
    )(*operands, *remote)


def finish_kernel(depth, refs):
    (low_ref, wself_ref, sum_ref, vec_ref) = refs[:4]
    attn_refs = refs[4 : 4 + depth]
    feed_refs = refs[4 + depth : 4 + 2 * depth]
    (tokens_ref, gain_ref, bias_ref, bada_ref, bdown_ref) = refs[4 + 2 * depth : 9 + 2 * depth]
    (qkv_ref, out_ref, ada_ref, up_ref, down_ref, self_ref) = refs[9 + 2 * depth :]
    step = pl.program_id(0)
    members = vec_ref.shape[0] // (8 * depth)
    width = vec_ref.shape[1]

    def pick(row):
        device = lax.broadcasted_iota(jnp.int32, (members, vec_ref.shape[0]), 0)
        column = lax.broadcasted_iota(jnp.int32, (members, vec_ref.shape[0]), 1)
        wanted = (column == device * 8 * depth + row).astype(F32).astype(BF)
        return dot(wanted, vec_ref[...]).astype(BF)

    rows = ada_ref.shape[1]
    times = pick(5)
    device = lax.broadcasted_iota(jnp.int32, (width, rows), 0)
    column = lax.broadcasted_iota(jnp.int32, (width, rows), 1)
    chosen = (device == column + step * rows).astype(F32).astype(BF)
    times = dot(times, chosen).astype(BF)
    for layer in range(depth):
        for place in range(2):
            ada_ref[layer, :, place * width : (place + 1) * width] = dot(
                times, pick(8 * layer + place), TN
            )
    self_ref[:, : width // 2] = sum_ref[0].astype(F32)
    self_ref[:, width // 2 :] = sum_ref[1].astype(F32)

    @pl.when(step == 0)
    def _():
        row = lax.broadcasted_iota(jnp.int32, (8 * depth, vec_ref.shape[0]), 0)
        column = lax.broadcasted_iota(jnp.int32, (8 * depth, vec_ref.shape[0]), 1)
        ones = (column % (8 * depth) == row).astype(F32).astype(BF)
        totals = dot(ones, vec_ref[...])
        for layer in range(depth):
            here = slice(layer, layer + 1)
            base = 8 * layer
            bada_ref[here, :width] = totals[base : base + 1]
            bada_ref[here, width:] = totals[base + 1 : base + 2]
            gain_ref[here, :] = totals[base + 2 : base + 3]
            bias_ref[here, :] = totals[base + 3 : base + 4]
            bdown_ref[here, :] = totals[base + 4 : base + 5]

    @pl.when(step == 1)
    def _():
        tokens_ref[...] = dot(low_ref[...].astype(BF), wself_ref[...], NT)

    @pl.when(step == 2)
    def _():
        for layer in range(depth):
            grads = attn_refs[layer][...]
            columns = grads.shape[1] // 4
            for place in range(3):
                qkv_ref[layer, place] = grads[:, place * columns : (place + 1) * columns]
            out_ref[layer] = grads[:, 3 * columns :].T

    @pl.when(step == 3)
    def _():
        for layer in range(depth):
            up_ref[layer] = feed_refs[layer][0]
            down_ref[layer] = feed_refs[layer][1]


def finish(depth, low, w_self, sums, vectors, attn_shards, feed_shards):
    block, width = low.shape
    part, columns = attn_shards[0].shape
    columns //= 4
    units = feed_shards[0].shape[2]
    steps = 4
    rows = 2 * width // steps

    def fixed(*shape):
        return pl.BlockSpec(shape, lambda step: (0,) * len(shape))

    def kernel(*refs):
        finish_kernel(depth, refs)

    fixed_shapes = [
        (block, width),
        (depth, width),
        (depth, width),
        (depth, 2 * width),
        (depth, width),
        (depth, 3, part, columns),
        (depth, columns, part),
    ]
    shard = (depth, part, units)
    return pl.pallas_call(
        kernel,
        grid=(steps,),
        out_shape=[
            *[jax.ShapeDtypeStruct(each, F32) for each in fixed_shapes],
            jax.ShapeDtypeStruct((depth, width, 2 * width), F32),
            jax.ShapeDtypeStruct(shard, F32),
            jax.ShapeDtypeStruct(shard, F32),
            jax.ShapeDtypeStruct((2 * width, width), F32),
        ],
        in_specs=[
            fixed(block, width),
            fixed(width, width),
            pl.BlockSpec((None, 2, rows, width // 2), lambda step: (step // 2, 0, step % 2, 0)),
            fixed(*vectors.shape),
            *[fixed(*each.shape) for each in attn_shards],
            *[fixed(*each.shape) for each in feed_shards],
        ],
        out_specs=[
            *[fixed(*each) for each in fixed_shapes],
            pl.BlockSpec((depth, width // steps, 2 * width), lambda step: (0, step, 0)),
            fixed(*shard),
            fixed(*shard),
            pl.BlockSpec((rows, width), lambda step: (step, 0)),
        ],
        compiler_params=pltpu.CompilerParams(vmem_limit_bytes=LIMIT),
        name="write_grads",
    )(low, w_self, sums, vectors, *attn_shards, *feed_shards)


def local(
    tokens,
    cotangent,
    lengths,
    timesteps,
    w_self,
    ln_gain,
    ln_bias,
    w_qkv,
    w_out,
    w_ada,
    b_ada,
    w_up,
    w_down,
    b_down,
):
    width = tokens.shape[1]
    depth = w_qkv.shape[0]
    heads = w_qkv.shape[3] // HD
    deep = 4 if lax.axis_size("dp") == 8 else 0
    weights = (jnp.swapaxes(w_qkv, 2, 3), w_out, w_up, w_down, w_ada)
    vectors = (ln_gain, ln_bias, b_down, b_ada, lengths, timesteps)
    made, kept = forward(heads, tokens, cotangent, w_self, vectors, weights)
    (activations, estimate, conds, cosine, sine, temb, grad_all) = made
    made = backward(
        heads,
        deep,
        cotangent,
        grad_all,
        ln_gain,
        lengths,
        (cosine, sine, temb, conds),
        weights,
        kept,
        (tokens, estimate),
    )
    grad_rows, smalls = made[:2]
    attn_shards = made[2 : 2 + depth]
    feed_shards = made[2 + depth : 2 + 2 * depth]
    if deep:
        sums, vectors = made[2 + 2 * depth :]
        vectors = vectors.reshape(-1, width)
    else:
        attn_shards = [
            lax.psum_scatter(each, "dp", scatter_dimension=0, tiled=True).astype(F32)
            for each in attn_shards
        ]
        feed_shards = [
            lax.psum_scatter(each, "dp", scatter_dimension=1, tiled=True).astype(F32)
            for each in feed_shards
        ]
        joined = jnp.concatenate([tokens, estimate], axis=1)
        sums = lax.psum(dot(joined, grad_rows.astype(BF), TN).astype(BF), ("dp", "tensor"))
        sums = sums.reshape(2, width, 2, width // 2).swapaxes(1, 2)
        vectors = smalls.at[5].set(temb[0]).astype(BF)
        vectors = lax.all_gather(vectors, ("dp", "tensor"), axis=0, tiled=True)
    made = finish(depth, grad_rows, w_self, sums, vectors, attn_shards, feed_shards)
    (grad_tokens, gain, bias, bias_ada, bias_down, qkv, out, ada, up, down, own) = made
    return (
        activations,
        grad_tokens,
        gain,
        bias,
        qkv,
        out,
        ada,
        bias_ada,
        up,
        jnp.swapaxes(down, 1, 2),
        bias_down,
        own,
    )


def solution(mesh):
    return jax.shard_map(
        local,
        mesh=mesh,
        in_specs=(
            P(("dp", "tensor"), None),
            P(("dp", "tensor"), None),
            P("dp", None),
            P("dp", None),
            P(),
            P(),
            P(),
            P(None, None, None, "tensor"),
            P(None, "tensor", None),
            P(),
            P(),
            P(None, None, "tensor"),
            P(None, "tensor", None),
            P(),
        ),
        out_specs=(
            P(("dp", "tensor"), None),
            P(("dp", "tensor"), None),
            P(),
            P(),
            P(None, None, "dp", "tensor"),
            P(None, "tensor", "dp"),
            P(),
            P(),
            P(None, "dp", "tensor"),
            P(None, "tensor", "dp"),
            P(),
            P(),
        ),
        check_vma=False,
    )
```

```python
import functools

import jax
import jax.numpy as jnp
from jax import lax
from jax.experimental import pallas as pl
from jax.experimental.pallas import tpu as pltpu
from jax.sharding import PartitionSpec as P

HD = 64
HALF = HD // 2
BF = jnp.bfloat16
F32 = jnp.float32
MESH = pl.DeviceIdType.MESH
EPS = 1e-05
LIMIT = 60 << 20

def norm(rows):
    centred = rows - jnp.mean(rows, axis=-1, keepdims=True)
    rstd = lax.rsqrt(jnp.mean(centred * centred, axis=-1, keepdims=True) + EPS)
    return (centred * rstd, rstd)


def norm_back(grad, hat, rstd):
    return rstd * (
        grad
        - jnp.mean(grad, axis=-1, keepdims=True)
        - hat * jnp.mean(grad * hat, axis=-1, keepdims=True)
    )


def dot(left, right, dims=((1,), (0,))):
    return lax.dot_general(left, right, (dims, ((), ())), preferred_element_type=F32)


NT = ((1,), (1,))
TN = ((0,), (0,))


def head_mask(head, columns, rotary):
    lane = lax.broadcasted_iota(jnp.int32, (1, columns), 1)
    if rotary:
        return (lane % 128) // HALF == head
    return lane // HD == head


def keep_head(rows, head, rotary):
    return jnp.where(head_mask(head, rows.shape[1], rotary), rows, jnp.zeros_like(rows))


def turned_place(columns, start, total):
    row = lax.broadcasted_iota(jnp.int32, (256, total), 0)
    column = lax.broadcasted_iota(jnp.int32, (256, total), 1) - start
    source = column // HD * HALF + column % HD // HALF * 128 + column % HALF
    fits = (source == row) & (column >= 0) & (column < columns)
    return fits.astype(F32).astype(BF)


def plain_place(columns, start, total):
    row = lax.broadcasted_iota(jnp.int32, (columns, total), 0)
    column = lax.broadcasted_iota(jnp.int32, (columns, total), 1) - start
    return (row == column).astype(F32).astype(BF)


def span(start, size):
    return pl.ds(pl.multiple_of(start, size), size)


class Gather:
    def __init__(self, sems, ids, rows):
        self.sems, self.ids, self.rows = sems, ids, rows
        self.half = rows.shape[0] // 8

    def copy(self, src, dst, kind, part, far):
        send, recv = self.sems
        return pltpu.make_async_remote_copy(
            src_ref=self.rows.at[span(src, self.half)],
            dst_ref=self.rows.at[span(dst, self.half)],
            send_sem=send.at[kind, part],
            recv_sem=recv.at[kind, part],
            device_id=self.ids[1] if far else self.ids[0],
            device_id_type=MESH,
        )

    def own(self, part):
        return span(2 * self.half * part, self.half)

    def pair(self, part):
        return 6 * self.half - 2 * self.half * part

    def far_copy(self, part):
        return self.copy(2 * self.half * part, self.pair(part), 0, part, True)

    def sibling_copy(self, part):
        start = 2 * self.half * part
        return self.copy(start, start + self.half, 1, part, False)

    def forward_copy(self, part):
        return self.copy(self.pair(part), self.pair(part) + self.half, 2, part, False)

    def send(self, part):
        self.far_copy(part).start()
        self.sibling_copy(part).start()

    def near(self, part):
        self.sibling_copy(part).wait_recv()

    def arrive(self, part):
        self.far_copy(part).wait_recv()
        self.forward_copy(part).start()

    def settle(self, part):
        self.forward_copy(part).wait()

    def far(self, part):
        self.arrive(part)
        self.settle(part)

    def receive(self, step):
        @pl.when(step < 2)
        def _():
            self.near(step)

        @pl.when(step >= 2)
        def _():
            self.far(step - 2)

    def finish(self, far=True):
        for part in range(2):
            self.sibling_copy(part).wait_send()
            if far:
                self.far_copy(part).wait_send()


class Scatter:
    def __init__(self, sems, ids, own, buffers):
        self.sems, self.ids, self.own_sum = sems, ids, own
        self.pair_out, self.pair_in, self.own_out, self.own_in, self.far_out, self.far_in = buffers
        self.half = self.pair_out.shape[1]

    def copy(self, src, dst, kind, part, far):
        send, recv = self.sems
        return pltpu.make_async_remote_copy(
            src_ref=src.at[part],
            dst_ref=dst.at[part],
            send_sem=send.at[kind, part],
            recv_sem=recv.at[kind, part],
            device_id=self.ids[1] if far else self.ids[0],
            device_id_type=MESH,
        )

    def pair_copy(self, part):
        return self.copy(self.pair_out, self.pair_in, 0, part, False)

    def own_copy(self, part):
        return self.copy(self.own_out, self.own_in, 1, part, False)

    def sum_copy(self, part):
        return self.copy(self.far_out, self.far_in, 2, part, True)

    def send(self, unit, total):
        @pl.when(unit < 2)
        def _():
            self.own_sum[span(self.half * unit, self.half), :] = total[: self.half, :]
            self.own_out[unit] = total[self.half :, :].astype(BF)
            self.own_copy(unit).start()

        @pl.when(unit >= 2)
        def _():
            part = 3 - unit
            self.pair_out[part] = total[self.half :, :].astype(BF)
            self.pair_copy(part).start()
            self.pair_copy(part).wait_recv()
            self.far_out[part] = (
                total[: self.half, :] + self.pair_in[part].astype(F32)
            ).astype(BF)
            self.sum_copy(part).start()

    def collect(self, part):
        self.own_copy(part).wait_recv()
        self.sum_copy(part).wait_recv()
        rows = pl.ds(part * self.half, self.half)
        made = self.own_sum[rows, :] + self.own_in[part].astype(F32)
        return made + self.far_in[part].astype(F32)

    def finish(self):
        for part in range(2):
            self.pair_copy(part).wait_send()
            self.own_copy(part).wait_send()
            self.sum_copy(part).wait_send()


class Near:
    def __init__(self, sems, ids, own, out, into):
        self.sems, self.ids = sems, ids
        self.own, self.out, self.into = own, out, into
        self.half = out.shape[1]

    def copy(self, part):
        return pltpu.make_async_remote_copy(
            src_ref=self.out.at[part],
            dst_ref=self.into.at[part],
            send_sem=self.sems.at[0, part],
            recv_sem=self.sems.at[1, part],
            device_id=self.ids[0],
            device_id_type=MESH,
        )

    def send(self, part, total):
        self.own[span(self.half * part, self.half), :] = total[: self.half, :]
        self.out[part] = total[self.half :, :].astype(BF)
        self.copy(part).start()

    def collect(self, part):
        self.copy(part).wait_recv()
        return self.own[pl.ds(part * self.half, self.half), :] + self.into[part].astype(F32)

    def drain(self):
        for part in range(2):
            self.copy(part).wait_send()


class Fetch:
    def __init__(self, sems, ids, square, shards):
        self.sems, self.shards = sems, shards
        self.far = ids[1]
        self.x, self.z, self.x_peer, self.z_peer = square
        self.piece = shards.shape[1] // 8

    def copy(self, index, src, start, size, device):
        place = span(start * self.piece, size * self.piece)
        return pltpu.make_async_remote_copy(
            src_ref=self.shards.at[src, place],
            dst_ref=self.shards.at[1, place],
            send_sem=self.sems.at[0, index],
            recv_sem=self.sems.at[1, index],
            device_id=device,
            device_id_type=MESH,
        )

    def hop(self, index):
        x_first = 2 * self.z + self.x
        z_first = 4 + 2 * self.x + self.z
        return (
            lambda: self.copy(0, 0, x_first, 1, self.far),
            lambda: self.copy(1, 0, z_first, 1, self.far),
            lambda: self.copy(2, 1, x_first, 1, self.x_peer),
            lambda: self.copy(3, 1, z_first, 1, self.z_peer),
            lambda: self.copy(4, 1, 2 * self.z, 2, self.z_peer),
            lambda: self.copy(5, 1, 4 + 2 * self.x, 2, self.x_peer),
        )[index]()

    def step(self, count):
        if count == 1:
            self.hop(0).start()
            self.hop(1).start()
        elif count < 4:
            for index in (2 * count - 4, 2 * count - 3):
                self.hop(index).wait_recv()
                self.hop(index + 2).start()
        else:
            self.hop(4).wait_recv()
            self.hop(5).wait_recv()

    def finish(self):
        for index in range(6):
            self.hop(index).wait_send()


def square():
    group = lax.axis_index("dp")
    place = lax.axis_index("tensor")
    x = lax.rem(group, 2)
    z = lax.rem(group // 2, 2)
    return (x, z, (group + 1 - 2 * x, place), (group + 2 - 4 * z, place))


def neighbours():
    group = lax.axis_index("dp")
    place = lax.axis_index("tensor")
    core = lax.rem(place, 2)
    return ((group, place + 1 - 2 * core), (group, lax.rem(place + 2, 4)))


class Spot:
    def __init__(self, deep):
        group = lax.axis_index("dp")
        self.place = lax.axis_index("tensor")
        self.deep = deep
        self.z = group // 2
        self.x = lax.rem(group, 2)
        self.across = (2 * self.z + 1 - self.x, self.place)

    def level(self, ahead):
        return lax.rem(self.z + ahead, self.deep)

    def along(self, ahead):
        return (2 * self.level(ahead) + self.x, self.place)

    def partners(self):
        return [self.across] + [self.along(ahead) for ahead in range(1, self.deep)]


def meet(ids):
    barrier = pltpu.get_barrier_semaphore()
    for device in ids:
        pl.semaphore_signal(barrier, inc=1, device_id=device, device_id_type=MESH)
    pl.semaphore_wait(barrier, len(ids))


class DpSum:
    def __init__(self, spot, src, out, scratch):
        self.spot, self.src, self.out = spot, src, out
        self.pairs, self.rest, self.sems = scratch
        self.block = self.pairs.shape[1]

    @staticmethod
    def scratch(deep, block, columns):
        return [
            pltpu.VMEM((deep, block, columns), BF),
            pltpu.VMEM((deep - 1, block, columns), BF),
            pltpu.SemaphoreType.DMA((4, deep)),
        ]

    def rows(self, ahead, x):
        start = (2 * self.spot.level(ahead) + x) * self.block
        return pl.ds(pl.multiple_of(start, self.block), self.block)

    def x_copy(self, ahead):
        return pltpu.make_async_remote_copy(
            src_ref=self.src.at[self.rows(ahead, 1 - self.spot.x)],
            dst_ref=self.pairs.at[ahead],
            send_sem=self.sems.at[0, ahead],
            recv_sem=self.sems.at[1, ahead],
            device_id=self.spot.across,
            device_id_type=MESH,
        )

    def z_copy(self, ahead):
        return pltpu.make_async_remote_copy(
            src_ref=self.pairs.at[ahead],
            dst_ref=self.rest.at[ahead - 1],
            send_sem=self.sems.at[2, ahead],
            recv_sem=self.sems.at[3, ahead],
            device_id=self.spot.along(ahead),
            device_id_type=MESH,
        )

    def order(self):
        return [*range(1, self.spot.deep), 0]

    def start(self):
        for ahead in self.order():
            self.x_copy(ahead).start()

    def middle(self):
        for ahead in self.order():
            self.x_copy(ahead).wait_recv()
            total = self.src[self.rows(ahead, self.spot.x), :].astype(F32)
            total = total + self.pairs[ahead].astype(F32)
            if ahead:
                self.pairs[ahead] = total.astype(BF)
                self.z_copy(ahead).start()
            else:
                self.out[...] = total
        for ahead in self.order():
            self.x_copy(ahead).wait_send()

    def end(self):
        for ahead in range(1, self.spot.deep):
            self.z_copy(ahead).wait_recv()
        total = self.out[...]
        for ahead in range(1, self.spot.deep):
            total = total + self.rest[ahead - 1].astype(F32)
        self.out[...] = total
        for ahead in range(1, self.spot.deep):
            self.z_copy(ahead).wait_send()


def scatter_scratch(rows, width):
    return [pltpu.VMEM((2, rows // 8, width), BF)] * 6


def gelu_parts(hidden):
    cdf = 0.5 * (1.0 + lax.erf(hidden * (0.5**0.5)))
    density = jnp.exp(hidden * hidden * -0.5) * 0.3989422804014327
    return (hidden * cdf, cdf + hidden * density)


def load_turned(wq, wk, wqk):
    turn = turned_place(wq.shape[0], 0, wq.shape[0])
    wqk[:256, :] = dot(turn, wq[...]).astype(BF)
    wqk[256:, :] = dot(turn, wk[...]).astype(BF)


def is_packed(lengths_ref, length):
    return (lengths_ref[:, 0:1] < length).astype(jnp.int32).astype(F32)


def owner(chunk):
    return 2 * (chunk // 4) + chunk % 2


def apart(keys, queries, packed):
    return (keys != queries).astype(jnp.int32).astype(F32) * (packed * -1e9)


def unit_owner(unit, half):
    return jnp.where(unit < 2, 0, 2) + half


SAVED = ("a", "q", "k", "v", "o", "o2", "x1", "m", "g", "slope", "x", "lse")


def forward_kernel(depth, heads, refs):
    refs = list(refs)

    def take(count):
        made = refs[:count]
        del refs[:count]
        return made

    (gain_ref, bias_ref, bdown_ref, bada_ref, lengths_ref, steps_ref) = take(6)
    (rotary_ref, time_ref, cot_ref) = take(3)
    (tokens_hbm, wself_hbm, wqkv_hbm, wout_hbm, wup_hbm, wdown_hbm, wada_hbm) = take(7)
    (acts_ref, est_ref, cond_ref, cos_ref, sin_ref, temb_ref, grad_hbm) = take(7)
    saved_hbm = [dict(zip(SAVED, take(len(SAVED)))) for _ in range(depth)]
    gather_sems = [take(2) for _ in range(5)]
    (near_a_sems, near_f_sems, fetch_sems, cross_send, cross_recv) = take(5)
    (load_sems, store_sems) = take(2)
    (tokens, wself, wada) = take(3)
    wa, wu, wd, wqk = take(depth), take(depth), take(depth), take(depth)
    abufs, mbufs, (ebuf,) = take(2), take(2), take(1)
    (q2, k2, v2, ob2, lse2, accs, stats, gb, gpb) = take(9)
    (x1, xb, start, own_a, own_f, sums) = take(6)
    near_a_bufs, near_f_bufs = take(2), take(2)
    ids = neighbours()
    corner = square()
    columns = heads * HD
    width = xb.shape[1]
    half = xb.shape[0] // 2
    unit_rows = 2 * half
    length = 8 * half
    part_a = [pl.ds(part * columns, columns) for part in range(4)]
    sources = [tokens_hbm, wself_hbm.at[0], wself_hbm.at[1]]
    places = [tokens, wself.at[0], wself.at[1]]
    for layer in range(depth):
        sources += [wqkv_hbm.at[layer, part] for part in range(3)] + [wout_hbm.at[layer]]
        places += [wa[layer].at[0, rows] for rows in part_a]
        sources += [wup_hbm.at[layer], wdown_hbm.at[layer]]
        places += [wu[layer].at[0], wd[layer].at[0]]
    loads = [
        pltpu.make_async_copy(src, dst, load_sems.at[i])
        for i, (src, dst) in enumerate(zip(sources, places))
    ]
    ada_loads = [
        pltpu.make_async_copy(wada_hbm.at[layer], wada, load_sems.at[len(loads)])
        for layer in range(depth)
    ]
    order = [0, 1, *range(3, 9)]
    for i in order:
        loads[i].start()
    ada_loads[0].start()
    for i in range(len(loads)):
        if i not in order:
            loads[i].start()
    meet([*ids, *corner[2:]])
    fetches = []
    for layer in range(depth):
        for shards in (wa[layer], wu[layer], wd[layer]):
            fetches.append(Fetch(fetch_sems.at[len(fetches)], ids, corner, shards))
    gathers = [Gather(gather_sems[i], ids, abufs[i]) for i in range(2)]
    mixes = [Gather(gather_sems[2 + i], ids, mbufs[i]) for i in range(2)]
    grads = Gather(gather_sems[4], ids, ebuf)
    near_a = Near(near_a_sems, ids, own_a, *near_a_bufs)
    near_f = Near(near_f_sems, ids, own_f, *near_f_bufs)
    packed = is_packed(lengths_ref, length)
    pending = []

    def store(name, src, dst):
        made = pltpu.make_async_copy(src, dst, store_sems.at[len(pending)])
        made.start()
        pending.append([name, made, False])

    def stored(*names):
        for each in pending:
            if each[0] in names and not each[2]:
                each[1].wait()
                each[2] = True

    def begin(number, part, made):
        layer = number % depth
        rows = pl.ds(part * half, half)
        if number >= 2 and part == 0:
            gathers[number % 2].finish()
        xb[rows, :] = made
        hat = norm(made)[0]
        gain = gain_ref[layer : layer + 1, :]
        normed = hat * gain + bias_ref[layer : layer + 1, :]
        abufs[number % 2][pl.ds(2 * half * part, half), :] = normed.astype(BF)
        gathers[number % 2].send(part)

    for i in (3, 4, 5, 6):
        loads[i].wait()
    fetches[0].step(1)
    loads[0].wait()
    loads[1].wait()
    for part in range(2):
        rows = pl.ds(part * half, half)
        made = dot(tokens[rows, :], wself[0])
        start[rows, :] = made
        begin(0, part, made)

    def make_tables():
        place = lax.axis_index("tensor")
        sibling = ids[0][1]
        far = ids[1][1]
        far_other = lax.rem(sibling + 2, 4)
        row = lax.broadcasted_iota(jnp.int32, (half, 128), 0).astype(F32)
        for chunk, (block, part) in enumerate(
            zip(
                (place, sibling, place, sibling, far, far_other, far, far_other),
                (0, 0, 1, 1, 1, 1, 0, 0),
            )
        ):
            rows = pl.ds(chunk * half, half)
            offset = (block * unit_rows).astype(F32)
            position = row + part * half + (1.0 - packed) * offset
            angle = position * rotary_ref[...]
            cos_ref[rows, :] = jnp.cos(angle)
            sin_ref[rows, :] = jnp.sin(angle)
        steps = steps_ref[...].astype(F32)
        slot = lax.broadcasted_iota(jnp.int32, steps.shape, 1)
        mine = jnp.sum(jnp.where(slot == place, steps, 0.0), axis=1, keepdims=True)
        step = packed * mine + (1.0 - packed) * steps[:, 0:1]
        angle = jnp.broadcast_to(step * time_ref[...], (8, width // 2))
        temb_ref[:, : width // 2] = jnp.cos(angle)
        temb_ref[:, width // 2 :] = jnp.sin(angle)

    def make_cond(layer):
        ada_loads[layer].wait()
        column = temb_ref[...].T[:, 0:1]
        made = jnp.sum(wada[...] * column, axis=0, keepdims=True)
        made = made + bada_ref[layer : layer + 1, :]
        cond_ref[8 * layer : 8 * layer + 8, :] = jnp.broadcast_to(made, (8, 2 * width))
        if layer + 1 < depth:
            ada_loads[layer + 1].start()

    def project(number, count, pick, before):
        layer = number % depth
        abuf = abufs[number % 2]

        def body(step, carry):
            before(step)
            shard, unit = pick(step)
            rows = span(unit * unit_rows, unit_rows)
            normed = abuf[rows, :]
            mixed = dot(normed, wqk[layer][shard], NT)
            cosine = cos_ref[rows, :]
            sine = sin_ref[rows, :]
            for place, dst, scale in ((0, q2, HD**-0.5), (256, k2, 1.0)):
                first = mixed[:, place : place + 128]
                second = mixed[:, place + 128 : place + 256]
                dst[shard, rows, :128] = ((first * cosine - second * sine) * scale).astype(BF)
                dst[shard, rows, 128:] = ((second * cosine + first * sine) * scale).astype(BF)
            v2[shard, rows, :] = dot(normed, wa[layer][shard, part_a[2], :], NT).astype(BF)
            return carry

        lax.fori_loop(0, count, body, 0)

    lane = lax.broadcasted_iota(jnp.int32, (1, 128), 1)

    def scores_of(shard, unit, head, keys):
        rows = span(unit * unit_rows, unit_rows)
        made = dot(keep_head(q2[shard, rows, :], head, True), k2[shard, keys, :], NT)
        part = lax.broadcasted_iota(jnp.int32, (2, 1, length // 2), 0)
        chunk = lax.broadcasted_iota(jnp.int32, (2, 1, length // 2), 2) // half
        neg = apart(owner(chunk + keys.start // half), part, packed.reshape(1, 1, 1))
        return (made.reshape(2, half, length // 2) + neg).reshape(unit_rows, length // 2)

    def attend_near(number, count, pick, before):
        keys = pl.ds(0, length // 2)

        def body(step, carry):
            before(step)
            shard, unit = pick(step)
            place = 2 * unit + shard
            attended = jnp.zeros((unit_rows, columns), F32)
            tops = jnp.zeros((unit_rows, 128), F32)
            totals = jnp.zeros((unit_rows, 128), F32)
            for head in range(heads):
                scores = scores_of(shard, unit, head, keys)
                largest = jnp.max(scores, axis=-1, keepdims=True)
                shares = jnp.exp(scores - largest)
                output = dot(shares.astype(BF), v2[shard, keys, :])
                attended = jnp.where(head_mask(head, columns, False), output, attended)
                tops = jnp.where(lane == head, largest, tops)
                totals = jnp.where(lane == head, jnp.sum(shares, axis=-1, keepdims=True), totals)
            accs[place] = attended
            stats[place, 0] = tops
            stats[place, 1] = totals
            return carry

        lax.fori_loop(0, count, body, 0)

    def attend_far(number, save, count, pick, before):
        keys = pl.ds(length // 2, length // 2)
        layer, slot = number % depth, number % 2

        def body(step, carry):
            before(step)
            shard, unit = pick(step)
            place = 2 * unit + shard
            rows = span(unit * unit_rows, unit_rows)
            attended = jnp.zeros((unit_rows, columns), F32)
            logs = jnp.zeros((unit_rows, 128), F32)
            for head in range(heads):
                scores = scores_of(shard, unit, head, keys)
                earlier = stats[place, 0][:, head : head + 1]
                largest = jnp.maximum(earlier, jnp.max(scores, axis=-1, keepdims=True))
                shares = jnp.exp(scores - largest)
                shrink = jnp.exp(earlier - largest)
                totals = stats[place, 1][:, head : head + 1] * shrink
                totals = totals + jnp.sum(shares, axis=-1, keepdims=True)
                output = dot(shares.astype(BF), v2[shard, keys, :])
                output = (accs[place] * shrink + output) * (1.0 / totals)
                attended = jnp.where(head_mask(head, columns, False), output, attended)
                if save:
                    logs = jnp.where(lane == head, largest + jnp.log(totals), logs)
            if save:
                lse2[slot, shard, unit] = logs.T[:8, :]
            attended = attended.astype(BF)
            ob2[slot, shard, rows, :] = attended

            @pl.when(shard == 1)
            def _():
                total = dot(ob2[slot, 0, rows, :], wa[layer][0, part_a[3], :])
                near_a.send(unit, total + dot(attended, wa[layer][1, part_a[3], :]))

            return carry

        lax.fori_loop(0, count, body, 0)

    def feed(number, save, pick, before):
        layer = number % depth
        mbuf = mbufs[number % 2]

        def body(step, carry):
            before(step)
            shard, unit = pick(step)
            rows = span(unit * unit_rows, unit_rows)
            hidden = dot(mbuf[rows, :], wu[layer][shard])
            gated, slope = gelu_parts(hidden)
            gated = gated.astype(BF)
            made = dot(gated, wd[layer][shard])

            @pl.when(shard == 0)
            def _():
                if save:
                    gb[rows, :] = gated
                    gpb[rows, :] = slope.astype(BF)
                sums[rows, :] = made

            @pl.when(shard == 1)
            def _():
                near_f.send(unit, sums[rows, :] + made)

            return carry

        lax.fori_loop(0, 4, body, 0)

    crossings = {}

    def cross(number):
        slot = number % 2
        made = []
        for part in range(2):
            made.append(
                pltpu.make_async_remote_copy(
                    src_ref=lse2.at[slot, 1, part],
                    dst_ref=lse2.at[slot, 0, 3 - part],
                    send_sem=cross_send.at[2 * slot + part],
                    recv_sem=cross_recv.at[2 * slot + part],
                    device_id=ids[1],
                    device_id_type=MESH,
                )
            )
            made[-1].start()
        crossings[number] = made

    def late(number):
        slot = number % 2
        saved = saved_hbm[number % depth]
        for part in range(2):
            mixes[slot].far(part)
        store("m", mbufs[slot], saved["m"])
        for each in crossings[number]:
            each.wait_recv()
        store("lse", lse2.at[slot, 0], saved["lse"])

    def events(table):
        def before(step):
            for when, actions in table.items():

                @pl.when(step == when)
                def _():
                    for action in actions:
                        if isinstance(action, tuple):
                            if action[0] < len(fetches):
                                fetches[action[0]].step(action[1])
                        else:
                            action()

        return before

    def waits(*indices):
        def action():
            for index in indices:
                loads[index].wait()

        return action

    def by_unit(step):
        return (lax.rem(step, 2), step // 2)

    def by_shard(step):
        return (step // 2, lax.rem(step, 2))

    def run(number, after_layer):
        layer, slot = number % depth, number % 2
        save = number >= depth
        group, mix = gathers[slot], mixes[slot]
        mix_rows = mbufs[slot]
        base = 3 * layer

        def after_attend(part):
            def action():
                if part == 0 and number >= 2:
                    mix.finish(far=False)
                if part == 0:
                    stored("x1")
                rows = pl.ds(part * half, half)
                after = xb[rows, :] + near_a.collect(part)
                x1[rows, :] = after
                shift = cond_ref[8 * layer : 8 * layer + 1, :width]
                scale = cond_ref[8 * layer : 8 * layer + 1, width:]
                made = norm(after)[0] * (1.0 + scale) + shift
                mix_rows[pl.ds(2 * half * part, half), :] = made.astype(BF)
                mix.sibling_copy(part).start()
                if number == 2 * depth - 1:
                    mix.far_copy(part).start()

            return action

        def after_feed(part):
            def action():
                if part == 0:
                    stored("x")
                rows = pl.ds(part * half, half)
                made = x1[rows, :] + near_f.collect(part) + bdown_ref[layer : layer + 1, :]
                after_layer(part, rows, made)

            return action

        def near_rows(part):
            return lambda: group.near(part)

        def far_rows(part):
            return lambda: group.far(part)

        def mixed(part):
            return lambda: mix.near(part)

        if number:
            near_a.drain()
            near_f.drain()
        stored("q", "k", "v")

        def turn(shard):
            rows = wa[layer].at[shard, part_a[0]], wa[layer].at[shard, part_a[1]]
            load_turned(*rows, wqk[layer].at[shard])

        far_table = {3: [after_attend(0)]}
        feed_table = {
            0: [mixed(0)],
            1: [after_attend(1)],
            2: [mixed(1)],
            3: [after_feed(0)],
        }
        order = by_unit
        if number == 0:
            make_tables()
            turn(0)
            arrive = {
                0: [near_rows(0)],
                1: [near_rows(1)],
                2: [(0, 2), waits(7), (1, 1), far_rows(0)],
                3: [far_rows(1), waits(8), (2, 1)],
            }

            def in_order(step):
                return jnp.where(step < 2, step, 5 - step)

            project(number, 4, lambda step: (0, in_order(step)), events(arrive))
            attend_near(number, 2, lambda step: (0, step), events({1: [(0, 3)]}))
            make_cond(layer)
            first = {1: [(1, 2), waits(9, 10, 11, 12), (3, 1)]}
            attend_far(number, save, 2, lambda step: (0, step), events(first))
            fetches[0].step(4)
            turn(1)
            second = {3: [(1, 3), (2, 2), waits(13), (4, 1)]}
            project(number, 4, lambda step: (1, in_order(step)), events(second))
            attend_near(number, 2, lambda step: (1, step), events({}))
            far_table = {1: [after_attend(0)]}
            attend_far(number, save, 2, lambda step: (1, step), events(far_table))
            feed_table = {
                0: [mixed(0), (2, 3), (3, 2), waits(14), (5, 1)],
                1: [after_attend(1), mixed(1)],
                2: [(1, 4), (3, 3), (4, 2), (2, 4)],
                3: [after_feed(0)],
            }
            order = by_shard
        else:
            own_table = {0: [near_rows(0)], 1: [near_rows(1)]}
            near_table = {3: [lambda: group.arrive(0)]}
            if not save:
                turn(0)
                own_table[0] += [(base + 1, 3), (base + 2, 2)]
                own_table[2] = [(base, 4), lambda: turn(1)]
                near_table[3] = [(base + 2, 3), lambda: group.arrive(0)]
                feed_table[0] += [(base + 1, 4)]
                feed_table[1] += [(base + 2, 4)]
            project(number, 4, by_shard, events(own_table))
            attend_near(number, 4, by_unit, events(near_table))
            if not save:
                make_cond(layer)
            if number == depth:
                for part in range(2):
                    grads.near(part)
                    grads.far(part)
                store("grad", ebuf, grad_hbm)
            arrive = {
                0: [lambda: group.settle(0)],
                1: [lambda: group.arrive(1)],
                2: [lambda: group.settle(1)],
            }
            project(number, 4, lambda step: (lax.rem(step, 2), 3 - step // 2), events(arrive))
            if number == depth - 1:
                for part in range(2):
                    ebuf[grads.own(part), :] = cot_ref[pl.ds(part * half, half), :]
                    grads.send(part)
            if number > depth:
                for part in range(2):
                    mixes[(number - 1) % 2].far_copy(part).start()
            if save:
                store("a", abufs[slot], saved_hbm[layer]["a"])
                store("x", xb, saved_hbm[layer]["x"])
                for name, src in (("q", q2), ("k", k2), ("v", v2)):
                    store(name, src.at[0], saved_hbm[layer][name])
            attend_far(number, save, 4, by_unit, events(far_table))
        if save:
            cross(number)
            rows = pl.ds(0, length // 2)
            store("o", ob2.at[slot, 0, rows], saved_hbm[layer]["o"])
            store("o2", ob2.at[slot, 1, rows], saved_hbm[layer]["o2"])
        stored("g", "slope")
        feed(number, save, order, events(feed_table))
        if save:
            store("x1", x1, saved_hbm[layer]["x1"])
            store("g", gb, saved_hbm[layer]["g"])
            store("slope", gpb, saved_hbm[layer]["slope"])
        after_feed(1)()

    def between(part, rows, made):
        estimate = made.astype(BF)
        est_ref[rows, :] = estimate
        begin(depth, part, start[rows, :] + dot(estimate, wself[1]))

    def close(part, rows, made):
        acts_ref[rows, :] = made.astype(BF)

    def enter(number):
        return lambda part, rows, made: begin(number, part, made)

    for number in range(2 * depth):
        if number + 1 == 2 * depth:
            run(number, close)
        elif number + 1 == depth:
            loads[2].wait()
            run(number, between)
        else:
            run(number, enter(number + 1))
    for number in range(depth, 2 * depth):
        late(number)
    for each in gathers:
        each.finish()
    for each in (*mixes, grads):
        each.finish()
    near_a.drain()
    near_f.drain()
    for each in fetches:
        each.finish()
    for each in crossings.values():
        for copy in each:
            copy.wait_send()
    stored("grad", *SAVED)


def any_spec():
    return pl.BlockSpec(memory_space=pl.ANY)


def vmem_spec():
    return pl.BlockSpec(memory_space=pltpu.VMEM)


def forward(heads, tokens, cotangent, w_self, vectors, weights):
    depth = weights[0].shape[0]
    block, width = tokens.shape
    length = 4 * block
    half = block // 2
    columns = heads * HD
    units = weights[2].shape[2]
    lanes = jnp.arange(128) % HALF
    rotary = jnp.exp(-jnp.log(10000.0) * lanes.astype(F32) / HALF)[None]
    halves = jnp.arange(width // 2).astype(F32)
    times = jnp.exp(-jnp.log(10000.0) * halves / (width // 2))[None]
    kept = {
        "a": ((length, width), BF),
        "q": ((length, 256), BF),
        "k": ((length, 256), BF),
        "v": ((length, columns), BF),
        "o": ((length // 2, columns), BF),
        "o2": ((length // 2, columns), BF),
        "x1": ((block, width), F32),
        "m": ((length, width), BF),
        "g": ((length // 2, units), BF),
        "slope": ((length // 2, units), BF),
        "x": ((block, width), F32),
        "lse": ((4, 8, block), F32),
    }
    kept_shapes = [jax.ShapeDtypeStruct(*kept[name]) for name in SAVED]
    out_shape = [
        jax.ShapeDtypeStruct((block, width), BF),
        jax.ShapeDtypeStruct((block, width), BF),
        jax.ShapeDtypeStruct((8 * depth, 2 * width), F32),
        jax.ShapeDtypeStruct((length, 128), F32),
        jax.ShapeDtypeStruct((length, 128), F32),
        jax.ShapeDtypeStruct((8, width), F32),
        jax.ShapeDtypeStruct((length, width), BF),
    ] + kept_shapes * depth
    out_specs = [vmem_spec()] * 6 + [any_spec()] * (1 + depth * len(SAVED))
    dma = pltpu.SemaphoreType.DMA
    scratch = [dma((3, 2))] * 10
    scratch += [dma((2, 2))] * 2 + [dma((3 * depth, 2, 6)), dma((4,)), dma((4,))]
    scratch += [dma((4 + 6 * depth,)), dma((1 + depth * len(SAVED),))]
    scratch += [
        pltpu.VMEM((block, width), BF),
        pltpu.VMEM((2, width, width), BF),
        pltpu.VMEM((width, 2 * width), F32),
    ]
    scratch += [pltpu.VMEM((2, 4 * columns, width), BF)] * depth
    scratch += [pltpu.VMEM((2, width, units), BF)] * depth
    scratch += [pltpu.VMEM((2, units, width), BF)] * depth
    scratch += [pltpu.VMEM((2, 512, width), BF)] * depth
    scratch += [pltpu.VMEM((length, width), BF)] * 5
    scratch += [
        pltpu.VMEM((2, length, 256), BF),
        pltpu.VMEM((2, length, 256), BF),
        pltpu.VMEM((2, length, columns), BF),
        pltpu.VMEM((2, 2, length // 2, columns), BF),
        pltpu.VMEM((2, 2, 4, 8, block), F32),
        pltpu.VMEM((4, block, columns), F32),
        pltpu.VMEM((4, 2, block, 128), F32),
        pltpu.VMEM((length // 2, units), BF),
        pltpu.VMEM((length // 2, units), BF),
    ]
    scratch += [pltpu.VMEM((block, width), F32)] * 5
    scratch += [pltpu.VMEM((2 * block, width), F32)]
    scratch += [pltpu.VMEM((2, half, width), BF)] * 4

    def kernel(*refs):
        forward_kernel(depth, heads, refs)

    operands = [*vectors, rotary, times, cotangent]
    remote = [tokens, w_self.reshape(2, width, width), *weights]
    made = pl.pallas_call(
        kernel,
        out_shape=out_shape,
        in_specs=[vmem_spec()] * len(operands) + [any_spec()] * len(remote),
        out_specs=out_specs,
        scratch_shapes=scratch,
        compiler_params=pltpu.CompilerParams(
            collective_id=1, has_side_effects=True, vmem_limit_bytes=LIMIT
        ),
        name="layers_forward",
    )(*operands, *remote)
    count = len(SAVED)
    saved = [made[7 + count * layer : 7 + count * (layer + 1)] for layer in range(depth)]
    return (made[:7], [dict(zip(SAVED, each)) for each in saved])


class Ladder:
    def __init__(self, sems):
        self.send, self.recv = sems
        self.used = 0
        self.open = []

    def copy(self, src, dst, device):
        made = pltpu.make_async_remote_copy(
            src_ref=src,
            dst_ref=dst,
            send_sem=self.send.at[self.used],
            recv_sem=self.recv.at[self.used],
            device_id=device,
            device_id_type=MESH,
        )
        self.used += 1
        assert self.used <= LADDER_COPIES
        made.start()
        self.open.append(made)
        return made

    def finish(self):
        for each in self.open:
            each.wait_send()


LADDER_COPIES = 34


class Loads:
    def __init__(self, sems):
        self.sems = sems
        self.names = {}

    def add(self, name, sources, buffer):
        self.names[name] = (sources, buffer, len(self.names))
        return buffer

    def copy(self, name, layer):
        sources, buffer, place = self.names[name]
        return pltpu.make_async_copy(sources[layer], buffer, self.sems.at[place])

    def start(self, layer, *names):
        if layer >= 0:
            for name in names:
                self.copy(name, layer).start()

    def wait(self, layer, *names):
        for name in names:
            self.copy(name, layer).wait()


def backward_kernel(depth, heads, deep, refs):
    refs = list(refs)

    def take(count):
        made = refs[:count]
        del refs[:count]
        return made

    cot_ref, gain_ref, lengths_ref, cos_ref, sin_ref, temb_ref, cond_ref = take(7)
    joined_hbm = take(2)
    (grad_hbm,) = take(1)
    wqkv_hbm, wout_hbm, wup_hbm, wdown_hbm, _ = take(5)
    saved_hbm = [dict(zip(SAVED, take(len(SAVED)))) for _ in range(depth)]
    (out_ref, small_ref) = take(2)
    attn_outs, feed_outs = take(depth), take(depth)
    if deep:
        sum_ref, vec_ref = take(2)
    feed_sems, attn_sems = [take(2), take(2)], [take(2), take(2)]
    load_sems, store_sems, out_sems = take(3)
    loads = Loads(load_sems)
    wq, wk, wv = (
        loads.add(name, [wqkv_hbm.at[layer, part] for layer in range(depth)], take(1)[0])
        for part, name in enumerate(("wq", "wk", "wv"))
    )
    wout, wup, wdown = (
        loads.add(name, [src.at[layer] for layer in range(depth)], take(1)[0])
        for name, src in (("wout", wout_hbm), ("wup", wup_hbm), ("wdown", wdown_hbm))
    )
    buffers = dict(zip(SAVED, take(len(SAVED))))
    outs = [take(2) for _ in range(depth)]
    for name in SAVED:
        if name in ("o", "o2"):
            continue
        rows = saved_hbm[0][name].shape[0]
        buffer = buffers[name]
        if rows < buffer.shape[0]:
            buffer = buffer.at[pl.ds(0, rows)]
        loads.add(name, [saved_hbm[layer][name] for layer in range(depth)], buffer)
    abuf, qb, kb, vb, _, _, x1b, mbuf, gb, gpb, xb, lse = (buffers[name] for name in SAVED)
    ebuf, fbuf = take(2)
    feed_bufs, attn_bufs = take(6), take(6)
    (wqk, dhb, qmask, domask, dsb, pb, dkb, dvb, dqk, dvv, work, dxb) = take(12)
    (feed_grads, attn_grads) = take(2)
    ids = neighbours()
    sums = {}
    if deep:
        spot = Spot(deep)
        meet([*ids, *spot.partners()])
        for layer in range(depth):
            for name, src, out in (
                ("up", feed_grads.at[0], feed_outs[layer].at[0]),
                ("down", feed_grads.at[1], feed_outs[layer].at[1]),
                ("attn", attn_grads, attn_outs[layer]),
            ):
                sums[name, layer] = DpSum(spot, src, out, take(3))
        tail_refs = take(10)
        joined = tail_refs[0]
        joined_loads = [
            pltpu.make_async_copy(src, joined.at[i], store_sems.at[i])
            for i, src in enumerate(joined_hbm)
        ]
        for each in joined_loads:
            each.start()
    else:
        meet(ids)
    width = cot_ref.shape[1]
    half = cot_ref.shape[0] // 2
    unit_rows = 2 * half
    total, own, dx1 = (work.at[pl.ds(i * unit_rows, unit_rows)] for i in range(3))
    feed_rows = Gather(feed_sems[0], ids, ebuf)
    feed_sum = Scatter(feed_sems[1], ids, own, feed_bufs)
    attn_rows = Gather(attn_sems[0], ids, fbuf)
    attn_sum = Scatter(attn_sems[1], ids, own, attn_bufs)
    columns = heads * HD
    tiles = width // 256
    top = depth - 1
    packed = is_packed(lengths_ref, 8 * half)
    loads.add("grad", [grad_hbm] * depth, ebuf)
    loads.start(top, "m", "wup", "grad", "wdown", "slope", "x1", "wout", "q", "k", "v", "lse", "g")
    loads.start(top, "wq", "wk", "wv", "a", "x")
    out_loads = []
    out_sends = []
    for layer in range(depth):
        rows = outs[layer][0].at[pl.ds(0, 4 * half)]
        pairs = ((saved_hbm[layer]["o"], rows), (saved_hbm[layer]["o2"], outs[layer][1]))
        out_loads.append(
            [
                pltpu.make_async_copy(src, dst, out_sems.at[layer, 4 + i])
                for i, (src, dst) in enumerate(pairs)
            ]
        )
        out_sends.append(
            [
                pltpu.make_async_remote_copy(
                    src_ref=outs[layer][1].at[pl.ds(part * unit_rows, unit_rows)],
                    dst_ref=outs[layer][0].at[pl.ds((3 - part) * unit_rows, unit_rows)],
                    send_sem=out_sems.at[layer, part],
                    recv_sem=out_sems.at[layer, 2 + part],
                    device_id=ids[1],
                    device_id_type=MESH,
                )
                for part in range(2)
            ]
        )
        for each in out_loads[layer]:
            each.start()

    def send_outs(layer):
        out_loads[layer][1].wait()
        for each in out_sends[layer]:
            each.start()

    send_outs(top)
    dxb[...] = cot_ref[...].astype(F32)
    small_ref[...] = jnp.zeros_like(small_ref)

    def outer(left, right, dst):
        def tile(index, carry):
            place = span(index * 256, 256)
            dst[place, :] = dot(left[:, place], right[...], TN).astype(BF)
            return carry

        lax.fori_loop(0, tiles, tile, 0)

    def turn_back(grad, rows, scale):
        cosine = cos_ref[rows, :]
        sine = sin_ref[rows, :]
        first_half = grad[:, :128]
        second_half = grad[:, 128:]
        return (
            ((first_half * cosine + second_half * sine) * scale).astype(BF),
            ((second_half * cosine - first_half * sine) * scale).astype(BF),
        )

    def event(name, layer, kind):
        if (name, layer) in sums:
            getattr(sums[name, layer], kind)()

    for layer in reversed(range(depth)):
        def note(row, value):
            small_ref[8 * layer + row : 8 * layer + row + 1, :] = value

        note(4, jnp.sum(dxb[...], axis=0, keepdims=True))
        dkb[...] = jnp.zeros_like(dkb)
        dvb[...] = jnp.zeros_like(dvb)
        loads.wait(layer, "m", "wup")

        def expand(step, carry):
            rows = span((3 - step) * unit_rows, unit_rows)
            gated, slope = gelu_parts(dot(mbuf[rows, :], wup[...]))
            gb[rows, :] = gated.astype(BF)
            gpb[rows, :] = slope.astype(BF)
            return carry

        lax.fori_loop(0, 2, expand, 0)
        loads.wait(layer, "wdown", "slope")
        if layer == top:
            loads.wait(layer, "grad")

        def contract(step, carry):
            if layer == top:
                unit = jnp.where(step < 2, 3 - step, step - 2)
            else:
                feed_rows.receive(step)
                unit = jnp.where(step < 2, step, 5 - step)
            rows = span(unit * unit_rows, unit_rows)
            grad = dot(ebuf[rows, :], wdown[...], NT)
            grad = (grad * gpb[rows, :].astype(F32)).astype(BF)
            dhb[rows, :] = grad
            total[...] = dot(grad, wup[...], NT)
            feed_sum.send(unit, total)
            return carry

        lax.fori_loop(0, 4, contract, 0)
        loads.start(layer - 1, "wdown", "slope")
        event("attn", layer + 1, "middle")
        event("up", layer + 1, "end")
        if layer < top:
            attn_rows.finish()
            attn_sum.finish()
        shift_sum = jnp.zeros((1, width), F32)
        scale_sum = jnp.zeros((1, width), F32)
        for part in range(2):
            if part == 0:
                loads.wait(layer, "x1")
                outer(mbuf, dhb, feed_grads.at[0])
                event("up", layer, "start")
            else:
                loads.wait(layer, "g")
                outer(ebuf, gb, feed_grads.at[1])
                event("down", layer, "start")
            rows = pl.ds(part * half, half)
            grad = feed_sum.collect(part)
            hat, rstd = norm(x1b[rows, :])
            shift_sum += jnp.sum(grad, axis=0, keepdims=True)
            scale_sum += jnp.sum(grad * hat, axis=0, keepdims=True)
            after = dxb[rows, :]
            after = after + norm_back(grad * (1.0 + cond_ref[8 * layer : 8 * layer + 1, width:]), hat, rstd)
            dx1[rows, :] = after
            fbuf[attn_rows.own(part), :] = after.astype(BF)
            attn_rows.send(part)
        note(0, shift_sum)
        note(1, scale_sum)
        loads.start(layer - 1, "m", "g", "x1", "wup")
        loads.wait(layer, "wout", "q", "k", "v", "lse")

        def attend(step, carry):
            attn_rows.receive(step)
            if layer:

                @pl.when(step == 3)
                def _():
                    send_outs(layer - 1)

            unit = jnp.where(step < 2, step, 5 - step)
            rows = span(unit * unit_rows, unit_rows)
            grad_out = dot(fbuf[rows, :], wout[...], NT).astype(BF)
            queries = qb[rows, :]
            grad_queries = jnp.zeros((unit_rows, 256), F32)
            chunk = lax.broadcasted_iota(jnp.int32, (8, 1, unit_rows), 0)
            part = lax.broadcasted_iota(jnp.int32, (8, 1, unit_rows), 2) // half
            neg = apart(owner(chunk), unit_owner(unit, part), packed.reshape(1, 1, 1))
            for head in range(heads):
                place = pl.ds(head * unit_rows, unit_rows)
                masked = keep_head(queries, head, True)
                masked_out = keep_head(grad_out, head, False)
                qmask[place, :] = masked
                domask[place, :] = masked_out
                scores = dot(kb[...], masked, NT).reshape(8, half, unit_rows)
                shares = jnp.exp(scores - (lse[unit, head : head + 1, :] - neg))
                shares = shares.reshape(8 * half, unit_rows)
                grad_shares = dot(vb[...], masked_out, NT)
                centre = jnp.sum(shares * grad_shares, axis=0, keepdims=True)
                grad_scores = (shares * (grad_shares - centre)).astype(BF)
                pb[:, place] = shares.astype(BF)
                dsb[:, place] = grad_scores
                grad_queries = grad_queries + dot(grad_scores, keep_head(kb[...], head, True), TN)
            dkb[...] += dot(dsb[...], qmask[...])
            dvb[...] += dot(pb[...], domask[...])
            low, high = turn_back(grad_queries, rows, HD**-0.5)
            dqk[rows, :128] = low
            dqk[rows, 128:256] = high
            return carry

        lax.fori_loop(0, 4, attend, 0)
        loads.start(layer - 1, "wout", "q", "k", "v", "lse")
        event("down", layer + 1, "end")
        event("attn", layer + 1, "end")
        event("up", layer, "middle")
        loads.wait(layer, "wq", "wk", "wv")
        load_turned(wq, wk, wqk)

        def spread(step, carry):
            unit = jnp.where(step < 2, 3 - step, step - 2)
            rows = span(unit * unit_rows, unit_rows)
            low, high = turn_back(dkb[rows, :], rows, 1.0)
            dqk[rows, 256:384] = low
            dqk[rows, 384:512] = high
            values = dvb[rows, :].astype(BF)
            dvv[rows, :] = values
            total[...] = dot(dqk[rows, :], wqk[...]) + dot(values, wv[...])
            attn_sum.send(unit, total)
            return carry

        lax.fori_loop(0, 4, spread, 0)
        loads.start(layer - 1, "wq", "wk", "wv")
        event("down", layer, "middle")
        loads.wait(layer, "a")
        out_loads[layer][0].wait()
        for each in out_sends[layer]:
            each.wait()
        ob = outs[layer][0]
        places = (
            turned_place(columns, 0, 4 * columns),
            turned_place(columns, columns, 4 * columns),
            plain_place(columns, 2 * columns, 4 * columns),
            plain_place(columns, 3 * columns, 4 * columns),
        )

        def attn_tile(index, carry):
            place = span(index * 256, 256)
            normed = abuf[:, place]
            both = dot(normed, dqk[...], TN).astype(BF)
            made = dot(both[:, :256], places[0]) + dot(both[:, 256:], places[1])
            made = made + dot(dot(normed, dvv[...], TN).astype(BF), places[2])
            outs = dot(fbuf[:, place], ob[...], TN).astype(BF)
            attn_grads[place, :] = (made + dot(outs, places[3])).astype(BF)
            return carry

        lax.fori_loop(0, tiles, attn_tile, 0)
        loads.start(layer - 1, "a")
        event("attn", layer, "start")
        if not deep:
            stores = [
                pltpu.make_async_copy(attn_grads, attn_outs[layer], store_sems.at[0]),
                pltpu.make_async_copy(feed_grads, feed_outs[layer], store_sems.at[1]),
            ]
            for each in stores:
                each.start()
            for each in stores:
                each.wait()
        if layer < top:
            feed_rows.finish()
        feed_sum.finish()
        loads.wait(layer, "x")
        gain_sum = jnp.zeros((1, width), F32)
        bias_sum = jnp.zeros((1, width), F32)
        for part in range(2):
            rows = pl.ds(part * half, half)
            grad = attn_sum.collect(part)
            hat, rstd = norm(xb[rows, :])
            gain_sum += jnp.sum(grad * hat, axis=0, keepdims=True)
            bias_sum += jnp.sum(grad, axis=0, keepdims=True)
            made = dx1[rows, :] + norm_back(
                grad * gain_ref[layer : layer + 1, :], hat, rstd
            )
            dxb[rows, :] = made
            if layer:
                ebuf[feed_rows.own(part), :] = made.astype(BF)
                feed_rows.send(part)
        note(2, gain_sum)
        note(3, bias_sum)
        loads.start(layer - 1, "x")
    out_ref[...] = dxb[...]
    if deep:
        for each in joined_loads:
            each.wait()
        tail(deep, spot, ids, sums, dxb, small_ref, temb_ref, work, dsb, tail_refs,
             sum_ref, vec_ref, store_sems)
    attn_rows.finish()
    attn_sum.finish()


def tail(deep, spot, ids, sums, dxb, small_ref, temb_ref, work, dsb, scratch, sum_ref, vec_ref,
         store_sems):
    (joined, ebuf, jbuf, near_in, next_in, z_in, result, vecs, send, recv) = scratch
    sibling, far = ids
    place = lax.axis_index("tensor")
    core = lax.rem(place, 2)
    y = place // 2
    x, z = spot.x, spot.z
    width = dxb.shape[1]
    ladder = Ladder((send, recv))
    ebuf[0] = dxb[...].astype(BF)
    rows_copy = ladder.copy(ebuf.at[0], ebuf.at[1], sibling)
    joined_copy = ladder.copy(joined.at[1 - core], jbuf, sibling)
    mine = vecs.at[core, y, x, z]
    row = lax.broadcasted_iota(jnp.int32, small_ref.shape, 0)
    mine[...] = jnp.where(row == 5, temb_ref[0:1, :], small_ref[...]).astype(BF)
    vec_z = [ladder.copy(mine, mine, spot.along(ahead)) for ahead in range(1, deep)]
    rows_copy.wait_recv()
    joined_copy.wait_recv()
    rest = width // 2

    def tile(index, carry):
        rows = span(index * 256, 256)
        made = dot(joined[core, :, rows], ebuf[0], TN)
        work[rows, :] = made + dot(jbuf[:, rows], ebuf[1], TN)
        return carry

    lax.fori_loop(0, width // 256, tile, 0)
    half, quarter = width // 2, width // 4
    piece = quarter // deep
    ways = (((far, y), (spot.across, x)), ((spot.across, x), (far, y)))
    lanes = (pl.ds(0, rest), pl.ds(rest, rest))
    firsts = []
    for side, ((device, bit), _) in enumerate(ways):
        out = dsb.at[pl.ds(0, half), lanes[side]]
        out[...] = work[span((1 - bit) * half, half), lanes[side]].astype(BF)
        firsts.append(ladder.copy(out, near_in.at[side], device))
    for each in vec_z:
        each.wait_recv()
    row_z = vecs.at[core, y, x]
    vec_x = ladder.copy(row_z, row_z, spot.across)
    seconds = []
    for side, ((_, bit), (device, bit2)) in enumerate(ways):
        firsts[side].wait_recv()
        kept = work.at[span(bit * half, half), lanes[side]]
        kept[...] = kept[...] + near_in[side].astype(F32)
        out = dsb.at[pl.ds(half, quarter), lanes[side]]
        out[...] = work[span(bit * half + (1 - bit2) * quarter, quarter), lanes[side]].astype(BF)
        seconds.append(ladder.copy(out, next_in.at[side], device))
    vec_x.wait_recv()
    plane = vecs.at[core, y]
    vec_y = ladder.copy(plane, plane, far)
    sums["attn", 0].middle()
    thirds = []
    for side, ((_, bit), (_, bit2)) in enumerate(ways):
        seconds[side].wait_recv()
        kept = work.at[span(bit * half + bit2 * quarter, quarter), lanes[side]]
        kept[...] = kept[...] + next_in[side].astype(F32)
        out = dsb.at[pl.ds(half + quarter, quarter), lanes[side]]
        out[...] = kept[...].astype(BF)
        for ahead in range(1, deep):
            start = half + quarter + spot.level(ahead) * piece
            thirds.append(
                ladder.copy(
                    dsb.at[span(start, piece), lanes[side]],
                    z_in.at[side, ahead - 1],
                    spot.along(ahead),
                )
            )
    sums["up", 0].end()
    sums["down", 0].end()
    vec_y.wait_recv()
    every = vecs.at[core]
    vec_core = ladder.copy(every, every, sibling)
    lasts = []
    for side, ((_, bit), (_, bit2)) in enumerate(ways):
        for ahead in range(1, deep):
            thirds[side * (deep - 1) + ahead - 1].wait_recv()
        start = bit * half + bit2 * quarter + z * piece
        made = work[span(start, piece), lanes[side]]
        for ahead in range(1, deep):
            made = made + z_in[side, ahead - 1].astype(F32)
        own = result.at[core, side, span(start, piece)]
        own[...] = made.astype(BF)
        lasts += [ladder.copy(own, own, spot.along(ahead)) for ahead in range(1, deep)]
    backs = []
    for side, ((_, bit), (device, bit2)) in enumerate(ways):
        for ahead in range(1, deep):
            lasts[side * (deep - 1) + ahead - 1].wait_recv()
        own = result.at[core, side, span(bit * half + bit2 * quarter, quarter)]
        backs.append(ladder.copy(own, own, device))
    ends = []
    for side, ((device, bit), _) in enumerate(ways):
        backs[side].wait_recv()
        own = result.at[core, side, span(bit * half, half)]
        ends.append(ladder.copy(own, own, device))
    sums["attn", 0].end()
    vec_core.wait_recv()
    vec_store = pltpu.make_async_copy(vecs, vec_ref, store_sems.at[0])
    vec_store.start()
    for each in ends:
        each.wait_recv()
    whole = ladder.copy(result.at[core], result.at[core], sibling)
    whole.wait_recv()
    sum_store = pltpu.make_async_copy(result, sum_ref, store_sems.at[1])
    sum_store.start()
    ladder.finish()
    vec_store.wait()
    sum_store.wait()


def backward(heads, deep, cotangent, grad_all, gains, lengths, tables, weights, kept, joined):
    depth = len(kept)
    block, width = cotangent.shape
    length = 4 * block
    units = weights[2].shape[2]
    columns = heads * HD
    part = width // (2 * deep) if deep else width
    half, quarter = width // 2, width // 4
    held = [[each[name] for name in SAVED] for each in kept]
    scratch = [pltpu.SemaphoreType.DMA((3, 2))] * 8
    scratch += [pltpu.SemaphoreType.DMA((7 + len(SAVED),)), pltpu.SemaphoreType.DMA((2,))]
    scratch += [pltpu.SemaphoreType.DMA((depth, 6))]
    scratch += [pltpu.VMEM((columns, width), BF)] * 3
    scratch += [pltpu.VMEM(each.shape[1:], BF) for each in weights[1:4]]
    for name, each in zip(SAVED, held[0]):
        shape = (length, units) if name in ("g", "slope") else each.shape
        scratch.append(pltpu.VMEM((16, 128) if name in ("o", "o2") else shape, each.dtype))
    scratch += [pltpu.VMEM((length, columns), BF), pltpu.VMEM((length // 2, columns), BF)] * depth
    scratch += [pltpu.VMEM((length, width), BF)] * 2
    scratch += scatter_scratch(length, width) + scatter_scratch(length, width)
    scratch += [
        pltpu.VMEM((512, width), BF),
        pltpu.VMEM((length, units), BF),
        pltpu.VMEM((heads * block, 256), BF),
        pltpu.VMEM((heads * block, columns), BF),
        pltpu.VMEM((length, heads * block), BF),
        pltpu.VMEM((length, heads * block), BF),
        pltpu.VMEM((length, 256), F32),
        pltpu.VMEM((length, columns), F32),
        pltpu.VMEM((length, 512), BF),
        pltpu.VMEM((length, columns), BF),
        pltpu.VMEM((3 * block, width), F32),
        pltpu.VMEM((block, width), F32),
        pltpu.VMEM((2, width, units), BF),
        pltpu.VMEM((width, 4 * columns), BF),
    ]
    out_shape = [
        jax.ShapeDtypeStruct((block, width), F32),
        jax.ShapeDtypeStruct((8 * depth, width), F32),
    ]
    kind = F32 if deep else BF
    out_shape += [jax.ShapeDtypeStruct((part, 4 * columns), kind)] * depth
    out_shape += [jax.ShapeDtypeStruct((2, part, units), kind)] * depth
    out_specs = [vmem_spec()] * 2 + [vmem_spec() if deep else any_spec()] * (2 * depth)
    if deep:
        for _ in range(depth):
            scratch += DpSum.scratch(deep, part, units) + DpSum.scratch(deep, part, units)
            scratch += DpSum.scratch(deep, part, 4 * columns)
        vec_shape = (2, 2, 2, deep, 8 * depth, width)
        scratch += [
            pltpu.VMEM((2, block, width), BF),
            pltpu.VMEM((2, block, width), BF),
            pltpu.VMEM((block, width), BF),
            pltpu.VMEM((2, half, half), BF),
            pltpu.VMEM((2, quarter, half), BF),
            pltpu.VMEM((2, deep - 1, quarter // deep, half), BF),
            pltpu.VMEM((2, 2, width, half), BF),
            pltpu.VMEM(vec_shape, BF),
            pltpu.SemaphoreType.DMA((LADDER_COPIES,)),
            pltpu.SemaphoreType.DMA((LADDER_COPIES,)),
        ]
        out_shape += [
            jax.ShapeDtypeStruct((2, 2, width, half), BF),
            jax.ShapeDtypeStruct(vec_shape, BF),
        ]
        out_specs += [any_spec(), any_spec()]

    def kernel(*refs):
        backward_kernel(depth, heads, deep, refs)

    operands = [cotangent, gains, lengths, *tables]
    in_specs = [vmem_spec()] * len(operands)
    remote = [*joined, grad_all, *weights, *[each for layer in held for each in layer]]
    in_specs += [any_spec()] * len(remote)
    return pl.pallas_call(
        kernel,
        out_shape=out_shape,
        in_specs=in_specs,
        out_specs=out_specs,
        scratch_shapes=scratch,
        compiler_params=pltpu.CompilerParams(
            collective_id=9, has_side_effects=True, vmem_limit_bytes=LIMIT
        ),
        name="layers_backward",
    )(*operands, *remote)


def finish_kernel(depth, refs):
    (low_ref, wself_ref, sum_ref, vec_ref) = refs[:4]
    attn_refs = refs[4 : 4 + depth]
    feed_refs = refs[4 + depth : 4 + 2 * depth]
    (tokens_ref, gain_ref, bias_ref, bada_ref, bdown_ref) = refs[4 + 2 * depth : 9 + 2 * depth]
    (qkv_ref, out_ref, ada_ref, up_ref, down_ref, self_ref) = refs[9 + 2 * depth :]
    step = pl.program_id(0)
    members = vec_ref.shape[0] // (8 * depth)
    width = vec_ref.shape[1]

    def pick(row):
        device = lax.broadcasted_iota(jnp.int32, (members, vec_ref.shape[0]), 0)
        column = lax.broadcasted_iota(jnp.int32, (members, vec_ref.shape[0]), 1)
        wanted = (column == device * 8 * depth + row).astype(F32).astype(BF)
        return dot(wanted, vec_ref[...]).astype(BF)

    rows = ada_ref.shape[1]
    times = pick(5)
    device = lax.broadcasted_iota(jnp.int32, (width, rows), 0)
    column = lax.broadcasted_iota(jnp.int32, (width, rows), 1)
    chosen = (device == column + step * rows).astype(F32).astype(BF)
    times = dot(times, chosen).astype(BF)
    for layer in range(depth):
        for place in range(2):
            ada_ref[layer, :, place * width : (place + 1) * width] = dot(
                times, pick(8 * layer + place), TN
            )
    self_ref[:, : width // 2] = sum_ref[0].astype(F32)
    self_ref[:, width // 2 :] = sum_ref[1].astype(F32)

    @pl.when(step == 0)
    def _():
        row = lax.broadcasted_iota(jnp.int32, (8 * depth, vec_ref.shape[0]), 0)
        column = lax.broadcasted_iota(jnp.int32, (8 * depth, vec_ref.shape[0]), 1)
        ones = (column % (8 * depth) == row).astype(F32).astype(BF)
        totals = dot(ones, vec_ref[...])
        for layer in range(depth):
            here = slice(layer, layer + 1)
            base = 8 * layer
            bada_ref[here, :width] = totals[base : base + 1]
            bada_ref[here, width:] = totals[base + 1 : base + 2]
            gain_ref[here, :] = totals[base + 2 : base + 3]
            bias_ref[here, :] = totals[base + 3 : base + 4]
            bdown_ref[here, :] = totals[base + 4 : base + 5]

    @pl.when(step == 1)
    def _():
        tokens_ref[...] = dot(low_ref[...].astype(BF), wself_ref[...], NT)

    @pl.when(step == 2)
    def _():
        for layer in range(depth):
            grads = attn_refs[layer][...]
            columns = grads.shape[1] // 4
            for place in range(3):
                qkv_ref[layer, place] = grads[:, place * columns : (place + 1) * columns]
            out_ref[layer] = grads[:, 3 * columns :].T

    @pl.when(step == 3)
    def _():
        for layer in range(depth):
            up_ref[layer] = feed_refs[layer][0]
            down_ref[layer] = feed_refs[layer][1]


def finish(depth, low, w_self, sums, vectors, attn_shards, feed_shards):
    block, width = low.shape
    part, columns = attn_shards[0].shape
    columns //= 4
    units = feed_shards[0].shape[2]
    steps = 4
    rows = 2 * width // steps

    def fixed(*shape):
        return pl.BlockSpec(shape, lambda step: (0,) * len(shape))

    def kernel(*refs):
        finish_kernel(depth, refs)

    fixed_shapes = [
        (block, width),
        (depth, width),
        (depth, width),
        (depth, 2 * width),
        (depth, width),
        (depth, 3, part, columns),
        (depth, columns, part),
    ]
    shard = (depth, part, units)
    return pl.pallas_call(
        kernel,
        grid=(steps,),
        out_shape=[
            *[jax.ShapeDtypeStruct(each, F32) for each in fixed_shapes],
            jax.ShapeDtypeStruct((depth, width, 2 * width), F32),
            jax.ShapeDtypeStruct(shard, F32),
            jax.ShapeDtypeStruct(shard, F32),
            jax.ShapeDtypeStruct((2 * width, width), F32),
        ],
        in_specs=[
            fixed(block, width),
            fixed(width, width),
            pl.BlockSpec((None, 2, rows, width // 2), lambda step: (step // 2, 0, step % 2, 0)),
            fixed(*vectors.shape),
            *[fixed(*each.shape) for each in attn_shards],
            *[fixed(*each.shape) for each in feed_shards],
        ],
        out_specs=[
            *[fixed(*each) for each in fixed_shapes],
            pl.BlockSpec((depth, width // steps, 2 * width), lambda step: (0, step, 0)),
            fixed(*shard),
            fixed(*shard),
            pl.BlockSpec((rows, width), lambda step: (step, 0)),
        ],
        compiler_params=pltpu.CompilerParams(vmem_limit_bytes=LIMIT),
        name="write_grads",
    )(low, w_self, sums, vectors, *attn_shards, *feed_shards)


def local(
    tokens,
    cotangent,
    lengths,
    timesteps,
    w_self,
    ln_gain,
    ln_bias,
    w_qkv,
    w_out,
    w_ada,
    b_ada,
    w_up,
    w_down,
    b_down,
):
    width = tokens.shape[1]
    depth = w_qkv.shape[0]
    heads = w_qkv.shape[3] // HD
    deep = 4 if lax.axis_size("dp") == 8 else 0
    weights = (jnp.swapaxes(w_qkv, 2, 3), w_out, w_up, w_down, w_ada)
    vectors = (ln_gain, ln_bias, b_down, b_ada, lengths, timesteps)
    made, kept = forward(heads, tokens, cotangent, w_self, vectors, weights)
    (activations, estimate, conds, cosine, sine, temb, grad_all) = made
    made = backward(
        heads,
        deep,
        cotangent,
        grad_all,
        ln_gain,
        lengths,
        (cosine, sine, temb, conds),
        weights,
        kept,
        (tokens, estimate),
    )
    grad_rows, smalls = made[:2]
    attn_shards = made[2 : 2 + depth]
    feed_shards = made[2 + depth : 2 + 2 * depth]
    if deep:
        sums, vectors = made[2 + 2 * depth :]
        vectors = vectors.reshape(-1, width)
    else:
        attn_shards = [
            lax.psum_scatter(each, "dp", scatter_dimension=0, tiled=True).astype(F32)
            for each in attn_shards
        ]
        feed_shards = [
            lax.psum_scatter(each, "dp", scatter_dimension=1, tiled=True).astype(F32)
            for each in feed_shards
        ]
        joined = jnp.concatenate([tokens, estimate], axis=1)
        sums = lax.psum(dot(joined, grad_rows.astype(BF), TN).astype(BF), ("dp", "tensor"))
        sums = sums.reshape(2, width, 2, width // 2).swapaxes(1, 2)
        vectors = smalls.at[5].set(temb[0]).astype(BF)
        vectors = lax.all_gather(vectors, ("dp", "tensor"), axis=0, tiled=True)
    made = finish(depth, grad_rows, w_self, sums, vectors, attn_shards, feed_shards)
    (grad_tokens, gain, bias, bias_ada, bias_down, qkv, out, ada, up, down, own) = made
    return (
        activations,
        grad_tokens,
        gain,
        bias,
        qkv,
        out,
        ada,
        bias_ada,
        up,
        jnp.swapaxes(down, 1, 2),
        bias_down,
        own,
    )


def solution(mesh):
    return jax.shard_map(
        local,
        mesh=mesh,
        in_specs=(
            P(("dp", "tensor"), None),
            P(("dp", "tensor"), None),
            P("dp", None),
            P("dp", None),
            P(),
            P(),
            P(),
            P(None, None, None, "tensor"),
            P(None, "tensor", None),
            P(),
            P(),
            P(None, None, "tensor"),
            P(None, "tensor", None),
            P(),
        ),
        out_specs=(
            P(("dp", "tensor"), None),
            P(("dp", "tensor"), None),
            P(),
            P(),
            P(None, None, "dp", "tensor"),
            P(None, "tensor", "dp"),
            P(),
            P(),
            P(None, "dp", "tensor"),
            P(None, "tensor", "dp"),
            P(),
            P(),
        ),
        check_vma=False,
    )
```

```python
import functools

import jax
import jax.numpy as jnp
from jax import lax
from jax.experimental import pallas as pl
from jax.experimental.pallas import tpu as pltpu
from jax.sharding import PartitionSpec as P

HD = 64
HALF = HD // 2
BF = jnp.bfloat16
F32 = jnp.float32
MESH = pl.DeviceIdType.MESH
EPS = 1e-05
LIMIT = 60 << 20

def norm(rows):
    centred = rows - jnp.mean(rows, axis=-1, keepdims=True)
    rstd = lax.rsqrt(jnp.mean(centred * centred, axis=-1, keepdims=True) + EPS)
    return (centred * rstd, rstd)


def norm_back(grad, hat, rstd):
    return rstd * (
        grad
        - jnp.mean(grad, axis=-1, keepdims=True)
        - hat * jnp.mean(grad * hat, axis=-1, keepdims=True)
    )


def dot(left, right, dims=((1,), (0,))):
    return lax.dot_general(left, right, (dims, ((), ())), preferred_element_type=F32)


NT = ((1,), (1,))
TN = ((0,), (0,))


def head_mask(head, columns, rotary):
    lane = lax.broadcasted_iota(jnp.int32, (1, columns), 1)
    if rotary:
        return (lane % 128) // HALF == head
    return lane // HD == head


def keep_head(rows, head, rotary):
    return jnp.where(head_mask(head, rows.shape[1], rotary), rows, jnp.zeros_like(rows))


def turned_place(columns, start, total):
    row = lax.broadcasted_iota(jnp.int32, (256, total), 0)
    column = lax.broadcasted_iota(jnp.int32, (256, total), 1) - start
    source = column // HD * HALF + column % HD // HALF * 128 + column % HALF
    fits = (source == row) & (column >= 0) & (column < columns)
    return fits.astype(F32).astype(BF)


def plain_place(columns, start, total):
    row = lax.broadcasted_iota(jnp.int32, (columns, total), 0)
    column = lax.broadcasted_iota(jnp.int32, (columns, total), 1) - start
    return (row == column).astype(F32).astype(BF)


def span(start, size):
    return pl.ds(pl.multiple_of(start, size), size)


class Gather:
    def __init__(self, sems, ids, rows):
        self.sems, self.ids, self.rows = sems, ids, rows
        self.half = rows.shape[0] // 8

    def copy(self, src, dst, kind, part, far):
        send, recv = self.sems
        return pltpu.make_async_remote_copy(
            src_ref=self.rows.at[span(src, self.half)],
            dst_ref=self.rows.at[span(dst, self.half)],
            send_sem=send.at[kind, part],
            recv_sem=recv.at[kind, part],
            device_id=self.ids[1] if far else self.ids[0],
            device_id_type=MESH,
        )

    def own(self, part):
        return span(2 * self.half * part, self.half)

    def pair(self, part):
        return 6 * self.half - 2 * self.half * part

    def far_copy(self, part):
        return self.copy(2 * self.half * part, self.pair(part), 0, part, True)

    def sibling_copy(self, part):
        start = 2 * self.half * part
        return self.copy(start, start + self.half, 1, part, False)

    def forward_copy(self, part):
        return self.copy(self.pair(part), self.pair(part) + self.half, 2, part, False)

    def send(self, part):
        self.far_copy(part).start()
        self.sibling_copy(part).start()

    def near(self, part):
        self.sibling_copy(part).wait_recv()

    def arrive(self, part):
        self.far_copy(part).wait_recv()
        self.forward_copy(part).start()

    def settle(self, part):
        self.forward_copy(part).wait()

    def far(self, part):
        self.arrive(part)
        self.settle(part)

    def receive(self, step):
        @pl.when(step < 2)
        def _():
            self.near(step)

        @pl.when(step >= 2)
        def _():
            self.far(step - 2)

    def finish(self, far=True):
        for part in range(2):
            self.sibling_copy(part).wait_send()
            if far:
                self.far_copy(part).wait_send()


class Scatter:
    def __init__(self, sems, ids, own, buffers):
        self.sems, self.ids, self.own_sum = sems, ids, own
        self.pair_out, self.pair_in, self.own_out, self.own_in, self.far_out, self.far_in = buffers
        self.half = self.pair_out.shape[1]

    def copy(self, src, dst, kind, part, far):
        send, recv = self.sems
        return pltpu.make_async_remote_copy(
            src_ref=src.at[part],
            dst_ref=dst.at[part],
            send_sem=send.at[kind, part],
            recv_sem=recv.at[kind, part],
            device_id=self.ids[1] if far else self.ids[0],
            device_id_type=MESH,
        )

    def pair_copy(self, part):
        return self.copy(self.pair_out, self.pair_in, 0, part, False)

    def own_copy(self, part):
        return self.copy(self.own_out, self.own_in, 1, part, False)

    def sum_copy(self, part):
        return self.copy(self.far_out, self.far_in, 2, part, True)

    def send(self, unit, total):
        @pl.when(unit < 2)
        def _():
            self.own_sum[span(self.half * unit, self.half), :] = total[: self.half, :]
            self.own_out[unit] = total[self.half :, :].astype(BF)
            self.own_copy(unit).start()

        @pl.when(unit >= 2)
        def _():
            part = 3 - unit
            self.pair_out[part] = total[self.half :, :].astype(BF)
            self.pair_copy(part).start()
            self.pair_copy(part).wait_recv()
            self.far_out[part] = (
                total[: self.half, :] + self.pair_in[part].astype(F32)
            ).astype(BF)
            self.sum_copy(part).start()

    def collect(self, part):
        self.own_copy(part).wait_recv()
        self.sum_copy(part).wait_recv()
        rows = pl.ds(part * self.half, self.half)
        made = self.own_sum[rows, :] + self.own_in[part].astype(F32)
        return made + self.far_in[part].astype(F32)

    def finish(self):
        for part in range(2):
            self.pair_copy(part).wait_send()
            self.own_copy(part).wait_send()
            self.sum_copy(part).wait_send()


class Near:
    def __init__(self, sems, ids, own, out, into):
        self.sems, self.ids = sems, ids
        self.own, self.out, self.into = own, out, into
        self.half = out.shape[1]

    def copy(self, part):
        return pltpu.make_async_remote_copy(
            src_ref=self.out.at[part],
            dst_ref=self.into.at[part],
            send_sem=self.sems.at[0, part],
            recv_sem=self.sems.at[1, part],
            device_id=self.ids[0],
            device_id_type=MESH,
        )

    def send(self, part, total):
        self.own[span(self.half * part, self.half), :] = total[: self.half, :]
        self.out[part] = total[self.half :, :].astype(BF)
        self.copy(part).start()

    def collect(self, part):
        self.copy(part).wait_recv()
        return self.own[pl.ds(part * self.half, self.half), :] + self.into[part].astype(F32)

    def drain(self):
        for part in range(2):
            self.copy(part).wait_send()


class Fetch:
    def __init__(self, sems, ids, square, shards):
        self.sems, self.shards = sems, shards
        self.far = ids[1]
        self.x, self.z, self.x_peer, self.z_peer = square
        self.piece = shards.shape[1] // 8

    def copy(self, index, src, start, size, device):
        place = span(start * self.piece, size * self.piece)
        return pltpu.make_async_remote_copy(
            src_ref=self.shards.at[src, place],
            dst_ref=self.shards.at[1, place],
            send_sem=self.sems.at[0, index],
            recv_sem=self.sems.at[1, index],
            device_id=device,
            device_id_type=MESH,
        )

    def hop(self, index):
        x_first = 2 * self.z + self.x
        z_first = 4 + 2 * self.x + self.z
        return (
            lambda: self.copy(0, 0, x_first, 1, self.far),
            lambda: self.copy(1, 0, z_first, 1, self.far),
            lambda: self.copy(2, 1, x_first, 1, self.x_peer),
            lambda: self.copy(3, 1, z_first, 1, self.z_peer),
            lambda: self.copy(4, 1, 2 * self.z, 2, self.z_peer),
            lambda: self.copy(5, 1, 4 + 2 * self.x, 2, self.x_peer),
        )[index]()

    def step(self, count):
        if count == 1:
            self.hop(0).start()
            self.hop(1).start()
        elif count < 4:
            for index in (2 * count - 4, 2 * count - 3):
                self.hop(index).wait_recv()
                self.hop(index + 2).start()
        else:
            self.hop(4).wait_recv()
            self.hop(5).wait_recv()

    def finish(self):
        for index in range(6):
            self.hop(index).wait_send()


def square():
    group = lax.axis_index("dp")
    place = lax.axis_index("tensor")
    x = lax.rem(group, 2)
    z = lax.rem(group // 2, 2)
    return (x, z, (group + 1 - 2 * x, place), (group + 2 - 4 * z, place))


def neighbours():
    group = lax.axis_index("dp")
    place = lax.axis_index("tensor")
    core = lax.rem(place, 2)
    return ((group, place + 1 - 2 * core), (group, lax.rem(place + 2, 4)))


class Spot:
    def __init__(self, deep):
        group = lax.axis_index("dp")
        self.place = lax.axis_index("tensor")
        self.deep = deep
        self.z = group // 2
        self.x = lax.rem(group, 2)
        self.across = (2 * self.z + 1 - self.x, self.place)

    def level(self, ahead):
        return lax.rem(self.z + ahead, self.deep)

    def along(self, ahead):
        return (2 * self.level(ahead) + self.x, self.place)

    def partners(self):
        return [self.across] + [self.along(ahead) for ahead in range(1, self.deep)]


def meet(ids):
    barrier = pltpu.get_barrier_semaphore()
    for device in ids:
        pl.semaphore_signal(barrier, inc=1, device_id=device, device_id_type=MESH)
    pl.semaphore_wait(barrier, len(ids))


class DpSum:
    def __init__(self, spot, src, out, scratch):
        self.spot, self.src, self.out = spot, src, out
        self.pairs, self.rest, self.sems = scratch
        self.block = self.pairs.shape[1]

    @staticmethod
    def scratch(deep, block, columns):
        return [
            pltpu.VMEM((deep, block, columns), BF),
            pltpu.VMEM((deep - 1, block, columns), BF),
            pltpu.SemaphoreType.DMA((4, deep)),
        ]

    def rows(self, ahead, x):
        start = (2 * self.spot.level(ahead) + x) * self.block
        return pl.ds(pl.multiple_of(start, self.block), self.block)

    def x_copy(self, ahead):
        return pltpu.make_async_remote_copy(
            src_ref=self.src.at[self.rows(ahead, 1 - self.spot.x)],
            dst_ref=self.pairs.at[ahead],
            send_sem=self.sems.at[0, ahead],
            recv_sem=self.sems.at[1, ahead],
            device_id=self.spot.across,
            device_id_type=MESH,
        )

    def z_copy(self, ahead):
        return pltpu.make_async_remote_copy(
            src_ref=self.pairs.at[ahead],
            dst_ref=self.rest.at[ahead - 1],
            send_sem=self.sems.at[2, ahead],
            recv_sem=self.sems.at[3, ahead],
            device_id=self.spot.along(ahead),
            device_id_type=MESH,
        )

    def order(self):
        return [*range(1, self.spot.deep), 0]

    def start(self):
        for ahead in self.order():
            self.x_copy(ahead).start()

    def middle(self):
        for ahead in self.order():
            self.x_copy(ahead).wait_recv()
            total = self.src[self.rows(ahead, self.spot.x), :].astype(F32)
            total = total + self.pairs[ahead].astype(F32)
            if ahead:
                self.pairs[ahead] = total.astype(BF)
                self.z_copy(ahead).start()
            else:
                self.out[...] = total
        for ahead in self.order():
            self.x_copy(ahead).wait_send()

    def end(self):
        for ahead in range(1, self.spot.deep):
            self.z_copy(ahead).wait_recv()
        total = self.out[...]
        for ahead in range(1, self.spot.deep):
            total = total + self.rest[ahead - 1].astype(F32)
        self.out[...] = total
        for ahead in range(1, self.spot.deep):
            self.z_copy(ahead).wait_send()


def scatter_scratch(rows, width):
    return [pltpu.VMEM((2, rows // 8, width), BF)] * 6


def gelu_parts(hidden):
    cdf = 0.5 * (1.0 + lax.erf(hidden * (0.5**0.5)))
    density = jnp.exp(hidden * hidden * -0.5) * 0.3989422804014327
    return (hidden * cdf, cdf + hidden * density)


def load_turned(wq, wk, wqk):
    turn = turned_place(wq.shape[0], 0, wq.shape[0])
    wqk[:256, :] = dot(turn, wq[...]).astype(BF)
    wqk[256:, :] = dot(turn, wk[...]).astype(BF)


def is_packed(lengths_ref, length):
    return (lengths_ref[:, 0:1] < length).astype(jnp.int32).astype(F32)


def owner(chunk):
    return 2 * (chunk // 4) + chunk % 2


def apart(keys, queries, packed):
    return (keys != queries).astype(jnp.int32).astype(F32) * (packed * -1e9)


def unit_owner(unit, half):
    return jnp.where(unit < 2, 0, 2) + half


SAVED = ("a", "q", "k", "v", "o", "o2", "x1", "m", "g", "slope", "x", "lse")


def forward_kernel(depth, heads, refs):
    refs = list(refs)

    def take(count):
        made = refs[:count]
        del refs[:count]
        return made

    (gain_ref, bias_ref, bdown_ref, bada_ref, lengths_ref, steps_ref) = take(6)
    (rotary_ref, time_ref, cot_ref) = take(3)
    (tokens_hbm, wself_hbm, wqkv_hbm, wout_hbm, wup_hbm, wdown_hbm, wada_hbm) = take(7)
    (acts_ref, est_ref, cond_ref, cos_ref, sin_ref, temb_ref, grad_hbm) = take(7)
    saved_hbm = [dict(zip(SAVED, take(len(SAVED)))) for _ in range(depth)]
    gather_sems = [take(2) for _ in range(5)]
    (near_a_sems, near_f_sems, fetch_sems, cross_send, cross_recv) = take(5)
    (load_sems, store_sems) = take(2)
    (tokens, wself, wada) = take(3)
    wa, wu, wd, wqk = take(depth), take(depth), take(depth), take(depth)
    abufs, mbufs, (ebuf,) = take(2), take(2), take(1)
    (q2, k2, v2, ob2, lse2, accs, stats, gb, gpb) = take(9)
    (x1, xb, start, own_a, own_f, sums) = take(6)
    near_a_bufs, near_f_bufs = take(2), take(2)
    ids = neighbours()
    corner = square()
    columns = heads * HD
    width = xb.shape[1]
    half = xb.shape[0] // 2
    unit_rows = 2 * half
    length = 8 * half
    part_a = [pl.ds(part * columns, columns) for part in range(4)]
    sources = [tokens_hbm, wself_hbm.at[0], wself_hbm.at[1]]
    places = [tokens, wself.at[0], wself.at[1]]
    for layer in range(depth):
        sources += [wqkv_hbm.at[layer, part] for part in range(3)] + [wout_hbm.at[layer]]
        places += [wa[layer].at[0, rows] for rows in part_a]
        sources += [wup_hbm.at[layer], wdown_hbm.at[layer]]
        places += [wu[layer].at[0], wd[layer].at[0]]
    loads = [
        pltpu.make_async_copy(src, dst, load_sems.at[i])
        for i, (src, dst) in enumerate(zip(sources, places))
    ]
    ada_loads = [
        pltpu.make_async_copy(wada_hbm.at[layer], wada, load_sems.at[len(loads)])
        for layer in range(depth)
    ]
    order = [0, 1, *range(3, 9)]
    for i in order:
        loads[i].start()
    ada_loads[0].start()
    for i in range(len(loads)):
        if i not in order:
            loads[i].start()
    meet([*ids, *corner[2:]])
    fetches = []
    for layer in range(depth):
        for shards in (wa[layer], wu[layer], wd[layer]):
            fetches.append(Fetch(fetch_sems.at[len(fetches)], ids, corner, shards))
    gathers = [Gather(gather_sems[i], ids, abufs[i]) for i in range(2)]
    mixes = [Gather(gather_sems[2 + i], ids, mbufs[i]) for i in range(2)]
    grads = Gather(gather_sems[4], ids, ebuf)
    near_a = Near(near_a_sems, ids, own_a, *near_a_bufs)
    near_f = Near(near_f_sems, ids, own_f, *near_f_bufs)
    packed = is_packed(lengths_ref, length)
    pending = []

    def store(name, src, dst):
        made = pltpu.make_async_copy(src, dst, store_sems.at[len(pending)])
        made.start()
        pending.append([name, made, False])

    def stored(*names):
        for each in pending:
            if each[0] in names and not each[2]:
                each[1].wait()
                each[2] = True

    def begin(number, part, made):
        layer = number % depth
        rows = pl.ds(part * half, half)
        if number >= 2 and part == 0:
            gathers[number % 2].finish()
        xb[rows, :] = made
        hat = norm(made)[0]
        gain = gain_ref[layer : layer + 1, :]
        normed = hat * gain + bias_ref[layer : layer + 1, :]
        abufs[number % 2][pl.ds(2 * half * part, half), :] = normed.astype(BF)
        gathers[number % 2].send(part)

    for i in (3, 4, 5, 6):
        loads[i].wait()
    fetches[0].step(1)
    loads[0].wait()
    loads[1].wait()
    for part in range(2):
        rows = pl.ds(part * half, half)
        made = dot(tokens[rows, :], wself[0])
        start[rows, :] = made
        begin(0, part, made)

    def make_tables():
        place = lax.axis_index("tensor")
        sibling = ids[0][1]
        far = ids[1][1]
        far_other = lax.rem(sibling + 2, 4)
        row = lax.broadcasted_iota(jnp.int32, (half, 128), 0).astype(F32)
        for chunk, (block, part) in enumerate(
            zip(
                (place, sibling, place, sibling, far, far_other, far, far_other),
                (0, 0, 1, 1, 1, 1, 0, 0),
            )
        ):
            rows = pl.ds(chunk * half, half)
            offset = (block * unit_rows).astype(F32)
            position = row + part * half + (1.0 - packed) * offset
            angle = position * rotary_ref[...]
            cos_ref[rows, :] = jnp.cos(angle)
            sin_ref[rows, :] = jnp.sin(angle)
        steps = steps_ref[...].astype(F32)
        slot = lax.broadcasted_iota(jnp.int32, steps.shape, 1)
        mine = jnp.sum(jnp.where(slot == place, steps, 0.0), axis=1, keepdims=True)
        step = packed * mine + (1.0 - packed) * steps[:, 0:1]
        angle = jnp.broadcast_to(step * time_ref[...], (8, width // 2))
        temb_ref[:, : width // 2] = jnp.cos(angle)
        temb_ref[:, width // 2 :] = jnp.sin(angle)

    def make_cond(layer):
        ada_loads[layer].wait()
        column = temb_ref[...].T[:, 0:1]
        made = jnp.sum(wada[...] * column, axis=0, keepdims=True)
        made = made + bada_ref[layer : layer + 1, :]
        cond_ref[8 * layer : 8 * layer + 8, :] = jnp.broadcast_to(made, (8, 2 * width))
        if layer + 1 < depth:
            ada_loads[layer + 1].start()

    def project(number, count, pick, before):
        layer = number % depth
        abuf = abufs[number % 2]

        def body(step, carry):
            before(step)
            shard, unit = pick(step)
            rows = span(unit * unit_rows, unit_rows)
            normed = abuf[rows, :]
            mixed = dot(normed, wqk[layer][shard], NT)
            cosine = cos_ref[rows, :]
            sine = sin_ref[rows, :]
            for place, dst, scale in ((0, q2, HD**-0.5), (256, k2, 1.0)):
                first = mixed[:, place : place + 128]
                second = mixed[:, place + 128 : place + 256]
                dst[shard, rows, :128] = ((first * cosine - second * sine) * scale).astype(BF)
                dst[shard, rows, 128:] = ((second * cosine + first * sine) * scale).astype(BF)
            v2[shard, rows, :] = dot(normed, wa[layer][shard, part_a[2], :], NT).astype(BF)
            return carry

        lax.fori_loop(0, count, body, 0)

    lane = lax.broadcasted_iota(jnp.int32, (1, 128), 1)

    def scores_of(shard, unit, head, keys):
        rows = span(unit * unit_rows, unit_rows)
        made = dot(keep_head(q2[shard, rows, :], head, True), k2[shard, keys, :], NT)
        part = lax.broadcasted_iota(jnp.int32, (2, 1, length // 2), 0)
        chunk = lax.broadcasted_iota(jnp.int32, (2, 1, length // 2), 2) // half
        neg = apart(owner(chunk + keys.start // half), part, packed.reshape(1, 1, 1))
        return (made.reshape(2, half, length // 2) + neg).reshape(unit_rows, length // 2)

    def attend_near(number, count, pick, before):
        keys = pl.ds(0, length // 2)

        def body(step, carry):
            before(step)
            shard, unit = pick(step)
            place = 2 * unit + shard
            attended = jnp.zeros((unit_rows, columns), F32)
            tops = jnp.zeros((unit_rows, 128), F32)
            totals = jnp.zeros((unit_rows, 128), F32)
            for head in range(heads):
                scores = scores_of(shard, unit, head, keys)
                largest = jnp.max(scores, axis=-1, keepdims=True)
                shares = jnp.exp(scores - largest)
                output = dot(shares.astype(BF), v2[shard, keys, :])
                attended = jnp.where(head_mask(head, columns, False), output, attended)
                tops = jnp.where(lane == head, largest, tops)
                totals = jnp.where(lane == head, jnp.sum(shares, axis=-1, keepdims=True), totals)
            accs[place] = attended
            stats[place, 0] = tops
            stats[place, 1] = totals
            return carry

        lax.fori_loop(0, count, body, 0)

    def attend_far(number, save, count, pick, before):
        keys = pl.ds(length // 2, length // 2)
        layer, slot = number % depth, number % 2

        def body(step, carry):
            before(step)
            shard, unit = pick(step)
            place = 2 * unit + shard
            rows = span(unit * unit_rows, unit_rows)
            attended = jnp.zeros((unit_rows, columns), F32)
            logs = jnp.zeros((unit_rows, 128), F32)
            for head in range(heads):
                scores = scores_of(shard, unit, head, keys)
                earlier = stats[place, 0][:, head : head + 1]
                largest = jnp.maximum(earlier, jnp.max(scores, axis=-1, keepdims=True))
                shares = jnp.exp(scores - largest)
                shrink = jnp.exp(earlier - largest)
                totals = stats[place, 1][:, head : head + 1] * shrink
                totals = totals + jnp.sum(shares, axis=-1, keepdims=True)
                output = dot(shares.astype(BF), v2[shard, keys, :])
                output = (accs[place] * shrink + output) * (1.0 / totals)
                attended = jnp.where(head_mask(head, columns, False), output, attended)
                if save:
                    logs = jnp.where(lane == head, largest + jnp.log(totals), logs)
            if save:
                lse2[slot, shard, unit] = logs.T[:8, :]
            attended = attended.astype(BF)
            ob2[slot, shard, rows, :] = attended

            @pl.when(shard == 1)
            def _():
                total = dot(ob2[slot, 0, rows, :], wa[layer][0, part_a[3], :])
                near_a.send(unit, total + dot(attended, wa[layer][1, part_a[3], :]))

            return carry

        lax.fori_loop(0, count, body, 0)

    def feed(number, save, pick, before):
        layer = number % depth
        mbuf = mbufs[number % 2]

        def body(step, carry):
            before(step)
            shard, unit = pick(step)
            rows = span(unit * unit_rows, unit_rows)
            hidden = dot(mbuf[rows, :], wu[layer][shard])
            gated, slope = gelu_parts(hidden)
            gated = gated.astype(BF)
            made = dot(gated, wd[layer][shard])

            @pl.when(shard == 0)
            def _():
                if save:
                    gb[rows, :] = gated
                    gpb[rows, :] = slope.astype(BF)
                sums[rows, :] = made

            @pl.when(shard == 1)
            def _():
                near_f.send(unit, sums[rows, :] + made)

            return carry

        lax.fori_loop(0, 4, body, 0)

    crossings = {}

    def cross(number):
        slot = number % 2
        made = []
        for part in range(2):
            made.append(
                pltpu.make_async_remote_copy(
                    src_ref=lse2.at[slot, 1, part],
                    dst_ref=lse2.at[slot, 0, 3 - part],
                    send_sem=cross_send.at[2 * slot + part],
                    recv_sem=cross_recv.at[2 * slot + part],
                    device_id=ids[1],
                    device_id_type=MESH,
                )
            )
            made[-1].start()
        crossings[number] = made

    def late(number):
        slot = number % 2
        saved = saved_hbm[number % depth]
        for part in range(2):
            mixes[slot].far(part)
        store("m", mbufs[slot], saved["m"])
        for each in crossings[number]:
            each.wait_recv()
        store("lse", lse2.at[slot, 0], saved["lse"])

    def events(table):
        def before(step):
            for when, actions in table.items():

                @pl.when(step == when)
                def _():
                    for action in actions:
                        if isinstance(action, tuple):
                            if action[0] < len(fetches):
                                fetches[action[0]].step(action[1])
                        else:
                            action()

        return before

    def waits(*indices):
        def action():
            for index in indices:
                loads[index].wait()

        return action

    def by_unit(step):
        return (lax.rem(step, 2), step // 2)

    def by_shard(step):
        return (step // 2, lax.rem(step, 2))

    def run(number, after_layer):
        layer, slot = number % depth, number % 2
        save = number >= depth
        group, mix = gathers[slot], mixes[slot]
        mix_rows = mbufs[slot]
        base = 3 * layer

        def after_attend(part):
            def action():
                if part == 0 and number >= 2:
                    mix.finish(far=False)
                if part == 0:
                    stored("x1")
                rows = pl.ds(part * half, half)
                after = xb[rows, :] + near_a.collect(part)
                x1[rows, :] = after
                shift = cond_ref[8 * layer : 8 * layer + 1, :width]
                scale = cond_ref[8 * layer : 8 * layer + 1, width:]
                made = norm(after)[0] * (1.0 + scale) + shift
                mix_rows[pl.ds(2 * half * part, half), :] = made.astype(BF)
                mix.sibling_copy(part).start()
                if number == 2 * depth - 1:
                    mix.far_copy(part).start()

            return action

        def after_feed(part):
            def action():
                if part == 0:
                    stored("x")
                rows = pl.ds(part * half, half)
                made = x1[rows, :] + near_f.collect(part) + bdown_ref[layer : layer + 1, :]
                after_layer(part, rows, made)

            return action

        def near_rows(part):
            return lambda: group.near(part)

        def far_rows(part):
            return lambda: group.far(part)

        def mixed(part):
            return lambda: mix.near(part)

        if number:
            near_a.drain()
            near_f.drain()
        stored("q", "k", "v")

        def turn(shard):
            rows = wa[layer].at[shard, part_a[0]], wa[layer].at[shard, part_a[1]]
            load_turned(*rows, wqk[layer].at[shard])

        far_table = {3: [after_attend(0)]}
        feed_table = {
            0: [mixed(0)],
            1: [after_attend(1)],
            2: [mixed(1)],
            3: [after_feed(0)],
        }
        order = by_unit
        if number == 0:
            make_tables()
            turn(0)
            arrive = {
                0: [near_rows(0)],
                1: [near_rows(1)],
                2: [(0, 2), waits(7), (1, 1), far_rows(0)],
                3: [far_rows(1), waits(8), (2, 1)],
            }

            def in_order(step):
                return jnp.where(step < 2, step, 5 - step)

            project(number, 4, lambda step: (0, in_order(step)), events(arrive))
            attend_near(number, 2, lambda step: (0, step), events({1: [(0, 3)]}))
            make_cond(layer)
            first = {1: [(1, 2), waits(9, 10, 11, 12), (3, 1)]}
            attend_far(number, save, 2, lambda step: (0, step), events(first))
            fetches[0].step(4)
            turn(1)
            second = {3: [(1, 3), (2, 2), waits(13), (4, 1)]}
            project(number, 4, lambda step: (1, in_order(step)), events(second))
            attend_near(number, 2, lambda step: (1, step), events({}))
            far_table = {1: [after_attend(0)]}
            attend_far(number, save, 2, lambda step: (1, step), events(far_table))
            feed_table = {
                0: [mixed(0), (2, 3), (3, 2), waits(14), (5, 1)],
                1: [after_attend(1), mixed(1)],
                2: [(1, 4), (3, 3), (4, 2), (2, 4)],
                3: [after_feed(0)],
            }
            order = by_shard
        else:
            own_table = {0: [near_rows(0)], 1: [near_rows(1)]}
            near_table = {3: [lambda: group.arrive(0)]}
            if not save:
                turn(0)
                own_table[0] += [(base + 1, 3), (base + 2, 2)]
                own_table[2] = [(base, 4), lambda: turn(1)]
                near_table[3] = [(base + 2, 3), lambda: group.arrive(0)]
                feed_table[0] += [(base + 1, 4)]
                feed_table[1] += [(base + 2, 4)]
            project(number, 4, by_shard, events(own_table))
            attend_near(number, 4, by_unit, events(near_table))
            if not save:
                make_cond(layer)
            if number == depth:
                for part in range(2):
                    grads.near(part)
                    grads.far(part)
                store("grad", ebuf, grad_hbm)
            arrive = {
                0: [lambda: group.settle(0)],
                1: [lambda: group.arrive(1)],
                2: [lambda: group.settle(1)],
            }
            project(number, 4, lambda step: (lax.rem(step, 2), 3 - step // 2), events(arrive))
            if number == depth - 1:
                for part in range(2):
                    ebuf[grads.own(part), :] = cot_ref[pl.ds(part * half, half), :]
                    grads.send(part)
            if number > depth:
                for part in range(2):
                    mixes[(number - 1) % 2].far_copy(part).start()
            if save:
                store("a", abufs[slot], saved_hbm[layer]["a"])
                store("x", xb, saved_hbm[layer]["x"])
                for name, src in (("q", q2), ("k", k2), ("v", v2)):
                    store(name, src.at[0], saved_hbm[layer][name])
            attend_far(number, save, 4, by_unit, events(far_table))
        if save:
            cross(number)
            rows = pl.ds(0, length // 2)
            store("o", ob2.at[slot, 0, rows], saved_hbm[layer]["o"])
            store("o2", ob2.at[slot, 1, rows], saved_hbm[layer]["o2"])
        stored("g", "slope")
        feed(number, save, order, events(feed_table))
        if save:
            store("x1", x1, saved_hbm[layer]["x1"])
            store("g", gb, saved_hbm[layer]["g"])
            store("slope", gpb, saved_hbm[layer]["slope"])
        after_feed(1)()

    def between(part, rows, made):
        estimate = made.astype(BF)
        est_ref[rows, :] = estimate
        begin(depth, part, start[rows, :] + dot(estimate, wself[1]))

    def close(part, rows, made):
        acts_ref[rows, :] = made.astype(BF)

    def enter(number):
        return lambda part, rows, made: begin(number, part, made)

    for number in range(2 * depth):
        if number + 1 == 2 * depth:
            run(number, close)
        elif number + 1 == depth:
            loads[2].wait()
            run(number, between)
        else:
            run(number, enter(number + 1))
    for number in range(depth, 2 * depth):
        late(number)
    for each in gathers:
        each.finish()
    for each in (*mixes, grads):
        each.finish()
    near_a.drain()
    near_f.drain()
    for each in fetches:
        each.finish()
    for each in crossings.values():
        for copy in each:
            copy.wait_send()
    stored("grad", *SAVED)


def any_spec():
    return pl.BlockSpec(memory_space=pl.ANY)


def vmem_spec():
    return pl.BlockSpec(memory_space=pltpu.VMEM)


def forward(heads, tokens, cotangent, w_self, vectors, weights):
    depth = weights[0].shape[0]
    block, width = tokens.shape
    length = 4 * block
    half = block // 2
    columns = heads * HD
    units = weights[2].shape[2]
    lanes = jnp.arange(128) % HALF
    rotary = jnp.exp(-jnp.log(10000.0) * lanes.astype(F32) / HALF)[None]
    halves = jnp.arange(width // 2).astype(F32)
    times = jnp.exp(-jnp.log(10000.0) * halves / (width // 2))[None]
    kept = {
        "a": ((length, width), BF),
        "q": ((length, 256), BF),
        "k": ((length, 256), BF),
        "v": ((length, columns), BF),
        "o": ((length // 2, columns), BF),
        "o2": ((length // 2, columns), BF),
        "x1": ((block, width), F32),
        "m": ((length, width), BF),
        "g": ((length // 2, units), BF),
        "slope": ((length // 2, units), BF),
        "x": ((block, width), F32),
        "lse": ((4, 8, block), F32),
    }
    kept_shapes = [jax.ShapeDtypeStruct(*kept[name]) for name in SAVED]
    out_shape = [
        jax.ShapeDtypeStruct((block, width), BF),
        jax.ShapeDtypeStruct((block, width), BF),
        jax.ShapeDtypeStruct((8 * depth, 2 * width), F32),
        jax.ShapeDtypeStruct((length, 128), F32),
        jax.ShapeDtypeStruct((length, 128), F32),
        jax.ShapeDtypeStruct((8, width), F32),
        jax.ShapeDtypeStruct((length, width), BF),
    ] + kept_shapes * depth
    out_specs = [vmem_spec()] * 6 + [any_spec()] * (1 + depth * len(SAVED))
    dma = pltpu.SemaphoreType.DMA
    scratch = [dma((3, 2))] * 10
    scratch += [dma((2, 2))] * 2 + [dma((3 * depth, 2, 6)), dma((4,)), dma((4,))]
    scratch += [dma((4 + 6 * depth,)), dma((1 + depth * len(SAVED),))]
    scratch += [
        pltpu.VMEM((block, width), BF),
        pltpu.VMEM((2, width, width), BF),
        pltpu.VMEM((width, 2 * width), F32),
    ]
    scratch += [pltpu.VMEM((2, 4 * columns, width), BF)] * depth
    scratch += [pltpu.VMEM((2, width, units), BF)] * depth
    scratch += [pltpu.VMEM((2, units, width), BF)] * depth
    scratch += [pltpu.VMEM((2, 512, width), BF)] * depth
    scratch += [pltpu.VMEM((length, width), BF)] * 5
    scratch += [
        pltpu.VMEM((2, length, 256), BF),
        pltpu.VMEM((2, length, 256), BF),
        pltpu.VMEM((2, length, columns), BF),
        pltpu.VMEM((2, 2, length // 2, columns), BF),
        pltpu.VMEM((2, 2, 4, 8, block), F32),
        pltpu.VMEM((4, block, columns), F32),
        pltpu.VMEM((4, 2, block, 128), F32),
        pltpu.VMEM((length // 2, units), BF),
        pltpu.VMEM((length // 2, units), BF),
    ]
    scratch += [pltpu.VMEM((block, width), F32)] * 5
    scratch += [pltpu.VMEM((2 * block, width), F32)]
    scratch += [pltpu.VMEM((2, half, width), BF)] * 4

    def kernel(*refs):
        forward_kernel(depth, heads, refs)

    operands = [*vectors, rotary, times, cotangent]
    remote = [tokens, w_self.reshape(2, width, width), *weights]
    made = pl.pallas_call(
        kernel,
        out_shape=out_shape,
        in_specs=[vmem_spec()] * len(operands) + [any_spec()] * len(remote),
        out_specs=out_specs,
        scratch_shapes=scratch,
        compiler_params=pltpu.CompilerParams(
            collective_id=1, has_side_effects=True, vmem_limit_bytes=LIMIT
        ),
        name="layers_forward",
    )(*operands, *remote)
    count = len(SAVED)
    saved = [made[7 + count * layer : 7 + count * (layer + 1)] for layer in range(depth)]
    return (made[:7], [dict(zip(SAVED, each)) for each in saved])


class Ladder:
    def __init__(self, sems):
        self.send, self.recv = sems
        self.used = 0
        self.open = []

    def copy(self, src, dst, device):
        made = pltpu.make_async_remote_copy(
            src_ref=src,
            dst_ref=dst,
            send_sem=self.send.at[self.used],
            recv_sem=self.recv.at[self.used],
            device_id=device,
            device_id_type=MESH,
        )
        self.used += 1
        assert self.used <= LADDER_COPIES
        made.start()
        self.open.append(made)
        return made

    def finish(self):
        for each in self.open:
            each.wait_send()


LADDER_COPIES = 34


class Loads:
    def __init__(self, sems):
        self.sems = sems
        self.names = {}

    def add(self, name, sources, buffer):
        self.names[name] = (sources, buffer, len(self.names))
        return buffer

    def copy(self, name, layer):
        sources, buffer, place = self.names[name]
        return pltpu.make_async_copy(sources[layer], buffer, self.sems.at[place])

    def start(self, layer, *names):
        if layer >= 0:
            for name in names:
                self.copy(name, layer).start()

    def wait(self, layer, *names):
        for name in names:
            self.copy(name, layer).wait()


def backward_kernel(depth, heads, deep, refs):
    refs = list(refs)

    def take(count):
        made = refs[:count]
        del refs[:count]
        return made

    cot_ref, gain_ref, lengths_ref, cos_ref, sin_ref, temb_ref, cond_ref = take(7)
    joined_hbm = take(2)
    (grad_hbm,) = take(1)
    wqkv_hbm, wout_hbm, wup_hbm, wdown_hbm, _ = take(5)
    saved_hbm = [dict(zip(SAVED, take(len(SAVED)))) for _ in range(depth)]
    (out_ref, small_ref) = take(2)
    attn_outs, feed_outs = take(depth), take(depth)
    if deep:
        sum_ref, vec_ref = take(2)
    feed_sems, attn_sems = [take(2), take(2)], [take(2), take(2)]
    load_sems, store_sems, out_sems = take(3)
    loads = Loads(load_sems)
    wq, wk, wv = (
        loads.add(name, [wqkv_hbm.at[layer, part] for layer in range(depth)], take(1)[0])
        for part, name in enumerate(("wq", "wk", "wv"))
    )
    wout, wup, wdown = (
        loads.add(name, [src.at[layer] for layer in range(depth)], take(1)[0])
        for name, src in (("wout", wout_hbm), ("wup", wup_hbm), ("wdown", wdown_hbm))
    )
    buffers = dict(zip(SAVED, take(len(SAVED))))
    outs = [take(2) for _ in range(depth)]
    for name in SAVED:
        if name in ("o", "o2"):
            continue
        rows = saved_hbm[0][name].shape[0]
        buffer = buffers[name]
        if rows < buffer.shape[0]:
            buffer = buffer.at[pl.ds(0, rows)]
        loads.add(name, [saved_hbm[layer][name] for layer in range(depth)], buffer)
    abuf, qb, kb, vb, _, _, x1b, mbuf, gb, gpb, xb, lse = (buffers[name] for name in SAVED)
    ebuf, fbuf = take(2)
    feed_bufs, attn_bufs = take(6), take(6)
    (wqk, dhb, qmask, domask, dsb, pb, dkb, dvb, dqk, dvv, work, dxb) = take(12)
    (feed_grads, attn_grads) = take(2)
    ids = neighbours()
    sums = {}
    if deep:
        spot = Spot(deep)
        meet([*ids, *spot.partners()])
        for layer in range(depth):
            for name, src, out in (
                ("up", feed_grads.at[0], feed_outs[layer].at[0]),
                ("down", feed_grads.at[1], feed_outs[layer].at[1]),
                ("attn", attn_grads, attn_outs[layer]),
            ):
                sums[name, layer] = DpSum(spot, src, out, take(3))
        tail_refs = take(10)
        joined = tail_refs[0]
        joined_loads = [
            pltpu.make_async_copy(src, joined.at[i], store_sems.at[i])
            for i, src in enumerate(joined_hbm)
        ]
        for each in joined_loads:
            each.start()
    else:
        meet(ids)
    width = cot_ref.shape[1]
    half = cot_ref.shape[0] // 2
    unit_rows = 2 * half
    total, own, dx1 = (work.at[pl.ds(i * unit_rows, unit_rows)] for i in range(3))
    feed_rows = Gather(feed_sems[0], ids, ebuf)
    feed_sum = Scatter(feed_sems[1], ids, own, feed_bufs)
    attn_rows = Gather(attn_sems[0], ids, fbuf)
    attn_sum = Scatter(attn_sems[1], ids, own, attn_bufs)
    columns = heads * HD
    tiles = width // 256
    top = depth - 1
    packed = is_packed(lengths_ref, 8 * half)
    loads.add("grad", [grad_hbm] * depth, ebuf)
    loads.start(top, "m", "wup", "grad", "wdown", "slope", "x1", "wout", "q", "k", "v", "lse", "g")
    loads.start(top, "wq", "wk", "wv", "a", "x")
    out_loads = []
    out_sends = []
    for layer in range(depth):
        rows = outs[layer][0].at[pl.ds(0, 4 * half)]
        pairs = ((saved_hbm[layer]["o"], rows), (saved_hbm[layer]["o2"], outs[layer][1]))
        out_loads.append(
            [
                pltpu.make_async_copy(src, dst, out_sems.at[layer, 4 + i])
                for i, (src, dst) in enumerate(pairs)
            ]
        )
        out_sends.append(
            [
                pltpu.make_async_remote_copy(
                    src_ref=outs[layer][1].at[pl.ds(part * unit_rows, unit_rows)],
                    dst_ref=outs[layer][0].at[pl.ds((3 - part) * unit_rows, unit_rows)],
                    send_sem=out_sems.at[layer, part],
                    recv_sem=out_sems.at[layer, 2 + part],
                    device_id=ids[1],
                    device_id_type=MESH,
                )
                for part in range(2)
            ]
        )
        for each in out_loads[layer]:
            each.start()

    def send_outs(layer):
        out_loads[layer][1].wait()
        for each in out_sends[layer]:
            each.start()

    send_outs(top)
    dxb[...] = cot_ref[...].astype(F32)
    small_ref[...] = jnp.zeros_like(small_ref)

    def outer(left, right, dst):
        def tile(index, carry):
            place = span(index * 256, 256)
            dst[place, :] = dot(left[:, place], right[...], TN).astype(BF)
            return carry

        lax.fori_loop(0, tiles, tile, 0)

    def turn_back(grad, rows, scale):
        cosine = cos_ref[rows, :]
        sine = sin_ref[rows, :]
        first_half = grad[:, :128]
        second_half = grad[:, 128:]
        return (
            ((first_half * cosine + second_half * sine) * scale).astype(BF),
            ((second_half * cosine - first_half * sine) * scale).astype(BF),
        )

    def event(name, layer, kind):
        if (name, layer) in sums:
            getattr(sums[name, layer], kind)()

    for layer in reversed(range(depth)):
        def note(row, value):
            small_ref[8 * layer + row : 8 * layer + row + 1, :] = value

        note(4, jnp.sum(dxb[...], axis=0, keepdims=True))
        dkb[...] = jnp.zeros_like(dkb)
        dvb[...] = jnp.zeros_like(dvb)
        loads.wait(layer, "m", "wup")

        def expand(step, carry):
            rows = span((3 - step) * unit_rows, unit_rows)
            gated, slope = gelu_parts(dot(mbuf[rows, :], wup[...]))
            gb[rows, :] = gated.astype(BF)
            gpb[rows, :] = slope.astype(BF)
            return carry

        lax.fori_loop(0, 2, expand, 0)
        loads.wait(layer, "wdown", "slope")
        if layer == top:
            loads.wait(layer, "grad")

        def contract(step, carry):
            if layer == top:
                unit = jnp.where(step < 2, 3 - step, step - 2)
            else:
                feed_rows.receive(step)
                unit = jnp.where(step < 2, step, 5 - step)
            rows = span(unit * unit_rows, unit_rows)
            grad = dot(ebuf[rows, :], wdown[...], NT)
            grad = (grad * gpb[rows, :].astype(F32)).astype(BF)
            dhb[rows, :] = grad
            total[...] = dot(grad, wup[...], NT)
            feed_sum.send(unit, total)
            return carry

        lax.fori_loop(0, 4, contract, 0)
        loads.start(layer - 1, "wdown", "slope")
        event("attn", layer + 1, "middle")
        event("up", layer + 1, "end")
        if layer < top:
            attn_rows.finish()
            attn_sum.finish()
        shift_sum = jnp.zeros((1, width), F32)
        scale_sum = jnp.zeros((1, width), F32)
        for part in range(2):
            if part == 0:
                loads.wait(layer, "x1")
                outer(mbuf, dhb, feed_grads.at[0])
                event("up", layer, "start")
            else:
                loads.wait(layer, "g")
                outer(ebuf, gb, feed_grads.at[1])
                event("down", layer, "start")
            rows = pl.ds(part * half, half)
            grad = feed_sum.collect(part)
            hat, rstd = norm(x1b[rows, :])
            shift_sum += jnp.sum(grad, axis=0, keepdims=True)
            scale_sum += jnp.sum(grad * hat, axis=0, keepdims=True)
            after = dxb[rows, :]
            after = after + norm_back(grad * (1.0 + cond_ref[8 * layer : 8 * layer + 1, width:]), hat, rstd)
            dx1[rows, :] = after
            fbuf[attn_rows.own(part), :] = after.astype(BF)
            attn_rows.send(part)
        note(0, shift_sum)
        note(1, scale_sum)
        loads.start(layer - 1, "m", "g", "x1", "wup")
        loads.wait(layer, "wout", "q", "k", "v", "lse")

        def attend(step, carry):
            attn_rows.receive(step)
            if layer:

                @pl.when(step == 3)
                def _():
                    send_outs(layer - 1)

            unit = jnp.where(step < 2, step, 5 - step)
            rows = span(unit * unit_rows, unit_rows)
            grad_out = dot(fbuf[rows, :], wout[...], NT).astype(BF)
            queries = qb[rows, :]
            grad_queries = jnp.zeros((unit_rows, 256), F32)
            chunk = lax.broadcasted_iota(jnp.int32, (8, 1, unit_rows), 0)
            part = lax.broadcasted_iota(jnp.int32, (8, 1, unit_rows), 2) // half
            neg = apart(owner(chunk), unit_owner(unit, part), packed.reshape(1, 1, 1))
            for head in range(heads):
                place = pl.ds(head * unit_rows, unit_rows)
                masked = keep_head(queries, head, True)
                masked_out = keep_head(grad_out, head, False)
                qmask[place, :] = masked
                domask[place, :] = masked_out
                scores = dot(kb[...], masked, NT).reshape(8, half, unit_rows)
                shares = jnp.exp(scores - (lse[unit, head : head + 1, :] - neg))
                shares = shares.reshape(8 * half, unit_rows)
                grad_shares = dot(vb[...], masked_out, NT)
                centre = jnp.sum(shares * grad_shares, axis=0, keepdims=True)
                grad_scores = (shares * (grad_shares - centre)).astype(BF)
                pb[:, place] = shares.astype(BF)
                dsb[:, place] = grad_scores
                grad_queries = grad_queries + dot(grad_scores, keep_head(kb[...], head, True), TN)
            dkb[...] += dot(dsb[...], qmask[...])
            dvb[...] += dot(pb[...], domask[...])
            low, high = turn_back(grad_queries, rows, HD**-0.5)
            dqk[rows, :128] = low
            dqk[rows, 128:256] = high
            return carry

        lax.fori_loop(0, 4, attend, 0)
        loads.start(layer - 1, "wout", "q", "k", "v", "lse")
        event("down", layer + 1, "end")
        event("attn", layer + 1, "end")
        event("up", layer, "middle")
        loads.wait(layer, "wq", "wk", "wv")
        load_turned(wq, wk, wqk)

        def spread(step, carry):
            unit = jnp.where(step < 2, 3 - step, step - 2)
            rows = span(unit * unit_rows, unit_rows)
            low, high = turn_back(dkb[rows, :], rows, 1.0)
            dqk[rows, 256:384] = low
            dqk[rows, 384:512] = high
            values = dvb[rows, :].astype(BF)
            dvv[rows, :] = values
            total[...] = dot(dqk[rows, :], wqk[...]) + dot(values, wv[...])
            attn_sum.send(unit, total)
            return carry

        lax.fori_loop(0, 4, spread, 0)
        loads.start(layer - 1, "wq", "wk", "wv")
        if layer:
            event("down", layer, "middle")
        loads.wait(layer, "a")
        out_loads[layer][0].wait()
        for each in out_sends[layer]:
            each.wait()
        ob = outs[layer][0]
        places = (
            turned_place(columns, 0, 4 * columns),
            turned_place(columns, columns, 4 * columns),
            plain_place(columns, 2 * columns, 4 * columns),
            plain_place(columns, 3 * columns, 4 * columns),
        )

        def attn_tile(index, carry):
            place = span(index * 256, 256)
            normed = abuf[:, place]
            both = dot(normed, dqk[...], TN).astype(BF)
            made = dot(both[:, :256], places[0]) + dot(both[:, 256:], places[1])
            made = made + dot(dot(normed, dvv[...], TN).astype(BF), places[2])
            outs = dot(fbuf[:, place], ob[...], TN).astype(BF)
            attn_grads[place, :] = (made + dot(outs, places[3])).astype(BF)
            return carry

        lax.fori_loop(0, tiles, attn_tile, 0)
        loads.start(layer - 1, "a")
        if layer:
            event("attn", layer, "start")
        if not deep:
            stores = [
                pltpu.make_async_copy(attn_grads, attn_outs[layer], store_sems.at[0]),
                pltpu.make_async_copy(feed_grads, feed_outs[layer], store_sems.at[1]),
            ]
            for each in stores:
                each.start()
            for each in stores:
                each.wait()
        if layer < top:
            feed_rows.finish()
        feed_sum.finish()
        loads.wait(layer, "x")
        gain_sum = jnp.zeros((1, width), F32)
        bias_sum = jnp.zeros((1, width), F32)
        for part in range(2):
            rows = pl.ds(part * half, half)
            grad = attn_sum.collect(part)
            hat, rstd = norm(xb[rows, :])
            gain_sum += jnp.sum(grad * hat, axis=0, keepdims=True)
            bias_sum += jnp.sum(grad, axis=0, keepdims=True)
            made = dx1[rows, :] + norm_back(
                grad * gain_ref[layer : layer + 1, :], hat, rstd
            )
            dxb[rows, :] = made
            if layer:
                ebuf[feed_rows.own(part), :] = made.astype(BF)
                feed_rows.send(part)
        note(2, gain_sum)
        note(3, bias_sum)
        loads.start(layer - 1, "x")
    out_ref[...] = dxb[...]
    if deep:
        for each in joined_loads:
            each.wait()
        tail(deep, spot, ids, sums, dxb, small_ref, temb_ref, work, dsb, tail_refs,
             sum_ref, vec_ref, store_sems)
    attn_rows.finish()
    attn_sum.finish()


def tail(deep, spot, ids, sums, dxb, small_ref, temb_ref, work, dsb, scratch, sum_ref, vec_ref,
         store_sems):
    (joined, ebuf, jbuf, near_in, next_in, z_in, result, vecs, send, recv) = scratch
    sibling, far = ids
    place = lax.axis_index("tensor")
    core = lax.rem(place, 2)
    y = place // 2
    x, z = spot.x, spot.z
    width = dxb.shape[1]
    ladder = Ladder((send, recv))
    ebuf[0] = dxb[...].astype(BF)
    rows_copy = ladder.copy(ebuf.at[0], ebuf.at[1], sibling)
    joined_copy = ladder.copy(joined.at[1 - core], jbuf, sibling)
    mine = vecs.at[core, y, x, z]
    row = lax.broadcasted_iota(jnp.int32, small_ref.shape, 0)
    mine[...] = jnp.where(row == 5, temb_ref[0:1, :], small_ref[...]).astype(BF)
    vec_z = [ladder.copy(mine, mine, spot.along(ahead)) for ahead in range(1, deep)]
    rows_copy.wait_recv()
    joined_copy.wait_recv()
    rest = width // 2

    def tile(index, carry):
        rows = span(index * 256, 256)
        made = dot(joined[core, :, rows], ebuf[0], TN)
        work[rows, :] = made + dot(jbuf[:, rows], ebuf[1], TN)
        return carry

    lax.fori_loop(0, width // 256, tile, 0)
    half, quarter = width // 2, width // 4
    piece = quarter // deep
    ways = (((far, y), (spot.across, x)), ((spot.across, x), (far, y)))
    lanes = (pl.ds(0, rest), pl.ds(rest, rest))
    firsts = []
    for side, ((device, bit), _) in enumerate(ways):
        out = dsb.at[pl.ds(0, half), lanes[side]]
        out[...] = work[span((1 - bit) * half, half), lanes[side]].astype(BF)
        firsts.append(ladder.copy(out, near_in.at[side], device))
    sums["down", 0].middle()
    for each in vec_z:
        each.wait_recv()
    row_z = vecs.at[core, y, x]
    vec_x = ladder.copy(row_z, row_z, spot.across)
    seconds = []
    for side, ((_, bit), (device, bit2)) in enumerate(ways):
        firsts[side].wait_recv()
        kept = work.at[span(bit * half, half), lanes[side]]
        kept[...] = kept[...] + near_in[side].astype(F32)
        out = dsb.at[pl.ds(half, quarter), lanes[side]]
        out[...] = work[span(bit * half + (1 - bit2) * quarter, quarter), lanes[side]].astype(BF)
        seconds.append(ladder.copy(out, next_in.at[side], device))
    sums["attn", 0].start()
    vec_x.wait_recv()
    plane = vecs.at[core, y]
    vec_y = ladder.copy(plane, plane, far)
    thirds = []
    for side, ((_, bit), (_, bit2)) in enumerate(ways):
        seconds[side].wait_recv()
        kept = work.at[span(bit * half + bit2 * quarter, quarter), lanes[side]]
        kept[...] = kept[...] + next_in[side].astype(F32)
        out = dsb.at[pl.ds(half + quarter, quarter), lanes[side]]
        out[...] = kept[...].astype(BF)
        for ahead in range(1, deep):
            start = half + quarter + spot.level(ahead) * piece
            thirds.append(
                ladder.copy(
                    dsb.at[span(start, piece), lanes[side]],
                    z_in.at[side, ahead - 1],
                    spot.along(ahead),
                )
            )
    sums["up", 0].end()
    sums["down", 0].end()
    vec_y.wait_recv()
    every = vecs.at[core]
    vec_core = ladder.copy(every, every, sibling)
    lasts = []
    for side, ((_, bit), (_, bit2)) in enumerate(ways):
        for ahead in range(1, deep):
            thirds[side * (deep - 1) + ahead - 1].wait_recv()
        start = bit * half + bit2 * quarter + z * piece
        made = work[span(start, piece), lanes[side]]
        for ahead in range(1, deep):
            made = made + z_in[side, ahead - 1].astype(F32)
        own = result.at[core, side, span(start, piece)]
        own[...] = made.astype(BF)
        lasts += [ladder.copy(own, own, spot.along(ahead)) for ahead in range(1, deep)]
    backs = []
    for side, ((_, bit), (device, bit2)) in enumerate(ways):
        for ahead in range(1, deep):
            lasts[side * (deep - 1) + ahead - 1].wait_recv()
        own = result.at[core, side, span(bit * half + bit2 * quarter, quarter)]
        backs.append(ladder.copy(own, own, device))
    sums["attn", 0].middle()
    ends = []
    for side, ((device, bit), _) in enumerate(ways):
        backs[side].wait_recv()
        own = result.at[core, side, span(bit * half, half)]
        ends.append(ladder.copy(own, own, device))
    sums["attn", 0].end()
    vec_core.wait_recv()
    vec_store = pltpu.make_async_copy(vecs, vec_ref, store_sems.at[0])
    vec_store.start()
    for each in ends:
        each.wait_recv()
    whole = ladder.copy(result.at[core], result.at[core], sibling)
    whole.wait_recv()
    sum_store = pltpu.make_async_copy(result, sum_ref, store_sems.at[1])
    sum_store.start()
    ladder.finish()
    vec_store.wait()
    sum_store.wait()


def backward(heads, deep, cotangent, grad_all, gains, lengths, tables, weights, kept, joined):
    depth = len(kept)
    block, width = cotangent.shape
    length = 4 * block
    units = weights[2].shape[2]
    columns = heads * HD
    part = width // (2 * deep) if deep else width
    half, quarter = width // 2, width // 4
    held = [[each[name] for name in SAVED] for each in kept]
    scratch = [pltpu.SemaphoreType.DMA((3, 2))] * 8
    scratch += [pltpu.SemaphoreType.DMA((7 + len(SAVED),)), pltpu.SemaphoreType.DMA((2,))]
    scratch += [pltpu.SemaphoreType.DMA((depth, 6))]
    scratch += [pltpu.VMEM((columns, width), BF)] * 3
    scratch += [pltpu.VMEM(each.shape[1:], BF) for each in weights[1:4]]
    for name, each in zip(SAVED, held[0]):
        shape = (length, units) if name in ("g", "slope") else each.shape
        scratch.append(pltpu.VMEM((16, 128) if name in ("o", "o2") else shape, each.dtype))
    scratch += [pltpu.VMEM((length, columns), BF), pltpu.VMEM((length // 2, columns), BF)] * depth
    scratch += [pltpu.VMEM((length, width), BF)] * 2
    scratch += scatter_scratch(length, width) + scatter_scratch(length, width)
    scratch += [
        pltpu.VMEM((512, width), BF),
        pltpu.VMEM((length, units), BF),
        pltpu.VMEM((heads * block, 256), BF),
        pltpu.VMEM((heads * block, columns), BF),
        pltpu.VMEM((length, heads * block), BF),
        pltpu.VMEM((length, heads * block), BF),
        pltpu.VMEM((length, 256), F32),
        pltpu.VMEM((length, columns), F32),
        pltpu.VMEM((length, 512), BF),
        pltpu.VMEM((length, columns), BF),
        pltpu.VMEM((3 * block, width), F32),
        pltpu.VMEM((block, width), F32),
        pltpu.VMEM((2, width, units), BF),
        pltpu.VMEM((width, 4 * columns), BF),
    ]
    out_shape = [
        jax.ShapeDtypeStruct((block, width), F32),
        jax.ShapeDtypeStruct((8 * depth, width), F32),
    ]
    kind = F32 if deep else BF
    out_shape += [jax.ShapeDtypeStruct((part, 4 * columns), kind)] * depth
    out_shape += [jax.ShapeDtypeStruct((2, part, units), kind)] * depth
    out_specs = [vmem_spec()] * 2 + [vmem_spec() if deep else any_spec()] * (2 * depth)
    if deep:
        for _ in range(depth):
            scratch += DpSum.scratch(deep, part, units) + DpSum.scratch(deep, part, units)
            scratch += DpSum.scratch(deep, part, 4 * columns)
        vec_shape = (2, 2, 2, deep, 8 * depth, width)
        scratch += [
            pltpu.VMEM((2, block, width), BF),
            pltpu.VMEM((2, block, width), BF),
            pltpu.VMEM((block, width), BF),
            pltpu.VMEM((2, half, half), BF),
            pltpu.VMEM((2, quarter, half), BF),
            pltpu.VMEM((2, deep - 1, quarter // deep, half), BF),
            pltpu.VMEM((2, 2, width, half), BF),
            pltpu.VMEM(vec_shape, BF),
            pltpu.SemaphoreType.DMA((LADDER_COPIES,)),
            pltpu.SemaphoreType.DMA((LADDER_COPIES,)),
        ]
        out_shape += [
            jax.ShapeDtypeStruct((2, 2, width, half), BF),
            jax.ShapeDtypeStruct(vec_shape, BF),
        ]
        out_specs += [any_spec(), any_spec()]

    def kernel(*refs):
        backward_kernel(depth, heads, deep, refs)

    operands = [cotangent, gains, lengths, *tables]
    in_specs = [vmem_spec()] * len(operands)
    remote = [*joined, grad_all, *weights, *[each for layer in held for each in layer]]
    in_specs += [any_spec()] * len(remote)
    return pl.pallas_call(
        kernel,
        out_shape=out_shape,
        in_specs=in_specs,
        out_specs=out_specs,
        scratch_shapes=scratch,
        compiler_params=pltpu.CompilerParams(
            collective_id=9, has_side_effects=True, vmem_limit_bytes=LIMIT
        ),
        name="layers_backward",
    )(*operands, *remote)


def finish_kernel(depth, refs):
    (low_ref, wself_ref, sum_ref, vec_ref) = refs[:4]
    attn_refs = refs[4 : 4 + depth]
    feed_refs = refs[4 + depth : 4 + 2 * depth]
    (tokens_ref, gain_ref, bias_ref, bada_ref, bdown_ref) = refs[4 + 2 * depth : 9 + 2 * depth]
    (qkv_ref, out_ref, ada_ref, up_ref, down_ref, self_ref, picked) = refs[9 + 2 * depth :]
    step = pl.program_id(0)
    members = vec_ref.shape[0] // (8 * depth)
    width = vec_ref.shape[1]

    def pick(row):
        device = lax.broadcasted_iota(jnp.int32, (members, vec_ref.shape[0]), 0)
        column = lax.broadcasted_iota(jnp.int32, (members, vec_ref.shape[0]), 1)
        wanted = (column == device * 8 * depth + row).astype(F32).astype(BF)
        return dot(wanted, vec_ref[...]).astype(BF)

    rows = ada_ref.shape[1]

    @pl.when(step == 0)
    def _():
        picked[2 * depth] = pick(5)
        for layer in range(depth):
            for place in range(2):
                picked[2 * layer + place] = pick(8 * layer + place)

    device = lax.broadcasted_iota(jnp.int32, (width, rows), 0)
    column = lax.broadcasted_iota(jnp.int32, (width, rows), 1)
    chosen = (device == column + step * rows).astype(F32).astype(BF)
    times = dot(picked[2 * depth], chosen).astype(BF)
    for layer in range(depth):
        for place in range(2):
            ada_ref[layer, :, place * width : (place + 1) * width] = dot(
                times, picked[2 * layer + place], TN
            )
    self_ref[:, : width // 2] = sum_ref[0].astype(F32)
    self_ref[:, width // 2 :] = sum_ref[1].astype(F32)

    @pl.when(step == 0)
    def _():
        row = lax.broadcasted_iota(jnp.int32, (8 * depth, vec_ref.shape[0]), 0)
        column = lax.broadcasted_iota(jnp.int32, (8 * depth, vec_ref.shape[0]), 1)
        ones = (column % (8 * depth) == row).astype(F32).astype(BF)
        totals = dot(ones, vec_ref[...])
        for layer in range(depth):
            here = slice(layer, layer + 1)
            base = 8 * layer
            bada_ref[here, :width] = totals[base : base + 1]
            bada_ref[here, width:] = totals[base + 1 : base + 2]
            gain_ref[here, :] = totals[base + 2 : base + 3]
            bias_ref[here, :] = totals[base + 3 : base + 4]
            bdown_ref[here, :] = totals[base + 4 : base + 5]

    @pl.when(step == 1)
    def _():
        tokens_ref[...] = dot(low_ref[...].astype(BF), wself_ref[...], NT)

    @pl.when(step == 2)
    def _():
        for layer in range(depth):
            grads = attn_refs[layer][...]
            columns = grads.shape[1] // 4
            for place in range(3):
                qkv_ref[layer, place] = grads[:, place * columns : (place + 1) * columns]
            out_ref[layer] = grads[:, 3 * columns :].T

    @pl.when(step == 3)
    def _():
        for layer in range(depth):
            up_ref[layer] = feed_refs[layer][0]
            down_ref[layer] = feed_refs[layer][1]


def finish(depth, low, w_self, sums, vectors, attn_shards, feed_shards):
    block, width = low.shape
    part, columns = attn_shards[0].shape
    columns //= 4
    units = feed_shards[0].shape[2]
    steps = 4
    rows = 2 * width // steps

    def fixed(*shape):
        return pl.BlockSpec(shape, lambda step: (0,) * len(shape))

    def kernel(*refs):
        finish_kernel(depth, refs)

    fixed_shapes = [
        (block, width),
        (depth, width),
        (depth, width),
        (depth, 2 * width),
        (depth, width),
        (depth, 3, part, columns),
        (depth, columns, part),
    ]
    shard = (depth, part, units)
    return pl.pallas_call(
        kernel,
        grid=(steps,),
        out_shape=[
            *[jax.ShapeDtypeStruct(each, F32) for each in fixed_shapes],
            jax.ShapeDtypeStruct((depth, width, 2 * width), F32),
            jax.ShapeDtypeStruct(shard, F32),
            jax.ShapeDtypeStruct(shard, F32),
            jax.ShapeDtypeStruct((2 * width, width), F32),
        ],
        in_specs=[
            fixed(block, width),
            fixed(width, width),
            pl.BlockSpec((None, 2, rows, width // 2), lambda step: (step // 2, 0, step % 2, 0)),
            fixed(*vectors.shape),
            *[fixed(*each.shape) for each in attn_shards],
            *[fixed(*each.shape) for each in feed_shards],
        ],
        out_specs=[
            *[fixed(*each) for each in fixed_shapes],
            pl.BlockSpec((depth, width // steps, 2 * width), lambda step: (0, step, 0)),
            fixed(*shard),
            fixed(*shard),
            pl.BlockSpec((rows, width), lambda step: (step, 0)),
        ],
        scratch_shapes=[
            pltpu.VMEM((2 * depth + 1, vectors.shape[0] // (8 * depth), width), BF)
        ],
        compiler_params=pltpu.CompilerParams(vmem_limit_bytes=LIMIT),
        name="write_grads",
    )(low, w_self, sums, vectors, *attn_shards, *feed_shards)


def local(
    tokens,
    cotangent,
    lengths,
    timesteps,
    w_self,
    ln_gain,
    ln_bias,
    w_qkv,
    w_out,
    w_ada,
    b_ada,
    w_up,
    w_down,
    b_down,
):
    width = tokens.shape[1]
    depth = w_qkv.shape[0]
    heads = w_qkv.shape[3] // HD
    deep = 4 if lax.axis_size("dp") == 8 else 0
    weights = (jnp.swapaxes(w_qkv, 2, 3), w_out, w_up, w_down, w_ada)
    vectors = (ln_gain, ln_bias, b_down, b_ada, lengths, timesteps)
    made, kept = forward(heads, tokens, cotangent, w_self, vectors, weights)
    (activations, estimate, conds, cosine, sine, temb, grad_all) = made
    made = backward(
        heads,
        deep,
        cotangent,
        grad_all,
        ln_gain,
        lengths,
        (cosine, sine, temb, conds),
        weights,
        kept,
        (tokens, estimate),
    )
    grad_rows, smalls = made[:2]
    attn_shards = made[2 : 2 + depth]
    feed_shards = made[2 + depth : 2 + 2 * depth]
    if deep:
        sums, vectors = made[2 + 2 * depth :]
        vectors = vectors.reshape(-1, width)
    else:
        attn_shards = [
            lax.psum_scatter(each, "dp", scatter_dimension=0, tiled=True).astype(F32)
            for each in attn_shards
        ]
        feed_shards = [
            lax.psum_scatter(each, "dp", scatter_dimension=1, tiled=True).astype(F32)
            for each in feed_shards
        ]
        joined = jnp.concatenate([tokens, estimate], axis=1)
        sums = lax.psum(dot(joined, grad_rows.astype(BF), TN).astype(BF), ("dp", "tensor"))
        sums = sums.reshape(2, width, 2, width // 2).swapaxes(1, 2)
        vectors = smalls.at[5].set(temb[0]).astype(BF)
        vectors = lax.all_gather(vectors, ("dp", "tensor"), axis=0, tiled=True)
    made = finish(depth, grad_rows, w_self, sums, vectors, attn_shards, feed_shards)
    (grad_tokens, gain, bias, bias_ada, bias_down, qkv, out, ada, up, down, own) = made
    return (
        activations,
        grad_tokens,
        gain,
        bias,
        qkv,
        out,
        ada,
        bias_ada,
        up,
        jnp.swapaxes(down, 1, 2),
        bias_down,
        own,
    )


def solution(mesh):
    return jax.shard_map(
        local,
        mesh=mesh,
        in_specs=(
            P(("dp", "tensor"), None),
            P(("dp", "tensor"), None),
            P("dp", None),
            P("dp", None),
            P(),
            P(),
            P(),
            P(None, None, None, "tensor"),
            P(None, "tensor", None),
            P(),
            P(),
            P(None, None, "tensor"),
            P(None, "tensor", None),
            P(),
        ),
        out_specs=(
            P(("dp", "tensor"), None),
            P(("dp", "tensor"), None),
            P(),
            P(),
            P(None, None, "dp", "tensor"),
            P(None, "tensor", "dp"),
            P(),
            P(),
            P(None, "dp", "tensor"),
            P(None, "tensor", "dp"),
            P(),
            P(),
        ),
        check_vma=False,
    )
```

```python
import functools

import jax
import jax.numpy as jnp
from jax import lax
from jax.experimental import pallas as pl
from jax.experimental.pallas import tpu as pltpu
from jax.sharding import PartitionSpec as P

HD = 64
HALF = HD // 2
BF = jnp.bfloat16
F32 = jnp.float32
MESH = pl.DeviceIdType.MESH
EPS = 1e-05
LIMIT = 60 << 20

def norm(rows):
    centred = rows - jnp.mean(rows, axis=-1, keepdims=True)
    rstd = lax.rsqrt(jnp.mean(centred * centred, axis=-1, keepdims=True) + EPS)
    return (centred * rstd, rstd)


def norm_back(grad, hat, rstd):
    return rstd * (
        grad
        - jnp.mean(grad, axis=-1, keepdims=True)
        - hat * jnp.mean(grad * hat, axis=-1, keepdims=True)
    )


def dot(left, right, dims=((1,), (0,))):
    return lax.dot_general(left, right, (dims, ((), ())), preferred_element_type=F32)


NT = ((1,), (1,))
TN = ((0,), (0,))


def head_mask(head, columns, rotary):
    lane = lax.broadcasted_iota(jnp.int32, (1, columns), 1)
    if rotary:
        return (lane % 128) // HALF == head
    return lane // HD == head


def keep_head(rows, head, rotary):
    return jnp.where(head_mask(head, rows.shape[1], rotary), rows, jnp.zeros_like(rows))


def turned_place(columns, start, total):
    row = lax.broadcasted_iota(jnp.int32, (256, total), 0)
    column = lax.broadcasted_iota(jnp.int32, (256, total), 1) - start
    source = column // HD * HALF + column % HD // HALF * 128 + column % HALF
    fits = (source == row) & (column >= 0) & (column < columns)
    return fits.astype(F32).astype(BF)


def plain_place(columns, start, total):
    row = lax.broadcasted_iota(jnp.int32, (columns, total), 0)
    column = lax.broadcasted_iota(jnp.int32, (columns, total), 1) - start
    return (row == column).astype(F32).astype(BF)


def span(start, size):
    return pl.ds(pl.multiple_of(start, size), size)


class Gather:
    def __init__(self, sems, ids, rows):
        self.sems, self.ids, self.rows = sems, ids, rows
        self.half = rows.shape[0] // 8

    def copy(self, src, dst, kind, part, far):
        send, recv = self.sems
        return pltpu.make_async_remote_copy(
            src_ref=self.rows.at[span(src, self.half)],
            dst_ref=self.rows.at[span(dst, self.half)],
            send_sem=send.at[kind, part],
            recv_sem=recv.at[kind, part],
            device_id=self.ids[1] if far else self.ids[0],
            device_id_type=MESH,
        )

    def own(self, part):
        return span(2 * self.half * part, self.half)

    def pair(self, part):
        return 6 * self.half - 2 * self.half * part

    def far_copy(self, part):
        return self.copy(2 * self.half * part, self.pair(part), 0, part, True)

    def sibling_copy(self, part):
        start = 2 * self.half * part
        return self.copy(start, start + self.half, 1, part, False)

    def forward_copy(self, part):
        return self.copy(self.pair(part), self.pair(part) + self.half, 2, part, False)

    def send(self, part):
        self.far_copy(part).start()
        self.sibling_copy(part).start()

    def near(self, part):
        self.sibling_copy(part).wait_recv()

    def arrive(self, part):
        self.far_copy(part).wait_recv()
        self.forward_copy(part).start()

    def settle(self, part):
        self.forward_copy(part).wait()

    def far(self, part):
        self.arrive(part)
        self.settle(part)

    def receive(self, step):
        @pl.when(step < 2)
        def _():
            self.near(step)

        @pl.when(step >= 2)
        def _():
            self.far(step - 2)

    def finish(self, far=True):
        for part in range(2):
            self.sibling_copy(part).wait_send()
            if far:
                self.far_copy(part).wait_send()


class Scatter:
    def __init__(self, sems, ids, own, buffers):
        self.sems, self.ids, self.own_sum = sems, ids, own
        self.pair_out, self.pair_in, self.own_out, self.own_in, self.far_out, self.far_in = buffers
        self.half = self.pair_out.shape[1]

    def copy(self, src, dst, kind, part, far):
        send, recv = self.sems
        return pltpu.make_async_remote_copy(
            src_ref=src.at[part],
            dst_ref=dst.at[part],
            send_sem=send.at[kind, part],
            recv_sem=recv.at[kind, part],
            device_id=self.ids[1] if far else self.ids[0],
            device_id_type=MESH,
        )

    def pair_copy(self, part):
        return self.copy(self.pair_out, self.pair_in, 0, part, False)

    def own_copy(self, part):
        return self.copy(self.own_out, self.own_in, 1, part, False)

    def sum_copy(self, part):
        return self.copy(self.far_out, self.far_in, 2, part, True)

    def send(self, unit, total):
        @pl.when(unit < 2)
        def _():
            self.own_sum[span(self.half * unit, self.half), :] = total[: self.half, :]
            self.own_out[unit] = total[self.half :, :].astype(BF)
            self.own_copy(unit).start()

        @pl.when(unit >= 2)
        def _():
            part = 3 - unit
            self.pair_out[part] = total[self.half :, :].astype(BF)
            self.pair_copy(part).start()
            self.pair_copy(part).wait_recv()
            self.far_out[part] = (
                total[: self.half, :] + self.pair_in[part].astype(F32)
            ).astype(BF)
            self.sum_copy(part).start()

    def collect(self, part):
        self.own_copy(part).wait_recv()
        self.sum_copy(part).wait_recv()
        rows = pl.ds(part * self.half, self.half)
        made = self.own_sum[rows, :] + self.own_in[part].astype(F32)
        return made + self.far_in[part].astype(F32)

    def finish(self):
        for part in range(2):
            self.pair_copy(part).wait_send()
            self.own_copy(part).wait_send()
            self.sum_copy(part).wait_send()


class Near:
    def __init__(self, sems, ids, own, out, into):
        self.sems, self.ids = sems, ids
        self.own, self.out, self.into = own, out, into
        self.half = out.shape[1]

    def copy(self, part):
        return pltpu.make_async_remote_copy(
            src_ref=self.out.at[part],
            dst_ref=self.into.at[part],
            send_sem=self.sems.at[0, part],
            recv_sem=self.sems.at[1, part],
            device_id=self.ids[0],
            device_id_type=MESH,
        )

    def send(self, part, total):
        self.own[span(self.half * part, self.half), :] = total[: self.half, :]
        self.out[part] = total[self.half :, :].astype(BF)
        self.copy(part).start()

    def collect(self, part):
        self.copy(part).wait_recv()
        return self.own[pl.ds(part * self.half, self.half), :] + self.into[part].astype(F32)

    def drain(self):
        for part in range(2):
            self.copy(part).wait_send()


class Fetch:
    def __init__(self, sems, ids, square, shards):
        self.sems, self.shards = sems, shards
        self.far = ids[1]
        self.x, self.z, self.x_peer, self.z_peer = square
        self.piece = shards.shape[1] // 8

    def copy(self, index, src, start, size, device):
        place = span(start * self.piece, size * self.piece)
        return pltpu.make_async_remote_copy(
            src_ref=self.shards.at[src, place],
            dst_ref=self.shards.at[1, place],
            send_sem=self.sems.at[0, index],
            recv_sem=self.sems.at[1, index],
            device_id=device,
            device_id_type=MESH,
        )

    def hop(self, index):
        x_first = 2 * self.z + self.x
        z_first = 4 + 2 * self.x + self.z
        return (
            lambda: self.copy(0, 0, x_first, 1, self.far),
            lambda: self.copy(1, 0, z_first, 1, self.far),
            lambda: self.copy(2, 1, x_first, 1, self.x_peer),
            lambda: self.copy(3, 1, z_first, 1, self.z_peer),
            lambda: self.copy(4, 1, 2 * self.z, 2, self.z_peer),
            lambda: self.copy(5, 1, 4 + 2 * self.x, 2, self.x_peer),
        )[index]()

    def step(self, count):
        if count == 1:
            self.hop(0).start()
            self.hop(1).start()
        elif count < 4:
            for index in (2 * count - 4, 2 * count - 3):
                self.hop(index).wait_recv()
                self.hop(index + 2).start()
        else:
            self.hop(4).wait_recv()
            self.hop(5).wait_recv()

    def finish(self):
        for index in range(6):
            self.hop(index).wait_send()


def square():
    group = lax.axis_index("dp")
    place = lax.axis_index("tensor")
    x = lax.rem(group, 2)
    z = lax.rem(group // 2, 2)
    return (x, z, (group + 1 - 2 * x, place), (group + 2 - 4 * z, place))


def neighbours():
    group = lax.axis_index("dp")
    place = lax.axis_index("tensor")
    core = lax.rem(place, 2)
    return ((group, place + 1 - 2 * core), (group, lax.rem(place + 2, 4)))


class Spot:
    def __init__(self, deep):
        group = lax.axis_index("dp")
        self.place = lax.axis_index("tensor")
        self.deep = deep
        self.z = group // 2
        self.x = lax.rem(group, 2)
        self.across = (2 * self.z + 1 - self.x, self.place)

    def level(self, ahead):
        return lax.rem(self.z + ahead, self.deep)

    def along(self, ahead):
        return (2 * self.level(ahead) + self.x, self.place)

    def partners(self):
        return [self.across] + [self.along(ahead) for ahead in range(1, self.deep)]


def meet(ids):
    barrier = pltpu.get_barrier_semaphore()
    for device in ids:
        pl.semaphore_signal(barrier, inc=1, device_id=device, device_id_type=MESH)
    pl.semaphore_wait(barrier, len(ids))


class DpSum:
    def __init__(self, spot, src, out, scratch):
        self.spot, self.src, self.out = spot, src, out
        self.pairs, self.rest, self.sems = scratch
        self.block = self.pairs.shape[1]

    @staticmethod
    def scratch(deep, block, columns):
        return [
            pltpu.VMEM((deep, block, columns), BF),
            pltpu.VMEM((deep - 1, block, columns), BF),
            pltpu.SemaphoreType.DMA((4, deep)),
        ]

    def rows(self, ahead, x):
        start = (2 * self.spot.level(ahead) + x) * self.block
        return pl.ds(pl.multiple_of(start, self.block), self.block)

    def x_copy(self, ahead):
        return pltpu.make_async_remote_copy(
            src_ref=self.src.at[self.rows(ahead, 1 - self.spot.x)],
            dst_ref=self.pairs.at[ahead],
            send_sem=self.sems.at[0, ahead],
            recv_sem=self.sems.at[1, ahead],
            device_id=self.spot.across,
            device_id_type=MESH,
        )

    def z_copy(self, ahead):
        return pltpu.make_async_remote_copy(
            src_ref=self.pairs.at[ahead],
            dst_ref=self.rest.at[ahead - 1],
            send_sem=self.sems.at[2, ahead],
            recv_sem=self.sems.at[3, ahead],
            device_id=self.spot.along(ahead),
            device_id_type=MESH,
        )

    def order(self):
        return [*range(1, self.spot.deep), 0]

    def start(self):
        for ahead in self.order():
            self.x_copy(ahead).start()

    def middle(self):
        for ahead in self.order():
            self.x_copy(ahead).wait_recv()
            total = self.src[self.rows(ahead, self.spot.x), :].astype(F32)
            total = total + self.pairs[ahead].astype(F32)
            if ahead:
                self.pairs[ahead] = total.astype(BF)
                self.z_copy(ahead).start()
            else:
                self.out[...] = total
        for ahead in self.order():
            self.x_copy(ahead).wait_send()

    def end(self):
        for ahead in range(1, self.spot.deep):
            self.z_copy(ahead).wait_recv()
        total = self.out[...]
        for ahead in range(1, self.spot.deep):
            total = total + self.rest[ahead - 1].astype(F32)
        self.out[...] = total
        for ahead in range(1, self.spot.deep):
            self.z_copy(ahead).wait_send()


def scatter_scratch(rows, width):
    return [pltpu.VMEM((2, rows // 8, width), BF)] * 6


def gelu_parts(hidden):
    cdf = 0.5 * (1.0 + lax.erf(hidden * (0.5**0.5)))
    density = jnp.exp(hidden * hidden * -0.5) * 0.3989422804014327
    return (hidden * cdf, cdf + hidden * density)


def load_turned(wq, wk, wqk):
    turn = turned_place(wq.shape[0], 0, wq.shape[0])
    wqk[:256, :] = dot(turn, wq[...]).astype(BF)
    wqk[256:, :] = dot(turn, wk[...]).astype(BF)


def is_packed(lengths_ref, length):
    return (lengths_ref[:, 0:1] < length).astype(jnp.int32).astype(F32)


def owner(chunk):
    return 2 * (chunk // 4) + chunk % 2


def apart(keys, queries, packed):
    return (keys != queries).astype(jnp.int32).astype(F32) * (packed * -1e9)


def unit_owner(unit, half):
    return jnp.where(unit < 2, 0, 2) + half


SAVED = ("a", "q", "k", "v", "o", "o2", "x1", "m", "g", "slope", "x", "lse")


def forward_kernel(depth, heads, refs):
    refs = list(refs)

    def take(count):
        made = refs[:count]
        del refs[:count]
        return made

    (gain_ref, bias_ref, bdown_ref, bada_ref, lengths_ref, steps_ref) = take(6)
    (rotary_ref, time_ref, cot_ref) = take(3)
    (tokens_hbm, wself_hbm, wqkv_hbm, wout_hbm, wup_hbm, wdown_hbm, wada_hbm) = take(7)
    (acts_ref, est_ref, cond_ref, cos_ref, sin_ref, temb_ref, grad_hbm) = take(7)
    saved_hbm = [dict(zip(SAVED, take(len(SAVED)))) for _ in range(depth)]
    gather_sems = [take(2) for _ in range(5)]
    (near_a_sems, near_f_sems, fetch_sems, cross_send, cross_recv) = take(5)
    (load_sems, store_sems) = take(2)
    (tokens, wself, wada) = take(3)
    wa, wu, wd, wqk = take(depth), take(depth), take(depth), take(depth)
    abufs, mbufs, (ebuf,) = take(2), take(2), take(1)
    (q2, k2, v2, ob2, lse2, accs, stats, gb, gpb) = take(9)
    (x1, xb, start, own_a, own_f, sums) = take(6)
    near_a_bufs, near_f_bufs = take(2), take(2)
    ids = neighbours()
    corner = square()
    columns = heads * HD
    width = xb.shape[1]
    half = xb.shape[0] // 2
    unit_rows = 2 * half
    length = 8 * half
    part_a = [pl.ds(part * columns, columns) for part in range(4)]
    sources = [tokens_hbm, wself_hbm.at[0], wself_hbm.at[1]]
    places = [tokens, wself.at[0], wself.at[1]]
    for layer in range(depth):
        sources += [wqkv_hbm.at[layer, part] for part in range(3)] + [wout_hbm.at[layer]]
        places += [wa[layer].at[0, rows] for rows in part_a]
        sources += [wup_hbm.at[layer], wdown_hbm.at[layer]]
        places += [wu[layer].at[0], wd[layer].at[0]]
    loads = [
        pltpu.make_async_copy(src, dst, load_sems.at[i])
        for i, (src, dst) in enumerate(zip(sources, places))
    ]
    ada_loads = [
        pltpu.make_async_copy(wada_hbm.at[layer], wada, load_sems.at[len(loads)])
        for layer in range(depth)
    ]
    order = [0, 1, *range(3, 9)]
    for i in order:
        loads[i].start()
    ada_loads[0].start()
    for i in range(len(loads)):
        if i not in order:
            loads[i].start()
    meet([*ids, *corner[2:]])
    fetches = []
    for layer in range(depth):
        for shards in (wa[layer], wu[layer], wd[layer]):
            fetches.append(Fetch(fetch_sems.at[len(fetches)], ids, corner, shards))
    gathers = [Gather(gather_sems[i], ids, abufs[i]) for i in range(2)]
    mixes = [Gather(gather_sems[2 + i], ids, mbufs[i]) for i in range(2)]
    grads = Gather(gather_sems[4], ids, ebuf)
    near_a = Near(near_a_sems, ids, own_a, *near_a_bufs)
    near_f = Near(near_f_sems, ids, own_f, *near_f_bufs)
    packed = is_packed(lengths_ref, length)
    pending = []

    def store(name, src, dst):
        made = pltpu.make_async_copy(src, dst, store_sems.at[len(pending)])
        made.start()
        pending.append([name, made, False])

    def stored(*names):
        for each in pending:
            if each[0] in names and not each[2]:
                each[1].wait()
                each[2] = True

    def begin(number, part, made):
        layer = number % depth
        rows = pl.ds(part * half, half)
        if number >= 2 and part == 0:
            gathers[number % 2].finish()
        xb[rows, :] = made
        hat = norm(made)[0]
        gain = gain_ref[layer : layer + 1, :]
        normed = hat * gain + bias_ref[layer : layer + 1, :]
        abufs[number % 2][pl.ds(2 * half * part, half), :] = normed.astype(BF)
        gathers[number % 2].send(part)

    for i in (3, 4, 5, 6):
        loads[i].wait()
    fetches[0].step(1)
    loads[0].wait()
    loads[1].wait()
    for part in range(2):
        rows = pl.ds(part * half, half)
        made = dot(tokens[rows, :], wself[0])
        start[rows, :] = made
        begin(0, part, made)

    def make_tables():
        place = lax.axis_index("tensor")
        sibling = ids[0][1]
        far = ids[1][1]
        far_other = lax.rem(sibling + 2, 4)
        row = lax.broadcasted_iota(jnp.int32, (half, 128), 0).astype(F32)
        for chunk, (block, part) in enumerate(
            zip(
                (place, sibling, place, sibling, far, far_other, far, far_other),
                (0, 0, 1, 1, 1, 1, 0, 0),
            )
        ):
            rows = pl.ds(chunk * half, half)
            offset = (block * unit_rows).astype(F32)
            position = row + part * half + (1.0 - packed) * offset
            angle = position * rotary_ref[...]
            cos_ref[rows, :] = jnp.cos(angle)
            sin_ref[rows, :] = jnp.sin(angle)
        steps = steps_ref[...].astype(F32)
        slot = lax.broadcasted_iota(jnp.int32, steps.shape, 1)
        mine = jnp.sum(jnp.where(slot == place, steps, 0.0), axis=1, keepdims=True)
        step = packed * mine + (1.0 - packed) * steps[:, 0:1]
        angle = jnp.broadcast_to(step * time_ref[...], (8, width // 2))
        temb_ref[:, : width // 2] = jnp.cos(angle)
        temb_ref[:, width // 2 :] = jnp.sin(angle)

    def make_cond(layer):
        ada_loads[layer].wait()
        column = temb_ref[...].T[:, 0:1]
        made = jnp.sum(wada[...] * column, axis=0, keepdims=True)
        made = made + bada_ref[layer : layer + 1, :]
        cond_ref[8 * layer : 8 * layer + 8, :] = jnp.broadcast_to(made, (8, 2 * width))
        if layer + 1 < depth:
            ada_loads[layer + 1].start()

    def project(number, count, pick, before):
        layer = number % depth
        abuf = abufs[number % 2]

        def body(step, carry):
            before(step)
            shard, unit = pick(step)
            rows = span(unit * unit_rows, unit_rows)
            normed = abuf[rows, :]
            mixed = dot(normed, wqk[layer][shard], NT)
            cosine = cos_ref[rows, :]
            sine = sin_ref[rows, :]
            for place, dst, scale in ((0, q2, HD**-0.5), (256, k2, 1.0)):
                first = mixed[:, place : place + 128]
                second = mixed[:, place + 128 : place + 256]
                dst[shard, rows, :128] = ((first * cosine - second * sine) * scale).astype(BF)
                dst[shard, rows, 128:] = ((second * cosine + first * sine) * scale).astype(BF)
            v2[shard, rows, :] = dot(normed, wa[layer][shard, part_a[2], :], NT).astype(BF)
            return carry

        lax.fori_loop(0, count, body, 0)

    lane = lax.broadcasted_iota(jnp.int32, (1, 128), 1)

    def scores_of(shard, unit, head, keys):
        rows = span(unit * unit_rows, unit_rows)
        made = dot(keep_head(q2[shard, rows, :], head, True), k2[shard, keys, :], NT)
        part = lax.broadcasted_iota(jnp.int32, (2, 1, length // 2), 0)
        chunk = lax.broadcasted_iota(jnp.int32, (2, 1, length // 2), 2) // half
        neg = apart(owner(chunk + keys.start // half), part, packed.reshape(1, 1, 1))
        return (made.reshape(2, half, length // 2) + neg).reshape(unit_rows, length // 2)

    def attend_near(number, count, pick, before):
        keys = pl.ds(0, length // 2)

        def body(step, carry):
            before(step)
            shard, unit = pick(step)
            place = 2 * unit + shard
            attended = jnp.zeros((unit_rows, columns), F32)
            tops = jnp.zeros((unit_rows, 128), F32)
            totals = jnp.zeros((unit_rows, 128), F32)
            for head in range(heads):
                scores = scores_of(shard, unit, head, keys)
                largest = jnp.max(scores, axis=-1, keepdims=True)
                shares = jnp.exp(scores - largest)
                output = dot(shares.astype(BF), v2[shard, keys, :])
                attended = jnp.where(head_mask(head, columns, False), output, attended)
                tops = jnp.where(lane == head, largest, tops)
                totals = jnp.where(lane == head, jnp.sum(shares, axis=-1, keepdims=True), totals)
            accs[place] = attended
            stats[place, 0] = tops
            stats[place, 1] = totals
            return carry

        lax.fori_loop(0, count, body, 0)

    def attend_far(number, save, count, pick, before):
        keys = pl.ds(length // 2, length // 2)
        layer, slot = number % depth, number % 2

        def body(step, carry):
            before(step)
            shard, unit = pick(step)
            place = 2 * unit + shard
            rows = span(unit * unit_rows, unit_rows)
            attended = jnp.zeros((unit_rows, columns), F32)
            logs = jnp.zeros((unit_rows, 128), F32)
            for head in range(heads):
                scores = scores_of(shard, unit, head, keys)
                earlier = stats[place, 0][:, head : head + 1]
                largest = jnp.maximum(earlier, jnp.max(scores, axis=-1, keepdims=True))
                shares = jnp.exp(scores - largest)
                shrink = jnp.exp(earlier - largest)
                totals = stats[place, 1][:, head : head + 1] * shrink
                totals = totals + jnp.sum(shares, axis=-1, keepdims=True)
                output = dot(shares.astype(BF), v2[shard, keys, :])
                output = (accs[place] * shrink + output) * (1.0 / totals)
                attended = jnp.where(head_mask(head, columns, False), output, attended)
                if save:
                    logs = jnp.where(lane == head, largest + jnp.log(totals), logs)
            if save:
                lse2[slot, shard, unit] = logs.T[:8, :]
            attended = attended.astype(BF)
            ob2[slot, shard, rows, :] = attended

            @pl.when(shard == 1)
            def _():
                total = dot(ob2[slot, 0, rows, :], wa[layer][0, part_a[3], :])
                near_a.send(unit, total + dot(attended, wa[layer][1, part_a[3], :]))

            return carry

        lax.fori_loop(0, count, body, 0)

    def feed(number, save, pick, before):
        layer = number % depth
        mbuf = mbufs[number % 2]

        def body(step, carry):
            before(step)
            shard, unit = pick(step)
            rows = span(unit * unit_rows, unit_rows)
            hidden = dot(mbuf[rows, :], wu[layer][shard])
            gated, slope = gelu_parts(hidden)
            gated = gated.astype(BF)
            made = dot(gated, wd[layer][shard])

            @pl.when(shard == 0)
            def _():
                if save:
                    gb[rows, :] = gated
                    gpb[rows, :] = slope.astype(BF)
                sums[rows, :] = made

            @pl.when(shard == 1)
            def _():
                near_f.send(unit, sums[rows, :] + made)

            return carry

        lax.fori_loop(0, 4, body, 0)

    crossings = {}

    def cross(number):
        slot = number % 2
        made = []
        for part in range(2):
            made.append(
                pltpu.make_async_remote_copy(
                    src_ref=lse2.at[slot, 1, part],
                    dst_ref=lse2.at[slot, 0, 3 - part],
                    send_sem=cross_send.at[2 * slot + part],
                    recv_sem=cross_recv.at[2 * slot + part],
                    device_id=ids[1],
                    device_id_type=MESH,
                )
            )
            made[-1].start()
        crossings[number] = made

    def late(number):
        slot = number % 2
        saved = saved_hbm[number % depth]
        for part in range(2):
            mixes[slot].far(part)
        store("m", mbufs[slot], saved["m"])
        for each in crossings[number]:
            each.wait_recv()
        store("lse", lse2.at[slot, 0], saved["lse"])

    def events(table):
        def before(step):
            for when, actions in table.items():

                @pl.when(step == when)
                def _():
                    for action in actions:
                        if isinstance(action, tuple):
                            if action[0] < len(fetches):
                                fetches[action[0]].step(action[1])
                        else:
                            action()

        return before

    def waits(*indices):
        def action():
            for index in indices:
                loads[index].wait()

        return action

    def by_unit(step):
        return (lax.rem(step, 2), step // 2)

    def by_shard(step):
        return (step // 2, lax.rem(step, 2))

    def run(number, after_layer):
        layer, slot = number % depth, number % 2
        save = number >= depth
        group, mix = gathers[slot], mixes[slot]
        mix_rows = mbufs[slot]
        base = 3 * layer

        def after_attend(part):
            def action():
                if part == 0 and number >= 2:
                    mix.finish(far=False)
                if part == 0:
                    stored("x1")
                rows = pl.ds(part * half, half)
                after = xb[rows, :] + near_a.collect(part)
                x1[rows, :] = after
                shift = cond_ref[8 * layer : 8 * layer + 1, :width]
                scale = cond_ref[8 * layer : 8 * layer + 1, width:]
                made = norm(after)[0] * (1.0 + scale) + shift
                mix_rows[pl.ds(2 * half * part, half), :] = made.astype(BF)
                mix.sibling_copy(part).start()
                if number == 2 * depth - 1:
                    mix.far_copy(part).start()

            return action

        def after_feed(part):
            def action():
                if part == 0:
                    stored("x")
                rows = pl.ds(part * half, half)
                made = x1[rows, :] + near_f.collect(part) + bdown_ref[layer : layer + 1, :]
                after_layer(part, rows, made)

            return action

        def near_rows(part):
            return lambda: group.near(part)

        def far_rows(part):
            return lambda: group.far(part)

        def mixed(part):
            return lambda: mix.near(part)

        if number:
            near_a.drain()
            near_f.drain()
        stored("q", "k", "v")

        def turn(shard):
            rows = wa[layer].at[shard, part_a[0]], wa[layer].at[shard, part_a[1]]
            load_turned(*rows, wqk[layer].at[shard])

        far_table = {3: [after_attend(0)]}
        feed_table = {
            0: [mixed(0)],
            1: [after_attend(1)],
            2: [mixed(1)],
            3: [after_feed(0)],
        }
        order = by_unit
        if number == 0:
            make_tables()
            turn(0)
            arrive = {
                0: [near_rows(0)],
                1: [near_rows(1)],
                2: [(0, 2), waits(7), (1, 1), far_rows(0)],
                3: [far_rows(1), waits(8), (2, 1)],
            }

            def in_order(step):
                return jnp.where(step < 2, step, 5 - step)

            project(number, 4, lambda step: (0, in_order(step)), events(arrive))
            attend_near(number, 2, lambda step: (0, step), events({1: [(0, 3)]}))
            make_cond(layer)
            first = {1: [(1, 2), waits(9, 10, 11, 12), (3, 1)]}
            attend_far(number, save, 2, lambda step: (0, step), events(first))
            fetches[0].step(4)
            turn(1)
            second = {3: [(1, 3), (2, 2), waits(13), (4, 1)]}
            project(number, 4, lambda step: (1, in_order(step)), events(second))
            attend_near(number, 2, lambda step: (1, step), events({}))
            far_table = {1: [after_attend(0)]}
            attend_far(number, save, 2, lambda step: (1, step), events(far_table))
            feed_table = {
                0: [mixed(0), (2, 3), (3, 2), waits(14), (5, 1)],
                1: [after_attend(1), mixed(1)],
                2: [(1, 4), (3, 3), (4, 2), (2, 4)],
                3: [after_feed(0)],
            }
            order = by_shard
        else:
            own_table = {0: [near_rows(0)], 1: [near_rows(1)]}
            near_table = {3: [lambda: group.arrive(0)]}
            if not save:
                turn(0)
                own_table[0] += [(base + 1, 3)]
                near_table[1] = [(base + 2, 2)]
                own_table[2] = [(base, 4), lambda: turn(1)]
                far_table[0] = [(base + 2, 3)]
                feed_table[0] += [(base + 1, 4)]
                feed_table[1] += [(base + 2, 4)]
            project(number, 4, by_shard, events(own_table))
            attend_near(number, 4, by_unit, events(near_table))
            if not save:
                make_cond(layer)
            if number == depth:
                for part in range(2):
                    grads.near(part)
                    grads.far(part)
                store("grad", ebuf, grad_hbm)
            arrive = {
                0: [lambda: group.settle(0)],
                1: [lambda: group.arrive(1)],
                2: [lambda: group.settle(1)],
            }
            project(number, 4, lambda step: (lax.rem(step, 2), 3 - step // 2), events(arrive))
            if number == depth - 1:
                for part in range(2):
                    ebuf[grads.own(part), :] = cot_ref[pl.ds(part * half, half), :]
                    grads.send(part)
            if number > depth:
                for part in range(2):
                    mixes[(number - 1) % 2].far_copy(part).start()
            if save:
                store("a", abufs[slot], saved_hbm[layer]["a"])
                store("x", xb, saved_hbm[layer]["x"])
                for name, src in (("q", q2), ("k", k2), ("v", v2)):
                    store(name, src.at[0], saved_hbm[layer][name])
            attend_far(number, save, 4, by_unit, events(far_table))
        if save:
            cross(number)
            rows = pl.ds(0, length // 2)
            store("o", ob2.at[slot, 0, rows], saved_hbm[layer]["o"])
            store("o2", ob2.at[slot, 1, rows], saved_hbm[layer]["o2"])
        stored("g", "slope")
        feed(number, save, order, events(feed_table))
        if save:
            store("x1", x1, saved_hbm[layer]["x1"])
            store("g", gb, saved_hbm[layer]["g"])
            store("slope", gpb, saved_hbm[layer]["slope"])
        after_feed(1)()

    def between(part, rows, made):
        estimate = made.astype(BF)
        est_ref[rows, :] = estimate
        begin(depth, part, start[rows, :] + dot(estimate, wself[1]))

    def close(part, rows, made):
        acts_ref[rows, :] = made.astype(BF)

    def enter(number):
        return lambda part, rows, made: begin(number, part, made)

    for number in range(2 * depth):
        if number + 1 == 2 * depth:
            run(number, close)
        elif number + 1 == depth:
            loads[2].wait()
            run(number, between)
        else:
            run(number, enter(number + 1))
    for number in range(depth, 2 * depth):
        late(number)
    for each in gathers:
        each.finish()
    for each in (*mixes, grads):
        each.finish()
    near_a.drain()
    near_f.drain()
    for each in fetches:
        each.finish()
    for each in crossings.values():
        for copy in each:
            copy.wait_send()
    stored("grad", *SAVED)


def any_spec():
    return pl.BlockSpec(memory_space=pl.ANY)


def vmem_spec():
    return pl.BlockSpec(memory_space=pltpu.VMEM)


def forward(heads, tokens, cotangent, w_self, vectors, weights):
    depth = weights[0].shape[0]
    block, width = tokens.shape
    length = 4 * block
    half = block // 2
    columns = heads * HD
    units = weights[2].shape[2]
    lanes = jnp.arange(128) % HALF
    rotary = jnp.exp(-jnp.log(10000.0) * lanes.astype(F32) / HALF)[None]
    halves = jnp.arange(width // 2).astype(F32)
    times = jnp.exp(-jnp.log(10000.0) * halves / (width // 2))[None]
    kept = {
        "a": ((length, width), BF),
        "q": ((length, 256), BF),
        "k": ((length, 256), BF),
        "v": ((length, columns), BF),
        "o": ((length // 2, columns), BF),
        "o2": ((length // 2, columns), BF),
        "x1": ((block, width), F32),
        "m": ((length, width), BF),
        "g": ((length // 2, units), BF),
        "slope": ((length // 2, units), BF),
        "x": ((block, width), F32),
        "lse": ((4, 8, block), F32),
    }
    kept_shapes = [jax.ShapeDtypeStruct(*kept[name]) for name in SAVED]
    out_shape = [
        jax.ShapeDtypeStruct((block, width), BF),
        jax.ShapeDtypeStruct((block, width), BF),
        jax.ShapeDtypeStruct((8 * depth, 2 * width), F32),
        jax.ShapeDtypeStruct((length, 128), F32),
        jax.ShapeDtypeStruct((length, 128), F32),
        jax.ShapeDtypeStruct((8, width), F32),
        jax.ShapeDtypeStruct((length, width), BF),
    ] + kept_shapes * depth
    out_specs = [vmem_spec()] * 6 + [any_spec()] * (1 + depth * len(SAVED))
    dma = pltpu.SemaphoreType.DMA
    scratch = [dma((3, 2))] * 10
    scratch += [dma((2, 2))] * 2 + [dma((3 * depth, 2, 6)), dma((4,)), dma((4,))]
    scratch += [dma((4 + 6 * depth,)), dma((1 + depth * len(SAVED),))]
    scratch += [
        pltpu.VMEM((block, width), BF),
        pltpu.VMEM((2, width, width), BF),
        pltpu.VMEM((width, 2 * width), F32),
    ]
    scratch += [pltpu.VMEM((2, 4 * columns, width), BF)] * depth
    scratch += [pltpu.VMEM((2, width, units), BF)] * depth
    scratch += [pltpu.VMEM((2, units, width), BF)] * depth
    scratch += [pltpu.VMEM((2, 512, width), BF)] * depth
    scratch += [pltpu.VMEM((length, width), BF)] * 5
    scratch += [
        pltpu.VMEM((2, length, 256), BF),
        pltpu.VMEM((2, length, 256), BF),
        pltpu.VMEM((2, length, columns), BF),
        pltpu.VMEM((2, 2, length // 2, columns), BF),
        pltpu.VMEM((2, 2, 4, 8, block), F32),
        pltpu.VMEM((4, block, columns), F32),
        pltpu.VMEM((4, 2, block, 128), F32),
        pltpu.VMEM((length // 2, units), BF),
        pltpu.VMEM((length // 2, units), BF),
    ]
    scratch += [pltpu.VMEM((block, width), F32)] * 5
    scratch += [pltpu.VMEM((2 * block, width), F32)]
    scratch += [pltpu.VMEM((2, half, width), BF)] * 4

    def kernel(*refs):
        forward_kernel(depth, heads, refs)

    operands = [*vectors, rotary, times, cotangent]
    remote = [tokens, w_self.reshape(2, width, width), *weights]
    made = pl.pallas_call(
        kernel,
        out_shape=out_shape,
        in_specs=[vmem_spec()] * len(operands) + [any_spec()] * len(remote),
        out_specs=out_specs,
        scratch_shapes=scratch,
        compiler_params=pltpu.CompilerParams(
            collective_id=1, has_side_effects=True, vmem_limit_bytes=LIMIT
        ),
        name="layers_forward",
    )(*operands, *remote)
    count = len(SAVED)
    saved = [made[7 + count * layer : 7 + count * (layer + 1)] for layer in range(depth)]
    return (made[:7], [dict(zip(SAVED, each)) for each in saved])


class Ladder:
    def __init__(self, sems):
        self.send, self.recv = sems
        self.used = 0
        self.open = []

    def copy(self, src, dst, device):
        made = pltpu.make_async_remote_copy(
            src_ref=src,
            dst_ref=dst,
            send_sem=self.send.at[self.used],
            recv_sem=self.recv.at[self.used],
            device_id=device,
            device_id_type=MESH,
        )
        self.used += 1
        assert self.used <= LADDER_COPIES
        made.start()
        self.open.append(made)
        return made

    def finish(self):
        for each in self.open:
            each.wait_send()


LADDER_COPIES = 34


class Loads:
    def __init__(self, sems):
        self.sems = sems
        self.names = {}

    def add(self, name, sources, buffer):
        self.names[name] = (sources, buffer, len(self.names))
        return buffer

    def copy(self, name, layer):
        sources, buffer, place = self.names[name]
        return pltpu.make_async_copy(sources[layer], buffer, self.sems.at[place])

    def start(self, layer, *names):
        if layer >= 0:
            for name in names:
                self.copy(name, layer).start()

    def wait(self, layer, *names):
        for name in names:
            self.copy(name, layer).wait()


def backward_kernel(depth, heads, deep, refs):
    refs = list(refs)

    def take(count):
        made = refs[:count]
        del refs[:count]
        return made

    cot_ref, gain_ref, lengths_ref, cos_ref, sin_ref, temb_ref, cond_ref = take(7)
    joined_hbm = take(2)
    (grad_hbm,) = take(1)
    wqkv_hbm, wout_hbm, wup_hbm, wdown_hbm, _ = take(5)
    saved_hbm = [dict(zip(SAVED, take(len(SAVED)))) for _ in range(depth)]
    (out_ref, small_ref) = take(2)
    attn_outs, feed_outs = take(depth), take(depth)
    if deep:
        sum_ref, vec_ref = take(2)
    feed_sems, attn_sems = [take(2), take(2)], [take(2), take(2)]
    load_sems, store_sems, out_sems = take(3)
    loads = Loads(load_sems)
    wq, wk, wv = (
        loads.add(name, [wqkv_hbm.at[layer, part] for layer in range(depth)], take(1)[0])
        for part, name in enumerate(("wq", "wk", "wv"))
    )
    wout, wup, wdown = (
        loads.add(name, [src.at[layer] for layer in range(depth)], take(1)[0])
        for name, src in (("wout", wout_hbm), ("wup", wup_hbm), ("wdown", wdown_hbm))
    )
    buffers = dict(zip(SAVED, take(len(SAVED))))
    outs = [take(2) for _ in range(depth)]
    for name in SAVED:
        if name in ("o", "o2"):
            continue
        rows = saved_hbm[0][name].shape[0]
        buffer = buffers[name]
        if rows < buffer.shape[0]:
            buffer = buffer.at[pl.ds(0, rows)]
        loads.add(name, [saved_hbm[layer][name] for layer in range(depth)], buffer)
    abuf, qb, kb, vb, _, _, x1b, mbuf, gb, gpb, xb, lse = (buffers[name] for name in SAVED)
    ebuf, fbuf = take(2)
    feed_bufs, attn_bufs = take(6), take(6)
    (wqk, dhb, qmask, domask, dsb, pb, dkb, dvb, dqk, dvv, work, dxb) = take(12)
    (feed_grads, attn_grads) = take(2)
    ids = neighbours()
    sums = {}
    if deep:
        spot = Spot(deep)
        meet([*ids, *spot.partners()])
        for layer in range(depth):
            for name, src, out in (
                ("up", feed_grads.at[0], feed_outs[layer].at[0]),
                ("down", feed_grads.at[1], feed_outs[layer].at[1]),
                ("attn", attn_grads, attn_outs[layer]),
            ):
                sums[name, layer] = DpSum(spot, src, out, take(3))
        tail_refs = take(10)
        joined = tail_refs[0]
        joined_loads = [
            pltpu.make_async_copy(src, joined.at[i], store_sems.at[i])
            for i, src in enumerate(joined_hbm)
        ]
        for each in joined_loads:
            each.start()
    else:
        meet(ids)
    width = cot_ref.shape[1]
    half = cot_ref.shape[0] // 2
    unit_rows = 2 * half
    total, own, dx1 = (work.at[pl.ds(i * unit_rows, unit_rows)] for i in range(3))
    feed_rows = Gather(feed_sems[0], ids, ebuf)
    feed_sum = Scatter(feed_sems[1], ids, own, feed_bufs)
    attn_rows = Gather(attn_sems[0], ids, fbuf)
    attn_sum = Scatter(attn_sems[1], ids, own, attn_bufs)
    columns = heads * HD
    tiles = width // 256
    top = depth - 1
    packed = is_packed(lengths_ref, 8 * half)
    loads.add("grad", [grad_hbm] * depth, ebuf)
    loads.start(top, "m", "wup", "grad", "wdown", "slope", "x1", "wout", "q", "k", "v", "lse", "g")
    loads.start(top, "wq", "wk", "wv", "a", "x")
    out_loads = []
    out_sends = []
    for layer in range(depth):
        rows = outs[layer][0].at[pl.ds(0, 4 * half)]
        pairs = ((saved_hbm[layer]["o"], rows), (saved_hbm[layer]["o2"], outs[layer][1]))
        out_loads.append(
            [
                pltpu.make_async_copy(src, dst, out_sems.at[layer, 4 + i])
                for i, (src, dst) in enumerate(pairs)
            ]
        )
        out_sends.append(
            [
                pltpu.make_async_remote_copy(
                    src_ref=outs[layer][1].at[pl.ds(part * unit_rows, unit_rows)],
                    dst_ref=outs[layer][0].at[pl.ds((3 - part) * unit_rows, unit_rows)],
                    send_sem=out_sems.at[layer, part],
                    recv_sem=out_sems.at[layer, 2 + part],
                    device_id=ids[1],
                    device_id_type=MESH,
                )
                for part in range(2)
            ]
        )
        for each in out_loads[layer]:
            each.start()

    def send_outs(layer):
        out_loads[layer][1].wait()
        for each in out_sends[layer]:
            each.start()

    send_outs(top)
    dxb[...] = cot_ref[...].astype(F32)
    small_ref[...] = jnp.zeros_like(small_ref)

    def outer(left, right, dst):
        def tile(index, carry):
            place = span(index * 256, 256)
            dst[place, :] = dot(left[:, place], right[...], TN).astype(BF)
            return carry

        lax.fori_loop(0, tiles, tile, 0)

    def turn_back(grad, rows, scale):
        cosine = cos_ref[rows, :]
        sine = sin_ref[rows, :]
        first_half = grad[:, :128]
        second_half = grad[:, 128:]
        return (
            ((first_half * cosine + second_half * sine) * scale).astype(BF),
            ((second_half * cosine - first_half * sine) * scale).astype(BF),
        )

    def event(name, layer, kind):
        if (name, layer) in sums:
            getattr(sums[name, layer], kind)()

    for layer in reversed(range(depth)):
        def note(row, value):
            small_ref[8 * layer + row : 8 * layer + row + 1, :] = value

        note(4, jnp.sum(dxb[...], axis=0, keepdims=True))
        dkb[...] = jnp.zeros_like(dkb)
        dvb[...] = jnp.zeros_like(dvb)
        loads.wait(layer, "m", "wup")

        def expand(step, carry):
            rows = span((3 - step) * unit_rows, unit_rows)
            gated, slope = gelu_parts(dot(mbuf[rows, :], wup[...]))
            gb[rows, :] = gated.astype(BF)
            gpb[rows, :] = slope.astype(BF)
            return carry

        lax.fori_loop(0, 2, expand, 0)
        loads.wait(layer, "wdown", "slope")
        if layer == top:
            loads.wait(layer, "grad")

        def contract(step, carry):
            if layer == top:
                unit = jnp.where(step < 2, 3 - step, step - 2)
            else:
                feed_rows.receive(step)
                unit = jnp.where(step < 2, step, 5 - step)
            rows = span(unit * unit_rows, unit_rows)
            grad = dot(ebuf[rows, :], wdown[...], NT)
            grad = (grad * gpb[rows, :].astype(F32)).astype(BF)
            dhb[rows, :] = grad
            total[...] = dot(grad, wup[...], NT)
            feed_sum.send(unit, total)
            return carry

        lax.fori_loop(0, 4, contract, 0)
        loads.start(layer - 1, "wdown", "slope")
        event("attn", layer + 1, "middle")
        event("up", layer + 1, "end")
        if layer < top:
            attn_rows.finish()
            attn_sum.finish()
        shift_sum = jnp.zeros((1, width), F32)
        scale_sum = jnp.zeros((1, width), F32)
        for part in range(2):
            if part == 0:
                loads.wait(layer, "x1")
                outer(mbuf, dhb, feed_grads.at[0])
                event("up", layer, "start")
            else:
                loads.wait(layer, "g")
                outer(ebuf, gb, feed_grads.at[1])
                event("down", layer, "start")
            rows = pl.ds(part * half, half)
            grad = feed_sum.collect(part)
            hat, rstd = norm(x1b[rows, :])
            shift_sum += jnp.sum(grad, axis=0, keepdims=True)
            scale_sum += jnp.sum(grad * hat, axis=0, keepdims=True)
            after = dxb[rows, :]
            after = after + norm_back(grad * (1.0 + cond_ref[8 * layer : 8 * layer + 1, width:]), hat, rstd)
            dx1[rows, :] = after
            fbuf[attn_rows.own(part), :] = after.astype(BF)
            attn_rows.send(part)
        note(0, shift_sum)
        note(1, scale_sum)
        loads.start(layer - 1, "m", "g", "x1", "wup")
        loads.wait(layer, "wout", "q", "k", "v", "lse")

        def attend(step, carry):
            attn_rows.receive(step)
            if layer:

                @pl.when(step == 3)
                def _():
                    send_outs(layer - 1)

            unit = jnp.where(step < 2, step, 5 - step)
            rows = span(unit * unit_rows, unit_rows)
            grad_out = dot(fbuf[rows, :], wout[...], NT).astype(BF)
            queries = qb[rows, :]
            grad_queries = jnp.zeros((unit_rows, 256), F32)
            chunk = lax.broadcasted_iota(jnp.int32, (8, 1, unit_rows), 0)
            part = lax.broadcasted_iota(jnp.int32, (8, 1, unit_rows), 2) // half
            neg = apart(owner(chunk), unit_owner(unit, part), packed.reshape(1, 1, 1))
            for head in range(heads):
                place = pl.ds(head * unit_rows, unit_rows)
                masked = keep_head(queries, head, True)
                masked_out = keep_head(grad_out, head, False)
                qmask[place, :] = masked
                domask[place, :] = masked_out
                scores = dot(kb[...], masked, NT).reshape(8, half, unit_rows)
                shares = jnp.exp(scores - (lse[unit, head : head + 1, :] - neg))
                shares = shares.reshape(8 * half, unit_rows)
                grad_shares = dot(vb[...], masked_out, NT)
                centre = jnp.sum(shares * grad_shares, axis=0, keepdims=True)
                grad_scores = (shares * (grad_shares - centre)).astype(BF)
                pb[:, place] = shares.astype(BF)
                dsb[:, place] = grad_scores
                grad_queries = grad_queries + dot(grad_scores, keep_head(kb[...], head, True), TN)
            dkb[...] += dot(dsb[...], qmask[...])
            dvb[...] += dot(pb[...], domask[...])
            low, high = turn_back(grad_queries, rows, HD**-0.5)
            dqk[rows, :128] = low
            dqk[rows, 128:256] = high
            return carry

        lax.fori_loop(0, 4, attend, 0)
        loads.start(layer - 1, "wout", "q", "k", "v", "lse")
        event("down", layer + 1, "end")
        event("attn", layer + 1, "end")
        event("up", layer, "middle")
        loads.wait(layer, "wq", "wk", "wv")
        load_turned(wq, wk, wqk)

        def spread(step, carry):
            unit = jnp.where(step < 2, 3 - step, step - 2)
            rows = span(unit * unit_rows, unit_rows)
            low, high = turn_back(dkb[rows, :], rows, 1.0)
            dqk[rows, 256:384] = low
            dqk[rows, 384:512] = high
            values = dvb[rows, :].astype(BF)
            dvv[rows, :] = values
            total[...] = dot(dqk[rows, :], wqk[...]) + dot(values, wv[...])
            attn_sum.send(unit, total)
            return carry

        lax.fori_loop(0, 4, spread, 0)
        loads.start(layer - 1, "wq", "wk", "wv")
        if layer:
            event("down", layer, "middle")
        loads.wait(layer, "a")
        out_loads[layer][0].wait()
        for each in out_sends[layer]:
            each.wait()
        ob = outs[layer][0]
        places = (
            turned_place(columns, 0, 4 * columns),
            turned_place(columns, columns, 4 * columns),
            plain_place(columns, 2 * columns, 4 * columns),
            plain_place(columns, 3 * columns, 4 * columns),
        )

        def attn_tile(index, carry):
            place = span(index * 256, 256)
            normed = abuf[:, place]
            both = dot(normed, dqk[...], TN).astype(BF)
            made = dot(both[:, :256], places[0]) + dot(both[:, 256:], places[1])
            made = made + dot(dot(normed, dvv[...], TN).astype(BF), places[2])
            outs = dot(fbuf[:, place], ob[...], TN).astype(BF)
            attn_grads[place, :] = (made + dot(outs, places[3])).astype(BF)
            return carry

        lax.fori_loop(0, tiles, attn_tile, 0)
        loads.start(layer - 1, "a")
        if layer:
            event("attn", layer, "start")
        if not deep:
            stores = [
                pltpu.make_async_copy(attn_grads, attn_outs[layer], store_sems.at[0]),
                pltpu.make_async_copy(feed_grads, feed_outs[layer], store_sems.at[1]),
            ]
            for each in stores:
                each.start()
            for each in stores:
                each.wait()
        if layer < top:
            feed_rows.finish()
        feed_sum.finish()
        loads.wait(layer, "x")
        gain_sum = jnp.zeros((1, width), F32)
        bias_sum = jnp.zeros((1, width), F32)
        for part in range(2):
            rows = pl.ds(part * half, half)
            grad = attn_sum.collect(part)
            hat, rstd = norm(xb[rows, :])
            gain_sum += jnp.sum(grad * hat, axis=0, keepdims=True)
            bias_sum += jnp.sum(grad, axis=0, keepdims=True)
            made = dx1[rows, :] + norm_back(
                grad * gain_ref[layer : layer + 1, :], hat, rstd
            )
            dxb[rows, :] = made
            if layer:
                ebuf[feed_rows.own(part), :] = made.astype(BF)
                feed_rows.send(part)
        note(2, gain_sum)
        note(3, bias_sum)
        loads.start(layer - 1, "x")
    out_ref[...] = dxb[...]
    if deep:
        for each in joined_loads:
            each.wait()
        tail(deep, spot, ids, sums, dxb, small_ref, temb_ref, work, dsb, tail_refs,
             sum_ref, vec_ref, store_sems)
    attn_rows.finish()
    attn_sum.finish()


def tail(deep, spot, ids, sums, dxb, small_ref, temb_ref, work, dsb, scratch, sum_ref, vec_ref,
         store_sems):
    (joined, ebuf, jbuf, near_in, next_in, z_in, result, vecs, send, recv) = scratch
    sibling, far = ids
    place = lax.axis_index("tensor")
    core = lax.rem(place, 2)
    y = place // 2
    x, z = spot.x, spot.z
    width = dxb.shape[1]
    ladder = Ladder((send, recv))
    ebuf[0] = dxb[...].astype(BF)
    rows_copy = ladder.copy(ebuf.at[0], ebuf.at[1], sibling)
    joined_copy = ladder.copy(joined.at[1 - core], jbuf, sibling)
    mine = vecs.at[core, y, x, z]
    row = lax.broadcasted_iota(jnp.int32, small_ref.shape, 0)
    mine[...] = jnp.where(row == 5, temb_ref[0:1, :], small_ref[...]).astype(BF)
    vec_z = [ladder.copy(mine, mine, spot.along(ahead)) for ahead in range(1, deep)]
    rows_copy.wait_recv()
    joined_copy.wait_recv()
    rest = width // 2

    def tile(index, carry):
        rows = span(index * 256, 256)
        made = dot(joined[core, :, rows], ebuf[0], TN)
        work[rows, :] = made + dot(jbuf[:, rows], ebuf[1], TN)
        return carry

    lax.fori_loop(0, width // 256, tile, 0)
    half, quarter = width // 2, width // 4
    piece = quarter // deep
    ways = (((far, y), (spot.across, x)), ((spot.across, x), (far, y)))
    lanes = (pl.ds(0, rest), pl.ds(rest, rest))
    firsts = []
    for side, ((device, bit), _) in enumerate(ways):
        out = dsb.at[pl.ds(0, half), lanes[side]]
        out[...] = work[span((1 - bit) * half, half), lanes[side]].astype(BF)
        firsts.append(ladder.copy(out, near_in.at[side], device))
    sums["down", 0].middle()
    for each in vec_z:
        each.wait_recv()
    row_z = vecs.at[core, y, x]
    vec_x = ladder.copy(row_z, row_z, spot.across)
    seconds = []
    for side, ((_, bit), (device, bit2)) in enumerate(ways):
        firsts[side].wait_recv()
        kept = work.at[span(bit * half, half), lanes[side]]
        kept[...] = kept[...] + near_in[side].astype(F32)
        out = dsb.at[pl.ds(half, quarter), lanes[side]]
        out[...] = work[span(bit * half + (1 - bit2) * quarter, quarter), lanes[side]].astype(BF)
        seconds.append(ladder.copy(out, next_in.at[side], device))
    sums["attn", 0].start()
    vec_x.wait_recv()
    plane = vecs.at[core, y]
    vec_y = ladder.copy(plane, plane, far)
    thirds = []
    for side, ((_, bit), (_, bit2)) in enumerate(ways):
        seconds[side].wait_recv()
        kept = work.at[span(bit * half + bit2 * quarter, quarter), lanes[side]]
        kept[...] = kept[...] + next_in[side].astype(F32)
        out = dsb.at[pl.ds(half + quarter, quarter), lanes[side]]
        out[...] = kept[...].astype(BF)
        for ahead in range(1, deep):
            start = half + quarter + spot.level(ahead) * piece
            thirds.append(
                ladder.copy(
                    dsb.at[span(start, piece), lanes[side]],
                    z_in.at[side, ahead - 1],
                    spot.along(ahead),
                )
            )
    sums["up", 0].end()
    sums["down", 0].end()
    vec_y.wait_recv()
    every = vecs.at[core]
    vec_core = ladder.copy(every, every, sibling)
    lasts = []
    for side, ((_, bit), (_, bit2)) in enumerate(ways):
        for ahead in range(1, deep):
            thirds[side * (deep - 1) + ahead - 1].wait_recv()
        start = bit * half + bit2 * quarter + z * piece
        made = work[span(start, piece), lanes[side]]
        for ahead in range(1, deep):
            made = made + z_in[side, ahead - 1].astype(F32)
        own = result.at[core, side, span(start, piece)]
        own[...] = made.astype(BF)
        lasts += [ladder.copy(own, own, spot.along(ahead)) for ahead in range(1, deep)]
    backs = []
    for side, ((_, bit), (device, bit2)) in enumerate(ways):
        for ahead in range(1, deep):
            lasts[side * (deep - 1) + ahead - 1].wait_recv()
        own = result.at[core, side, span(bit * half + bit2 * quarter, quarter)]
        backs.append(ladder.copy(own, own, device))
    sums["attn", 0].middle()
    ends = []
    for side, ((device, bit), _) in enumerate(ways):
        backs[side].wait_recv()
        own = result.at[core, side, span(bit * half, half)]
        ends.append(ladder.copy(own, own, device))
    sums["attn", 0].end()
    vec_core.wait_recv()
    vec_store = pltpu.make_async_copy(vecs, vec_ref, store_sems.at[0])
    vec_store.start()
    for each in ends:
        each.wait_recv()
    whole = ladder.copy(result.at[core], result.at[core], sibling)
    whole.wait_recv()
    sum_store = pltpu.make_async_copy(result, sum_ref, store_sems.at[1])
    sum_store.start()
    ladder.finish()
    vec_store.wait()
    sum_store.wait()


def backward(heads, deep, cotangent, grad_all, gains, lengths, tables, weights, kept, joined):
    depth = len(kept)
    block, width = cotangent.shape
    length = 4 * block
    units = weights[2].shape[2]
    columns = heads * HD
    part = width // (2 * deep) if deep else width
    half, quarter = width // 2, width // 4
    held = [[each[name] for name in SAVED] for each in kept]
    scratch = [pltpu.SemaphoreType.DMA((3, 2))] * 8
    scratch += [pltpu.SemaphoreType.DMA((7 + len(SAVED),)), pltpu.SemaphoreType.DMA((2,))]
    scratch += [pltpu.SemaphoreType.DMA((depth, 6))]
    scratch += [pltpu.VMEM((columns, width), BF)] * 3
    scratch += [pltpu.VMEM(each.shape[1:], BF) for each in weights[1:4]]
    for name, each in zip(SAVED, held[0]):
        shape = (length, units) if name in ("g", "slope") else each.shape
        scratch.append(pltpu.VMEM((16, 128) if name in ("o", "o2") else shape, each.dtype))
    scratch += [pltpu.VMEM((length, columns), BF), pltpu.VMEM((length // 2, columns), BF)] * depth
    scratch += [pltpu.VMEM((length, width), BF)] * 2
    scratch += scatter_scratch(length, width) + scatter_scratch(length, width)
    scratch += [
        pltpu.VMEM((512, width), BF),
        pltpu.VMEM((length, units), BF),
        pltpu.VMEM((heads * block, 256), BF),
        pltpu.VMEM((heads * block, columns), BF),
        pltpu.VMEM((length, heads * block), BF),
        pltpu.VMEM((length, heads * block), BF),
        pltpu.VMEM((length, 256), F32),
        pltpu.VMEM((length, columns), F32),
        pltpu.VMEM((length, 512), BF),
        pltpu.VMEM((length, columns), BF),
        pltpu.VMEM((3 * block, width), F32),
        pltpu.VMEM((block, width), F32),
        pltpu.VMEM((2, width, units), BF),
        pltpu.VMEM((width, 4 * columns), BF),
    ]
    out_shape = [
        jax.ShapeDtypeStruct((block, width), F32),
        jax.ShapeDtypeStruct((8 * depth, width), F32),
    ]
    kind = F32 if deep else BF
    out_shape += [jax.ShapeDtypeStruct((part, 4 * columns), kind)] * depth
    out_shape += [jax.ShapeDtypeStruct((2, part, units), kind)] * depth
    out_specs = [vmem_spec()] * 2 + [vmem_spec() if deep else any_spec()] * (2 * depth)
    if deep:
        for _ in range(depth):
            scratch += DpSum.scratch(deep, part, units) + DpSum.scratch(deep, part, units)
            scratch += DpSum.scratch(deep, part, 4 * columns)
        vec_shape = (2, 2, 2, deep, 8 * depth, width)
        scratch += [
            pltpu.VMEM((2, block, width), BF),
            pltpu.VMEM((2, block, width), BF),
            pltpu.VMEM((block, width), BF),
            pltpu.VMEM((2, half, half), BF),
            pltpu.VMEM((2, quarter, half), BF),
            pltpu.VMEM((2, deep - 1, quarter // deep, half), BF),
            pltpu.VMEM((2, 2, width, half), BF),
            pltpu.VMEM(vec_shape, BF),
            pltpu.SemaphoreType.DMA((LADDER_COPIES,)),
            pltpu.SemaphoreType.DMA((LADDER_COPIES,)),
        ]
        out_shape += [
            jax.ShapeDtypeStruct((2, 2, width, half), BF),
            jax.ShapeDtypeStruct(vec_shape, BF),
        ]
        out_specs += [any_spec(), any_spec()]

    def kernel(*refs):
        backward_kernel(depth, heads, deep, refs)

    operands = [cotangent, gains, lengths, *tables]
    in_specs = [vmem_spec()] * len(operands)
    remote = [*joined, grad_all, *weights, *[each for layer in held for each in layer]]
    in_specs += [any_spec()] * len(remote)
    return pl.pallas_call(
        kernel,
        out_shape=out_shape,
        in_specs=in_specs,
        out_specs=out_specs,
        scratch_shapes=scratch,
        compiler_params=pltpu.CompilerParams(
            collective_id=9, has_side_effects=True, vmem_limit_bytes=LIMIT
        ),
        name="layers_backward",
    )(*operands, *remote)


def finish_kernel(depth, refs):
    (low_ref, wself_ref, sum_ref, vec_ref) = refs[:4]
    attn_refs = refs[4 : 4 + depth]
    feed_refs = refs[4 + depth : 4 + 2 * depth]
    (tokens_ref, gain_ref, bias_ref, bada_ref, bdown_ref) = refs[4 + 2 * depth : 9 + 2 * depth]
    (qkv_ref, out_ref, ada_ref, up_ref, down_ref, self_ref, picked) = refs[9 + 2 * depth :]
    step = pl.program_id(0)
    members = vec_ref.shape[0] // (8 * depth)
    width = vec_ref.shape[1]

    def pick(row):
        device = lax.broadcasted_iota(jnp.int32, (members, vec_ref.shape[0]), 0)
        column = lax.broadcasted_iota(jnp.int32, (members, vec_ref.shape[0]), 1)
        wanted = (column == device * 8 * depth + row).astype(F32).astype(BF)
        return dot(wanted, vec_ref[...]).astype(BF)

    rows = ada_ref.shape[1]

    @pl.when(step == 0)
    def _():
        picked[2 * depth] = pick(5)
        for layer in range(depth):
            for place in range(2):
                picked[2 * layer + place] = pick(8 * layer + place)

    device = lax.broadcasted_iota(jnp.int32, (width, rows), 0)
    column = lax.broadcasted_iota(jnp.int32, (width, rows), 1)
    chosen = (device == column + step * rows).astype(F32).astype(BF)
    times = dot(picked[2 * depth], chosen).astype(BF)
    for layer in range(depth):
        for place in range(2):
            ada_ref[layer, :, place * width : (place + 1) * width] = dot(
                times, picked[2 * layer + place], TN
            )
    self_ref[:, : width // 2] = sum_ref[0].astype(F32)
    self_ref[:, width // 2 :] = sum_ref[1].astype(F32)

    @pl.when(step == 0)
    def _():
        row = lax.broadcasted_iota(jnp.int32, (8 * depth, vec_ref.shape[0]), 0)
        column = lax.broadcasted_iota(jnp.int32, (8 * depth, vec_ref.shape[0]), 1)
        ones = (column % (8 * depth) == row).astype(F32).astype(BF)
        totals = dot(ones, vec_ref[...])
        for layer in range(depth):
            here = slice(layer, layer + 1)
            base = 8 * layer
            bada_ref[here, :width] = totals[base : base + 1]
            bada_ref[here, width:] = totals[base + 1 : base + 2]
            gain_ref[here, :] = totals[base + 2 : base + 3]
            bias_ref[here, :] = totals[base + 3 : base + 4]
            bdown_ref[here, :] = totals[base + 4 : base + 5]

    @pl.when(step == 1)
    def _():
        tokens_ref[...] = dot(low_ref[...].astype(BF), wself_ref[...], NT)

    @pl.when(step == 2)
    def _():
        for layer in range(depth):
            grads = attn_refs[layer][...]
            columns = grads.shape[1] // 4
            for place in range(3):
                qkv_ref[layer, place] = grads[:, place * columns : (place + 1) * columns]
            out_ref[layer] = grads[:, 3 * columns :].T

    @pl.when(step == 3)
    def _():
        for layer in range(depth):
            up_ref[layer] = feed_refs[layer][0]
            down_ref[layer] = feed_refs[layer][1]


def finish(depth, low, w_self, sums, vectors, attn_shards, feed_shards):
    block, width = low.shape
    part, columns = attn_shards[0].shape
    columns //= 4
    units = feed_shards[0].shape[2]
    steps = 4
    rows = 2 * width // steps

    def fixed(*shape):
        return pl.BlockSpec(shape, lambda step: (0,) * len(shape))

    def kernel(*refs):
        finish_kernel(depth, refs)

    fixed_shapes = [
        (block, width),
        (depth, width),
        (depth, width),
        (depth, 2 * width),
        (depth, width),
        (depth, 3, part, columns),
        (depth, columns, part),
    ]
    shard = (depth, part, units)
    return pl.pallas_call(
        kernel,
        grid=(steps,),
        out_shape=[
            *[jax.ShapeDtypeStruct(each, F32) for each in fixed_shapes],
            jax.ShapeDtypeStruct((depth, width, 2 * width), F32),
            jax.ShapeDtypeStruct(shard, F32),
            jax.ShapeDtypeStruct(shard, F32),
            jax.ShapeDtypeStruct((2 * width, width), F32),
        ],
        in_specs=[
            fixed(block, width),
            fixed(width, width),
            pl.BlockSpec((None, 2, rows, width // 2), lambda step: (step // 2, 0, step % 2, 0)),
            fixed(*vectors.shape),
            *[fixed(*each.shape) for each in attn_shards],
            *[fixed(*each.shape) for each in feed_shards],
        ],
        out_specs=[
            *[fixed(*each) for each in fixed_shapes],
            pl.BlockSpec((depth, width // steps, 2 * width), lambda step: (0, step, 0)),
            fixed(*shard),
            fixed(*shard),
            pl.BlockSpec((rows, width), lambda step: (step, 0)),
        ],
        scratch_shapes=[
            pltpu.VMEM((2 * depth + 1, vectors.shape[0] // (8 * depth), width), BF)
        ],
        compiler_params=pltpu.CompilerParams(vmem_limit_bytes=LIMIT),
        name="write_grads",
    )(low, w_self, sums, vectors, *attn_shards, *feed_shards)


def local(
    tokens,
    cotangent,
    lengths,
    timesteps,
    w_self,
    ln_gain,
    ln_bias,
    w_qkv,
    w_out,
    w_ada,
    b_ada,
    w_up,
    w_down,
    b_down,
):
    width = tokens.shape[1]
    depth = w_qkv.shape[0]
    heads = w_qkv.shape[3] // HD
    deep = 4 if lax.axis_size("dp") == 8 else 0
    weights = (jnp.swapaxes(w_qkv, 2, 3), w_out, w_up, w_down, w_ada)
    vectors = (ln_gain, ln_bias, b_down, b_ada, lengths, timesteps)
    made, kept = forward(heads, tokens, cotangent, w_self, vectors, weights)
    (activations, estimate, conds, cosine, sine, temb, grad_all) = made
    made = backward(
        heads,
        deep,
        cotangent,
        grad_all,
        ln_gain,
        lengths,
        (cosine, sine, temb, conds),
        weights,
        kept,
        (tokens, estimate),
    )
    grad_rows, smalls = made[:2]
    attn_shards = made[2 : 2 + depth]
    feed_shards = made[2 + depth : 2 + 2 * depth]
    if deep:
        sums, vectors = made[2 + 2 * depth :]
        vectors = vectors.reshape(-1, width)
    else:
        attn_shards = [
            lax.psum_scatter(each, "dp", scatter_dimension=0, tiled=True).astype(F32)
            for each in attn_shards
        ]
        feed_shards = [
            lax.psum_scatter(each, "dp", scatter_dimension=1, tiled=True).astype(F32)
            for each in feed_shards
        ]
        joined = jnp.concatenate([tokens, estimate], axis=1)
        sums = lax.psum(dot(joined, grad_rows.astype(BF), TN).astype(BF), ("dp", "tensor"))
        sums = sums.reshape(2, width, 2, width // 2).swapaxes(1, 2)
        vectors = smalls.at[5].set(temb[0]).astype(BF)
        vectors = lax.all_gather(vectors, ("dp", "tensor"), axis=0, tiled=True)
    made = finish(depth, grad_rows, w_self, sums, vectors, attn_shards, feed_shards)
    (grad_tokens, gain, bias, bias_ada, bias_down, qkv, out, ada, up, down, own) = made
    return (
        activations,
        grad_tokens,
        gain,
        bias,
        qkv,
        out,
        ada,
        bias_ada,
        up,
        jnp.swapaxes(down, 1, 2),
        bias_down,
        own,
    )


def solution(mesh):
    return jax.shard_map(
        local,
        mesh=mesh,
        in_specs=(
            P(("dp", "tensor"), None),
            P(("dp", "tensor"), None),
            P("dp", None),
            P("dp", None),
            P(),
            P(),
            P(),
            P(None, None, None, "tensor"),
            P(None, "tensor", None),
            P(),
            P(),
            P(None, None, "tensor"),
            P(None, "tensor", None),
            P(),
        ),
        out_specs=(
            P(("dp", "tensor"), None),
            P(("dp", "tensor"), None),
            P(),
            P(),
            P(None, None, "dp", "tensor"),
            P(None, "tensor", "dp"),
            P(),
            P(),
            P(None, "dp", "tensor"),
            P(None, "tensor", "dp"),
            P(),
            P(),
        ),
        check_vma=False,
    )
```

```python
import functools

import jax
import jax.numpy as jnp
from jax import lax
from jax.experimental import pallas as pl
from jax.experimental.pallas import tpu as pltpu
from jax.sharding import PartitionSpec as P

HD = 64
HALF = HD // 2
BF = jnp.bfloat16
F32 = jnp.float32
MESH = pl.DeviceIdType.MESH
EPS = 1e-05
LIMIT = 60 << 20

def norm(rows):
    centred = rows - jnp.mean(rows, axis=-1, keepdims=True)
    rstd = lax.rsqrt(jnp.mean(centred * centred, axis=-1, keepdims=True) + EPS)
    return (centred * rstd, rstd)


def norm_back(grad, hat, rstd):
    return rstd * (
        grad
        - jnp.mean(grad, axis=-1, keepdims=True)
        - hat * jnp.mean(grad * hat, axis=-1, keepdims=True)
    )


def dot(left, right, dims=((1,), (0,))):
    return lax.dot_general(left, right, (dims, ((), ())), preferred_element_type=F32)


NT = ((1,), (1,))
TN = ((0,), (0,))


def head_mask(head, columns, rotary):
    lane = lax.broadcasted_iota(jnp.int32, (1, columns), 1)
    if rotary:
        return (lane % 128) // HALF == head
    return lane // HD == head


def keep_head(rows, head, rotary):
    return jnp.where(head_mask(head, rows.shape[1], rotary), rows, jnp.zeros_like(rows))


def turned_place(columns, start, total):
    row = lax.broadcasted_iota(jnp.int32, (256, total), 0)
    column = lax.broadcasted_iota(jnp.int32, (256, total), 1) - start
    source = column // HD * HALF + column % HD // HALF * 128 + column % HALF
    fits = (source == row) & (column >= 0) & (column < columns)
    return fits.astype(F32).astype(BF)


def plain_place(columns, start, total):
    row = lax.broadcasted_iota(jnp.int32, (columns, total), 0)
    column = lax.broadcasted_iota(jnp.int32, (columns, total), 1) - start
    return (row == column).astype(F32).astype(BF)


def span(start, size):
    return pl.ds(pl.multiple_of(start, size), size)


class Gather:
    def __init__(self, sems, ids, rows):
        self.sems, self.ids, self.rows = sems, ids, rows
        self.half = rows.shape[0] // 8

    def copy(self, src, dst, kind, part, far):
        send, recv = self.sems
        return pltpu.make_async_remote_copy(
            src_ref=self.rows.at[span(src, self.half)],
            dst_ref=self.rows.at[span(dst, self.half)],
            send_sem=send.at[kind, part],
            recv_sem=recv.at[kind, part],
            device_id=self.ids[1] if far else self.ids[0],
            device_id_type=MESH,
        )

    def own(self, part):
        return span(2 * self.half * part, self.half)

    def pair(self, part):
        return 6 * self.half - 2 * self.half * part

    def far_copy(self, part):
        return self.copy(2 * self.half * part, self.pair(part), 0, part, True)

    def sibling_copy(self, part):
        start = 2 * self.half * part
        return self.copy(start, start + self.half, 1, part, False)

    def forward_copy(self, part):
        return self.copy(self.pair(part), self.pair(part) + self.half, 2, part, False)

    def send(self, part):
        self.far_copy(part).start()
        self.sibling_copy(part).start()

    def near(self, part):
        self.sibling_copy(part).wait_recv()

    def arrive(self, part):
        self.far_copy(part).wait_recv()
        self.forward_copy(part).start()

    def settle(self, part):
        self.forward_copy(part).wait()

    def far(self, part):
        self.arrive(part)
        self.settle(part)

    def receive(self, step):
        @pl.when(step < 2)
        def _():
            self.near(step)

        @pl.when(step >= 2)
        def _():
            self.far(step - 2)

    def finish(self, far=True):
        for part in range(2):
            self.sibling_copy(part).wait_send()
            if far:
                self.far_copy(part).wait_send()


class Scatter:
    def __init__(self, sems, ids, own, buffers):
        self.sems, self.ids, self.own_sum = sems, ids, own
        self.pair_out, self.pair_in, self.own_out, self.own_in, self.far_out, self.far_in = buffers
        self.half = self.pair_out.shape[1]

    def copy(self, src, dst, kind, part, far):
        send, recv = self.sems
        return pltpu.make_async_remote_copy(
            src_ref=src.at[part],
            dst_ref=dst.at[part],
            send_sem=send.at[kind, part],
            recv_sem=recv.at[kind, part],
            device_id=self.ids[1] if far else self.ids[0],
            device_id_type=MESH,
        )

    def pair_copy(self, part):
        return self.copy(self.pair_out, self.pair_in, 0, part, False)

    def own_copy(self, part):
        return self.copy(self.own_out, self.own_in, 1, part, False)

    def sum_copy(self, part):
        return self.copy(self.far_out, self.far_in, 2, part, True)

    def send(self, unit, total):
        @pl.when(unit < 2)
        def _():
            self.own_sum[span(self.half * unit, self.half), :] = total[: self.half, :]
            self.own_out[unit] = total[self.half :, :].astype(BF)
            self.own_copy(unit).start()

        @pl.when(unit >= 2)
        def _():
            part = 3 - unit
            self.pair_out[part] = total[self.half :, :].astype(BF)
            self.pair_copy(part).start()
            self.pair_copy(part).wait_recv()
            self.far_out[part] = (
                total[: self.half, :] + self.pair_in[part].astype(F32)
            ).astype(BF)
            self.sum_copy(part).start()

    def collect(self, part):
        self.own_copy(part).wait_recv()
        self.sum_copy(part).wait_recv()
        rows = pl.ds(part * self.half, self.half)
        made = self.own_sum[rows, :] + self.own_in[part].astype(F32)
        return made + self.far_in[part].astype(F32)

    def finish(self):
        for part in range(2):
            self.pair_copy(part).wait_send()
            self.own_copy(part).wait_send()
            self.sum_copy(part).wait_send()


class Near:
    def __init__(self, sems, ids, own, out, into):
        self.sems, self.ids = sems, ids
        self.own, self.out, self.into = own, out, into
        self.half = out.shape[1]

    def copy(self, part):
        return pltpu.make_async_remote_copy(
            src_ref=self.out.at[part],
            dst_ref=self.into.at[part],
            send_sem=self.sems.at[0, part],
            recv_sem=self.sems.at[1, part],
            device_id=self.ids[0],
            device_id_type=MESH,
        )

    def send(self, part, total):
        self.own[span(self.half * part, self.half), :] = total[: self.half, :]
        self.out[part] = total[self.half :, :].astype(BF)
        self.copy(part).start()

    def collect(self, part):
        self.copy(part).wait_recv()
        return self.own[pl.ds(part * self.half, self.half), :] + self.into[part].astype(F32)

    def drain(self):
        for part in range(2):
            self.copy(part).wait_send()


class Fetch:
    def __init__(self, sems, ids, square, shards):
        self.sems, self.shards = sems, shards
        self.far = ids[1]
        self.x, self.z, self.x_peer, self.z_peer = square
        self.piece = shards.shape[1] // 8

    def copy(self, index, src, start, size, device):
        place = span(start * self.piece, size * self.piece)
        return pltpu.make_async_remote_copy(
            src_ref=self.shards.at[src, place],
            dst_ref=self.shards.at[1, place],
            send_sem=self.sems.at[0, index],
            recv_sem=self.sems.at[1, index],
            device_id=device,
            device_id_type=MESH,
        )

    def hop(self, index):
        x_first = 2 * self.z + self.x
        z_first = 4 + 2 * self.x + self.z
        return (
            lambda: self.copy(0, 0, x_first, 1, self.far),
            lambda: self.copy(1, 0, z_first, 1, self.far),
            lambda: self.copy(2, 1, x_first, 1, self.x_peer),
            lambda: self.copy(3, 1, z_first, 1, self.z_peer),
            lambda: self.copy(4, 1, 2 * self.z, 2, self.z_peer),
            lambda: self.copy(5, 1, 4 + 2 * self.x, 2, self.x_peer),
        )[index]()

    def step(self, count):
        if count == 1:
            self.hop(0).start()
            self.hop(1).start()
        elif count < 4:
            for index in (2 * count - 4, 2 * count - 3):
                self.hop(index).wait_recv()
                self.hop(index + 2).start()
        else:
            self.hop(4).wait_recv()
            self.hop(5).wait_recv()

    def finish(self):
        for index in range(6):
            self.hop(index).wait_send()


def square():
    group = lax.axis_index("dp")
    place = lax.axis_index("tensor")
    x = lax.rem(group, 2)
    z = lax.rem(group // 2, 2)
    return (x, z, (group + 1 - 2 * x, place), (group + 2 - 4 * z, place))


def neighbours():
    group = lax.axis_index("dp")
    place = lax.axis_index("tensor")
    core = lax.rem(place, 2)
    return ((group, place + 1 - 2 * core), (group, lax.rem(place + 2, 4)))


class Spot:
    def __init__(self, deep):
        group = lax.axis_index("dp")
        self.place = lax.axis_index("tensor")
        self.deep = deep
        self.z = group // 2
        self.x = lax.rem(group, 2)
        self.across = (2 * self.z + 1 - self.x, self.place)

    def level(self, ahead):
        return lax.rem(self.z + ahead, self.deep)

    def along(self, ahead):
        return (2 * self.level(ahead) + self.x, self.place)

    def partners(self):
        return [self.across] + [self.along(ahead) for ahead in range(1, self.deep)]


def meet(ids):
    barrier = pltpu.get_barrier_semaphore()
    for device in ids:
        pl.semaphore_signal(barrier, inc=1, device_id=device, device_id_type=MESH)
    pl.semaphore_wait(barrier, len(ids))


class DpSum:
    def __init__(self, spot, src, out, scratch):
        self.spot, self.src, self.out = spot, src, out
        self.pairs, self.rest, self.sems = scratch
        self.block = self.pairs.shape[1]

    @staticmethod
    def scratch(deep, block, columns):
        return [
            pltpu.VMEM((deep, block, columns), BF),
            pltpu.VMEM((deep - 1, block, columns), BF),
            pltpu.SemaphoreType.DMA((4, deep)),
        ]

    def rows(self, ahead, x):
        start = (2 * self.spot.level(ahead) + x) * self.block
        return pl.ds(pl.multiple_of(start, self.block), self.block)

    def x_copy(self, ahead):
        return pltpu.make_async_remote_copy(
            src_ref=self.src.at[self.rows(ahead, 1 - self.spot.x)],
            dst_ref=self.pairs.at[ahead],
            send_sem=self.sems.at[0, ahead],
            recv_sem=self.sems.at[1, ahead],
            device_id=self.spot.across,
            device_id_type=MESH,
        )

    def z_copy(self, ahead):
        return pltpu.make_async_remote_copy(
            src_ref=self.pairs.at[ahead],
            dst_ref=self.rest.at[ahead - 1],
            send_sem=self.sems.at[2, ahead],
            recv_sem=self.sems.at[3, ahead],
            device_id=self.spot.along(ahead),
            device_id_type=MESH,
        )

    def order(self):
        return [*range(1, self.spot.deep), 0]

    def start(self):
        for ahead in self.order():
            self.x_copy(ahead).start()

    def middle(self):
        for ahead in self.order():
            self.x_copy(ahead).wait_recv()
            total = self.src[self.rows(ahead, self.spot.x), :].astype(F32)
            total = total + self.pairs[ahead].astype(F32)
            if ahead:
                self.pairs[ahead] = total.astype(BF)
                self.z_copy(ahead).start()
            else:
                self.out[...] = total
        for ahead in self.order():
            self.x_copy(ahead).wait_send()

    def end(self):
        for ahead in range(1, self.spot.deep):
            self.z_copy(ahead).wait_recv()
        total = self.out[...]
        for ahead in range(1, self.spot.deep):
            total = total + self.rest[ahead - 1].astype(F32)
        self.out[...] = total
        for ahead in range(1, self.spot.deep):
            self.z_copy(ahead).wait_send()


def scatter_scratch(rows, width):
    return [pltpu.VMEM((2, rows // 8, width), BF)] * 6


def gelu_parts(hidden):
    cdf = 0.5 * (1.0 + lax.erf(hidden * (0.5**0.5)))
    density = jnp.exp(hidden * hidden * -0.5) * 0.3989422804014327
    return (hidden * cdf, cdf + hidden * density)


def load_turned(wq, wk, wqk):
    turn = turned_place(wq.shape[0], 0, wq.shape[0])
    wqk[:256, :] = dot(turn, wq[...]).astype(BF)
    wqk[256:, :] = dot(turn, wk[...]).astype(BF)


def is_packed(lengths_ref, length):
    return (lengths_ref[:, 0:1] < length).astype(jnp.int32).astype(F32)


def owner(chunk):
    return 2 * (chunk // 4) + chunk % 2


def apart(keys, queries, packed):
    return (keys != queries).astype(jnp.int32).astype(F32) * (packed * -1e9)


def unit_owner(unit, half):
    return jnp.where(unit < 2, 0, 2) + half


SAVED = ("a", "q", "k", "v", "o", "o2", "x1", "m", "g", "slope", "x", "lse")


def forward_kernel(depth, heads, refs):
    refs = list(refs)

    def take(count):
        made = refs[:count]
        del refs[:count]
        return made

    (gain_ref, bias_ref, bdown_ref, bada_ref, lengths_ref, steps_ref) = take(6)
    (rotary_ref, time_ref, cot_ref) = take(3)
    (tokens_hbm, wself_hbm, wqkv_hbm, wout_hbm, wup_hbm, wdown_hbm, wada_hbm) = take(7)
    (acts_ref, est_ref, cond_ref, cos_ref, sin_ref, temb_ref, grad_hbm) = take(7)
    saved_hbm = [dict(zip(SAVED, take(len(SAVED)))) for _ in range(depth)]
    gather_sems = [take(2) for _ in range(5)]
    (near_a_sems, near_f_sems, fetch_sems, cross_send, cross_recv) = take(5)
    (load_sems, store_sems) = take(2)
    (tokens, wself, wada) = take(3)
    wa, wu, wd, wqk = take(depth), take(depth), take(depth), take(depth)
    abufs, mbufs, (ebuf,) = take(2), take(2), take(1)
    (q2, k2, v2, ob2, lse2, accs, stats, gb, gpb) = take(9)
    (x1, xb, start, own_a, own_f, sums) = take(6)
    near_a_bufs, near_f_bufs = take(2), take(2)
    ids = neighbours()
    corner = square()
    columns = heads * HD
    width = xb.shape[1]
    half = xb.shape[0] // 2
    unit_rows = 2 * half
    length = 8 * half
    part_a = [pl.ds(part * columns, columns) for part in range(4)]
    sources = [tokens_hbm, wself_hbm.at[0], wself_hbm.at[1]]
    places = [tokens, wself.at[0], wself.at[1]]
    for layer in range(depth):
        sources += [wqkv_hbm.at[layer, part] for part in range(3)] + [wout_hbm.at[layer]]
        places += [wa[layer].at[0, rows] for rows in part_a]
        sources += [wup_hbm.at[layer], wdown_hbm.at[layer]]
        places += [wu[layer].at[0], wd[layer].at[0]]
    loads = [
        pltpu.make_async_copy(src, dst, load_sems.at[i])
        for i, (src, dst) in enumerate(zip(sources, places))
    ]
    ada_loads = [
        pltpu.make_async_copy(wada_hbm.at[layer], wada, load_sems.at[len(loads)])
        for layer in range(depth)
    ]
    order = [0, 1, *range(3, 9)]
    for i in order:
        loads[i].start()
    ada_loads[0].start()
    for i in range(len(loads)):
        if i not in order:
            loads[i].start()
    meet([*ids, *corner[2:]])
    fetches = []
    for layer in range(depth):
        for shards in (wa[layer], wu[layer], wd[layer]):
            fetches.append(Fetch(fetch_sems.at[len(fetches)], ids, corner, shards))
    gathers = [Gather(gather_sems[i], ids, abufs[i]) for i in range(2)]
    mixes = [Gather(gather_sems[2 + i], ids, mbufs[i]) for i in range(2)]
    grads = Gather(gather_sems[4], ids, ebuf)
    near_a = Near(near_a_sems, ids, own_a, *near_a_bufs)
    near_f = Near(near_f_sems, ids, own_f, *near_f_bufs)
    packed = is_packed(lengths_ref, length)
    pending = []

    def store(name, src, dst):
        made = pltpu.make_async_copy(src, dst, store_sems.at[len(pending)])
        made.start()
        pending.append([name, made, False])

    def stored(*names):
        for each in pending:
            if each[0] in names and not each[2]:
                each[1].wait()
                each[2] = True

    def begin(number, part, made):
        layer = number % depth
        rows = pl.ds(part * half, half)
        if number >= 2 and part == 0:
            gathers[number % 2].finish()
        xb[rows, :] = made
        hat = norm(made)[0]
        gain = gain_ref[layer : layer + 1, :]
        normed = hat * gain + bias_ref[layer : layer + 1, :]
        abufs[number % 2][pl.ds(2 * half * part, half), :] = normed.astype(BF)
        gathers[number % 2].send(part)

    for i in (3, 4, 5, 6):
        loads[i].wait()
    fetches[0].step(1)
    loads[0].wait()
    loads[1].wait()
    for part in range(2):
        rows = pl.ds(part * half, half)
        made = dot(tokens[rows, :], wself[0])
        start[rows, :] = made
        begin(0, part, made)

    def make_tables():
        place = lax.axis_index("tensor")
        sibling = ids[0][1]
        far = ids[1][1]
        far_other = lax.rem(sibling + 2, 4)
        row = lax.broadcasted_iota(jnp.int32, (half, 128), 0).astype(F32)
        for chunk, (block, part) in enumerate(
            zip(
                (place, sibling, place, sibling, far, far_other, far, far_other),
                (0, 0, 1, 1, 1, 1, 0, 0),
            )
        ):
            rows = pl.ds(chunk * half, half)
            offset = (block * unit_rows).astype(F32)
            position = row + part * half + (1.0 - packed) * offset
            angle = position * rotary_ref[...]
            cos_ref[rows, :] = jnp.cos(angle)
            sin_ref[rows, :] = jnp.sin(angle)
        steps = steps_ref[...].astype(F32)
        slot = lax.broadcasted_iota(jnp.int32, steps.shape, 1)
        mine = jnp.sum(jnp.where(slot == place, steps, 0.0), axis=1, keepdims=True)
        step = packed * mine + (1.0 - packed) * steps[:, 0:1]
        angle = jnp.broadcast_to(step * time_ref[...], (8, width // 2))
        temb_ref[:, : width // 2] = jnp.cos(angle)
        temb_ref[:, width // 2 :] = jnp.sin(angle)

    def make_cond(layer):
        ada_loads[layer].wait()
        column = temb_ref[...].T[:, 0:1]
        made = jnp.sum(wada[...] * column, axis=0, keepdims=True)
        made = made + bada_ref[layer : layer + 1, :]
        cond_ref[8 * layer : 8 * layer + 8, :] = jnp.broadcast_to(made, (8, 2 * width))
        if layer + 1 < depth:
            ada_loads[layer + 1].start()

    def project(number, count, pick, before):
        layer = number % depth
        abuf = abufs[number % 2]

        def body(step, carry):
            before(step)
            shard, unit = pick(step)
            rows = span(unit * unit_rows, unit_rows)
            normed = abuf[rows, :]
            mixed = dot(normed, wqk[layer][shard], NT)
            cosine = cos_ref[rows, :]
            sine = sin_ref[rows, :]
            for place, dst, scale in ((0, q2, HD**-0.5), (256, k2, 1.0)):
                first = mixed[:, place : place + 128]
                second = mixed[:, place + 128 : place + 256]
                dst[shard, rows, :128] = ((first * cosine - second * sine) * scale).astype(BF)
                dst[shard, rows, 128:] = ((second * cosine + first * sine) * scale).astype(BF)
            v2[shard, rows, :] = dot(normed, wa[layer][shard, part_a[2], :], NT).astype(BF)
            return carry

        lax.fori_loop(0, count, body, 0)

    lane = lax.broadcasted_iota(jnp.int32, (1, 128), 1)

    def scores_of(shard, unit, head, keys):
        rows = span(unit * unit_rows, unit_rows)
        made = dot(keep_head(q2[shard, rows, :], head, True), k2[shard, keys, :], NT)
        part = lax.broadcasted_iota(jnp.int32, (2, 1, length // 2), 0)
        chunk = lax.broadcasted_iota(jnp.int32, (2, 1, length // 2), 2) // half
        neg = apart(owner(chunk + keys.start // half), part, packed.reshape(1, 1, 1))
        return (made.reshape(2, half, length // 2) + neg).reshape(unit_rows, length // 2)

    def attend_near(number, count, pick, before):
        keys = pl.ds(0, length // 2)

        def body(step, carry):
            before(step)
            shard, unit = pick(step)
            place = 2 * unit + shard
            attended = jnp.zeros((unit_rows, columns), F32)
            tops = jnp.zeros((unit_rows, 128), F32)
            totals = jnp.zeros((unit_rows, 128), F32)
            for head in range(heads):
                scores = scores_of(shard, unit, head, keys)
                largest = jnp.max(scores, axis=-1, keepdims=True)
                shares = jnp.exp(scores - largest)
                output = dot(shares.astype(BF), v2[shard, keys, :])
                attended = jnp.where(head_mask(head, columns, False), output, attended)
                tops = jnp.where(lane == head, largest, tops)
                totals = jnp.where(lane == head, jnp.sum(shares, axis=-1, keepdims=True), totals)
            accs[place] = attended
            stats[place, 0] = tops
            stats[place, 1] = totals
            return carry

        lax.fori_loop(0, count, body, 0)

    def attend_far(number, save, count, pick, before):
        keys = pl.ds(length // 2, length // 2)
        layer, slot = number % depth, number % 2

        def body(step, carry):
            before(step)
            shard, unit = pick(step)
            place = 2 * unit + shard
            rows = span(unit * unit_rows, unit_rows)
            attended = jnp.zeros((unit_rows, columns), F32)
            logs = jnp.zeros((unit_rows, 128), F32)
            for head in range(heads):
                scores = scores_of(shard, unit, head, keys)
                earlier = stats[place, 0][:, head : head + 1]
                largest = jnp.maximum(earlier, jnp.max(scores, axis=-1, keepdims=True))
                shares = jnp.exp(scores - largest)
                shrink = jnp.exp(earlier - largest)
                totals = stats[place, 1][:, head : head + 1] * shrink
                totals = totals + jnp.sum(shares, axis=-1, keepdims=True)
                output = dot(shares.astype(BF), v2[shard, keys, :])
                output = (accs[place] * shrink + output) * (1.0 / totals)
                attended = jnp.where(head_mask(head, columns, False), output, attended)
                if save:
                    logs = jnp.where(lane == head, largest + jnp.log(totals), logs)
            if save:
                lse2[slot, shard, unit] = logs.T[:8, :]
            attended = attended.astype(BF)
            ob2[slot, shard, rows, :] = attended

            @pl.when(shard == 1)
            def _():
                total = dot(ob2[slot, 0, rows, :], wa[layer][0, part_a[3], :])
                near_a.send(unit, total + dot(attended, wa[layer][1, part_a[3], :]))

            return carry

        lax.fori_loop(0, count, body, 0)

    def feed(number, save, pick, before):
        layer = number % depth
        mbuf = mbufs[number % 2]

        def body(step, carry):
            before(step)
            shard, unit = pick(step)
            rows = span(unit * unit_rows, unit_rows)
            hidden = dot(mbuf[rows, :], wu[layer][shard])
            gated, slope = gelu_parts(hidden)
            gated = gated.astype(BF)
            made = dot(gated, wd[layer][shard])

            @pl.when(shard == 0)
            def _():
                if save:
                    gb[rows, :] = gated
                    gpb[rows, :] = slope.astype(BF)
                sums[rows, :] = made

            @pl.when(shard == 1)
            def _():
                near_f.send(unit, sums[rows, :] + made)

            return carry

        lax.fori_loop(0, 4, body, 0)

    crossings = {}

    def cross(number):
        slot = number % 2
        made = []
        for part in range(2):
            made.append(
                pltpu.make_async_remote_copy(
                    src_ref=lse2.at[slot, 1, part],
                    dst_ref=lse2.at[slot, 0, 3 - part],
                    send_sem=cross_send.at[2 * slot + part],
                    recv_sem=cross_recv.at[2 * slot + part],
                    device_id=ids[1],
                    device_id_type=MESH,
                )
            )
            made[-1].start()
        crossings[number] = made

    def late(number):
        slot = number % 2
        saved = saved_hbm[number % depth]
        for part in range(2):
            mixes[slot].far(part)
        store("m", mbufs[slot], saved["m"])
        for each in crossings[number]:
            each.wait_recv()
        store("lse", lse2.at[slot, 0], saved["lse"])

    def events(table):
        def before(step):
            for when, actions in table.items():

                @pl.when(step == when)
                def _():
                    for action in actions:
                        if isinstance(action, tuple):
                            if action[0] < len(fetches):
                                fetches[action[0]].step(action[1])
                        else:
                            action()

        return before

    def waits(*indices):
        def action():
            for index in indices:
                loads[index].wait()

        return action

    def by_unit(step):
        return (lax.rem(step, 2), step // 2)

    def by_shard(step):
        return (step // 2, lax.rem(step, 2))

    def run(number, after_layer):
        layer, slot = number % depth, number % 2
        save = number >= depth
        group, mix = gathers[slot], mixes[slot]
        mix_rows = mbufs[slot]
        base = 3 * layer

        def after_attend(part):
            def action():
                if part == 0 and number >= 2:
                    mix.finish(far=False)
                if part == 0:
                    stored("x1")
                rows = pl.ds(part * half, half)
                after = xb[rows, :] + near_a.collect(part)
                x1[rows, :] = after
                shift = cond_ref[8 * layer : 8 * layer + 1, :width]
                scale = cond_ref[8 * layer : 8 * layer + 1, width:]
                made = norm(after)[0] * (1.0 + scale) + shift
                mix_rows[pl.ds(2 * half * part, half), :] = made.astype(BF)
                mix.sibling_copy(part).start()
                if number == 2 * depth - 1:
                    mix.far_copy(part).start()

            return action

        def after_feed(part):
            def action():
                if part == 0:
                    stored("x")
                rows = pl.ds(part * half, half)
                made = x1[rows, :] + near_f.collect(part) + bdown_ref[layer : layer + 1, :]
                after_layer(part, rows, made)

            return action

        def near_rows(part):
            return lambda: group.near(part)

        def far_rows(part):
            return lambda: group.far(part)

        def mixed(part):
            return lambda: mix.near(part)

        if number:
            near_a.drain()
            near_f.drain()
        stored("q", "k", "v")

        def turn(shard):
            rows = wa[layer].at[shard, part_a[0]], wa[layer].at[shard, part_a[1]]
            load_turned(*rows, wqk[layer].at[shard])

        far_table = {3: [after_attend(0)]}
        feed_table = {
            0: [mixed(0)],
            1: [after_attend(1)],
            2: [mixed(1)],
            3: [after_feed(0)],
        }
        order = by_unit
        if number == 0:
            make_tables()
            turn(0)
            arrive = {
                0: [near_rows(0)],
                1: [near_rows(1)],
                2: [(0, 2), waits(7), (1, 1), far_rows(0)],
                3: [far_rows(1), waits(8), (2, 1)],
            }

            def in_order(step):
                return jnp.where(step < 2, step, 5 - step)

            project(number, 4, lambda step: (0, in_order(step)), events(arrive))
            attend_near(number, 2, lambda step: (0, step), events({1: [(0, 3)]}))
            make_cond(layer)
            first = {1: [(1, 2), waits(9, 10, 11, 12), (3, 1)]}
            attend_far(number, save, 2, lambda step: (0, step), events(first))
            fetches[0].step(4)
            turn(1)
            second = {3: [(1, 3), (2, 2), waits(13), (4, 1)]}
            project(number, 4, lambda step: (1, in_order(step)), events(second))
            attend_near(number, 2, lambda step: (1, step), events({}))
            far_table = {1: [after_attend(0)]}
            attend_far(number, save, 2, lambda step: (1, step), events(far_table))
            feed_table = {
                0: [mixed(0), (2, 3), (3, 2), waits(14), (5, 1)],
                1: [after_attend(1), mixed(1)],
                2: [(1, 4), (2, 4)],
                3: [(3, 3), (4, 2), after_feed(0)],
            }
            order = by_shard
        else:
            own_table = {0: [near_rows(0)], 1: [near_rows(1)]}
            near_table = {3: [lambda: group.arrive(0)]}
            if not save:
                turn(0)
                own_table[0] += [(base + 1, 3)]
                near_table[1] = [(base + 2, 2)]
                own_table[2] = [(base, 4), lambda: turn(1)]
                far_table[0] = [(base + 2, 3)]
                feed_table[0] += [(base + 1, 4)]
                feed_table[1] += [(base + 2, 4)]
            project(number, 4, by_shard, events(own_table))
            attend_near(number, 4, by_unit, events(near_table))
            if not save:
                make_cond(layer)
            if number == depth:
                for part in range(2):
                    grads.near(part)
                    grads.far(part)
                store("grad", ebuf, grad_hbm)
            arrive = {
                0: [lambda: group.settle(0)],
                1: [lambda: group.arrive(1)],
                2: [lambda: group.settle(1)],
            }
            project(number, 4, lambda step: (lax.rem(step, 2), 3 - step // 2), events(arrive))
            if number == depth - 1:
                for part in range(2):
                    ebuf[grads.own(part), :] = cot_ref[pl.ds(part * half, half), :]
                    grads.send(part)
            if number > depth:
                for part in range(2):
                    mixes[(number - 1) % 2].far_copy(part).start()
            if save:
                store("a", abufs[slot], saved_hbm[layer]["a"])
                store("x", xb, saved_hbm[layer]["x"])
                for name, src in (("q", q2), ("k", k2), ("v", v2)):
                    store(name, src.at[0], saved_hbm[layer][name])
            attend_far(number, save, 4, by_unit, events(far_table))
        if save:
            cross(number)
            rows = pl.ds(0, length // 2)
            store("o", ob2.at[slot, 0, rows], saved_hbm[layer]["o"])
            store("o2", ob2.at[slot, 1, rows], saved_hbm[layer]["o2"])
        stored("g", "slope")
        feed(number, save, order, events(feed_table))
        if save:
            store("x1", x1, saved_hbm[layer]["x1"])
            store("g", gb, saved_hbm[layer]["g"])
            store("slope", gpb, saved_hbm[layer]["slope"])
        after_feed(1)()

    def between(part, rows, made):
        estimate = made.astype(BF)
        est_ref[rows, :] = estimate
        begin(depth, part, start[rows, :] + dot(estimate, wself[1]))

    def close(part, rows, made):
        acts_ref[rows, :] = made.astype(BF)

    def enter(number):
        return lambda part, rows, made: begin(number, part, made)

    for number in range(2 * depth):
        if number + 1 == 2 * depth:
            run(number, close)
        elif number + 1 == depth:
            loads[2].wait()
            run(number, between)
        else:
            run(number, enter(number + 1))
    for number in range(depth, 2 * depth):
        late(number)
    for each in gathers:
        each.finish()
    for each in (*mixes, grads):
        each.finish()
    near_a.drain()
    near_f.drain()
    for each in fetches:
        each.finish()
    for each in crossings.values():
        for copy in each:
            copy.wait_send()
    stored("grad", *SAVED)


def any_spec():
    return pl.BlockSpec(memory_space=pl.ANY)


def vmem_spec():
    return pl.BlockSpec(memory_space=pltpu.VMEM)


def forward(heads, tokens, cotangent, w_self, vectors, weights):
    depth = weights[0].shape[0]
    block, width = tokens.shape
    length = 4 * block
    half = block // 2
    columns = heads * HD
    units = weights[2].shape[2]
    lanes = jnp.arange(128) % HALF
    rotary = jnp.exp(-jnp.log(10000.0) * lanes.astype(F32) / HALF)[None]
    halves = jnp.arange(width // 2).astype(F32)
    times = jnp.exp(-jnp.log(10000.0) * halves / (width // 2))[None]
    kept = {
        "a": ((length, width), BF),
        "q": ((length, 256), BF),
        "k": ((length, 256), BF),
        "v": ((length, columns), BF),
        "o": ((length // 2, columns), BF),
        "o2": ((length // 2, columns), BF),
        "x1": ((block, width), F32),
        "m": ((length, width), BF),
        "g": ((length // 2, units), BF),
        "slope": ((length // 2, units), BF),
        "x": ((block, width), F32),
        "lse": ((4, 8, block), F32),
    }
    kept_shapes = [jax.ShapeDtypeStruct(*kept[name]) for name in SAVED]
    out_shape = [
        jax.ShapeDtypeStruct((block, width), BF),
        jax.ShapeDtypeStruct((block, width), BF),
        jax.ShapeDtypeStruct((8 * depth, 2 * width), F32),
        jax.ShapeDtypeStruct((length, 128), F32),
        jax.ShapeDtypeStruct((length, 128), F32),
        jax.ShapeDtypeStruct((8, width), F32),
        jax.ShapeDtypeStruct((length, width), BF),
    ] + kept_shapes * depth
    out_specs = [vmem_spec()] * 6 + [any_spec()] * (1 + depth * len(SAVED))
    dma = pltpu.SemaphoreType.DMA
    scratch = [dma((3, 2))] * 10
    scratch += [dma((2, 2))] * 2 + [dma((3 * depth, 2, 6)), dma((4,)), dma((4,))]
    scratch += [dma((4 + 6 * depth,)), dma((1 + depth * len(SAVED),))]
    scratch += [
        pltpu.VMEM((block, width), BF),
        pltpu.VMEM((2, width, width), BF),
        pltpu.VMEM((width, 2 * width), F32),
    ]
    scratch += [pltpu.VMEM((2, 4 * columns, width), BF)] * depth
    scratch += [pltpu.VMEM((2, width, units), BF)] * depth
    scratch += [pltpu.VMEM((2, units, width), BF)] * depth
    scratch += [pltpu.VMEM((2, 512, width), BF)] * depth
    scratch += [pltpu.VMEM((length, width), BF)] * 5
    scratch += [
        pltpu.VMEM((2, length, 256), BF),
        pltpu.VMEM((2, length, 256), BF),
        pltpu.VMEM((2, length, columns), BF),
        pltpu.VMEM((2, 2, length // 2, columns), BF),
        pltpu.VMEM((2, 2, 4, 8, block), F32),
        pltpu.VMEM((4, block, columns), F32),
        pltpu.VMEM((4, 2, block, 128), F32),
        pltpu.VMEM((length // 2, units), BF),
        pltpu.VMEM((length // 2, units), BF),
    ]
    scratch += [pltpu.VMEM((block, width), F32)] * 5
    scratch += [pltpu.VMEM((2 * block, width), F32)]
    scratch += [pltpu.VMEM((2, half, width), BF)] * 4

    def kernel(*refs):
        forward_kernel(depth, heads, refs)

    operands = [*vectors, rotary, times, cotangent]
    remote = [tokens, w_self.reshape(2, width, width), *weights]
    made = pl.pallas_call(
        kernel,
        out_shape=out_shape,
        in_specs=[vmem_spec()] * len(operands) + [any_spec()] * len(remote),
        out_specs=out_specs,
        scratch_shapes=scratch,
        compiler_params=pltpu.CompilerParams(
            collective_id=1, has_side_effects=True, vmem_limit_bytes=LIMIT
        ),
        name="layers_forward",
    )(*operands, *remote)
    count = len(SAVED)
    saved = [made[7 + count * layer : 7 + count * (layer + 1)] for layer in range(depth)]
    return (made[:7], [dict(zip(SAVED, each)) for each in saved])


class Ladder:
    def __init__(self, sems):
        self.send, self.recv = sems
        self.used = 0
        self.open = []

    def copy(self, src, dst, device):
        made = pltpu.make_async_remote_copy(
            src_ref=src,
            dst_ref=dst,
            send_sem=self.send.at[self.used],
            recv_sem=self.recv.at[self.used],
            device_id=device,
            device_id_type=MESH,
        )
        self.used += 1
        assert self.used <= LADDER_COPIES
        made.start()
        self.open.append(made)
        return made

    def finish(self):
        for each in self.open:
            each.wait_send()


LADDER_COPIES = 34


class Loads:
    def __init__(self, sems):
        self.sems = sems
        self.names = {}

    def add(self, name, sources, buffer):
        self.names[name] = (sources, buffer, len(self.names))
        return buffer

    def copy(self, name, layer):
        sources, buffer, place = self.names[name]
        return pltpu.make_async_copy(sources[layer], buffer, self.sems.at[place])

    def start(self, layer, *names):
        if layer >= 0:
            for name in names:
                self.copy(name, layer).start()

    def wait(self, layer, *names):
        for name in names:
            self.copy(name, layer).wait()


def backward_kernel(depth, heads, deep, refs):
    refs = list(refs)

    def take(count):
        made = refs[:count]
        del refs[:count]
        return made

    cot_ref, gain_ref, lengths_ref, cos_ref, sin_ref, temb_ref, cond_ref = take(7)
    joined_hbm = take(2)
    (grad_hbm,) = take(1)
    wqkv_hbm, wout_hbm, wup_hbm, wdown_hbm, _ = take(5)
    saved_hbm = [dict(zip(SAVED, take(len(SAVED)))) for _ in range(depth)]
    (out_ref, small_ref) = take(2)
    attn_outs, feed_outs = take(depth), take(depth)
    if deep:
        sum_ref, vec_ref = take(2)
    feed_sems, attn_sems = [take(2), take(2)], [take(2), take(2)]
    load_sems, store_sems, out_sems = take(3)
    loads = Loads(load_sems)
    wq, wk, wv = (
        loads.add(name, [wqkv_hbm.at[layer, part] for layer in range(depth)], take(1)[0])
        for part, name in enumerate(("wq", "wk", "wv"))
    )
    wout, wup, wdown = (
        loads.add(name, [src.at[layer] for layer in range(depth)], take(1)[0])
        for name, src in (("wout", wout_hbm), ("wup", wup_hbm), ("wdown", wdown_hbm))
    )
    buffers = dict(zip(SAVED, take(len(SAVED))))
    outs = [take(2) for _ in range(depth)]
    for name in SAVED:
        if name in ("o", "o2"):
            continue
        rows = saved_hbm[0][name].shape[0]
        buffer = buffers[name]
        if rows < buffer.shape[0]:
            buffer = buffer.at[pl.ds(0, rows)]
        loads.add(name, [saved_hbm[layer][name] for layer in range(depth)], buffer)
    abuf, qb, kb, vb, _, _, x1b, mbuf, gb, gpb, xb, lse = (buffers[name] for name in SAVED)
    ebuf, fbuf = take(2)
    feed_bufs, attn_bufs = take(6), take(6)
    (wqk, dhb, qmask, domask, dsb, pb, dkb, dvb, dqk, dvv, work, dxb) = take(12)
    (feed_grads, attn_grads) = take(2)
    ids = neighbours()
    sums = {}
    if deep:
        spot = Spot(deep)
        meet([*ids, *spot.partners()])
        for layer in range(depth):
            for name, src, out in (
                ("up", feed_grads.at[0], feed_outs[layer].at[0]),
                ("down", feed_grads.at[1], feed_outs[layer].at[1]),
                ("attn", attn_grads, attn_outs[layer]),
            ):
                sums[name, layer] = DpSum(spot, src, out, take(3))
        tail_refs = take(10)
        joined = tail_refs[0]
        joined_loads = [
            pltpu.make_async_copy(src, joined.at[i], store_sems.at[i])
            for i, src in enumerate(joined_hbm)
        ]
        for each in joined_loads:
            each.start()
    else:
        meet(ids)
    width = cot_ref.shape[1]
    half = cot_ref.shape[0] // 2
    unit_rows = 2 * half
    total, own, dx1 = (work.at[pl.ds(i * unit_rows, unit_rows)] for i in range(3))
    feed_rows = Gather(feed_sems[0], ids, ebuf)
    feed_sum = Scatter(feed_sems[1], ids, own, feed_bufs)
    attn_rows = Gather(attn_sems[0], ids, fbuf)
    attn_sum = Scatter(attn_sems[1], ids, own, attn_bufs)
    columns = heads * HD
    tiles = width // 256
    top = depth - 1
    packed = is_packed(lengths_ref, 8 * half)
    loads.add("grad", [grad_hbm] * depth, ebuf)
    loads.start(top, "m", "wup", "grad", "wdown", "slope", "x1", "wout", "q", "k", "v", "lse", "g")
    loads.start(top, "wq", "wk", "wv", "a", "x")
    out_loads = []
    out_sends = []
    for layer in range(depth):
        rows = outs[layer][0].at[pl.ds(0, 4 * half)]
        pairs = ((saved_hbm[layer]["o"], rows), (saved_hbm[layer]["o2"], outs[layer][1]))
        out_loads.append(
            [
                pltpu.make_async_copy(src, dst, out_sems.at[layer, 4 + i])
                for i, (src, dst) in enumerate(pairs)
            ]
        )
        out_sends.append(
            [
                pltpu.make_async_remote_copy(
                    src_ref=outs[layer][1].at[pl.ds(part * unit_rows, unit_rows)],
                    dst_ref=outs[layer][0].at[pl.ds((3 - part) * unit_rows, unit_rows)],
                    send_sem=out_sems.at[layer, part],
                    recv_sem=out_sems.at[layer, 2 + part],
                    device_id=ids[1],
                    device_id_type=MESH,
                )
                for part in range(2)
            ]
        )
        for each in out_loads[layer]:
            each.start()

    def send_outs(layer):
        out_loads[layer][1].wait()
        for each in out_sends[layer]:
            each.start()

    send_outs(top)
    dxb[...] = cot_ref[...].astype(F32)
    small_ref[...] = jnp.zeros_like(small_ref)

    def outer(left, right, dst):
        def tile(index, carry):
            place = span(index * 256, 256)
            dst[place, :] = dot(left[:, place], right[...], TN).astype(BF)
            return carry

        lax.fori_loop(0, tiles, tile, 0)

    def turn_back(grad, rows, scale):
        cosine = cos_ref[rows, :]
        sine = sin_ref[rows, :]
        first_half = grad[:, :128]
        second_half = grad[:, 128:]
        return (
            ((first_half * cosine + second_half * sine) * scale).astype(BF),
            ((second_half * cosine - first_half * sine) * scale).astype(BF),
        )

    def event(name, layer, kind):
        if (name, layer) in sums:
            getattr(sums[name, layer], kind)()

    for layer in reversed(range(depth)):
        def note(row, value):
            small_ref[8 * layer + row : 8 * layer + row + 1, :] = value

        note(4, jnp.sum(dxb[...], axis=0, keepdims=True))
        dkb[...] = jnp.zeros_like(dkb)
        dvb[...] = jnp.zeros_like(dvb)
        loads.wait(layer, "m", "wup")

        def expand(step, carry):
            rows = span((3 - step) * unit_rows, unit_rows)
            gated, slope = gelu_parts(dot(mbuf[rows, :], wup[...]))
            gb[rows, :] = gated.astype(BF)
            gpb[rows, :] = slope.astype(BF)
            return carry

        lax.fori_loop(0, 2, expand, 0)
        loads.wait(layer, "wdown", "slope")
        if layer == top:
            loads.wait(layer, "grad")

        def contract(step, carry):
            if layer == top:
                unit = jnp.where(step < 2, 3 - step, step - 2)
            else:
                feed_rows.receive(step)
                unit = jnp.where(step < 2, step, 5 - step)
            rows = span(unit * unit_rows, unit_rows)
            grad = dot(ebuf[rows, :], wdown[...], NT)
            grad = (grad * gpb[rows, :].astype(F32)).astype(BF)
            dhb[rows, :] = grad
            total[...] = dot(grad, wup[...], NT)
            feed_sum.send(unit, total)
            return carry

        lax.fori_loop(0, 4, contract, 0)
        loads.start(layer - 1, "wdown", "slope")
        event("attn", layer + 1, "middle")
        event("up", layer + 1, "end")
        if layer < top:
            attn_rows.finish()
            attn_sum.finish()
        shift_sum = jnp.zeros((1, width), F32)
        scale_sum = jnp.zeros((1, width), F32)
        for part in range(2):
            if part == 0:
                loads.wait(layer, "x1")
                outer(mbuf, dhb, feed_grads.at[0])
                event("up", layer, "start")
            else:
                loads.wait(layer, "g")
                outer(ebuf, gb, feed_grads.at[1])
                event("down", layer, "start")
            rows = pl.ds(part * half, half)
            grad = feed_sum.collect(part)
            hat, rstd = norm(x1b[rows, :])
            shift_sum += jnp.sum(grad, axis=0, keepdims=True)
            scale_sum += jnp.sum(grad * hat, axis=0, keepdims=True)
            after = dxb[rows, :]
            after = after + norm_back(grad * (1.0 + cond_ref[8 * layer : 8 * layer + 1, width:]), hat, rstd)
            dx1[rows, :] = after
            fbuf[attn_rows.own(part), :] = after.astype(BF)
            attn_rows.send(part)
        note(0, shift_sum)
        note(1, scale_sum)
        loads.start(layer - 1, "m", "g", "x1", "wup")
        loads.wait(layer, "wout", "q", "k", "v", "lse")

        def attend(step, carry):
            attn_rows.receive(step)
            if layer:

                @pl.when(step == 3)
                def _():
                    send_outs(layer - 1)

            unit = jnp.where(step < 2, step, 5 - step)
            rows = span(unit * unit_rows, unit_rows)
            grad_out = dot(fbuf[rows, :], wout[...], NT).astype(BF)
            queries = qb[rows, :]
            grad_queries = jnp.zeros((unit_rows, 256), F32)
            chunk = lax.broadcasted_iota(jnp.int32, (8, 1, unit_rows), 0)
            part = lax.broadcasted_iota(jnp.int32, (8, 1, unit_rows), 2) // half
            neg = apart(owner(chunk), unit_owner(unit, part), packed.reshape(1, 1, 1))
            for head in range(heads):
                place = pl.ds(head * unit_rows, unit_rows)
                masked = keep_head(queries, head, True)
                masked_out = keep_head(grad_out, head, False)
                qmask[place, :] = masked
                domask[place, :] = masked_out
                scores = dot(kb[...], masked, NT).reshape(8, half, unit_rows)
                shares = jnp.exp(scores - (lse[unit, head : head + 1, :] - neg))
                shares = shares.reshape(8 * half, unit_rows)
                grad_shares = dot(vb[...], masked_out, NT)
                centre = jnp.sum(shares * grad_shares, axis=0, keepdims=True)
                grad_scores = (shares * (grad_shares - centre)).astype(BF)
                pb[:, place] = shares.astype(BF)
                dsb[:, place] = grad_scores
                grad_queries = grad_queries + dot(grad_scores, keep_head(kb[...], head, True), TN)
            dkb[...] += dot(dsb[...], qmask[...])
            dvb[...] += dot(pb[...], domask[...])
            low, high = turn_back(grad_queries, rows, HD**-0.5)
            dqk[rows, :128] = low
            dqk[rows, 128:256] = high
            return carry

        lax.fori_loop(0, 4, attend, 0)
        loads.start(layer - 1, "wout", "q", "k", "v", "lse")
        event("down", layer + 1, "end")
        event("attn", layer + 1, "end")
        event("up", layer, "middle")
        loads.wait(layer, "wq", "wk", "wv")
        load_turned(wq, wk, wqk)

        def spread(step, carry):
            unit = jnp.where(step < 2, 3 - step, step - 2)
            rows = span(unit * unit_rows, unit_rows)
            low, high = turn_back(dkb[rows, :], rows, 1.0)
            dqk[rows, 256:384] = low
            dqk[rows, 384:512] = high
            values = dvb[rows, :].astype(BF)
            dvv[rows, :] = values
            total[...] = dot(dqk[rows, :], wqk[...]) + dot(values, wv[...])
            attn_sum.send(unit, total)
            return carry

        lax.fori_loop(0, 4, spread, 0)
        loads.start(layer - 1, "wq", "wk", "wv")
        if layer:
            event("down", layer, "middle")
        loads.wait(layer, "a")
        out_loads[layer][0].wait()
        for each in out_sends[layer]:
            each.wait()
        ob = outs[layer][0]
        places = (
            turned_place(columns, 0, 4 * columns),
            turned_place(columns, columns, 4 * columns),
            plain_place(columns, 2 * columns, 4 * columns),
            plain_place(columns, 3 * columns, 4 * columns),
        )

        def attn_tile(index, carry):
            place = span(index * 256, 256)
            normed = abuf[:, place]
            both = dot(normed, dqk[...], TN).astype(BF)
            made = dot(both[:, :256], places[0]) + dot(both[:, 256:], places[1])
            made = made + dot(dot(normed, dvv[...], TN).astype(BF), places[2])
            outs = dot(fbuf[:, place], ob[...], TN).astype(BF)
            attn_grads[place, :] = (made + dot(outs, places[3])).astype(BF)
            return carry

        lax.fori_loop(0, tiles, attn_tile, 0)
        loads.start(layer - 1, "a")
        if layer:
            event("attn", layer, "start")
        if not deep:
            stores = [
                pltpu.make_async_copy(attn_grads, attn_outs[layer], store_sems.at[0]),
                pltpu.make_async_copy(feed_grads, feed_outs[layer], store_sems.at[1]),
            ]
            for each in stores:
                each.start()
            for each in stores:
                each.wait()
        if layer < top:
            feed_rows.finish()
        feed_sum.finish()
        loads.wait(layer, "x")
        gain_sum = jnp.zeros((1, width), F32)
        bias_sum = jnp.zeros((1, width), F32)
        for part in range(2):
            rows = pl.ds(part * half, half)
            grad = attn_sum.collect(part)
            hat, rstd = norm(xb[rows, :])
            gain_sum += jnp.sum(grad * hat, axis=0, keepdims=True)
            bias_sum += jnp.sum(grad, axis=0, keepdims=True)
            made = dx1[rows, :] + norm_back(
                grad * gain_ref[layer : layer + 1, :], hat, rstd
            )
            dxb[rows, :] = made
            if layer:
                ebuf[feed_rows.own(part), :] = made.astype(BF)
                feed_rows.send(part)
        note(2, gain_sum)
        note(3, bias_sum)
        loads.start(layer - 1, "x")
    out_ref[...] = dxb[...]
    if deep:
        for each in joined_loads:
            each.wait()
        tail(deep, spot, ids, sums, dxb, small_ref, temb_ref, work, dsb, tail_refs,
             sum_ref, vec_ref, store_sems)
    attn_rows.finish()
    attn_sum.finish()


def tail(deep, spot, ids, sums, dxb, small_ref, temb_ref, work, dsb, scratch, sum_ref, vec_ref,
         store_sems):
    (joined, ebuf, jbuf, near_in, next_in, z_in, result, vecs, send, recv) = scratch
    sibling, far = ids
    place = lax.axis_index("tensor")
    core = lax.rem(place, 2)
    y = place // 2
    x, z = spot.x, spot.z
    width = dxb.shape[1]
    ladder = Ladder((send, recv))
    ebuf[0] = dxb[...].astype(BF)
    rows_copy = ladder.copy(ebuf.at[0], ebuf.at[1], sibling)
    joined_copy = ladder.copy(joined.at[1 - core], jbuf, sibling)
    mine = vecs.at[core, y, x, z]
    row = lax.broadcasted_iota(jnp.int32, small_ref.shape, 0)
    mine[...] = jnp.where(row == 5, temb_ref[0:1, :], small_ref[...]).astype(BF)
    vec_z = [ladder.copy(mine, mine, spot.along(ahead)) for ahead in range(1, deep)]
    rows_copy.wait_recv()
    joined_copy.wait_recv()
    rest = width // 2

    def tile(index, carry):
        rows = span(index * 256, 256)
        made = dot(joined[core, :, rows], ebuf[0], TN)
        work[rows, :] = made + dot(jbuf[:, rows], ebuf[1], TN)
        return carry

    lax.fori_loop(0, width // 256, tile, 0)
    half, quarter = width // 2, width // 4
    piece = quarter // deep
    ways = (((far, y), (spot.across, x)), ((spot.across, x), (far, y)))
    lanes = (pl.ds(0, rest), pl.ds(rest, rest))
    firsts = []
    for side, ((device, bit), _) in enumerate(ways):
        out = dsb.at[pl.ds(0, half), lanes[side]]
        out[...] = work[span((1 - bit) * half, half), lanes[side]].astype(BF)
        firsts.append(ladder.copy(out, near_in.at[side], device))
    sums["down", 0].middle()
    for each in vec_z:
        each.wait_recv()
    row_z = vecs.at[core, y, x]
    vec_x = ladder.copy(row_z, row_z, spot.across)
    seconds = []
    for side, ((_, bit), (device, bit2)) in enumerate(ways):
        firsts[side].wait_recv()
        kept = work.at[span(bit * half, half), lanes[side]]
        kept[...] = kept[...] + near_in[side].astype(F32)
        out = dsb.at[pl.ds(half, quarter), lanes[side]]
        out[...] = work[span(bit * half + (1 - bit2) * quarter, quarter), lanes[side]].astype(BF)
        seconds.append(ladder.copy(out, next_in.at[side], device))
    sums["attn", 0].start()
    vec_x.wait_recv()
    plane = vecs.at[core, y]
    vec_y = ladder.copy(plane, plane, far)
    thirds = []
    for side, ((_, bit), (_, bit2)) in enumerate(ways):
        seconds[side].wait_recv()
        kept = work.at[span(bit * half + bit2 * quarter, quarter), lanes[side]]
        kept[...] = kept[...] + next_in[side].astype(F32)
        out = dsb.at[pl.ds(half + quarter, quarter), lanes[side]]
        out[...] = kept[...].astype(BF)
        for ahead in range(1, deep):
            start = half + quarter + spot.level(ahead) * piece
            thirds.append(
                ladder.copy(
                    dsb.at[span(start, piece), lanes[side]],
                    z_in.at[side, ahead - 1],
                    spot.along(ahead),
                )
            )
    sums["up", 0].end()
    sums["down", 0].end()
    vec_y.wait_recv()
    every = vecs.at[core]
    vec_core = ladder.copy(every, every, sibling)
    lasts = []
    for side, ((_, bit), (_, bit2)) in enumerate(ways):
        for ahead in range(1, deep):
            thirds[side * (deep - 1) + ahead - 1].wait_recv()
        start = bit * half + bit2 * quarter + z * piece
        made = work[span(start, piece), lanes[side]]
        for ahead in range(1, deep):
            made = made + z_in[side, ahead - 1].astype(F32)
        own = result.at[core, side, span(start, piece)]
        own[...] = made.astype(BF)
        lasts += [ladder.copy(own, own, spot.along(ahead)) for ahead in range(1, deep)]
    backs = []
    for side, ((_, bit), (device, bit2)) in enumerate(ways):
        for ahead in range(1, deep):
            lasts[side * (deep - 1) + ahead - 1].wait_recv()
        own = result.at[core, side, span(bit * half + bit2 * quarter, quarter)]
        backs.append(ladder.copy(own, own, device))
    sums["attn", 0].middle()
    ends = []
    for side, ((device, bit), _) in enumerate(ways):
        backs[side].wait_recv()
        own = result.at[core, side, span(bit * half, half)]
        ends.append(ladder.copy(own, own, device))
    sums["attn", 0].end()
    vec_core.wait_recv()
    vec_store = pltpu.make_async_copy(vecs, vec_ref, store_sems.at[0])
    vec_store.start()
    for each in ends:
        each.wait_recv()
    whole = ladder.copy(result.at[core], result.at[core], sibling)
    whole.wait_recv()
    sum_store = pltpu.make_async_copy(result, sum_ref, store_sems.at[1])
    sum_store.start()
    ladder.finish()
    vec_store.wait()
    sum_store.wait()


def backward(heads, deep, cotangent, grad_all, gains, lengths, tables, weights, kept, joined):
    depth = len(kept)
    block, width = cotangent.shape
    length = 4 * block
    units = weights[2].shape[2]
    columns = heads * HD
    part = width // (2 * deep) if deep else width
    half, quarter = width // 2, width // 4
    held = [[each[name] for name in SAVED] for each in kept]
    scratch = [pltpu.SemaphoreType.DMA((3, 2))] * 8
    scratch += [pltpu.SemaphoreType.DMA((7 + len(SAVED),)), pltpu.SemaphoreType.DMA((2,))]
    scratch += [pltpu.SemaphoreType.DMA((depth, 6))]
    scratch += [pltpu.VMEM((columns, width), BF)] * 3
    scratch += [pltpu.VMEM(each.shape[1:], BF) for each in weights[1:4]]
    for name, each in zip(SAVED, held[0]):
        shape = (length, units) if name in ("g", "slope") else each.shape
        scratch.append(pltpu.VMEM((16, 128) if name in ("o", "o2") else shape, each.dtype))
    scratch += [pltpu.VMEM((length, columns), BF), pltpu.VMEM((length // 2, columns), BF)] * depth
    scratch += [pltpu.VMEM((length, width), BF)] * 2
    scratch += scatter_scratch(length, width) + scatter_scratch(length, width)
    scratch += [
        pltpu.VMEM((512, width), BF),
        pltpu.VMEM((length, units), BF),
        pltpu.VMEM((heads * block, 256), BF),
        pltpu.VMEM((heads * block, columns), BF),
        pltpu.VMEM((length, heads * block), BF),
        pltpu.VMEM((length, heads * block), BF),
        pltpu.VMEM((length, 256), F32),
        pltpu.VMEM((length, columns), F32),
        pltpu.VMEM((length, 512), BF),
        pltpu.VMEM((length, columns), BF),
        pltpu.VMEM((3 * block, width), F32),
        pltpu.VMEM((block, width), F32),
        pltpu.VMEM((2, width, units), BF),
        pltpu.VMEM((width, 4 * columns), BF),
    ]
    out_shape = [
        jax.ShapeDtypeStruct((block, width), F32),
        jax.ShapeDtypeStruct((8 * depth, width), F32),
    ]
    kind = F32 if deep else BF
    out_shape += [jax.ShapeDtypeStruct((part, 4 * columns), kind)] * depth
    out_shape += [jax.ShapeDtypeStruct((2, part, units), kind)] * depth
    out_specs = [vmem_spec()] * 2 + [vmem_spec() if deep else any_spec()] * (2 * depth)
    if deep:
        for _ in range(depth):
            scratch += DpSum.scratch(deep, part, units) + DpSum.scratch(deep, part, units)
            scratch += DpSum.scratch(deep, part, 4 * columns)
        vec_shape = (2, 2, 2, deep, 8 * depth, width)
        scratch += [
            pltpu.VMEM((2, block, width), BF),
            pltpu.VMEM((2, block, width), BF),
            pltpu.VMEM((block, width), BF),
            pltpu.VMEM((2, half, half), BF),
            pltpu.VMEM((2, quarter, half), BF),
            pltpu.VMEM((2, deep - 1, quarter // deep, half), BF),
            pltpu.VMEM((2, 2, width, half), BF),
            pltpu.VMEM(vec_shape, BF),
            pltpu.SemaphoreType.DMA((LADDER_COPIES,)),
            pltpu.SemaphoreType.DMA((LADDER_COPIES,)),
        ]
        out_shape += [
            jax.ShapeDtypeStruct((2, 2, width, half), BF),
            jax.ShapeDtypeStruct(vec_shape, BF),
        ]
        out_specs += [any_spec(), any_spec()]

    def kernel(*refs):
        backward_kernel(depth, heads, deep, refs)

    operands = [cotangent, gains, lengths, *tables]
    in_specs = [vmem_spec()] * len(operands)
    remote = [*joined, grad_all, *weights, *[each for layer in held for each in layer]]
    in_specs += [any_spec()] * len(remote)
    return pl.pallas_call(
        kernel,
        out_shape=out_shape,
        in_specs=in_specs,
        out_specs=out_specs,
        scratch_shapes=scratch,
        compiler_params=pltpu.CompilerParams(
            collective_id=9, has_side_effects=True, vmem_limit_bytes=LIMIT
        ),
        name="layers_backward",
    )(*operands, *remote)


def finish_kernel(depth, refs):
    (low_ref, wself_ref, sum_ref, vec_ref) = refs[:4]
    attn_refs = refs[4 : 4 + depth]
    feed_refs = refs[4 + depth : 4 + 2 * depth]
    (tokens_ref, gain_ref, bias_ref, bada_ref, bdown_ref) = refs[4 + 2 * depth : 9 + 2 * depth]
    (qkv_ref, out_ref, ada_ref, up_ref, down_ref, self_ref, picked) = refs[9 + 2 * depth :]
    step = pl.program_id(0)
    members = vec_ref.shape[0] // (8 * depth)
    width = vec_ref.shape[1]

    def pick(row):
        device = lax.broadcasted_iota(jnp.int32, (members, vec_ref.shape[0]), 0)
        column = lax.broadcasted_iota(jnp.int32, (members, vec_ref.shape[0]), 1)
        wanted = (column == device * 8 * depth + row).astype(F32).astype(BF)
        return dot(wanted, vec_ref[...]).astype(BF)

    rows = ada_ref.shape[1]

    @pl.when(step == 0)
    def _():
        picked[2 * depth] = pick(5)
        for layer in range(depth):
            for place in range(2):
                picked[2 * layer + place] = pick(8 * layer + place)

    device = lax.broadcasted_iota(jnp.int32, (width, rows), 0)
    column = lax.broadcasted_iota(jnp.int32, (width, rows), 1)
    chosen = (device == column + step * rows).astype(F32).astype(BF)
    times = dot(picked[2 * depth], chosen).astype(BF)
    for layer in range(depth):
        for place in range(2):
            ada_ref[layer, :, place * width : (place + 1) * width] = dot(
                times, picked[2 * layer + place], TN
            )
    self_ref[:, : width // 2] = sum_ref[0].astype(F32)
    self_ref[:, width // 2 :] = sum_ref[1].astype(F32)

    @pl.when(step == 0)
    def _():
        row = lax.broadcasted_iota(jnp.int32, (8 * depth, vec_ref.shape[0]), 0)
        column = lax.broadcasted_iota(jnp.int32, (8 * depth, vec_ref.shape[0]), 1)
        ones = (column % (8 * depth) == row).astype(F32).astype(BF)
        totals = dot(ones, vec_ref[...])
        for layer in range(depth):
            here = slice(layer, layer + 1)
            base = 8 * layer
            bada_ref[here, :width] = totals[base : base + 1]
            bada_ref[here, width:] = totals[base + 1 : base + 2]
            gain_ref[here, :] = totals[base + 2 : base + 3]
            bias_ref[here, :] = totals[base + 3 : base + 4]
            bdown_ref[here, :] = totals[base + 4 : base + 5]

    @pl.when(step == 1)
    def _():
        tokens_ref[...] = dot(low_ref[...].astype(BF), wself_ref[...], NT)

    @pl.when(step == 2)
    def _():
        for layer in range(depth):
            grads = attn_refs[layer][...]
            columns = grads.shape[1] // 4
            for place in range(3):
                qkv_ref[layer, place] = grads[:, place * columns : (place + 1) * columns]
            out_ref[layer] = grads[:, 3 * columns :].T

    @pl.when(step == 3)
    def _():
        for layer in range(depth):
            up_ref[layer] = feed_refs[layer][0]
            down_ref[layer] = feed_refs[layer][1]


def finish(depth, low, w_self, sums, vectors, attn_shards, feed_shards):
    block, width = low.shape
    part, columns = attn_shards[0].shape
    columns //= 4
    units = feed_shards[0].shape[2]
    steps = 4
    rows = 2 * width // steps

    def fixed(*shape):
        return pl.BlockSpec(shape, lambda step: (0,) * len(shape))

    def kernel(*refs):
        finish_kernel(depth, refs)

    fixed_shapes = [
        (block, width),
        (depth, width),
        (depth, width),
        (depth, 2 * width),
        (depth, width),
        (depth, 3, part, columns),
        (depth, columns, part),
    ]
    shard = (depth, part, units)
    return pl.pallas_call(
        kernel,
        grid=(steps,),
        out_shape=[
            *[jax.ShapeDtypeStruct(each, F32) for each in fixed_shapes],
            jax.ShapeDtypeStruct((depth, width, 2 * width), F32),
            jax.ShapeDtypeStruct(shard, F32),
            jax.ShapeDtypeStruct(shard, F32),
            jax.ShapeDtypeStruct((2 * width, width), F32),
        ],
        in_specs=[
            fixed(block, width),
            fixed(width, width),
            pl.BlockSpec((None, 2, rows, width // 2), lambda step: (step // 2, 0, step % 2, 0)),
            fixed(*vectors.shape),
            *[fixed(*each.shape) for each in attn_shards],
            *[fixed(*each.shape) for each in feed_shards],
        ],
        out_specs=[
            *[fixed(*each) for each in fixed_shapes],
            pl.BlockSpec((depth, width // steps, 2 * width), lambda step: (0, step, 0)),
            fixed(*shard),
            fixed(*shard),
            pl.BlockSpec((rows, width), lambda step: (step, 0)),
        ],
        scratch_shapes=[
            pltpu.VMEM((2 * depth + 1, vectors.shape[0] // (8 * depth), width), BF)
        ],
        compiler_params=pltpu.CompilerParams(vmem_limit_bytes=LIMIT),
        name="write_grads",
    )(low, w_self, sums, vectors, *attn_shards, *feed_shards)


def local(
    tokens,
    cotangent,
    lengths,
    timesteps,
    w_self,
    ln_gain,
    ln_bias,
    w_qkv,
    w_out,
    w_ada,
    b_ada,
    w_up,
    w_down,
    b_down,
):
    width = tokens.shape[1]
    depth = w_qkv.shape[0]
    heads = w_qkv.shape[3] // HD
    deep = 4 if lax.axis_size("dp") == 8 else 0
    weights = (jnp.swapaxes(w_qkv, 2, 3), w_out, w_up, w_down, w_ada)
    vectors = (ln_gain, ln_bias, b_down, b_ada, lengths, timesteps)
    made, kept = forward(heads, tokens, cotangent, w_self, vectors, weights)
    (activations, estimate, conds, cosine, sine, temb, grad_all) = made
    made = backward(
        heads,
        deep,
        cotangent,
        grad_all,
        ln_gain,
        lengths,
        (cosine, sine, temb, conds),
        weights,
        kept,
        (tokens, estimate),
    )
    grad_rows, smalls = made[:2]
    attn_shards = made[2 : 2 + depth]
    feed_shards = made[2 + depth : 2 + 2 * depth]
    if deep:
        sums, vectors = made[2 + 2 * depth :]
        vectors = vectors.reshape(-1, width)
    else:
        attn_shards = [
            lax.psum_scatter(each, "dp", scatter_dimension=0, tiled=True).astype(F32)
            for each in attn_shards
        ]
        feed_shards = [
            lax.psum_scatter(each, "dp", scatter_dimension=1, tiled=True).astype(F32)
            for each in feed_shards
        ]
        joined = jnp.concatenate([tokens, estimate], axis=1)
        sums = lax.psum(dot(joined, grad_rows.astype(BF), TN).astype(BF), ("dp", "tensor"))
        sums = sums.reshape(2, width, 2, width // 2).swapaxes(1, 2)
        vectors = smalls.at[5].set(temb[0]).astype(BF)
        vectors = lax.all_gather(vectors, ("dp", "tensor"), axis=0, tiled=True)
    made = finish(depth, grad_rows, w_self, sums, vectors, attn_shards, feed_shards)
    (grad_tokens, gain, bias, bias_ada, bias_down, qkv, out, ada, up, down, own) = made
    return (
        activations,
        grad_tokens,
        gain,
        bias,
        qkv,
        out,
        ada,
        bias_ada,
        up,
        jnp.swapaxes(down, 1, 2),
        bias_down,
        own,
    )


def solution(mesh):
    return jax.shard_map(
        local,
        mesh=mesh,
        in_specs=(
            P(("dp", "tensor"), None),
            P(("dp", "tensor"), None),
            P("dp", None),
            P("dp", None),
            P(),
            P(),
            P(),
            P(None, None, None, "tensor"),
            P(None, "tensor", None),
            P(),
            P(),
            P(None, None, "tensor"),
            P(None, "tensor", None),
            P(),
        ),
        out_specs=(
            P(("dp", "tensor"), None),
            P(("dp", "tensor"), None),
            P(),
            P(),
            P(None, None, "dp", "tensor"),
            P(None, "tensor", "dp"),
            P(),
            P(),
            P(None, "dp", "tensor"),
            P(None, "tensor", "dp"),
            P(),
            P(),
        ),
        check_vma=False,
    )
```
